32 devices in a mesh: stream: 4 (over z), radial: 4 (over y, core), snap: 2 (over x).
Axes of the slice: x: 2, y: 2, z: 4, core: 2. Of those that a mesh axis runs over, the one named last changes fastest.
Arguments:
- fields: bfloat16 [2, 8, 32, 32, 128], P('snap', None, 'stream', 'radial'), may hold values from -6 to 6
- first_weight: bfloat16 [27, 16, 8], replicated, may hold values from -0.4375 to 0.4375
- first_bias: float32 [16], replicated, may hold values from -3 to 3
- second_weight: bfloat16 [27, 16, 16], replicated, may hold values from -0.3125 to 0.3125
- second_bias: float32 [16], replicated, may hold values from -3 to 3
- cotangent: bfloat16 [2, 16, 32, 32, 128], P('snap', None, 'stream', 'radial'), may hold values from -6 to 6
Outputs:
- closure: bfloat16 [2, 16, 32, 32, 128], P('snap', None, 'stream', 'radial')
- first_grad: float32 [27, 16, 8], replicated
- second_grad: float32 [27, 16, 16], replicated
- bias_grad: float32 [16], replicated
The draws below stay inside these ranges and needn't reach their ends.
All inputs are finite; a program needn't handle non-finite values.
Results may differ from the reference program's by a relative error of at most 0.017.
Values may be sent and summed in bfloat16 or wider, within the bound.
No kernel may reach another device: no remote copies, remote signals or barrier semaphores. Data moves between devices by JAX's collectives and lax.ppermute only.
A program may use at most 128 MiB of HBM per device.

```python
import jax
import jax.numpy as jnp
from jax import lax

CIN = 8
CH = 16
TAPS = 27
NZ = 128
SNAPS = 2
NX = 32
NY = 32


def levels(key, extent, pieces, low, high):
    def one(position, blocks):
        draws = jax.random.uniform(jax.random.fold_in(jax.random.fold_in(key, 6), position), (blocks,), jnp.float32, low / len(pieces), high / len(pieces))
        return jnp.repeat(jnp.exp(draws), extent[position] // blocks).reshape((-1,) + (1,) * (len(extent) - position - 1))

    level = one(*pieces[0])
    for cut in pieces[1:]:
        level = level * one(*cut)
    return level


def bell_draw(rng, extent, width, reach, shards=(), held_as=jnp.bfloat16):
    values = width * jax.random.normal(rng, extent, jnp.float32)
    if shards:
        values = values * levels(rng, extent, shards, -0.22, 0.18)
    return jnp.clip(values, -reach, reach).astype(held_as)


def setup_inputs(seed: int = 0) -> dict:
    seeds = jax.random.split(jax.random.key(seed), 7)
    fields = bell_draw(seeds[0], (SNAPS, CIN, NX, NY, NZ), 1.0, 6.0, ((0, 2), (2, 4), (3, 4)))
    first_weight = bell_draw(seeds[1], (TAPS, CH, CIN), (TAPS * CIN) ** -0.5, 0.4375)
    first_bias = bell_draw(seeds[2], (CH,), 0.6, 3.0, (), jnp.float32)
    second_weight = bell_draw(seeds[3], (TAPS, CH, CH), (TAPS * CH) ** -0.5, 0.3125)
    second_bias = bell_draw(seeds[4], (CH,), 0.6, 3.0, (), jnp.float32)
    cotangent = bell_draw(seeds[5], (SNAPS, CH, NX, NY, NZ), 1.0, 6.0, ((0, 2), (2, 4), (3, 4)))
    return dict(fields=fields, first_weight=first_weight, first_bias=first_bias, second_weight=second_weight, second_bias=second_bias, cotangent=cotangent)


stencil_taps = [(step_x, step_y, step_z) for step_x in (-1, 0, 1) for step_y in (-1, 0, 1) for step_z in (-1, 0, 1)]

def window(padded, offsets, sign, sizes):
    starts = [2 + 2 * sign * offset for offset in offsets]
    return padded[:, starts[0]:starts[0] + sizes[0], starts[1]:starts[1] + sizes[1], starts[2]:starts[2] + sizes[2]]

def pad_cells(field):
    return jnp.pad(field, ((0, 0), (2, 2), (2, 2), (2, 2)))

def convolve(padded, weight, sizes):
    total = jnp.zeros((weight.shape[1],) + sizes, jnp.float32)
    for number, offsets in enumerate(stencil_taps):
        piece = window(padded, offsets, 1, sizes).astype(jnp.float32)
        total = total + jnp.einsum('oi,ixyz->oxyz', weight[number].astype(jnp.float32), piece)
    return total

def gelu_slope(value):
    return 0.5 * (1.0 + lax.erf(value * 0.7071067811865476)) + value * jnp.exp(-0.5 * value * value) * 0.3989422804014327

def reference(fields, first_weight, first_bias, second_weight, second_bias, cotangent):
    sizes = (NX, NY, NZ)

    def one_snapshot(pair):
        inputs, upstream = pair
        padded_in = pad_cells(inputs)
        pre = convolve(padded_in, first_weight, sizes) + first_bias[:, None, None, None]
        hidden = jax.nn.gelu(pre, approximate=False).astype(jnp.bfloat16)
        padded_hidden = pad_cells(hidden)
        closure = (convolve(padded_hidden, second_weight, sizes) + second_bias[:, None, None, None]).astype(jnp.bfloat16)
        upstream_f = upstream.astype(jnp.float32)
        padded_up = pad_cells(upstream)
        back = jnp.zeros((CH,) + sizes, jnp.float32)
        second_terms = []
        for number, offsets in enumerate(stencil_taps):
            shifted = window(padded_hidden, offsets, 1, sizes).astype(jnp.float32)
            second_terms.append(jnp.einsum('oxyz,ixyz->oi', upstream_f, shifted))
            earlier = window(padded_up, offsets, -1, sizes).astype(jnp.float32)
            back = back + jnp.einsum('oi,oxyz->ixyz', second_weight[number].astype(jnp.float32), earlier)
        dpre = (back * gelu_slope(pre)).astype(jnp.bfloat16)
        dpre_f = dpre.astype(jnp.float32)
        first_terms = []
        for number, offsets in enumerate(stencil_taps):
            shifted = window(padded_in, offsets, 1, sizes).astype(jnp.float32)
            first_terms.append(jnp.einsum('oxyz,ixyz->oi', dpre_f, shifted))
        bias_term = lax.optimization_barrier(jnp.sum(dpre_f, axis=(1, 2, 3)))
        return (closure, jnp.stack(first_terms), jnp.stack(second_terms), bias_term)
    closure, first_all, second_all, bias_all = lax.map(one_snapshot, (fields, cotangent))
    norm = 1.0 / jnp.sqrt(jnp.float32(SNAPS * NX * NY * NZ))
    return (closure, lax.optimization_barrier(jnp.sum(first_all, axis=0)) * norm, lax.optimization_barrier(jnp.sum(second_all, axis=0)) * norm, lax.optimization_barrier(jnp.sum(bias_all, axis=0)) * norm)
```

```python
import functools

import numpy as np
import jax
import jax.numpy as jnp
from jax import lax
from jax.experimental import pallas as pl
from jax.experimental.pallas import tpu as pltpu
from jax.sharding import PartitionSpec as P

F32 = jnp.float32
BF16 = jnp.bfloat16
YB = 8
Z = 128
CI = 8
CH = 16
FR = CI * 16
HR = 256


def lane_rows():
    one = np.concatenate([np.tile(np.arange(8), CI), np.tile(np.arange(-4, 0), CI), np.tile(np.arange(8, 12), CI)])
    chan = np.concatenate([np.repeat(np.arange(CI), 8), np.repeat(np.arange(CI), 4), np.repeat(np.arange(CI), 4)])
    y1 = np.tile(one, 3)
    e1 = np.zeros((3 * CI, 3 * FR), np.float32)
    for c in range(3):
        e1[c * CI + chan, c * FR + np.arange(FR)] = 1
    halo_y = np.concatenate([np.tile([-2, -1], CH), np.tile([8, 9], CH)])
    halo_c = np.concatenate([np.repeat(np.arange(CH), 2)] * 2)
    y2 = np.concatenate([np.tile(np.tile(np.arange(8), CH), 3), np.tile(halo_y, 3), np.full(64, 100)])
    e2 = np.zeros((3 * CH, 640), np.float32)
    for c in range(3):
        e2[c * CH + np.repeat(np.arange(CH), 8), c * 128 + np.arange(128)] = 1
        e2[c * CH + halo_c, 384 + c * 64 + np.arange(64)] = 1
    rows_y = np.concatenate([np.tile(np.arange(8), CH), halo_y])
    rows_c = np.concatenate([np.repeat(np.arange(CH), 8), halo_c])
    expand = np.zeros((192, CH), np.float32)
    expand[np.arange(192), rows_c] = 1
    return e1, y1, e2, y2, rows_y, expand


def pick_rows():
    pick = np.zeros((128, 192), np.float32)
    row = 0
    for base in (0, 4):
        for ch in range(CI):
            for y in range(4):
                pick[row, ch * 8 + base + y] = 1
                row += 1
        for ch in range(CH):
            for y in range(2):
                pick[row, 64 + ch * 8 + (0 if base == 0 else 6) + y] = 1
                row += 1
    return pick


def plane(ref, x):
    v = ref[0, :, x].astype(F32)
    return v.reshape(v.shape[0] * v.shape[1], v.shape[2])


def pack_kernel(fields, cot, pick, low, high):
    for x in range(fields.shape[2]):
        rows = jnp.concatenate([plane(fields, x), plane(cot, x)], axis=0).astype(BF16)
        got = jnp.dot(pick[...], rows, preferred_element_type=F32).astype(BF16)
        low[x] = got[:64]
        high[x] = got[64:]


def band_kernel(w1, w2, wb, e1, e2, expand, y1, y2, rows_y, t1, t2, tb):
    ry = rows_y[...]
    for w, e, ys, t, rows in ((w1, e1, y1, t1, 192), (w2, e2, y2, t2, 128), (wb, e2, y2, tb, 128)):
        width = e.shape[1]
        wide = jnp.dot(w[...], e[...], preferred_element_type=F32).astype(BF16)
        for a in range(3):
            total = jnp.zeros((rows, width), F32)
            for b in range(3):
                part = jnp.dot(expand[:rows], wide[(a * 3 + b) * CH:(a * 3 + b + 1) * CH], preferred_element_type=F32)
                total = jnp.where(ys[...] == ry[:rows] + float(2 * (b - 1)), part, total)
            t[:, a * width:(a + 1) * width] = total.astype(BF16)


def shifted(v):
    lane = lax.broadcasted_iota(jnp.int32, v.shape, 1)
    before = jnp.where(lane >= 2, pltpu.roll(v, 2, 1), 0.0)
    after = jnp.where(lane < Z - 2, pltpu.roll(v, Z - 2, 1), 0.0)
    return before.astype(BF16), v.astype(BF16), after.astype(BF16)


def store_wide(ref, pair, side, v):
    at = slice(side * Z, (side + 1) * Z)
    for c, piece in enumerate(shifted(v)):
        base = pair * 640
        ref[base + c * 128:base + (c + 1) * 128, at] = piece[:128]
        ref[base + 384 + c * 64:base + 384 + (c + 1) * 64, at] = piece[128:]


def main_kernel(counts, fields, cot, rlo, rhi, xlo, xhi, t1, t2, tb, b1, b2, e1t, e2t, y1, y2, yo,
                closure, payload, fs, hs, cs, slope):
    stream, radial = lax.axis_index("stream"), lax.axis_index("radial")
    zeros = jnp.zeros((64, 256), BF16)
    for pair in range(6):
        hs[pair * 640 + 576:(pair + 1) * 640] = zeros
        cs[pair * 640 + 576:(pair + 1) * 640] = zeros
    for p in range(16):
        x = p - 4
        if x < 0:
            v = xlo[p * 128:(p + 1) * 128].astype(F32)
        elif x >= 8:
            v = xhi[(x - 8) * 128:(x - 7) * 128].astype(F32)
        else:
            v = jnp.concatenate([plane(fields, x), rlo[x, :32].astype(F32), rhi[x, :32].astype(F32)], axis=0)
        at = slice((p % 2) * Z, (p % 2 + 1) * Z)
        for c, piece in enumerate(shifted(v)):
            fs[(p // 2) * 384 + c * 128:(p // 2) * 384 + (c + 1) * 128, at] = piece
    for p in range(12):
        x = p - 2
        if x < 0:
            v = xlo[512 + p * 192:512 + (p + 1) * 192].astype(F32)
        elif x >= 8:
            v = xhi[512 + (x - 8) * 192:512 + (x - 7) * 192].astype(F32)
        else:
            v = jnp.concatenate([plane(cot, x), rlo[x, 32:].astype(F32), rhi[x, 32:].astype(F32)], axis=0)
        store_wide(cs, p // 2, p % 2, v)
    keep_low = jnp.where(radial > 0, 1.0, 0.0)
    keep_high = jnp.where(radial < counts[1] - 1, 1.0, 0.0)
    keep_first = jnp.where(stream > 0, 1.0, 0.0)
    keep_last = jnp.where(stream < counts[0] - 1, 1.0, 0.0)
    for k in range(6):
        pre = jnp.dot(t1[...], fs[k * 384:(k + 3) * 384], preferred_element_type=F32) + b1[...]
        phi = 0.5 * (1.0 + lax.erf(pre * 0.7071067811865476))
        hidden = pre * phi
        if 1 <= k <= 4:
            local, share = pre[:128], phi[:128]
            slope[k - 1] = share + local * jnp.exp(-0.5 * local * local) * 0.3989422804014327
        hidden = jnp.concatenate([hidden[:128], hidden[128:160] * keep_low, hidden[160:] * keep_high], axis=0)
        if k == 0:
            hidden = hidden * keep_first
        if k == 5:
            hidden = hidden * keep_last
        hidden = hidden.astype(BF16).astype(F32)
        for side in range(2):
            store_wide(hs, k, side, hidden[:, side * Z:(side + 1) * Z])
    g1 = jnp.zeros((128, 1152), F32)
    g2 = jnp.zeros((128, 1920), F32)
    bias = jnp.zeros((128, 256), F32)
    over_lanes = (((1,), (1,)), ((), ()))
    for k in range(4):
        back = jnp.dot(tb[...], cs[k * 640:(k + 3) * 640], preferred_element_type=F32)
        dpre = (back * slope[k]).astype(BF16)
        bias = bias + dpre.astype(F32)
        g1 = g1 + lax.dot_general(dpre, fs[(k + 1) * 384:(k + 4) * 384], over_lanes, preferred_element_type=F32)
        here = cs[(k + 1) * 640 + 128:(k + 1) * 640 + 256]
        g2 = g2 + lax.dot_general(here, hs[k * 640:(k + 3) * 640], over_lanes, preferred_element_type=F32)
    bias = jnp.sum(bias, axis=1, keepdims=True)
    spot = lax.broadcasted_iota(jnp.int32, (128, 128), 1) == 120
    for a in range(3):
        for b in range(3):
            off = float(2 * (b - 1))
            one = jnp.where(y1[...] == yo[...] + off, g1[:, a * 384:(a + 1) * 384], 0.0).astype(BF16)
            two = jnp.where(y2[...] == yo[...] + off, g2[:, a * 640:(a + 1) * 640], 0.0).astype(BF16)
            both = jnp.dot(one, e1t[...], preferred_element_type=F32) + jnp.dot(two, e2t[...], preferred_element_type=F32)
            if a == 0 and b == 0:
                both = jnp.where(spot, bias, both)
            payload[(a * 3 + b) * CH:(a * 3 + b + 1) * CH] = jnp.sum(both.reshape(CH, 8, 128), axis=1).astype(BF16)
    for k in range(4):
        out = (jnp.dot(t2[...], hs[k * 640:(k + 3) * 640], preferred_element_type=F32) + b2[...]).astype(BF16)
        for side in range(2):
            closure[0, :, 2 * k + side] = out[:, side * Z:(side + 1) * Z].reshape(CH, 8, Z)


def add_kernel(norm, parts, total):
    acc = parts[0].astype(F32)
    for d in range(1, parts.shape[0]):
        acc = acc + parts[d].astype(F32)
    total[...] = acc * norm


def call(kernel, outs, name, scratch=(), flops=10_000_000):
    return pl.pallas_call(
        kernel,
        out_shape=outs,
        scratch_shapes=list(scratch),
        compiler_params=pltpu.CompilerParams(vmem_limit_bytes=48 * 1024 * 1024),
        cost_estimate=pl.CostEstimate(flops=flops, bytes_accessed=1_000_000, transcendentals=0),
        name=name,
    )


def shape(*dims, dtype=BF16):
    return jax.ShapeDtypeStruct(dims, dtype)


def exchange(low, high, axis):
    count = lax.axis_size(axis)
    up = [(i, i + 1) for i in range(count - 1)]
    down = [(j, i) for i, j in up]
    return lax.ppermute(high, axis, up), lax.ppermute(low, axis, down)


def local(fields, first_weight, first_bias, second_weight, second_bias, cotangent):
    e1, y1, e2, y2, rows_y, expand = lane_rows()
    y1 = jnp.asarray(y1[None], F32)
    y2 = jnp.asarray(y2[None], F32)
    ry = jnp.asarray(rows_y[:, None], F32)
    lanes_x = fields.shape[2]
    low, high = call(pack_kernel, (shape(lanes_x, 64, Z),) * 2, "pack_strips")(fields, cotangent, jnp.asarray(pick_rows(), BF16))
    rlo, rhi = exchange(low, high, "radial")

    w1 = first_weight.reshape(3, 3, 3, CH, CI).transpose(0, 1, 3, 2, 4).reshape(9 * CH, 3 * CI)
    w2 = second_weight.reshape(3, 3, 3, CH, CH)
    wb = w2[::-1, ::-1, ::-1].transpose(0, 1, 4, 2, 3).reshape(9 * CH, 3 * CH)
    w2 = w2.transpose(0, 1, 3, 2, 4).reshape(9 * CH, 3 * CH)
    t1, t2, tb = call(band_kernel, (shape(192, 1152), shape(128, 1920), shape(128, 1920)), "band_weights")(
        w1, w2, wb, jnp.asarray(e1, BF16), jnp.asarray(e2, BF16), jnp.asarray(expand, BF16), y1, y2, ry)

    def strip(xs, qs):
        pieces = []
        for x in xs:
            pieces += [fields[0, :, x].reshape(64, Z), rlo[x, :32], rhi[x, :32]]
        for x in qs:
            pieces += [cotangent[0, :, x].reshape(128, Z), rlo[x, 32:], rhi[x, 32:]]
        return jnp.concatenate(pieces, axis=0)

    xlo, xhi = exchange(strip((0, 1, 2, 3), (0, 1)), strip((4, 5, 6, 7), (6, 7)), "stream")
    e1t = np.zeros((384, 128), np.float32)
    e1t[:, :24] = e1.T
    e2t = np.zeros((640, 128), np.float32)
    e2t[:, 64:112] = e2.T
    rows_o = np.argmax(expand, axis=1)
    b1 = first_bias[rows_o][:, None]
    b2 = second_bias[rows_o[:128]][:, None]
    counts = (lax.axis_size("stream"), lax.axis_size("radial"))
    closure, payload = call(
        functools.partial(main_kernel, counts),
        (shape(*cotangent.shape), shape(9 * CH, 128)),
        "layers",
        (
            pltpu.VMEM((8 * 384, 256), BF16),
            pltpu.VMEM((6 * 640, 256), BF16),
            pltpu.VMEM((6 * 640, 256), BF16),
            pltpu.VMEM((4, 128, 256), F32),
        ),
        flops=3_000_000_000,
    )(fields, cotangent, rlo, rhi, xlo, xhi, t1, t2, tb, b1, b2, jnp.asarray(e1t, BF16), jnp.asarray(e2t, BF16), y1, y2, ry[:128])
    parts = lax.all_gather(payload, ("stream", "radial", "snap"))
    count = fields.shape[0] * lax.axis_size("snap") * fields.shape[2] * counts[0] * fields.shape[3] * counts[1] * fields.shape[4]
    norm = float(1.0 / np.sqrt(np.float32(count)))
    total = call(functools.partial(add_kernel, norm), shape(9 * CH, 128, dtype=F32), "add_parts")(parts)
    total = total.reshape(3, 3, CH, 128)
    first = total[..., :24].reshape(3, 3, CH, 3, CI).transpose(0, 1, 3, 2, 4).reshape(27, CH, CI)
    second = total[..., 64:112].reshape(3, 3, CH, 3, CH).transpose(0, 1, 3, 2, 4).reshape(27, CH, CH)
    return (closure, first, second, total[0, 0, :, 120])


def solution(mesh):
    split = P("snap", None, "stream", "radial", None)
    return jax.shard_map(
        local,
        mesh=mesh,
        in_specs=(split, P(), P(), P(), P(), split),
        out_specs=(split, P(), P(), P()),
        check_vma=False,
    )
```

```python
import functools

import numpy as np
import jax
import jax.numpy as jnp
from jax import lax
from jax.experimental import pallas as pl
from jax.experimental.pallas import tpu as pltpu
from jax.sharding import PartitionSpec as P

F32 = jnp.float32
BF16 = jnp.bfloat16
YB = 8
Z = 128
CI = 8
CH = 16
FR = CI * 16
HR = 256


def lane_rows():
    one = np.concatenate([np.tile(np.arange(8), CI), np.tile(np.arange(-4, 0), CI), np.tile(np.arange(8, 12), CI)])
    chan = np.concatenate([np.repeat(np.arange(CI), 8), np.repeat(np.arange(CI), 4), np.repeat(np.arange(CI), 4)])
    y1 = np.tile(one, 3)
    e1 = np.zeros((3 * CI, 3 * FR), np.float32)
    for c in range(3):
        e1[c * CI + chan, c * FR + np.arange(FR)] = 1
    halo_y = np.concatenate([np.tile([-2, -1], CH), np.tile([8, 9], CH)])
    halo_c = np.concatenate([np.repeat(np.arange(CH), 2)] * 2)
    y2 = np.concatenate([np.tile(np.tile(np.arange(8), CH), 3), np.tile(halo_y, 3), np.full(64, 100)])
    e2 = np.zeros((3 * CH, 640), np.float32)
    for c in range(3):
        e2[c * CH + np.repeat(np.arange(CH), 8), c * 128 + np.arange(128)] = 1
        e2[c * CH + halo_c, 384 + c * 64 + np.arange(64)] = 1
    rows_y = np.concatenate([np.tile(np.arange(8), CH), halo_y])
    rows_c = np.concatenate([np.repeat(np.arange(CH), 8), halo_c])
    expand = np.zeros((192, CH), np.float32)
    expand[np.arange(192), rows_c] = 1
    return e1, y1, e2, y2, rows_y, expand


def plane(ref, x):
    v = ref[0, :, x].astype(F32)
    return v.reshape(v.shape[0] * v.shape[1], v.shape[2])


def pack_kernel(fields, cot, low, high, fields_here, cot_here, sems):
    copies = [
        pltpu.make_async_copy(fields, fields_here, sems.at[0]),
        pltpu.make_async_copy(cot, cot_here, sems.at[1]),
    ]
    for copy in copies:
        copy.start()
    row = lax.broadcasted_iota(jnp.int32, (128, 192), 0)
    col = lax.broadcasted_iota(jnp.int32, (128, 192), 1)
    side, q = row // 64, row % 64
    from_fields = (q // 4) * 8 + 4 * side + q % 4
    from_cot = 64 + ((q - 32) // 2) * 8 + 6 * side + q % 2
    pick = jnp.where(col == jnp.where(q < 32, from_fields, from_cot), 1.0, 0.0).astype(BF16)
    for copy in copies:
        copy.wait()
    for x in range(fields.shape[2]):
        rows = jnp.concatenate([plane(fields_here, x), plane(cot_here, x)], axis=0).astype(BF16)
        got = jnp.dot(pick, rows, preferred_element_type=F32).astype(BF16)
        low[x] = got[:64]
        high[x] = got[64:]


def join_kernel(fields, cot, rlo, rhi, low, high):
    for out, xs, qs in ((low, (0, 1, 2, 3), (0, 1)), (high, (4, 5, 6, 7), (6, 7))):
        for n, x in enumerate(xs):
            out[n * 128:n * 128 + 64] = plane(fields, x).astype(BF16)
            out[n * 128 + 64:n * 128 + 96] = rlo[x, :32]
            out[n * 128 + 96:n * 128 + 128] = rhi[x, :32]
        for n, x in enumerate(qs):
            base = 512 + n * 192
            out[base:base + 128] = plane(cot, x).astype(BF16)
            out[base + 128:base + 160] = rlo[x, 32:]
            out[base + 160:base + 192] = rhi[x, 32:]


def band_kernel(w1, w2, wb, e1, e2, expand, y1, y2, rows_y, first_bias, second_bias, t1, t2, tb, b1, b2):
    ry = rows_y[...]
    for w, e, ys, t, rows in ((w1, e1, y1, t1, 192), (w2, e2, y2, t2, 128), (wb, e2, y2, tb, 128)):
        width = e.shape[1]
        wide = jnp.dot(w[...], e[...], preferred_element_type=F32).astype(BF16)
        for a in range(3):
            total = jnp.zeros((rows, width), F32)
            for b in range(3):
                part = jnp.dot(expand[:rows], wide[(a * 3 + b) * CH:(a * 3 + b + 1) * CH], preferred_element_type=F32)
                total = jnp.where(ys[...] == ry[:rows] + float(2 * (b - 1)), part, total)
            t[:, a * width:(a + 1) * width] = total.astype(BF16)
    for bias, out in ((first_bias, b1), (second_bias, b2)):
        rows = out.shape[0]
        column = jnp.sum(expand[:rows].astype(F32) * bias[...], axis=1, keepdims=True)
        out[...] = jnp.broadcast_to(column, (rows, 256))


def shifted(v):
    lane = lax.broadcasted_iota(jnp.int32, v.shape, 1)
    before = jnp.where(lane >= 2, pltpu.roll(v, 2, 1), 0.0)
    after = jnp.where(lane < Z - 2, pltpu.roll(v, Z - 2, 1), 0.0)
    return before.astype(BF16), v.astype(BF16), after.astype(BF16)


def store_wide(ref, pair, side, v):
    at = slice(side * Z, (side + 1) * Z)
    for c, piece in enumerate(shifted(v)):
        base = pair * 640
        ref[base + c * 128:base + (c + 1) * 128, at] = piece[:128]
        ref[base + 384 + c * 64:base + 384 + (c + 1) * 64, at] = piece[128:]


def main_kernel(counts, fields, cot, rlo, rhi, xlo, xhi, t1, t2, tb, b1, b2, er1, er2, y1, y2, yo,
                closure, payload, fs, hs, cs, slope):
    stream, radial = lax.axis_index("stream"), lax.axis_index("radial")
    zeros = jnp.zeros((64, 256), BF16)
    for pair in range(6):
        hs[pair * 640 + 576:(pair + 1) * 640] = zeros
        cs[pair * 640 + 576:(pair + 1) * 640] = zeros
    for p in range(16):
        x = p - 4
        if x < 0:
            v = xlo[p * 128:(p + 1) * 128].astype(F32)
        elif x >= 8:
            v = xhi[(x - 8) * 128:(x - 7) * 128].astype(F32)
        else:
            v = jnp.concatenate([plane(fields, x), rlo[x, :32].astype(F32), rhi[x, :32].astype(F32)], axis=0)
        at = slice((p % 2) * Z, (p % 2 + 1) * Z)
        for c, piece in enumerate(shifted(v)):
            fs[(p // 2) * 384 + c * 128:(p // 2) * 384 + (c + 1) * 128, at] = piece
    for p in range(12):
        x = p - 2
        if x < 0:
            v = xlo[512 + p * 192:512 + (p + 1) * 192].astype(F32)
        elif x >= 8:
            v = xhi[512 + (x - 8) * 192:512 + (x - 7) * 192].astype(F32)
        else:
            v = jnp.concatenate([plane(cot, x), rlo[x, 32:].astype(F32), rhi[x, 32:].astype(F32)], axis=0)
        store_wide(cs, p // 2, p % 2, v)
    keep_low = jnp.where(radial > 0, 1.0, 0.0)
    keep_high = jnp.where(radial < counts[1] - 1, 1.0, 0.0)
    keep_first = jnp.where(stream > 0, 1.0, 0.0)
    keep_last = jnp.where(stream < counts[0] - 1, 1.0, 0.0)
    for k in range(6):
        pre = jnp.dot(t1[...], fs[k * 384:(k + 3) * 384], preferred_element_type=F32) + b1[...]
        phi = 0.5 * (1.0 + lax.erf(pre * 0.7071067811865476))
        hidden = pre * phi
        if 1 <= k <= 4:
            local, share = pre[:128], phi[:128]
            slope[k - 1] = share + local * jnp.exp(-0.5 * local * local) * 0.3989422804014327
        hidden = jnp.concatenate([hidden[:128], hidden[128:160] * keep_low, hidden[160:] * keep_high], axis=0)
        if k == 0:
            hidden = hidden * keep_first
        if k == 5:
            hidden = hidden * keep_last
        hidden = hidden.astype(BF16).astype(F32)
        for side in range(2):
            store_wide(hs, k, side, hidden[:, side * Z:(side + 1) * Z])
    g1 = jnp.zeros((128, 1152), F32)
    g2 = jnp.zeros((128, 1920), F32)
    bias = jnp.zeros((128, 256), F32)
    over_lanes = (((1,), (1,)), ((), ()))
    for k in range(4):
        back = jnp.dot(tb[...], cs[k * 640:(k + 3) * 640], preferred_element_type=F32)
        dpre = (back * slope[k]).astype(BF16)
        bias = bias + dpre.astype(F32)
        g1 = g1 + lax.dot_general(dpre, fs[(k + 1) * 384:(k + 4) * 384], over_lanes, preferred_element_type=F32)
        here = cs[(k + 1) * 640 + 128:(k + 1) * 640 + 256]
        g2 = g2 + lax.dot_general(here, hs[k * 640:(k + 3) * 640], over_lanes, preferred_element_type=F32)
    bias = jnp.sum(bias, axis=1, keepdims=True)
    lane = lax.broadcasted_iota(jnp.int32, (8, 256), 1)

    def diagonal(rows, place):
        total = jnp.zeros((8, rows.shape[1]), F32)
        for o in range(CH):
            total = jnp.where(place == o, rows[o * 8:(o + 1) * 8], total)
        return jnp.sum(total, axis=0, keepdims=True)

    payload[24:] = jnp.zeros((8, 384), F32)
    payload[27:28, :128] = diagonal(jnp.broadcast_to(bias, (128, 128)), lane[:, :128])
    for a in range(3):
        for b in range(3):
            off = float(2 * (b - 1))
            one = jnp.where(y1[...] == yo[...] + off, g1[:, a * 384:(a + 1) * 384], 0.0).astype(BF16)
            two = jnp.where(y2[...] == yo[...] + off, g2[:, a * 640:(a + 1) * 640], 0.0).astype(BF16)
            for c in range(3):
                tap = (a * 3 + b) * 3 + c
                r1 = jnp.dot(one[:, c * 128:(c + 1) * 128], er1[...], preferred_element_type=F32)
                rim = 384 + (c // 2) * 128
                both = jnp.concatenate([two[:, c * 128:(c + 1) * 128], two[:, rim:rim + 128]], axis=1)
                r2 = jnp.dot(both, er2[c % 2], preferred_element_type=F32)
                payload[tap:tap + 1, :128] = diagonal(r1, lane[:, :128] // CI)
                payload[tap:tap + 1, 128:] = diagonal(r2, lane // CH)
    for k in range(4):
        out = (jnp.dot(t2[...], hs[k * 640:(k + 3) * 640], preferred_element_type=F32) + b2[...]).astype(BF16)
        for side in range(2):
            closure[0, :, 2 * k + side] = out[:, side * Z:(side + 1) * Z].reshape(CH, 8, Z)


def finish_kernel(norm, total, first, second, bias):
    scaled = total[...] * norm
    flipped = jnp.transpose(scaled)
    first[...] = flipped[:128, :27]
    second[...] = flipped[128:, :27]
    bias[...] = scaled[27:28, :CH]


def call(kernel, outs, name, scratch=(), flops=10_000_000, **specs):
    return pl.pallas_call(
        kernel,
        out_shape=outs,
        **specs,
        scratch_shapes=list(scratch),
        compiler_params=pltpu.CompilerParams(vmem_limit_bytes=48 * 1024 * 1024),
        cost_estimate=pl.CostEstimate(flops=flops, bytes_accessed=1_000_000, transcendentals=0),
        name=name,
    )


def shape(*dims, dtype=BF16):
    return jax.ShapeDtypeStruct(dims, dtype)


def exchange(low, high, axis):
    count = lax.axis_size(axis)
    up = [(i, i + 1) for i in range(count - 1)]
    down = [(j, i) for i, j in up]
    return lax.ppermute(high, axis, up), lax.ppermute(low, axis, down)


def reduce_all(v, axes):
    for axis in axes:
        count = lax.axis_size(axis)
        step = 1
        while step < count:
            v = v + lax.ppermute(v, axis, [(i, i ^ step) for i in range(count)])
            step *= 2
    return v


def local(fields, first_weight, first_bias, second_weight, second_bias, cotangent):
    e1, y1, e2, y2, rows_y, expand = lane_rows()
    y1 = jnp.asarray(y1[None], F32)
    y2 = jnp.asarray(y2[None], F32)
    ry = jnp.asarray(rows_y[:, None], F32)
    low, high = call(
        pack_kernel,
        (shape(fields.shape[2], 64, Z),) * 2,
        "pack_strips",
        (pltpu.VMEM(fields.shape, BF16), pltpu.VMEM(cotangent.shape, BF16), pltpu.SemaphoreType.DMA((2,))),
        in_specs=[pl.BlockSpec(memory_space=pl.ANY)] * 2,
    )(fields, cotangent)
    rlo, rhi = exchange(low, high, "radial")

    w1 = first_weight.reshape(3, 3, 3, CH, CI).transpose(0, 1, 3, 2, 4).reshape(9 * CH, 3 * CI)
    w2 = second_weight.reshape(3, 3, 3, CH, CH)
    wb = w2[::-1, ::-1, ::-1].transpose(0, 1, 4, 2, 3).reshape(9 * CH, 3 * CH)
    w2 = w2.transpose(0, 1, 3, 2, 4).reshape(9 * CH, 3 * CH)
    t1, t2, tb, b1, b2 = call(
        band_kernel,
        (shape(192, 1152), shape(128, 1920), shape(128, 1920), shape(192, 256, dtype=F32), shape(128, 256, dtype=F32)),
        "band_weights",
    )(w1, w2, wb, jnp.asarray(e1, BF16), jnp.asarray(e2, BF16), jnp.asarray(expand, BF16), y1, y2, ry, first_bias[None], second_bias[None])

    low, high = call(join_kernel, (shape(896, Z),) * 2, "join_strips")(fields, cotangent, rlo, rhi)
    xlo, xhi = exchange(low, high, "stream")
    er1 = np.tile(e1[:CI, :128].T, (1, CH))
    er2 = np.zeros((2, 256, 256), np.float32)
    for half in range(2):
        er2[half, :128] = np.tile(e2[:CH, :128].T, (1, CH))
        er2[half, 128 + half * 64:192 + half * 64] = np.tile(e2[:CH, 384:448].T, (1, CH))
    counts = (lax.axis_size("stream"), lax.axis_size("radial"))
    closure, payload = call(
        functools.partial(main_kernel, counts),
        (shape(*cotangent.shape), shape(32, 384, dtype=F32)),
        "layers",
        (
            pltpu.VMEM((8 * 384, 256), BF16),
            pltpu.VMEM((6 * 640, 256), BF16),
            pltpu.VMEM((6 * 640, 256), BF16),
            pltpu.VMEM((4, 128, 256), F32),
        ),
        flops=3_000_000_000,
    )(fields, cotangent, rlo, rhi, xlo, xhi, t1, t2, tb, b1, b2, jnp.asarray(er1, BF16), jnp.asarray(er2, BF16), y1, y2, ry[:128])
    total = reduce_all(payload, ("radial", "snap", "stream"))
    count = fields.shape[0] * lax.axis_size("snap") * fields.shape[2] * counts[0] * fields.shape[3] * counts[1] * fields.shape[4]
    norm = float(1.0 / np.sqrt(np.float32(count)))
    first, second, bias = call(
        functools.partial(finish_kernel, norm),
        (shape(CH * CI, 27, dtype=F32), shape(CH * CH, 27, dtype=F32), shape(1, CH, dtype=F32)),
        "finish",
    )(total)
    first = first.reshape(CH, CI, 27).transpose(2, 0, 1)
    second = second.reshape(CH, CH, 27).transpose(2, 0, 1)
    return (closure, first, second, bias[0])


def solution(mesh):
    split = P("snap", None, "stream", "radial", None)
    return jax.shard_map(
        local,
        mesh=mesh,
        in_specs=(split, P(), P(), P(), P(), split),
        out_specs=(split, P(), P(), P()),
        check_vma=False,
    )
```

```python
import functools

import numpy as np
import jax
import jax.numpy as jnp
from jax import lax
from jax.experimental import pallas as pl
from jax.experimental.pallas import tpu as pltpu
from jax.sharding import PartitionSpec as P

F32 = jnp.float32
BF16 = jnp.bfloat16
Z = 128
CI = 8
CH = 16
FAR = 100


def block(channels, width):
    own = (np.repeat(np.arange(channels), 8), np.tile(np.arange(8), channels))
    rim_c = np.concatenate([np.repeat(np.arange(channels), 2)] * 2)
    rim_y = np.concatenate([np.tile([-2, -1], channels), np.tile([8, 9], channels)])
    return own, (rim_c, rim_y)


def tables():
    own, rim = block(CI, 128)
    e1 = np.zeros((3 * CI, 384), np.float32)
    y1 = np.full(384, FAR)
    for c in range(3):
        for (ch, y), at in ((own, c * 128), (rim, c * 128 + 64)):
            e1[c * CI + ch, at + np.arange(len(ch))] = 1
            y1[at:at + len(ch)] = y
    own, rim = block(CH, 192)
    e2 = np.zeros((3 * CH, 640), np.float32)
    y2 = np.full(640, FAR)
    for c in range(3):
        for (ch, y), at in ((own, c * 128), (rim, 384 + c * 64)):
            e2[c * CH + ch, at + np.arange(len(ch))] = 1
            y2[at:at + len(ch)] = y
    expand = np.zeros((128, CH), np.float32)
    expand[np.arange(128), own[0]] = 1
    return e1, y1, e2, y2, own[1], expand


def plane(ref, x):
    v = ref[0, :, x].astype(F32)
    return v.reshape(v.shape[0] * v.shape[1], v.shape[2])


def pick_rows(rims, rows):
    half = rims // 2
    row = lax.broadcasted_iota(jnp.int32, (rims, rows), 0)
    col = lax.broadcasted_iota(jnp.int32, (rims, rows), 1)
    side = jnp.where(row >= half, 1, 0)
    q = row - side * half
    return jnp.where(col == (q // 2) * 8 + 6 * side + q % 2, 1.0, 0.0).astype(BF16)


def pack_kernel(fields, cot, low, high, fields_here, cot_here, sems):
    copies = [
        pltpu.make_async_copy(fields, fields_here, sems.at[0]),
        pltpu.make_async_copy(cot, cot_here, sems.at[1]),
    ]
    for copy in copies:
        copy.start()
    for copy in copies:
        copy.wait()
    last = fields.shape[2] - 2
    for out, x in ((low, 0), (high, last)):
        for n in range(2):
            out[n, :64] = plane(fields_here, x + n).astype(BF16)
            out[n, 64:] = plane(cot_here, x + n).astype(BF16)


def join_kernel(fields, cot, xlo, xhi, low, high):
    pick = pick_rows(96, 192)
    count = fields.shape[2]
    for p in range(count + 4):
        x = p - 2
        if x < 0:
            rows = xlo[p]
        elif x >= count:
            rows = xhi[x - count]
        else:
            rows = jnp.concatenate([plane(fields, x), plane(cot, x)], axis=0).astype(BF16)
        got = jnp.dot(pick, rows, preferred_element_type=F32).astype(BF16)
        low[p] = got[:48]
        high[p] = got[48:]


def join_hidden_kernel(hidden, xlo, xhi, low, high):
    pick = pick_rows(64, 128)
    count = hidden.shape[0]
    for p in range(count + 4):
        x = p - 2
        rows = xlo[p] if x < 0 else xhi[x - count] if x >= count else hidden[x]
        got = jnp.dot(pick, rows, preferred_element_type=F32).astype(BF16)
        low[p] = got[:32]
        high[p] = got[32:]


def band(w, e, expand, ys, rows_y, t):
    width = e.shape[1]
    wide = jnp.dot(w[...], e[...], preferred_element_type=F32).astype(BF16)
    for a in range(3):
        total = jnp.zeros((128, width), F32)
        for b in range(3):
            part = jnp.dot(expand[...], wide[(a * 3 + b) * CH:(a * 3 + b + 1) * CH], preferred_element_type=F32)
            total = jnp.where(ys[...] == rows_y[...] + float(2 * (b - 1)), part, total)
        t[:, a * width:(a + 1) * width] = total.astype(BF16)


def repeat_bias(bias, expand, out):
    column = jnp.sum(expand[...].astype(F32) * bias[...], axis=1, keepdims=True)
    out[...] = jnp.broadcast_to(column, out.shape)


def band_first_kernel(w1, wb, bias, e1, e2, expand, y1, y2, rows_y, t1, tb, b1):
    band(w1, e1, expand, y1, rows_y, t1)
    band(wb, e2, expand, y2, rows_y, tb)
    repeat_bias(bias, expand, b1)


def band_second_kernel(w2, bias, e2, expand, y2, rows_y, t2, b2):
    band(w2, e2, expand, y2, rows_y, t2)
    repeat_bias(bias, expand, b2)


def shifted(v):
    lane = lax.broadcasted_iota(jnp.int32, v.shape, 1)
    before = jnp.where(lane >= 2, pltpu.roll(v, 2, 1), 0.0)
    after = jnp.where(lane < Z - 2, pltpu.roll(v, Z - 2, 1), 0.0)
    return before.astype(BF16), v.astype(BF16), after.astype(BF16)


def store_wide(ref, p, v):
    at = slice(p * Z, (p + 1) * Z)
    for c, piece in enumerate(shifted(v)):
        ref[c * 128:(c + 1) * 128, at] = piece[:128]
        ref[384 + c * 64:384 + (c + 1) * 64, at] = piece[128:]
    ref[576:, at] = jnp.zeros((64, Z), BF16)


def stacked(ref, lanes):
    return jnp.concatenate([ref[:, a * 256:a * 256 + lanes] for a in range(3)], axis=0)


def first_kernel(fields, cot, xlo, xhi, rlo, rhi, t1, tb, b1, er1, er2, y1, y2, yo,
                 hidden_out, hidden_low, hidden_high, payload, fs, cs):
    count = fields.shape[2]
    lanes = count * Z
    zeros = jnp.zeros((32, Z), F32)
    for p in range(count + 4):
        x = p - 2
        if x < 0:
            own = xlo[p].astype(F32)
        elif x >= count:
            own = xhi[x - count].astype(F32)
        else:
            own = jnp.concatenate([plane(fields, x), plane(cot, x)], axis=0)
        low, high = rlo[p].astype(F32), rhi[p].astype(F32)
        for c, piece in enumerate(shifted(jnp.concatenate([own[:64], low[:16], high[:16], zeros], axis=0))):
            fs[c * 128:(c + 1) * 128, p * Z:(p + 1) * Z] = piece
        store_wide(cs, p, jnp.concatenate([own[64:], low[16:], high[16:]], axis=0))
    pre = jnp.dot(t1[...], stacked(fs, lanes), preferred_element_type=F32) + b1[...]
    share = 0.5 * (1.0 + lax.erf(pre * 0.7071067811865476))
    hidden = (pre * share).astype(BF16)
    for x in range(count):
        hidden_out[x] = hidden[:, x * Z:(x + 1) * Z]
    for n in range(2):
        hidden_low[n] = hidden[:, n * Z:(n + 1) * Z]
        hidden_high[n] = hidden[:, (count - 2 + n) * Z:(count - 1 + n) * Z]
    back = jnp.dot(tb[...], stacked(cs, lanes), preferred_element_type=F32)
    dpre = (back * (share + pre * jnp.exp(-0.5 * pre * pre) * 0.3989422804014327)).astype(BF16)
    bias = jnp.sum(dpre.astype(F32), axis=1, keepdims=True)
    lane = lax.broadcasted_iota(jnp.int32, (8, 256), 1)

    def diagonal(rows, place):
        total = jnp.zeros((8, rows.shape[1]), F32)
        for o in range(CH):
            total = jnp.where(place == o, rows[o * 8:(o + 1) * 8], total)
        return jnp.sum(total, axis=0, keepdims=True)

    payload[24:] = jnp.zeros((8, 384), F32)
    payload[27:28, :128] = diagonal(jnp.broadcast_to(bias, (128, 128)), lane[:, :128])
    over_lanes = (((1,), (1,)), ((), ()))
    for a in range(3):
        g1 = lax.dot_general(dpre, fs[:, a * 256:a * 256 + lanes], over_lanes, preferred_element_type=F32)
        g2 = lax.dot_general(hidden, cs[:, a * 256:a * 256 + lanes], over_lanes, preferred_element_type=F32)
        for b in range(3):
            off = float(2 * (b - 1))
            one = jnp.where(y1[...] == yo[...] + off, g1, 0.0).astype(BF16)
            two = jnp.where(y2[...] == yo[...] + off, g2, 0.0).astype(BF16)
            for c in range(3):
                tap = (a * 3 + b) * 3 + c
                r1 = jnp.dot(one[:, c * 128:(c + 1) * 128], er1[...], preferred_element_type=F32)
                rim = 384 + (c // 2) * 128
                both = jnp.concatenate([two[:, c * 128:(c + 1) * 128], two[:, rim:rim + 128]], axis=1)
                r2 = jnp.dot(both, er2[c % 2], preferred_element_type=F32)
                payload[tap:tap + 1, :128] = diagonal(r1, lane[:, :128] // CI)
                payload[26 - tap:27 - tap, 128:] = diagonal(r2, lane % CH)


def closure_kernel(hidden, xlo, xhi, rlo, rhi, t2, b2, closure, hs):
    count = hidden.shape[0]
    for p in range(count + 4):
        x = p - 2
        own = xlo[p] if x < 0 else xhi[x - count] if x >= count else hidden[x]
        store_wide(hs, p, jnp.concatenate([own, rlo[p], rhi[p]], axis=0).astype(F32))
    out = (jnp.dot(t2[...], stacked(hs, count * Z), preferred_element_type=F32) + b2[...]).astype(BF16)
    for x in range(count):
        closure[0, :, x] = out[:, x * Z:(x + 1) * Z].reshape(CH, 8, Z)


def finish_kernel(norm, total, first, second, bias):
    scaled = total[...] * norm
    flipped = jnp.transpose(scaled)
    first[...] = flipped[:128, :27]
    second[...] = flipped[128:, :27]
    bias[...] = scaled[27:28, :CH]


def call(kernel, outs, name, scratch=(), flops=10_000_000, **specs):
    return pl.pallas_call(
        kernel,
        out_shape=outs,
        **specs,
        scratch_shapes=list(scratch),
        compiler_params=pltpu.CompilerParams(vmem_limit_bytes=48 * 1024 * 1024),
        cost_estimate=pl.CostEstimate(flops=flops, bytes_accessed=1_000_000, transcendentals=0),
        name=name,
    )


def shape(*dims, dtype=BF16):
    return jax.ShapeDtypeStruct(dims, dtype)


def exchange(low, high, axis):
    count = lax.axis_size(axis)
    up = [(i, i + 1) for i in range(count - 1)]
    down = [(j, i) for i, j in up]
    return lax.ppermute(high, axis, up), lax.ppermute(low, axis, down)


def reduce_all(v, axes):
    for axis in axes:
        count = lax.axis_size(axis)
        if count & (count - 1):
            v = lax.psum(v, axis)
            continue

        def swapped(mask):
            return lax.ppermute(v, axis, [(i, i ^ mask) for i in range(count)])

        step = 1
        while step < count:
            if step * 4 <= count:
                one, two, three = swapped(step), swapped(2 * step), swapped(3 * step)
                v = (v + one) + (two + three)
                step *= 4
            else:
                v = v + swapped(step)
                step *= 2
    return v


def local(fields, first_weight, first_bias, second_weight, second_bias, cotangent):
    e1, y1, e2, y2, rows_y, expand = tables()
    er1 = np.tile(e1[:CI, :128].T, (1, CH))
    er2 = np.zeros((2, 256, 256), np.float32)
    for half in range(2):
        er2[half, :128] = np.repeat(e2[:CH, :128].T, CH, axis=1)
        er2[half, 128 + half * 64:192 + half * 64] = np.repeat(e2[:CH, 384:448].T, CH, axis=1)
    e1, e2, er1, er2, expand = (jnp.asarray(v, BF16) for v in (e1, e2, er1, er2, expand))
    y1, y2, rows_y = (jnp.asarray(v, F32) for v in (y1[None], y2[None], rows_y[:, None]))
    planes = fields.shape[2]
    low, high = call(
        pack_kernel,
        (shape(2, 192, Z),) * 2,
        "pack_strips",
        (pltpu.VMEM(fields.shape, BF16), pltpu.VMEM(cotangent.shape, BF16), pltpu.SemaphoreType.DMA((2,))),
        in_specs=[pl.BlockSpec(memory_space=pl.ANY)] * 2,
    )(fields, cotangent)
    xlo, xhi = exchange(low, high, "stream")

    w1 = first_weight.reshape(3, 3, 3, CH, CI).transpose(0, 1, 3, 2, 4).reshape(9 * CH, 3 * CI)
    w2 = second_weight.reshape(3, 3, 3, CH, CH)
    wb = w2[::-1, ::-1, ::-1].transpose(0, 1, 4, 2, 3).reshape(9 * CH, 3 * CH)
    w2 = w2.transpose(0, 1, 3, 2, 4).reshape(9 * CH, 3 * CH)
    spread = shape(128, planes * Z, dtype=F32)
    t1, tb, b1 = call(band_first_kernel, (shape(128, 1152), shape(128, 1920), spread), "band_first")(
        w1, wb, first_bias[None], e1, e2, expand, y1, y2, rows_y)

    low, high = call(join_kernel, (shape(planes + 4, 48, Z),) * 2, "join_strips")(fields, cotangent, xlo, xhi)
    rlo, rhi = exchange(low, high, "radial")
    wide = (planes + 4) * Z
    hidden, low, high, payload = call(
        first_kernel,
        (shape(planes, 128, Z), shape(2, 128, Z), shape(2, 128, Z), shape(32, 384, dtype=F32)),
        "gradients",
        (pltpu.VMEM((384, wide), BF16), pltpu.VMEM((640, wide), BF16)),
        flops=2_000_000_000,
    )(fields, cotangent, xlo, xhi, rlo, rhi, t1, tb, b1, er1, er2, y1, y2, rows_y)
    total = reduce_all(payload, ("radial", "stream", "snap"))

    xlo, xhi = exchange(low, high, "stream")
    low, high = call(join_hidden_kernel, (shape(planes + 4, 32, Z),) * 2, "join_hidden")(hidden, xlo, xhi)
    rlo, rhi = exchange(low, high, "radial")
    t2, b2 = call(band_second_kernel, (shape(128, 1920), spread), "band_second")(
        w2, second_bias[None], e2, expand, y2, rows_y)
    closure = call(
        closure_kernel, shape(*cotangent.shape), "closure", (pltpu.VMEM((640, wide), BF16),), flops=1_000_000_000
    )(hidden, xlo, xhi, rlo, rhi, t2, b2)

    cells = fields.shape[0] * fields.shape[2] * fields.shape[3] * fields.shape[4]
    for axis in ("stream", "radial", "snap"):
        cells *= lax.axis_size(axis)
    norm = float(1.0 / np.sqrt(np.float32(cells)))
    first, second, bias = call(
        functools.partial(finish_kernel, norm),
        (shape(CH * CI, 27, dtype=F32), shape(CH * CH, 27, dtype=F32), shape(1, CH, dtype=F32)),
        "finish",
    )(total)
    first = first.reshape(CH, CI, 27).transpose(2, 0, 1)
    second = second.reshape(CH, CH, 27).transpose(2, 0, 1)
    return (closure, first, second, bias[0])


def solution(mesh):
    split = P("snap", None, "stream", "radial", None)
    return jax.shard_map(
        local,
        mesh=mesh,
        in_specs=(split, P(), P(), P(), P(), split),
        out_specs=(split, P(), P(), P()),
        check_vma=False,
    )
```

```python
import functools

import numpy as np
import jax
import jax.numpy as jnp
from jax import lax
from jax.experimental import pallas as pl
from jax.experimental.pallas import tpu as pltpu
from jax.sharding import PartitionSpec as P

F32 = jnp.float32
BF16 = jnp.bfloat16
Z = 128
CI = 8
CH = 16
FAR = 100


def block(channels, width):
    own = (np.repeat(np.arange(channels), 8), np.tile(np.arange(8), channels))
    rim_c = np.concatenate([np.repeat(np.arange(channels), width)] * 2)
    rim_y = np.concatenate([np.tile(np.arange(-width, 0), channels), np.tile(np.arange(8, 8 + width), channels)])
    return own, (rim_c, rim_y)


def tables():
    own, rim = block(CI, 4)
    e1 = np.zeros((3 * CI, 384), np.float32)
    y1 = np.full(384, FAR)
    for c in range(3):
        for (ch, y), at in ((own, c * 128), (rim, c * 128 + 64)):
            e1[c * CI + ch, at + np.arange(len(ch))] = 1
            y1[at:at + len(ch)] = y
    own, rim = block(CH, 2)
    e2 = np.zeros((3 * CH, 640), np.float32)
    y2 = np.full(640, FAR)
    for c in range(3):
        for (ch, y), at in ((own, c * 128), (rim, 384 + c * 64)):
            e2[c * CH + ch, at + np.arange(len(ch))] = 1
            y2[at:at + len(ch)] = y
    rows_y = np.concatenate([own[1], rim[1]])
    expand = np.zeros((192, CH), np.float32)
    expand[np.arange(192), np.concatenate([own[0], rim[0]])] = 1
    return e1, y1, e2, y2, rows_y, expand


def plane(ref, x):
    v = ref[0, :, x].astype(F32)
    return v.reshape(v.shape[0] * v.shape[1], v.shape[2])


def pick_rows(channels, width):
    half = channels * width
    row = lax.broadcasted_iota(jnp.int32, (2 * half, channels * 8), 0)
    col = lax.broadcasted_iota(jnp.int32, (2 * half, channels * 8), 1)
    side = jnp.where(row >= half, 1, 0)
    q = row - side * half
    return jnp.where(col == (q // width) * 8 + (8 - width) * side + q % width, 1.0, 0.0).astype(BF16)


def partners(index, count):
    return index % 2 == 0, index > 0, index < count - 1


def sides(index, count, near, far):
    near_above, below, above = partners(index, count)
    low = jnp.where(near_above, far, near).astype(F32)
    high = jnp.where(near_above, near, far).astype(F32)
    return jnp.where(below, low, 0.0), jnp.where(above, high, 0.0)


def pack_kernel(fields, cot, near, far, fields_here, cot_here, sems):
    copies = [
        pltpu.make_async_copy(fields, fields_here, sems.at[0]),
        pltpu.make_async_copy(cot, cot_here, sems.at[1]),
    ]
    for copy in copies:
        copy.start()
    for copy in copies:
        copy.wait()
    up_first = lax.axis_index("stream") % 2 == 0
    count = fields.shape[2]
    for here, width, at, rows in ((fields_here, 4, 0, 64), (cot_here, 2, 256, 128)):
        for n in range(width):
            low, high = plane(here, n), plane(here, count - width + n)
            part = slice(at + n * rows, at + (n + 1) * rows)
            near[part] = jnp.where(up_first, high, low).astype(BF16)
            far[part] = jnp.where(up_first, low, high).astype(BF16)


def x_planes(count, fields, cot, xnear, xfar, size):
    index = lax.axis_index("stream")
    inner = [plane(fields, x) for x in range(count)]
    rims = [sides(index, size, xnear[n * 64:(n + 1) * 64], xfar[n * 64:(n + 1) * 64]) for n in range(4)]
    f = [low for low, _ in rims] + inner + [high for _, high in rims]
    inner = [plane(cot, x) for x in range(count)]
    rims = [sides(index, size, xnear[256 + n * 128:384 + n * 128], xfar[256 + n * 128:384 + n * 128]) for n in range(2)]
    return f, [low for low, _ in rims] + inner + [high for _, high in rims]


def join_kernel(counts, fields, cot, xnear, xfar, near, far):
    up_first = lax.axis_index("radial") % 2 == 0
    f, c = x_planes(fields.shape[2], fields, cot, xnear, xfar, counts[0])
    at = 0
    for rows, pick in ((f, pick_rows(CI, 4)), (c, pick_rows(CH, 2))):
        for v in rows:
            got = jnp.dot(pick, v.astype(BF16), preferred_element_type=F32)
            near[at:at + 32] = jnp.where(up_first, got[32:], got[:32]).astype(BF16)
            far[at:at + 32] = jnp.where(up_first, got[:32], got[32:]).astype(BF16)
            at += 32


def band(w, e, expand, ys, rows_y, t):
    rows, width = t.shape[0], e.shape[1]
    wide = jnp.dot(w[...], e[...], preferred_element_type=F32).astype(BF16)
    for a in range(3):
        total = jnp.zeros((rows, width), F32)
        for b in range(3):
            part = jnp.dot(expand[:rows], wide[(a * 3 + b) * CH:(a * 3 + b + 1) * CH], preferred_element_type=F32)
            total = jnp.where(ys[...] == rows_y[:rows] + float(2 * (b - 1)), part, total)
        t[:, a * width:(a + 1) * width] = total.astype(BF16)


def repeat_bias(bias, expand, out):
    column = jnp.sum(expand[:out.shape[0]].astype(F32) * bias[...], axis=1, keepdims=True)
    out[...] = jnp.broadcast_to(column, out.shape)


def band_first_kernel(w1, wb, bias, e1, e2, expand, y1, y2, rows_y, t1, tb, b1):
    band(w1, e1, expand, y1, rows_y, t1)
    band(wb, e2, expand, y2, rows_y, tb)
    repeat_bias(bias, expand, b1)


def band_second_kernel(w2, bias, e2, expand, y2, rows_y, t2, b2):
    band(w2, e2, expand, y2, rows_y, t2)
    repeat_bias(bias, expand, b2)


def shifted(v):
    lane = lax.broadcasted_iota(jnp.int32, v.shape, 1)
    before = jnp.where(lane >= 2, pltpu.roll(v, 2, 1), 0.0)
    after = jnp.where(lane < Z - 2, pltpu.roll(v, Z - 2, 1), 0.0)
    return before.astype(BF16), v.astype(BF16), after.astype(BF16)


def store_wide(ref, p, v):
    at = slice(p * Z, (p + 1) * Z)
    for c, piece in enumerate(shifted(v)):
        ref[c * 128:(c + 1) * 128, at] = piece[:128]
        ref[384 + c * 64:384 + (c + 1) * 64, at] = piece[128:]
    ref[576:, at] = jnp.zeros((64, Z), BF16)


def stacked(ref, lanes):
    return jnp.concatenate([ref[:, a * 256:a * 256 + lanes] for a in range(3)], axis=0)


def first_kernel(counts, fields, cot, xnear, xfar, rnear, rfar, t1, tb, b1, er1, er2, y1, y2, yo,
                 hidden_out, payload, fs, cs):
    count = fields.shape[2]
    lanes = count * Z
    stream, radial = lax.axis_index("stream"), lax.axis_index("radial")
    f, c = x_planes(count, fields, cot, xnear, xfar, counts[0])
    at = 0
    for p, v in enumerate(f):
        low, high = sides(radial, counts[1], rnear[at:at + 32], rfar[at:at + 32])
        for n, piece in enumerate(shifted(jnp.concatenate([v, low, high], axis=0))):
            fs[n * 128:(n + 1) * 128, p * Z:(p + 1) * Z] = piece
        at += 32
    for p, v in enumerate(c):
        low, high = sides(radial, counts[1], rnear[at:at + 32], rfar[at:at + 32])
        store_wide(cs, p, jnp.concatenate([v, low, high], axis=0))
        at += 32
    pre = jnp.dot(t1[...], stacked(fs, lanes + 4 * Z), preferred_element_type=F32) + b1[...]
    share = 0.5 * (1.0 + lax.erf(pre * 0.7071067811865476))
    hidden = (pre * share).astype(BF16)
    zero = jnp.zeros((), BF16)
    rims = (jnp.where(radial > 0, hidden[128:160], zero), jnp.where(radial < counts[1] - 1, hidden[160:], zero))
    for p in range(count + 4):
        at = slice(p * Z, (p + 1) * Z)
        rows = jnp.concatenate([hidden[:128, at], rims[0][:, at], rims[1][:, at]], axis=0)
        if p < 2:
            rows = jnp.where(stream > 0, rows, zero)
        elif p >= count + 2:
            rows = jnp.where(stream < counts[0] - 1, rows, zero)
        hidden_out[p] = rows
    at = slice(2 * Z, 2 * Z + lanes)
    pre, share, hidden = pre[:128, at], share[:128, at], hidden[:128, at]
    back = jnp.dot(tb[...], stacked(cs, lanes), preferred_element_type=F32)
    dpre = (back * (share + pre * jnp.exp(-0.5 * pre * pre) * 0.3989422804014327)).astype(BF16)
    bias = jnp.sum(dpre.astype(F32), axis=1, keepdims=True)
    lane = lax.broadcasted_iota(jnp.int32, (8, 256), 1)

    def diagonal(rows, place):
        total = jnp.zeros((8, rows.shape[1]), F32)
        for o in range(CH):
            total = jnp.where(place == o, rows[o * 8:(o + 1) * 8], total)
        return jnp.sum(total, axis=0, keepdims=True)

    payload[...] = jnp.zeros(payload.shape, F32)
    payload[27, :1] = diagonal(jnp.broadcast_to(bias, (128, 128)), lane[:, :128])
    over_lanes = (((1,), (1,)), ((), ()))
    for a in range(3):
        g1 = lax.dot_general(dpre, fs[:, (a + 1) * 256:(a + 1) * 256 + lanes], over_lanes, preferred_element_type=F32)
        g2 = lax.dot_general(hidden, cs[:, a * 256:a * 256 + lanes], over_lanes, preferred_element_type=F32)
        for b in range(3):
            off = float(2 * (b - 1))
            one = jnp.where(y1[...] == yo[...] + off, g1, 0.0).astype(BF16)
            two = jnp.where(y2[...] == yo[...] + off, g2, 0.0).astype(BF16)
            for c in range(3):
                tap = (a * 3 + b) * 3 + c
                r1 = jnp.dot(one[:, c * 128:(c + 1) * 128], er1[...], preferred_element_type=F32)
                rim = 384 + (c // 2) * 128
                both = jnp.concatenate([two[:, c * 128:(c + 1) * 128], two[:, rim:rim + 128]], axis=1)
                r2 = jnp.dot(both, er2[c % 2], preferred_element_type=F32)
                payload[tap, :1] = diagonal(r1, lane[:, :128] // CI)
                second = diagonal(r2, lane % CH)
                payload[26 - tap, 1:2] = second[:, :128]
                payload[26 - tap, 2:3] = second[:, 128:]


def closure_kernel(hidden, t2, b2, closure, hs):
    count = closure.shape[2]
    for p in range(count + 4):
        store_wide(hs, p, hidden[p].astype(F32))
    out = (jnp.dot(t2[...], stacked(hs, count * Z), preferred_element_type=F32) + b2[...]).astype(BF16)
    for x in range(count):
        closure[0, :, x] = out[:, x * Z:(x + 1) * Z].reshape(CH, 8, Z)


def add_kernel(parts, total):
    acc = parts[0]
    for d in range(1, parts.shape[0]):
        acc = acc + parts[d]
    for d in range(total.shape[0]):
        total[d] = acc


def finish_kernel(norm, total, first, second, bias):
    parts = [total[:, n] * norm for n in range(3)]
    first[...] = jnp.transpose(parts[0])[:, :27]
    second[:128] = jnp.transpose(parts[1])[:, :27]
    second[128:] = jnp.transpose(parts[2])[:, :27]
    bias[...] = parts[0][27:28, :CH]


def call(kernel, outs, name, scratch=(), flops=10_000_000, **specs):
    return pl.pallas_call(
        kernel,
        out_shape=outs,
        **specs,
        scratch_shapes=list(scratch),
        compiler_params=pltpu.CompilerParams(vmem_limit_bytes=48 * 1024 * 1024),
        cost_estimate=pl.CostEstimate(flops=flops, bytes_accessed=1_000_000, transcendentals=0),
        name=name,
    )


def shape(*dims, dtype=BF16):
    return jax.ShapeDtypeStruct(dims, dtype)


def exchange(near, far, axis):
    count = lax.axis_size(axis)
    shifted_pairs = [(i, min(max(i - 1 + 2 * (i % 2), 0), count - 1)) for i in range(count)]
    return lax.ppermute(near, axis, [(i, i ^ 1) for i in range(count)]), lax.ppermute(far, axis, shifted_pairs)


def reduce_all(v, axes):
    devices = 1
    for axis in axes:
        devices *= lax.axis_size(axis)
    rows = v.reshape(devices, -1, *v.shape[-1:]) if v.size // v.shape[-1] % devices == 0 else v.reshape(devices, 1, -1)
    mine = lax.all_to_all(rows, axes, 0, 0, tiled=True)
    mine = call(add_kernel, shape(*rows.shape, dtype=F32), "add_rows")(mine)
    return lax.all_to_all(mine, axes, 0, 0, tiled=True).reshape(v.shape)


def local(fields, first_weight, first_bias, second_weight, second_bias, cotangent):
    e1, y1, e2, y2, rows_y, expand = tables()
    er1 = np.tile(e1[:CI, :128].T, (1, CH))
    er2 = np.zeros((2, 256, 256), np.float32)
    for half in range(2):
        er2[half, :128] = np.repeat(e2[:CH, :128].T, CH, axis=1)
        er2[half, 128 + half * 64:192 + half * 64] = np.repeat(e2[:CH, 384:448].T, CH, axis=1)
    e1, e2, er1, er2, expand = (jnp.asarray(v, BF16) for v in (e1, e2, er1, er2, expand))
    y1, y2, rows_y = (jnp.asarray(v, F32) for v in (y1[None], y2[None], rows_y[:, None]))
    planes = fields.shape[2]
    near, far = call(
        pack_kernel,
        (shape(512, Z),) * 2,
        "pack_strips",
        (pltpu.VMEM(fields.shape, BF16), pltpu.VMEM(cotangent.shape, BF16), pltpu.SemaphoreType.DMA((2,))),
        in_specs=[pl.BlockSpec(memory_space=pltpu.HBM)] * 2,
    )(fields, cotangent)
    xnear, xfar = exchange(near, far, "stream")

    w1 = first_weight.reshape(3, 3, 3, CH, CI).transpose(0, 1, 3, 2, 4).reshape(9 * CH, 3 * CI)
    w2 = second_weight.reshape(3, 3, 3, CH, CH)
    wb = w2[::-1, ::-1, ::-1].transpose(0, 1, 4, 2, 3).reshape(9 * CH, 3 * CH)
    w2 = w2.transpose(0, 1, 3, 2, 4).reshape(9 * CH, 3 * CH)
    wide = (planes + 4) * Z
    t1, tb, b1 = call(
        band_first_kernel, (shape(192, 1152), shape(128, 1920), shape(192, wide, dtype=F32)), "band_first"
    )(w1, wb, first_bias[None], e1, e2, expand, y1, y2, rows_y)

    counts = (lax.axis_size("stream"), lax.axis_size("radial"))
    near, far = call(functools.partial(join_kernel, counts), (shape((2 * planes + 12) * 32, Z),) * 2, "join_strips")(
        fields, cotangent, xnear, xfar)
    rnear, rfar = exchange(near, far, "radial")
    hidden, payload = call(
        functools.partial(first_kernel, counts),
        (shape(planes + 4, 192, Z), shape(32, 4, 128, dtype=F32)),
        "gradients",
        (pltpu.VMEM((384, wide + 4 * Z), BF16), pltpu.VMEM((640, wide), BF16)),
        flops=2_000_000_000,
    )(fields, cotangent, xnear, xfar, rnear, rfar, t1, tb, b1, er1, er2, y1, y2, rows_y[:128])
    total = reduce_all(payload, ("stream", "radial", "snap"))

    t2, b2 = call(band_second_kernel, (shape(128, 1920), shape(128, planes * Z, dtype=F32)), "band_second")(
        w2, second_bias[None], e2, expand, y2, rows_y)
    closure = call(
        closure_kernel, shape(*cotangent.shape), "closure", (pltpu.VMEM((640, wide), BF16),), flops=1_000_000_000
    )(hidden, t2, b2)

    cells = fields.shape[0] * fields.shape[2] * fields.shape[3] * fields.shape[4]
    for axis in ("stream", "radial", "snap"):
        cells *= lax.axis_size(axis)
    norm = float(1.0 / np.sqrt(np.float32(cells)))
    first, second, bias = call(
        functools.partial(finish_kernel, norm),
        (shape(CH * CI, 27, dtype=F32), shape(CH * CH, 27, dtype=F32), shape(1, CH, dtype=F32)),
        "finish",
    )(total)
    first = first.reshape(CH, CI, 27).transpose(2, 0, 1)
    second = second.reshape(CH, CH, 27).transpose(2, 0, 1)
    return (closure, first, second, bias[0])


def solution(mesh):
    split = P("snap", None, "stream", "radial", None)
    return jax.shard_map(
        local,
        mesh=mesh,
        in_specs=(split, P(), P(), P(), P(), split),
        out_specs=(split, P(), P(), P()),
        check_vma=False,
    )
```

```python
import functools

import numpy as np
import jax
import jax.numpy as jnp
from jax import lax
from jax.experimental import pallas as pl
from jax.experimental.pallas import tpu as pltpu
from jax.sharding import PartitionSpec as P

F32 = jnp.float32
BF16 = jnp.bfloat16
Z = 128
CI = 8
CH = 16
FAR = 100


def block(channels, width):
    own = (np.repeat(np.arange(channels), 8), np.tile(np.arange(8), channels))
    rim_c = np.concatenate([np.repeat(np.arange(channels), width)] * 2)
    rim_y = np.concatenate([np.tile(np.arange(-width, 0), channels), np.tile(np.arange(8, 8 + width), channels)])
    return own, (rim_c, rim_y)


def tables():
    own, rim = block(CI, 4)
    e1 = np.zeros((3 * CI, 384), np.float32)
    y1 = np.full(384, FAR)
    for c in range(3):
        for (ch, y), at in ((own, c * 128), (rim, c * 128 + 64)):
            e1[c * CI + ch, at + np.arange(len(ch))] = 1
            y1[at:at + len(ch)] = y
    own, rim = block(CH, 2)
    e2 = np.zeros((3 * CH, 640), np.float32)
    y2 = np.full(640, FAR)
    for c in range(3):
        for (ch, y), at in ((own, c * 128), (rim, 384 + c * 64)):
            e2[c * CH + ch, at + np.arange(len(ch))] = 1
            y2[at:at + len(ch)] = y
    rows_y = np.concatenate([own[1], rim[1]])
    expand = np.zeros((192, CH), np.float32)
    expand[np.arange(192), np.concatenate([own[0], rim[0]])] = 1
    return e1, y1, e2, y2, rows_y, expand


def plane(ref, x):
    v = ref[0, :, x].astype(F32)
    return v.reshape(v.shape[0] * v.shape[1], v.shape[2])


def pick_rows(channels, width):
    half = channels * width
    row = lax.broadcasted_iota(jnp.int32, (2 * half, channels * 8), 0)
    col = lax.broadcasted_iota(jnp.int32, (2 * half, channels * 8), 1)
    side = jnp.where(row >= half, 1, 0)
    q = row - side * half
    return jnp.where(col == (q // width) * 8 + (8 - width) * side + q % width, 1.0, 0.0).astype(BF16)


def partners(index, count):
    return index % 2 == 0, index > 0, index < count - 1


def sides(index, count, near, far):
    near_above, below, above = partners(index, count)
    low = jnp.where(near_above, far, near).astype(F32)
    high = jnp.where(near_above, near, far).astype(F32)
    return jnp.where(below, low, 0.0), jnp.where(above, high, 0.0)


def pack_kernel(fields, cot, near, far, fields_here, cot_here, sems):
    copies = [
        pltpu.make_async_copy(fields, fields_here, sems.at[0]),
        pltpu.make_async_copy(cot, cot_here, sems.at[1]),
    ]
    for copy in copies:
        copy.start()
    for copy in copies:
        copy.wait()
    up_first = lax.axis_index("stream") % 2 == 0
    count = fields.shape[2]
    for here, width, at, rows in ((fields_here, 4, 0, 64), (cot_here, 2, 256, 128)):
        for n in range(width):
            low, high = plane(here, n), plane(here, count - width + n)
            part = slice(at + n * rows, at + (n + 1) * rows)
            near[part] = jnp.where(up_first, high, low).astype(BF16)
            far[part] = jnp.where(up_first, low, high).astype(BF16)


def x_planes(count, fields, cot, xnear, xfar, size):
    index = lax.axis_index("stream")
    inner = [plane(fields, x) for x in range(count)]
    rims = [sides(index, size, xnear[n * 64:(n + 1) * 64], xfar[n * 64:(n + 1) * 64]) for n in range(4)]
    f = [low for low, _ in rims] + inner + [high for _, high in rims]
    inner = [plane(cot, x) for x in range(count)]
    rims = [sides(index, size, xnear[256 + n * 128:384 + n * 128], xfar[256 + n * 128:384 + n * 128]) for n in range(2)]
    return f, [low for low, _ in rims] + inner + [high for _, high in rims]


def join_kernel(counts, fields, cot, xnear, xfar, near, far):
    up_first = lax.axis_index("radial") % 2 == 0
    f, c = x_planes(fields.shape[2], fields, cot, xnear, xfar, counts[0])
    at = 0
    for rows, pick in ((f, pick_rows(CI, 4)), (c, pick_rows(CH, 2))):
        for v in rows:
            got = jnp.dot(pick, v.astype(BF16), preferred_element_type=F32)
            near[at:at + 32] = jnp.where(up_first, got[32:], got[:32]).astype(BF16)
            far[at:at + 32] = jnp.where(up_first, got[:32], got[32:]).astype(BF16)
            at += 32


def band(w, e, expand, ys, rows_y, t):
    rows, width = t.shape[0], e.shape[1]
    wide = jnp.dot(w[...], e[...], preferred_element_type=F32).astype(BF16)
    for a in range(3):
        total = jnp.zeros((rows, width), F32)
        for b in range(3):
            part = jnp.dot(expand[:rows], wide[(a * 3 + b) * CH:(a * 3 + b + 1) * CH], preferred_element_type=F32)
            total = jnp.where(ys[...] == rows_y[:rows] + float(2 * (b - 1)), part, total)
        t[:, a * width:(a + 1) * width] = total.astype(BF16)


def repeat_bias(bias, expand, out):
    column = jnp.sum(expand[:out.shape[0]].astype(F32) * bias[...], axis=1, keepdims=True)
    out[...] = jnp.broadcast_to(column, out.shape)


def band_first_kernel(w1, wb, bias, e1, e2, expand, y1, y2, rows_y, t1, tb, b1):
    band(w1, e1, expand, y1, rows_y, t1)
    band(wb, e2, expand, y2, rows_y, tb)
    repeat_bias(bias, expand, b1)


def band_second_kernel(w2, bias, e2, expand, y2, rows_y, t2, b2):
    band(w2, e2, expand, y2, rows_y, t2)
    repeat_bias(bias, expand, b2)


def shifted(v):
    lane = lax.broadcasted_iota(jnp.int32, v.shape, 1)
    before = jnp.where(lane >= 2, pltpu.roll(v, 2, 1), 0.0)
    after = jnp.where(lane < Z - 2, pltpu.roll(v, Z - 2, 1), 0.0)
    return before.astype(BF16), v.astype(BF16), after.astype(BF16)


def store_wide(ref, p, v):
    at = slice(p * Z, (p + 1) * Z)
    for c, piece in enumerate(shifted(v)):
        ref[c * 128:(c + 1) * 128, at] = piece[:128]
        ref[384 + c * 64:384 + (c + 1) * 64, at] = piece[128:]
    ref[576:, at] = jnp.zeros((64, Z), BF16)


def stacked(ref, lanes):
    return jnp.concatenate([ref[:, a * 256:a * 256 + lanes] for a in range(3)], axis=0)


def first_kernel(counts, fields, cot, xnear, xfar, rnear, rfar, t1, tb, b1, er1, er2, y1, y2, yo,
                 hidden_out, payload, fs, cs):
    count = fields.shape[2]
    lanes = count * Z
    stream, radial = lax.axis_index("stream"), lax.axis_index("radial")
    f, c = x_planes(count, fields, cot, xnear, xfar, counts[0])
    at = 0
    for p, v in enumerate(f):
        low, high = sides(radial, counts[1], rnear[at:at + 32], rfar[at:at + 32])
        for n, piece in enumerate(shifted(jnp.concatenate([v, low, high], axis=0))):
            fs[n * 128:(n + 1) * 128, p * Z:(p + 1) * Z] = piece
        at += 32
    for p, v in enumerate(c):
        low, high = sides(radial, counts[1], rnear[at:at + 32], rfar[at:at + 32])
        store_wide(cs, p, jnp.concatenate([v, low, high], axis=0))
        at += 32
    pre = jnp.dot(t1[...], stacked(fs, lanes + 4 * Z), preferred_element_type=F32) + b1[...]
    share = 0.5 * (1.0 + lax.erf(pre * 0.7071067811865476))
    hidden = (pre * share).astype(BF16)
    zero = jnp.zeros((), BF16)
    rims = (jnp.where(radial > 0, hidden[128:160], zero), jnp.where(radial < counts[1] - 1, hidden[160:], zero))
    for p in range(count + 4):
        at = slice(p * Z, (p + 1) * Z)
        rows = jnp.concatenate([hidden[:128, at], rims[0][:, at], rims[1][:, at]], axis=0)
        if p < 2:
            rows = jnp.where(stream > 0, rows, zero)
        elif p >= count + 2:
            rows = jnp.where(stream < counts[0] - 1, rows, zero)
        hidden_out[p] = rows
    at = slice(2 * Z, 2 * Z + lanes)
    pre, share, hidden = pre[:128, at], share[:128, at], hidden[:128, at]
    back = jnp.dot(tb[...], stacked(cs, lanes), preferred_element_type=F32)
    dpre = (back * (share + pre * jnp.exp(-0.5 * pre * pre) * 0.3989422804014327)).astype(BF16)
    bias = jnp.sum(dpre.astype(F32), axis=1, keepdims=True)
    lane = lax.broadcasted_iota(jnp.int32, (8, 256), 1)

    def diagonal(rows, place):
        total = jnp.zeros((8, rows.shape[1]), F32)
        for o in range(CH):
            total = jnp.where(place == o, rows[o * 8:(o + 1) * 8], total)
        return jnp.sum(total, axis=0, keepdims=True)

    ones, twos = [None] * 32, [None] * 32
    ones[27] = diagonal(jnp.broadcast_to(bias, (128, 128)), lane[:, :128])
    over_lanes = (((1,), (1,)), ((), ()))
    for a in range(3):
        g1 = lax.dot_general(dpre, fs[:, (a + 1) * 256:(a + 1) * 256 + lanes], over_lanes, preferred_element_type=F32)
        g2 = lax.dot_general(hidden, cs[:, a * 256:a * 256 + lanes], over_lanes, preferred_element_type=F32)
        for b in range(3):
            off = float(2 * (b - 1))
            one = jnp.where(y1[...] == yo[...] + off, g1, 0.0).astype(BF16)
            two = jnp.where(y2[...] == yo[...] + off, g2, 0.0).astype(BF16)
            for c in range(3):
                tap = (a * 3 + b) * 3 + c
                r1 = jnp.dot(one[:, c * 128:(c + 1) * 128], er1[...], preferred_element_type=F32)
                rim = 384 + (c // 2) * 128
                both = jnp.concatenate([two[:, c * 128:(c + 1) * 128], two[:, rim:rim + 128]], axis=1)
                r2 = jnp.dot(both, er2[c % 2], preferred_element_type=F32)
                ones[tap] = diagonal(r1, lane[:, :128] // CI)
                twos[26 - tap] = diagonal(r2, lane % CH)
    for rows, at, width in ((ones, 0, 128), (twos, 128, 256)):
        rows = [jnp.zeros((1, width), F32) if v is None else v for v in rows]
        payload[:, at:at + width] = jnp.concatenate(rows, axis=0).astype(BF16)


def closure_kernel(hidden, t2, b2, closure, hs):
    count = closure.shape[2]
    for p in range(count + 4):
        store_wide(hs, p, hidden[p].astype(F32))
    out = (jnp.dot(t2[...], stacked(hs, count * Z), preferred_element_type=F32) + b2[...]).astype(BF16)
    for x in range(count):
        closure[0, :, x] = out[:, x * Z:(x + 1) * Z].reshape(CH, 8, Z)


def finish_kernel(norm, total, last, first, second, bias):
    scaled = (total[...].astype(F32) + last[...].astype(F32)) * norm
    flipped = jnp.transpose(scaled)
    first[...] = flipped[:128, :27]
    second[...] = flipped[128:, :27]
    bias[...] = scaled[27:28, :CH]


def call(kernel, outs, name, scratch=(), flops=10_000_000, **specs):
    return pl.pallas_call(
        kernel,
        out_shape=outs,
        **specs,
        scratch_shapes=list(scratch),
        compiler_params=pltpu.CompilerParams(vmem_limit_bytes=48 * 1024 * 1024),
        cost_estimate=pl.CostEstimate(flops=flops, bytes_accessed=1_000_000, transcendentals=0),
        name=name,
    )


def shape(*dims, dtype=BF16):
    return jax.ShapeDtypeStruct(dims, dtype)


def exchange(near, far, axis):
    count = lax.axis_size(axis)
    shifted_pairs = [(i, min(max(i - 1 + 2 * (i % 2), 0), count - 1)) for i in range(count)]
    return lax.ppermute(near, axis, [(i, i ^ 1) for i in range(count)]), lax.ppermute(far, axis, shifted_pairs)


def swap(v, axis, mask):
    return lax.ppermute(v, axis, [(i, i ^ mask) for i in range(lax.axis_size(axis))])


def add(v, w):
    return (v.astype(F32) + w.astype(F32)).astype(BF16)


def local(fields, first_weight, first_bias, second_weight, second_bias, cotangent):
    e1, y1, e2, y2, rows_y, expand = tables()
    er1 = np.tile(e1[:CI, :128].T, (1, CH))
    er2 = np.zeros((2, 256, 256), np.float32)
    for half in range(2):
        er2[half, :128] = np.repeat(e2[:CH, :128].T, CH, axis=1)
        er2[half, 128 + half * 64:192 + half * 64] = np.repeat(e2[:CH, 384:448].T, CH, axis=1)
    e1, e2, er1, er2, expand = (jnp.asarray(v, BF16) for v in (e1, e2, er1, er2, expand))
    y1, y2, rows_y = (jnp.asarray(v, F32) for v in (y1[None], y2[None], rows_y[:, None]))
    planes = fields.shape[2]

    w1 = first_weight.reshape(3, 3, 3, CH, CI).transpose(0, 1, 3, 2, 4).reshape(9 * CH, 3 * CI)
    wb = second_weight.reshape(3, 3, 3, CH, CH)[::-1, ::-1, ::-1].transpose(0, 1, 4, 2, 3).reshape(9 * CH, 3 * CH)
    w1, wb, fields_first, cot_first = lax.optimization_barrier((w1, wb, fields, cotangent))
    near, far = call(
        pack_kernel,
        (shape(512, Z),) * 2,
        "pack_strips",
        (pltpu.VMEM(fields.shape, BF16), pltpu.VMEM(cotangent.shape, BF16), pltpu.SemaphoreType.DMA((2,))),
        in_specs=[pl.BlockSpec(memory_space=pltpu.HBM)] * 2,
    )(fields_first, cot_first)
    xnear, xfar = exchange(near, far, "stream")
    wide = (planes + 4) * Z
    t1, tb, b1 = call(
        band_first_kernel, (shape(192, 1152), shape(128, 1920), shape(192, wide, dtype=F32)), "band_first"
    )(w1, wb, first_bias[None], e1, e2, expand, y1, y2, rows_y)

    counts = (lax.axis_size("stream"), lax.axis_size("radial"))
    t1, tb, b1, xnear, xfar = lax.optimization_barrier((t1, tb, b1, xnear, xfar))
    near, far = call(functools.partial(join_kernel, counts), (shape((2 * planes + 12) * 32, Z),) * 2, "join_strips")(
        fields, cotangent, xnear, xfar)
    rnear, rfar = exchange(near, far, "radial")
    hidden, payload = call(
        functools.partial(first_kernel, counts),
        (shape(planes + 4, 192, Z), shape(32, 384)),
        "gradients",
        (pltpu.VMEM((384, wide + 4 * Z), BF16), pltpu.VMEM((640, wide), BF16)),
        flops=2_000_000_000,
    )(fields, cotangent, xnear, xfar, rnear, rfar, t1, tb, b1, er1, er2, y1, y2, rows_y[:128])

    steps = [(axis, 1 << n) for axis in ("radial", "stream", "snap") for n in range((lax.axis_size(axis) - 1).bit_length())]
    payload, weight = lax.optimization_barrier((payload, second_weight))
    arrived = swap(payload, *steps[0])
    w2 = weight.reshape(3, 3, 3, CH, CH).transpose(0, 1, 3, 2, 4).reshape(9 * CH, 3 * CH)
    t2, b2 = call(band_second_kernel, (shape(128, 1920), shape(128, planes * Z, dtype=F32)), "band_second")(
        w2, second_bias[None], e2, expand, y2, rows_y)
    payload, t2, b2 = lax.optimization_barrier((add(payload, arrived), t2, b2))
    arrived = swap(payload, *steps[1])
    closure = call(
        closure_kernel, shape(*cotangent.shape), "closure", (pltpu.VMEM((640, wide), BF16),), flops=1_000_000_000
    )(hidden, t2, b2)
    for step in steps[2:]:
        payload = add(payload, arrived)
        arrived = swap(payload, *step)

    cells = fields.shape[0] * fields.shape[2] * fields.shape[3] * fields.shape[4]
    for axis in ("stream", "radial", "snap"):
        cells *= lax.axis_size(axis)
    norm = float(1.0 / np.sqrt(np.float32(cells)))
    first, second, bias = call(
        functools.partial(finish_kernel, norm),
        (shape(CH * CI, 27, dtype=F32), shape(CH * CH, 27, dtype=F32), shape(1, CH, dtype=F32)),
        "finish",
    )(payload, arrived)
    first = first.reshape(CH, CI, 27).transpose(2, 0, 1)
    second = second.reshape(CH, CH, 27).transpose(2, 0, 1)
    return (closure, first, second, bias[0])


def solution(mesh):
    split = P("snap", None, "stream", "radial", None)
    return jax.shard_map(
        local,
        mesh=mesh,
        in_specs=(split, P(), P(), P(), P(), split),
        out_specs=(split, P(), P(), P()),
        check_vma=False,
    )
```

```python
import functools

import numpy as np
import jax
import jax.numpy as jnp
from jax import lax
from jax.experimental import pallas as pl
from jax.experimental.pallas import tpu as pltpu
from jax.sharding import PartitionSpec as P

F32 = jnp.float32
BF16 = jnp.bfloat16
Z = 128
CI = 8
CH = 16
FAR = 100


def block(channels, width):
    own = (np.repeat(np.arange(channels), 8), np.tile(np.arange(8), channels))
    rim_c = np.concatenate([np.repeat(np.arange(channels), width)] * 2)
    rim_y = np.concatenate([np.tile(np.arange(-width, 0), channels), np.tile(np.arange(8, 8 + width), channels)])
    return own, (rim_c, rim_y)


def tables():
    own, rim = block(CI, 4)
    e1 = np.zeros((3 * CI, 384), np.float32)
    y1 = np.full(384, FAR)
    for c in range(3):
        for (ch, y), at in ((own, c * 128), (rim, c * 128 + 64)):
            e1[c * CI + ch, at + np.arange(len(ch))] = 1
            y1[at:at + len(ch)] = y
    own, rim = block(CH, 2)
    e2 = np.zeros((3 * CH, 640), np.float32)
    y2 = np.full(640, FAR)
    for c in range(3):
        for (ch, y), at in ((own, c * 128), (rim, 384 + c * 64)):
            e2[c * CH + ch, at + np.arange(len(ch))] = 1
            y2[at:at + len(ch)] = y
    rows_y = np.concatenate([own[1], rim[1]])
    expand = np.zeros((192, CH), np.float32)
    expand[np.arange(192), np.concatenate([own[0], rim[0]])] = 1
    return e1, y1, e2, y2, rows_y, expand


def plane(ref, x):
    v = ref[0, :, x].astype(F32)
    return v.reshape(v.shape[0] * v.shape[1], v.shape[2])


def pick_rows(channels, width):
    half = channels * width
    row = lax.broadcasted_iota(jnp.int32, (2 * half, channels * 8), 0)
    col = lax.broadcasted_iota(jnp.int32, (2 * half, channels * 8), 1)
    side = jnp.where(row >= half, 1, 0)
    q = row - side * half
    return jnp.where(col == (q // width) * 8 + (8 - width) * side + q % width, 1.0, 0.0).astype(BF16)


def partners(index, count):
    return index % 2 == 0, index > 0, index < count - 1


def sides(index, count, near, far):
    near_above, below, above = partners(index, count)
    low = jnp.where(near_above, far, near).astype(F32)
    high = jnp.where(near_above, near, far).astype(F32)
    return jnp.where(below, low, 0.0), jnp.where(above, high, 0.0)


def pack_kernel(fields, cot, near, far, fields_here, cot_here, sems):
    copies = [
        pltpu.make_async_copy(fields, fields_here, sems.at[0]),
        pltpu.make_async_copy(cot, cot_here, sems.at[1]),
    ]
    for copy in copies:
        copy.start()
    for copy in copies:
        copy.wait()
    up_first = lax.axis_index("stream") % 2 == 0
    count = fields.shape[2]
    for here, width, at, rows in ((fields_here, 4, 0, 64), (cot_here, 2, 256, 128)):
        for n in range(width):
            low, high = plane(here, n), plane(here, count - width + n)
            part = slice(at + n * rows, at + (n + 1) * rows)
            near[part] = jnp.where(up_first, high, low).astype(BF16)
            far[part] = jnp.where(up_first, low, high).astype(BF16)


def x_planes(count, fields, cot, xnear, xfar, size):
    index = lax.axis_index("stream")
    inner = [plane(fields, x) for x in range(count)]
    rims = [sides(index, size, xnear[n * 64:(n + 1) * 64], xfar[n * 64:(n + 1) * 64]) for n in range(4)]
    f = [low for low, _ in rims] + inner + [high for _, high in rims]
    inner = [plane(cot, x) for x in range(count)]
    rims = [sides(index, size, xnear[256 + n * 128:384 + n * 128], xfar[256 + n * 128:384 + n * 128]) for n in range(2)]
    return f, [low for low, _ in rims] + inner + [high for _, high in rims]


def join_kernel(counts, fields, cot, xnear, xfar, near, far):
    up_first = lax.axis_index("radial") % 2 == 0
    f, c = x_planes(fields.shape[2], fields, cot, xnear, xfar, counts[0])
    at = 0
    for rows, pick in ((f, pick_rows(CI, 4)), (c, pick_rows(CH, 2))):
        for v in rows:
            got = jnp.dot(pick, v.astype(BF16), preferred_element_type=F32)
            near[at:at + 32] = jnp.where(up_first, got[32:], got[:32]).astype(BF16)
            far[at:at + 32] = jnp.where(up_first, got[:32], got[32:]).astype(BF16)
            at += 32


def band(w, e, expand, ys, rows_y, t):
    rows, width = t.shape[0], e.shape[1]
    wide = jnp.dot(w[...], e[...], preferred_element_type=F32).astype(BF16)
    for a in range(3):
        total = jnp.zeros((rows, width), F32)
        for b in range(3):
            part = jnp.dot(expand[:rows], wide[(a * 3 + b) * CH:(a * 3 + b + 1) * CH], preferred_element_type=F32)
            total = jnp.where(ys[...] == rows_y[:rows] + float(2 * (b - 1)), part, total)
        t[:, a * width:(a + 1) * width] = total.astype(BF16)


def repeat_bias(bias, expand, out):
    column = jnp.sum(expand[:out.shape[0]].astype(F32) * bias[...], axis=1, keepdims=True)
    out[...] = jnp.broadcast_to(column, out.shape)


def band_first_kernel(w1, wb, bias, e1, e2, expand, y1, y2, rows_y, t1, tb, b1):
    band(w1, e1, expand, y1, rows_y, t1)
    band(wb, e2, expand, y2, rows_y, tb)
    repeat_bias(bias, expand, b1)


def band_second_kernel(w2, bias, e2, expand, y2, rows_y, t2, b2):
    band(w2, e2, expand, y2, rows_y, t2)
    repeat_bias(bias, expand, b2)


def shifted(v):
    lane = lax.broadcasted_iota(jnp.int32, v.shape, 1)
    before = jnp.where(lane >= 2, pltpu.roll(v, 2, 1), 0.0)
    after = jnp.where(lane < Z - 2, pltpu.roll(v, Z - 2, 1), 0.0)
    return before.astype(BF16), v.astype(BF16), after.astype(BF16)


def store_wide(ref, p, v):
    at = slice(p * Z, (p + 1) * Z)
    for c, piece in enumerate(shifted(v)):
        ref[c * 128:(c + 1) * 128, at] = piece[:128]
        ref[384 + c * 64:384 + (c + 1) * 64, at] = piece[128:]
    ref[576:, at] = jnp.zeros((64, Z), BF16)


def stacked(ref, lanes):
    return jnp.concatenate([ref[:, a * 256:a * 256 + lanes] for a in range(3)], axis=0)


def first_kernel(counts, fields, cot, xnear, xfar, rnear, rfar, t1, tb, b1, er1, er2, y1, y2, yo,
                 hidden_out, payload, fs, cs):
    count = fields.shape[2]
    lanes = count * Z
    stream, radial = lax.axis_index("stream"), lax.axis_index("radial")
    f, c = x_planes(count, fields, cot, xnear, xfar, counts[0])
    at = 0
    for p, v in enumerate(f):
        low, high = sides(radial, counts[1], rnear[at:at + 32], rfar[at:at + 32])
        for n, piece in enumerate(shifted(jnp.concatenate([v, low, high], axis=0))):
            fs[n * 128:(n + 1) * 128, p * Z:(p + 1) * Z] = piece
        at += 32
    for p, v in enumerate(c):
        low, high = sides(radial, counts[1], rnear[at:at + 32], rfar[at:at + 32])
        store_wide(cs, p, jnp.concatenate([v, low, high], axis=0))
        at += 32
    pre = jnp.dot(t1[...], stacked(fs, lanes + 4 * Z), preferred_element_type=F32) + b1[...]
    share = 0.5 * (1.0 + lax.erf(pre * 0.7071067811865476))
    hidden = (pre * share).astype(BF16)
    zero = jnp.zeros((), BF16)
    rims = (jnp.where(radial > 0, hidden[128:160], zero), jnp.where(radial < counts[1] - 1, hidden[160:], zero))
    for p in range(count + 4):
        at = slice(p * Z, (p + 1) * Z)
        rows = jnp.concatenate([hidden[:128, at], rims[0][:, at], rims[1][:, at]], axis=0)
        if p < 2:
            rows = jnp.where(stream > 0, rows, zero)
        elif p >= count + 2:
            rows = jnp.where(stream < counts[0] - 1, rows, zero)
        hidden_out[p] = rows
    at = slice(2 * Z, 2 * Z + lanes)
    pre, share, hidden = pre[:128, at], share[:128, at], hidden[:128, at]
    back = jnp.dot(tb[...], stacked(cs, lanes), preferred_element_type=F32)
    dpre = (back * (share + pre * jnp.exp(-0.5 * pre * pre) * 0.3989422804014327)).astype(BF16)
    bias = jnp.sum(dpre.astype(F32), axis=1, keepdims=True)
    lane = lax.broadcasted_iota(jnp.int32, (8, 256), 1)

    def diagonal(rows, place):
        total = jnp.zeros((8, rows.shape[1]), F32)
        for o in range(CH):
            total = jnp.where(place == o, rows[o * 8:(o + 1) * 8], total)
        return jnp.sum(total, axis=0, keepdims=True)

    ones, twos = [None] * 32, [None] * 32
    ones[27] = diagonal(jnp.broadcast_to(bias, (128, 128)), lane[:, :128])
    over_lanes = (((1,), (1,)), ((), ()))
    for a in range(3):
        g1 = lax.dot_general(dpre, fs[:, (a + 1) * 256:(a + 1) * 256 + lanes], over_lanes, preferred_element_type=F32)
        g2 = lax.dot_general(hidden, cs[:, a * 256:a * 256 + lanes], over_lanes, preferred_element_type=F32)
        for b in range(3):
            off = float(2 * (b - 1))
            one = jnp.where(y1[...] == yo[...] + off, g1, 0.0).astype(BF16)
            two = jnp.where(y2[...] == yo[...] + off, g2, 0.0).astype(BF16)
            for c in range(3):
                tap = (a * 3 + b) * 3 + c
                r1 = jnp.dot(one[:, c * 128:(c + 1) * 128], er1[...], preferred_element_type=F32)
                rim = 384 + (c // 2) * 128
                both = jnp.concatenate([two[:, c * 128:(c + 1) * 128], two[:, rim:rim + 128]], axis=1)
                r2 = jnp.dot(both, er2[c % 2], preferred_element_type=F32)
                ones[tap] = diagonal(r1, lane[:, :128] // CI)
                twos[26 - tap] = diagonal(r2, lane % CH)
    for rows, at, width in ((ones, 0, 128), (twos, 128, 256)):
        rows = [jnp.zeros((1, width), F32) if v is None else v for v in rows]
        payload[:, at:at + width] = jnp.concatenate(rows, axis=0).astype(BF16)


def closure_kernel(hidden, t2, b2, closure, hs):
    count = closure.shape[2]
    for p in range(count + 4):
        store_wide(hs, p, hidden[p].astype(F32))
    out = (jnp.dot(t2[...], stacked(hs, count * Z), preferred_element_type=F32) + b2[...]).astype(BF16)
    for x in range(count):
        closure[0, :, x] = out[:, x * Z:(x + 1) * Z].reshape(CH, 8, Z)


def finish_kernel(norm, total, last, first, second, bias):
    scaled = (total[...].astype(F32) + last[...].astype(F32)) * norm
    flipped = jnp.transpose(scaled)
    first[...] = flipped[:128, :27]
    second[...] = flipped[128:, :27]
    bias[...] = scaled[27:28, :CH]


def call(kernel, outs, name, scratch=(), flops=10_000_000, **specs):
    return pl.pallas_call(
        kernel,
        out_shape=outs,
        **specs,
        scratch_shapes=list(scratch),
        compiler_params=pltpu.CompilerParams(vmem_limit_bytes=48 * 1024 * 1024),
        cost_estimate=pl.CostEstimate(flops=flops, bytes_accessed=1_000_000, transcendentals=0),
        name=name,
    )


def shape(*dims, dtype=BF16):
    return jax.ShapeDtypeStruct(dims, dtype)


def exchange(near, far, axis):
    count = lax.axis_size(axis)
    shifted_pairs = [(i, min(max(i - 1 + 2 * (i % 2), 0), count - 1)) for i in range(count)]
    return lax.ppermute(near, axis, [(i, i ^ 1) for i in range(count)]), lax.ppermute(far, axis, shifted_pairs)


def swap(v, axis, mask):
    return lax.ppermute(v, axis, [(i, i ^ mask) for i in range(lax.axis_size(axis))])


def add(v, w):
    return (v.astype(F32) + w.astype(F32)).astype(BF16)


def gather(v, axis):
    count = lax.axis_size(axis)
    return lax.all_to_all(jnp.broadcast_to(v[None], (count, *v.shape)), axis, 0, 0)


def merge(parts):
    return jnp.sum(parts.astype(F32), axis=0).astype(BF16)


def local(fields, first_weight, first_bias, second_weight, second_bias, cotangent):
    e1, y1, e2, y2, rows_y, expand = tables()
    er1 = np.tile(e1[:CI, :128].T, (1, CH))
    er2 = np.zeros((2, 256, 256), np.float32)
    for half in range(2):
        er2[half, :128] = np.repeat(e2[:CH, :128].T, CH, axis=1)
        er2[half, 128 + half * 64:192 + half * 64] = np.repeat(e2[:CH, 384:448].T, CH, axis=1)
    e1, e2, er1, er2, expand = (jnp.asarray(v, BF16) for v in (e1, e2, er1, er2, expand))
    y1, y2, rows_y = (jnp.asarray(v, F32) for v in (y1[None], y2[None], rows_y[:, None]))
    planes = fields.shape[2]

    w1 = first_weight.reshape(3, 3, 3, CH, CI).transpose(0, 1, 3, 2, 4).reshape(9 * CH, 3 * CI)
    wb = second_weight.reshape(3, 3, 3, CH, CH)[::-1, ::-1, ::-1].transpose(0, 1, 4, 2, 3).reshape(9 * CH, 3 * CH)
    w1, wb, fields_first, cot_first = lax.optimization_barrier((w1, wb, fields, cotangent))
    near, far = call(
        pack_kernel,
        (shape(512, Z),) * 2,
        "pack_strips",
        (pltpu.VMEM(fields.shape, BF16), pltpu.VMEM(cotangent.shape, BF16), pltpu.SemaphoreType.DMA((2,))),
        in_specs=[pl.BlockSpec(memory_space=pltpu.HBM)] * 2,
    )(fields_first, cot_first)
    xnear, xfar = exchange(near, far, "stream")
    wide = (planes + 4) * Z
    t1, tb, b1 = call(
        band_first_kernel, (shape(192, 1152), shape(128, 1920), shape(192, wide, dtype=F32)), "band_first"
    )(w1, wb, first_bias[None], e1, e2, expand, y1, y2, rows_y)

    counts = (lax.axis_size("stream"), lax.axis_size("radial"))
    t1, tb, b1, xnear, xfar = lax.optimization_barrier((t1, tb, b1, xnear, xfar))
    near, far = call(functools.partial(join_kernel, counts), (shape((2 * planes + 12) * 32, Z),) * 2, "join_strips")(
        fields, cotangent, xnear, xfar)
    rnear, rfar = exchange(near, far, "radial")
    hidden, payload = call(
        functools.partial(first_kernel, counts),
        (shape(planes + 4, 192, Z), shape(32, 384)),
        "gradients",
        (pltpu.VMEM((384, wide + 4 * Z), BF16), pltpu.VMEM((640, wide), BF16)),
        flops=2_000_000_000,
    )(fields, cotangent, xnear, xfar, rnear, rfar, t1, tb, b1, er1, er2, y1, y2, rows_y[:128])

    payload, weight = lax.optimization_barrier((payload, second_weight))
    parts = gather(payload, "radial")
    w2 = weight.reshape(3, 3, 3, CH, CH).transpose(0, 1, 3, 2, 4).reshape(9 * CH, 3 * CH)
    t2, b2 = call(band_second_kernel, (shape(128, 1920), shape(128, planes * Z, dtype=F32)), "band_second")(
        w2, second_bias[None], e2, expand, y2, rows_y)
    payload, t2, b2 = lax.optimization_barrier((merge(parts), t2, b2))
    parts = gather(payload, "stream")
    closure = call(
        closure_kernel, shape(*cotangent.shape), "closure", (pltpu.VMEM((640, wide), BF16),), flops=1_000_000_000
    )(hidden, t2, b2)
    payload = merge(parts)
    for n in range((lax.axis_size("snap") - 1).bit_length()):
        if n:
            payload = add(payload, arrived)
        arrived = swap(payload, "snap", 1 << n)

    cells = fields.shape[0] * fields.shape[2] * fields.shape[3] * fields.shape[4]
    for axis in ("stream", "radial", "snap"):
        cells *= lax.axis_size(axis)
    norm = float(1.0 / np.sqrt(np.float32(cells)))
    first, second, bias = call(
        functools.partial(finish_kernel, norm),
        (shape(CH * CI, 27, dtype=F32), shape(CH * CH, 27, dtype=F32), shape(1, CH, dtype=F32)),
        "finish",
    )(payload, arrived)
    first = first.reshape(CH, CI, 27).transpose(2, 0, 1)
    second = second.reshape(CH, CH, 27).transpose(2, 0, 1)
    return (closure, first, second, bias[0])


def solution(mesh):
    split = P("snap", None, "stream", "radial", None)
    return jax.shard_map(
        local,
        mesh=mesh,
        in_specs=(split, P(), P(), P(), P(), split),
        out_specs=(split, P(), P(), P()),
        check_vma=False,
    )
```

```python
import functools

import numpy as np
import jax
import jax.numpy as jnp
from jax import lax
from jax.experimental import pallas as pl
from jax.experimental.pallas import tpu as pltpu
from jax.sharding import PartitionSpec as P

F32 = jnp.float32
BF16 = jnp.bfloat16
Z = 128
CI = 8
CH = 16
FAR = 100


def block(channels, width, y_first=False):
    own = (np.repeat(np.arange(channels), 8), np.tile(np.arange(8), channels))
    if y_first:
        own = (np.tile(np.arange(channels), 8), np.repeat(np.arange(8), channels))
    rim_c = np.concatenate([np.repeat(np.arange(channels), width)] * 2)
    rim_y = np.concatenate([np.tile(np.arange(-width, 0), channels), np.tile(np.arange(8, 8 + width), channels)])
    return own, (rim_c, rim_y)


def lanes_of(channels, total, places):
    e = np.zeros((3 * channels, total), np.float32)
    ys = np.full((1, total), FAR, np.float32)
    for c in range(3):
        for (ch, y), start, step in places:
            at = start + c * step + np.arange(len(ch))
            e[c * channels + ch, at] = 1
            ys[0, at] = y
    return e, ys


def rows_of(own, rim):
    ch, y = (np.concatenate([a, b]) for a, b in zip(own, rim))
    return np.eye(CH, dtype=np.float32)[ch], y[:, None].astype(np.float32)


def plane(ref, x):
    v = ref[0, :, x].astype(F32)
    return v.reshape(v.shape[0] * v.shape[1], v.shape[2])


def pick_rows(channels, width):
    half = channels * width
    row = lax.broadcasted_iota(jnp.int32, (2 * half, channels * 8), 0)
    col = lax.broadcasted_iota(jnp.int32, (2 * half, channels * 8), 1)
    side = jnp.where(row >= half, 1, 0)
    q = row - side * half
    return jnp.where(col == (q // width) * 8 + (8 - width) * side + q % width, 1.0, 0.0).astype(BF16)


def partners(index, count):
    return index % 2 == 0, index > 0, index < count - 1


def sides(index, count, near, far):
    near_above, below, above = partners(index, count)
    low = jnp.where(near_above, far, near).astype(F32)
    high = jnp.where(near_above, near, far).astype(F32)
    return jnp.where(below, low, 0.0), jnp.where(above, high, 0.0)


def strips(here, width, near, far, at):
    up_first = lax.axis_index("stream") % 2 == 0
    count, rows = here.shape[2], here.shape[1] * here.shape[3]
    for n in range(width):
        low, high = plane(here, n), plane(here, count - width + n)
        part = slice(at + n * rows, at + (n + 1) * rows)
        near[part] = jnp.where(up_first, high, low).astype(BF16)
        far[part] = jnp.where(up_first, low, high).astype(BF16)


def pack_kernel(fields, cot, near, far):
    strips(fields, 4, near, far, 0)
    strips(cot, 2, near, far, 256)


def x_planes(count, fields, cot, xnear, xfar, size):
    index = lax.axis_index("stream")
    inner = [plane(fields, x) for x in range(count)]
    rims = [sides(index, size, xnear[n * 64:(n + 1) * 64], xfar[n * 64:(n + 1) * 64]) for n in range(4)]
    f = [low for low, _ in rims] + inner + [high for _, high in rims]
    inner = [plane(cot, x) for x in range(count)]
    rims = [sides(index, size, xnear[256 + n * 128:384 + n * 128], xfar[256 + n * 128:384 + n * 128]) for n in range(2)]
    return f, [low for low, _ in rims] + inner + [high for _, high in rims]


def join_kernel(counts, fields, cot, xnear, xfar, near, far):
    up_first = lax.axis_index("radial") % 2 == 0
    f, c = x_planes(fields.shape[2], fields, cot, xnear, xfar, counts[0])
    at = 0
    for rows, pick in ((f, pick_rows(CI, 4)), (c, pick_rows(CH, 2))):
        for v in rows:
            got = jnp.dot(pick, v.astype(BF16), preferred_element_type=F32)
            near[at:at + 32] = jnp.where(up_first, got[32:], got[:32]).astype(BF16)
            far[at:at + 32] = jnp.where(up_first, got[:32], got[32:]).astype(BF16)
            at += 32


def band(w, e, expand, ys, rows_y, t):
    rows, width = t.shape[0], e.shape[1]
    wide = jnp.dot(w[...], e[...], preferred_element_type=F32).astype(BF16)
    for a in range(3):
        total = jnp.zeros((rows, width), F32)
        for b in range(3):
            part = jnp.dot(expand[:rows], wide[(a * 3 + b) * CH:(a * 3 + b + 1) * CH], preferred_element_type=F32)
            total = jnp.where(ys[...] == rows_y[:rows] + float(2 * (b - 1)), part, total)
        t[:, a * width:(a + 1) * width] = total.astype(BF16)


def repeat_bias(bias, expand, out):
    column = jnp.sum(expand[:out.shape[0]].astype(F32) * bias[...], axis=1, keepdims=True)
    out[...] = jnp.broadcast_to(column, out.shape)


def band_first_kernel(w1, wb, bias, e1o, e1r, e2o, e2r, expand, y1o, y1r, y2o, y2r, rows_y, t1o, t1r, tbo, tbr, b1):
    band(w1, e1o, expand, y1o, rows_y, t1o)
    band(w1, e1r, expand, y1r, rows_y, t1r)
    band(wb, e2o, expand, y2o, rows_y, tbo)
    band(wb, e2r, expand, y2r, rows_y, tbr)
    repeat_bias(bias, expand, b1)


def band_second_kernel(w2, bias, e2, expand, y2, rows_y, t2, b2):
    band(w2, e2, expand, y2, rows_y, t2)
    repeat_bias(bias, expand, b2)


def shifted(v):
    lane = lax.broadcasted_iota(jnp.int32, v.shape, 1)
    before = jnp.where(lane >= 2, pltpu.roll(v, 2, 1), 0.0)
    after = jnp.where(lane < Z - 2, pltpu.roll(v, Z - 2, 1), 0.0)
    return before.astype(BF16), v.astype(BF16), after.astype(BF16)


def store_wide(ref, p, v):
    at = slice(p * Z, (p + 1) * Z)
    for c, piece in enumerate(shifted(v)):
        ref[c * 128:(c + 1) * 128, at] = piece[:128]
        ref[384 + c * 64:384 + (c + 1) * 64, at] = piece[128:]
    ref[576:, at] = jnp.zeros((64, Z), BF16)


def stacked(ref, lanes):
    return jnp.concatenate([ref[:, a * 256:a * 256 + lanes] for a in range(3)], axis=0)


def own_kernel(counts, fields, cot, xnear, xfar, t1, tb, b1, fs, cs, pre, back):
    count = fields.shape[2]
    f, c = x_planes(count, fields, cot, xnear, xfar, counts[0])
    for ref, rows in ((fs, f), (cs, c)):
        for p, v in enumerate(rows):
            for n, piece in enumerate(shifted(v)):
                ref[n * v.shape[0]:(n + 1) * v.shape[0], p * Z:(p + 1) * Z] = piece
    fs[192:] = jnp.zeros((64, fs.shape[1]), BF16)
    pre[...] = jnp.dot(t1[...], stacked(fs, pre.shape[1]), preferred_element_type=F32) + b1[...]
    back[...] = jnp.dot(tb[...], stacked(cs, back.shape[1]), preferred_element_type=F32)


def two_dots(v, w):
    high = v.astype(BF16)
    low = (v - high.astype(F32)).astype(BF16)
    return jnp.dot(high, w, preferred_element_type=F32) + jnp.dot(low, w, preferred_element_type=F32)


def rim_kernel(counts, rnear, rfar, fs, cs, pre_own, back_own, t1, tb, e1t, e2t, rep1, rep2, y1, y2,
               hidden_out, payload, fr, cr, taps):
    count = hidden_out.shape[0] - 4
    lanes = count * Z
    stream, radial = lax.axis_index("stream"), lax.axis_index("radial")
    at = 0
    for ref in (fr, cr):
        for p in range(ref.shape[1] // Z):
            low, high = sides(radial, counts[1], rnear[at:at + 32], rfar[at:at + 32])
            for n, piece in enumerate(shifted(jnp.concatenate([low, high], axis=0))):
                ref[n * 64:(n + 1) * 64, p * Z:(p + 1) * Z] = piece
            at += 32
        ref[192:] = jnp.zeros((64, ref.shape[1]), BF16)
    pre = pre_own[...] + jnp.dot(t1[...], stacked(fr, lanes + 4 * Z), preferred_element_type=F32)
    share = 0.5 * (1.0 + lax.erf(pre * 0.7071067811865476))
    hidden = (pre * share).astype(BF16)
    zero = jnp.zeros((), BF16)
    rims = (jnp.where(radial > 0, hidden[128:160], zero), jnp.where(radial < counts[1] - 1, hidden[160:], zero))
    for p in range(count + 4):
        at = slice(p * Z, (p + 1) * Z)
        rows = jnp.concatenate([hidden[:128, at], rims[0][:, at], rims[1][:, at]], axis=0)
        if p < 2:
            rows = jnp.where(stream > 0, rows, zero)
        elif p >= count + 2:
            rows = jnp.where(stream < counts[0] - 1, rows, zero)
        hidden_out[p] = rows
    at = slice(2 * Z, 2 * Z + lanes)
    pre, share, hidden = pre[:128, at], share[:128, at], hidden[:128, at]
    back = back_own[...] + jnp.dot(tb[...], stacked(cr, lanes), preferred_element_type=F32)
    dpre = (back * (share + pre * jnp.exp(-0.5 * pre * pre) * 0.3989422804014327)).astype(BF16)
    over_lanes = (((1,), (1,)), ((), ()))
    ones, twos = [], []
    for a in range(3):
        at = slice((a + 1) * 256, (a + 1) * 256 + lanes)
        rows = [ref[n * 64:(n + 1) * 64, at] for n in range(3) for ref in (fs, fr)]
        g1 = lax.dot_general(dpre, jnp.concatenate(rows, axis=0), over_lanes, preferred_element_type=F32)
        at = slice(a * 256, a * 256 + lanes)
        rows = jnp.concatenate([cs[:, at], cr[:, at]], axis=0)
        g2 = lax.dot_general(hidden, rows, over_lanes, preferred_element_type=F32)
        for b in range(3):
            for g, ys, out in ((g1, y1, ones), (g2, y2, twos)):
                total = jnp.zeros((CH, g.shape[1]), F32)
                for y in range(8):
                    total = jnp.where(ys[...] == float(y + 2 * (b - 1)), g[y * CH:(y + 1) * CH], total)
                out.append(total)
    taps[:, 24:] = jnp.zeros((3, 8, 128), F32)
    for parts, et, rep, at, width in ((ones, e1t, rep1, 0, 128), (twos[::-1], e2t, rep2, 1, 256)):
        sums = two_dots(jnp.concatenate(parts, axis=0), et[...])
        wide = two_dots(sums, rep[...])
        row = lax.broadcasted_iota(jnp.int32, wide.shape, 0) % CH
        lane = lax.broadcasted_iota(jnp.int32, wide.shape, 1) % width
        mine = row == (lane // CI if width == 128 else lane % CH)
        total = jnp.sum(jnp.where(mine, wide, 0.0).reshape(9, CH, 3 * width), axis=1)
        for c in range(3):
            first = c if width == 128 else 2 - c
            for n in range(width // 128):
                taps[at + n, pl.ds(first, 9, stride=3)] = total[:, c * width + n * 128:c * width + (n + 1) * 128]
    bias = jnp.sum(dpre.astype(F32), axis=1, keepdims=True)
    bias = sum(bias[y * CH:(y + 1) * CH] for y in range(8))
    row = lax.broadcasted_iota(jnp.int32, (CH, 128), 0)
    lane = lax.broadcasted_iota(jnp.int32, (CH, 128), 1)
    taps[0, 27:28] = jnp.sum(jnp.where(row == lane, bias, 0.0), axis=0, keepdims=True)
    payload[...] = jnp.concatenate([taps[n] for n in range(3)], axis=1)


def closure_kernel(hidden, t2, b2, closure, hs):
    count = closure.shape[2]
    for p in range(count + 4):
        store_wide(hs, p, hidden[p].astype(F32))
    out = (jnp.dot(t2[...], stacked(hs, count * Z), preferred_element_type=F32) + b2[...]).astype(BF16)
    for x in range(count):
        closure[0, :, x] = out[:, x * Z:(x + 1) * Z].reshape(CH, 8, Z)


def add_kernel(here, there, total):
    s = here[...].astype(F32) + there[...].astype(F32)
    lost = s - s.astype(BF16).astype(F32)
    row = lax.broadcasted_iota(jnp.int32, s.shape, 0)
    total[...] = (s + jnp.where(row == 28, pltpu.roll(lost, 1, 0), 0.0)).astype(BF16)


def finish_kernel(norm, total, last, first, second, bias):
    scaled = (total[...].astype(F32) + last[...].astype(F32)) * norm
    flipped = jnp.transpose(scaled)
    first[...] = flipped[:128, :27]
    second[...] = flipped[128:, :27]
    bias[...] = scaled[27:28, :CH] + scaled[28:29, :CH]


def call(kernel, outs, name, scratch=(), flops=10_000_000, **specs):
    return pl.pallas_call(
        kernel,
        out_shape=outs,
        **specs,
        scratch_shapes=list(scratch),
        compiler_params=pltpu.CompilerParams(vmem_limit_bytes=48 * 1024 * 1024),
        cost_estimate=pl.CostEstimate(flops=flops, bytes_accessed=1_000_000, transcendentals=0),
        name=name,
    )


def shape(*dims, dtype=BF16):
    return jax.ShapeDtypeStruct(dims, dtype)


def exchange(near, far, axis):
    count = lax.axis_size(axis)
    shifted_pairs = [(i, min(max(i - 1 + 2 * (i % 2), 0), count - 1)) for i in range(count)]
    far = lax.ppermute(far, axis, shifted_pairs)
    return lax.ppermute(near, axis, [(i, i ^ 1) for i in range(count)]), far


def swap(v, axis, mask):
    return lax.ppermute(v, axis, [(i, i ^ mask) for i in range(lax.axis_size(axis))])


def add(v, w):
    return call(add_kernel, shape(*v.shape), "add_parts")(v, w)


def local(fields, first_weight, first_bias, second_weight, second_bias, cotangent):
    own, rim = block(CI, 4)
    e1, y1 = lanes_of(CI, 384, ((own, 0, 128), (rim, 64, 128)))
    e1o, y1o = lanes_of(CI, 256, ((own, 0, 64),))
    e1r, y1r = lanes_of(CI, 256, ((rim, 0, 64),))
    own, rim = block(CH, 2)
    e2, y2 = lanes_of(CH, 640, ((own, 0, 128), (rim, 384, 64)))
    e2o, y2o, e2r, y2r = e2[:, :384], y2[:, :384], e2[:, 384:], y2[:, 384:]
    expand2, rows_y2 = rows_of(own, rim)
    own, _ = block(CH, 2, y_first=True)
    e2h, y2h = lanes_of(CH, 640, ((own, 0, 128), (rim, 384, 64)))
    expand1, rows_y1 = rows_of(own, rim)
    e1t, e2t = np.zeros((384, 128), np.float32), np.zeros((640, 128), np.float32)
    e1t[:, :3 * CI], e2t[:, :3 * CH] = e1.T, e2.T
    rep1, rep2 = np.zeros((128, 384), np.float32), np.zeros((128, 768), np.float32)
    for c in range(3):
        rep1[c * CI:(c + 1) * CI, c * 128:(c + 1) * 128] = np.tile(np.eye(CI), (1, CH))
        rep2[c * CH:(c + 1) * CH, c * 256:(c + 1) * 256] = np.repeat(np.eye(CH), CH, axis=1)

    def const(*arrays, dtype=BF16):
        return [jnp.asarray(v, dtype) for v in arrays]

    planes = fields.shape[2]

    w1 = first_weight.reshape(3, 3, 3, CH, CI).transpose(0, 1, 3, 2, 4).reshape(9 * CH, 3 * CI)
    near, far = call(pack_kernel, (shape(512, Z),) * 2, "pack_strips")(fields, cotangent)
    xnear, xfar = exchange(near, far, "stream")
    wide = (planes + 4) * Z
    counts = (lax.axis_size("stream"), lax.axis_size("radial"))
    near, far = call(functools.partial(join_kernel, counts), (shape((2 * planes + 12) * 32, Z),) * 2, "join_strips")(
        fields, cotangent, xnear, xfar)
    near, far, weight = lax.optimization_barrier((near, far, second_weight))
    rnear, rfar = exchange(near, far, "radial")
    wb = weight.reshape(3, 3, 3, CH, CH)[::-1, ::-1, ::-1].transpose(0, 1, 4, 2, 3).reshape(9 * CH, 3 * CH)
    t1o, t1r, tbo, tbr, b1 = call(
        band_first_kernel,
        (shape(192, 768), shape(192, 768), shape(128, 1152), shape(128, 768), shape(192, wide, dtype=F32)),
        "band_first",
    )(w1, wb, first_bias[None], *const(e1o, e1r, e2o, e2r, expand1), *const(y1o, y1r, y2o, y2r, rows_y1, dtype=F32))
    fs, cs, pre, back = call(
        functools.partial(own_kernel, counts),
        (shape(256, wide + 4 * Z), shape(384, wide), shape(192, wide, dtype=F32), shape(128, planes * Z, dtype=F32)),
        "own_rows",
        flops=1_000_000_000,
    )(fields, cotangent, xnear, xfar, t1o, tbo, b1)
    hidden, payload = call(
        functools.partial(rim_kernel, counts),
        (shape(planes + 4, 192, Z), shape(32, 384, dtype=F32)),
        "gradients",
        (pltpu.VMEM((256, wide + 4 * Z), BF16), pltpu.VMEM((256, wide), BF16), pltpu.VMEM((3, 32, 128), F32)),
        flops=2_000_000_000,
    )(rnear, rfar, fs, cs, pre, back, t1r, tbr, *const(e1t, e2t, rep1, rep2), *const(y1, y2, dtype=F32))

    steps = [(axis, 1 << n) for axis in ("radial", "stream", "snap") for n in range((lax.axis_size(axis) - 1).bit_length())]
    payload, weight = lax.optimization_barrier((payload, second_weight))
    arrived = swap(payload, *steps[0])
    w2 = weight.reshape(3, 3, 3, CH, CH).transpose(0, 1, 3, 2, 4).reshape(9 * CH, 3 * CH)
    t2, b2 = call(band_second_kernel, (shape(128, 1920), shape(128, planes * Z, dtype=F32)), "band_second")(
        w2, second_bias[None], *const(e2h, expand2), *const(y2h, rows_y2, dtype=F32))
    payload, t2, b2 = lax.optimization_barrier((add(payload, arrived), t2, b2))
    arrived = swap(payload, *steps[1])
    closure = call(
        closure_kernel, shape(*cotangent.shape), "closure", (pltpu.VMEM((640, wide), BF16),), flops=1_000_000_000
    )(hidden, t2, b2)
    for step in steps[2:]:
        payload = add(payload, arrived)
        arrived = swap(payload, *step)

    cells = fields.shape[0] * fields.shape[2] * fields.shape[3] * fields.shape[4]
    for axis in ("stream", "radial", "snap"):
        cells *= lax.axis_size(axis)
    norm = float(1.0 / np.sqrt(np.float32(cells)))
    first, second, bias = call(
        functools.partial(finish_kernel, norm),
        (shape(CH * CI, 27, dtype=F32), shape(CH * CH, 27, dtype=F32), shape(1, CH, dtype=F32)),
        "finish",
    )(payload, arrived)
    first = first.reshape(CH, CI, 27).transpose(2, 0, 1)
    second = second.reshape(CH, CH, 27).transpose(2, 0, 1)
    return (closure, first, second, bias[0])


def solution(mesh):
    split = P("snap", None, "stream", "radial", None)
    return jax.shard_map(
        local,
        mesh=mesh,
        in_specs=(split, P(), P(), P(), P(), split),
        out_specs=(split, P(), P(), P()),
        check_vma=False,
    )
```

```python
import functools

import numpy as np
import jax
import jax.numpy as jnp
from jax import lax
from jax.experimental import pallas as pl
from jax.experimental.pallas import tpu as pltpu
from jax.sharding import PartitionSpec as P

F32 = jnp.float32
BF16 = jnp.bfloat16
Z = 128
CI = 8
CH = 16
FAR = 100


def natural(n):
    return n // 8, n % 8


def y_first(n):
    return n % CH, n // CH


def rim(width):
    def of(n):
        side, n = n // 32, n % 32
        return n // width, n % width + side * (8 + width) - width
    return of


def table(channels, total, places):
    e = np.zeros((total, 128), np.float32)
    ys = np.full((1, total), FAR, np.float32)
    for c in range(3):
        for of, count, start in places:
            ch, y = of(np.arange(count))
            at = start + c * (128 if start == 0 or channels == CI else 64) + np.arange(count)
            e[at, c * channels + ch] = 1
            ys[0, at] = y
    return e, ys


def iota(rows, columns):
    return [lax.broadcasted_iota(jnp.int32, (rows, columns), d) for d in range(2)]


def one_hot(where):
    return jnp.where(where, 1.0, 0.0).astype(BF16)


def lane_y(of, width, step):
    lane = lax.broadcasted_iota(jnp.int32, (1, width), 1)
    return jnp.where(lane < 3 * step, of(lane % step)[1], FAR)


def place(rows, wanted, of, side=None):
    row, lane = iota(rows, 128)
    if side is None:
        return one_hot(of(lane)[0] == wanted(row))
    return one_hot((of(lane % 64)[0] == wanted(row)) & (lane // 64 == side))


def row_table(rows, own):
    row, lane = iota(rows, CH)
    own_c, own_y = own(row)
    rim_c, rim_y = rim(2)(row - 128)
    channel, y = jnp.where(row < 128, own_c, rim_c), jnp.where(row < 128, own_y, rim_y)
    return one_hot(channel == lane), y[:, :1]


def plane(ref, x):
    v = ref[0, :, x].astype(F32)
    return v.reshape(v.shape[0] * v.shape[1], v.shape[2])


def pick_rows(channels, width):
    half = channels * width
    row = lax.broadcasted_iota(jnp.int32, (2 * half, channels * 8), 0)
    col = lax.broadcasted_iota(jnp.int32, (2 * half, channels * 8), 1)
    side = jnp.where(row >= half, 1, 0)
    q = row - side * half
    return jnp.where(col == (q // width) * 8 + (8 - width) * side + q % width, 1.0, 0.0).astype(BF16)


def partners(index, count):
    return index % 2 == 0, index > 0, index < count - 1


def sides(index, count, near, far):
    near_above, below, above = partners(index, count)
    low = jnp.where(near_above, far, near).astype(F32)
    high = jnp.where(near_above, near, far).astype(F32)
    return jnp.where(below, low, 0.0), jnp.where(above, high, 0.0)


def pack_kernel(fields, cot, near, far, f_rows, c_rows):
    up_first = lax.axis_index("stream") % 2 == 0
    count, at = fields.shape[2], 0
    for ref, out, width in ((fields, f_rows, 4), (cot, c_rows, 2)):
        rows = [plane(ref, x) for x in range(count)]
        for x, v in enumerate(rows):
            out[x] = v.astype(BF16)
        for low, high in zip(rows[:width], rows[count - width:]):
            part = slice(at, at + low.shape[0])
            near[part] = jnp.where(up_first, high, low).astype(BF16)
            far[part] = jnp.where(up_first, low, high).astype(BF16)
            at += low.shape[0]


def x_planes(count, fields, cot, xnear, xfar, size):
    index = lax.axis_index("stream")
    inner = [fields[x].astype(F32) for x in range(count)]
    rims = [sides(index, size, xnear[n * 64:(n + 1) * 64], xfar[n * 64:(n + 1) * 64]) for n in range(4)]
    f = [low for low, _ in rims] + inner + [high for _, high in rims]
    inner = [cot[x].astype(F32) for x in range(count)]
    rims = [sides(index, size, xnear[256 + n * 128:384 + n * 128], xfar[256 + n * 128:384 + n * 128]) for n in range(2)]
    return f, [low for low, _ in rims] + inner + [high for _, high in rims]


def join_kernel(counts, xfar, xnear, fields, cot, near, far):
    up_first = lax.axis_index("radial") % 2 == 0
    f, c = x_planes(fields.shape[0], fields, cot, xnear, xfar, counts[0])
    at = 0
    for rows, pick in ((f, pick_rows(CI, 4)), (c, pick_rows(CH, 2))):
        for v in rows:
            got = jnp.dot(pick, v.astype(BF16), preferred_element_type=F32)
            near[at:at + 32] = jnp.where(up_first, got[32:], got[:32]).astype(BF16)
            far[at:at + 32] = jnp.where(up_first, got[:32], got[32:]).astype(BF16)
            at += 32


def spread(w, by_row, flip):
    taps = jnp.transpose(w[...].astype(F32))
    width = taps.shape[1]
    row = lax.broadcasted_iota(jnp.int32, (CH, width), 0)
    lane = lax.broadcasted_iota(jnp.int32, (CH, width), 1)
    mine = row == (lane // (width // CH) if by_row else lane % CH)
    found = []
    for c in range(3):
        rows = []
        for ab in range(9):
            t = 26 - (ab * 3 + c) if flip else ab * 3 + c
            rows.append(jnp.where(mine, jnp.broadcast_to(taps[t:t + 1], (CH, width)), 0.0))
        found.append(jnp.concatenate(rows, axis=0).astype(BF16))
    return found


def dots(pairs):
    total = None
    for v, w in pairs:
        part = jnp.dot(v, w, preferred_element_type=F32)
        total = part if total is None else total + part
    return total.astype(BF16)


def halves(parts, wanted, of):
    left, right = (place(parts[0].shape[1], wanted, of, side) for side in range(2))
    return jnp.concatenate([dots([(parts[0], left), (parts[1], right)]), dots([(parts[2], left)])], axis=1)


def wholes(parts, wanted, of):
    at = place(parts[0].shape[1], wanted, of)
    return jnp.concatenate([dots([(v, at)]) for v in parts], axis=1)


def band(wide, expand, ys, rows_y, t):
    rows, width = t.shape[0], wide.shape[1]
    for a in range(3):
        total = jnp.zeros((rows, width), F32)
        for b in range(3):
            part = jnp.dot(expand[:rows], wide[(a * 3 + b) * CH:(a * 3 + b + 1) * CH], preferred_element_type=F32)
            total = jnp.where(ys == rows_y[:rows] + 2 * (b - 1), part, total)
        t[:, a * width:(a + 1) * width] = total.astype(BF16)


def repeat_bias(bias, expand, out):
    column = jnp.sum(expand.astype(F32) * bias[...], axis=1, keepdims=True)
    out[...] = jnp.broadcast_to(column, out.shape)


def band_first_kernel(w1, w2, bias, t1o, t1r, tbo, tbr, b1):
    expand, rows_y = row_table(192, y_first)
    parts = spread(w1, True, False)
    band(halves(parts, lambda n: n % CI, natural), expand, lane_y(natural, 256, 64), rows_y, t1o)
    band(halves(parts, lambda n: n % CI, rim(4)), expand, lane_y(rim(4), 256, 64), rows_y, t1r)
    parts = spread(w2, False, True)
    band(wholes(parts, lambda n: n // CH, natural), expand, lane_y(natural, 384, 128), rows_y, tbo)
    band(halves(parts, lambda n: n // CH, rim(2)), expand, lane_y(rim(2), 256, 64), rows_y, tbr)
    repeat_bias(bias, expand, b1)


def band_second_kernel(w2, bias, t2, b2):
    expand, rows_y = row_table(128, natural)
    parts = spread(w2, True, False)
    wide = [wholes(parts, lambda n: n % CH, y_first), halves(parts, lambda n: n % CH, rim(2))]
    ys = jnp.concatenate([lane_y(y_first, 384, 128), lane_y(rim(2), 256, 64)], axis=1)
    band(jnp.concatenate(wide, axis=1), expand, ys, rows_y, t2)
    repeat_bias(bias, expand, b2)


def shifted(v):
    lane = lax.broadcasted_iota(jnp.int32, v.shape, 1)
    before = jnp.where(lane >= 2, pltpu.roll(v, 2, 1), 0.0)
    after = jnp.where(lane < Z - 2, pltpu.roll(v, Z - 2, 1), 0.0)
    return before.astype(BF16), v.astype(BF16), after.astype(BF16)


def store_wide(ref, p, v):
    at = slice(p * Z, (p + 1) * Z)
    for c, piece in enumerate(shifted(v)):
        ref[c * 128:(c + 1) * 128, at] = piece[:128]
        ref[384 + c * 64:384 + (c + 1) * 64, at] = piece[128:]
    ref[576:, at] = jnp.zeros((64, Z), BF16)


def stacked(ref, lanes):
    return jnp.concatenate([ref[:, a * 256:a * 256 + lanes] for a in range(3)], axis=0)


def own_kernel(counts, xfar, xnear, fields, cot, t1, tb, b1, fs, cs, pre, back):
    count = fields.shape[0]
    f, c = x_planes(count, fields, cot, xnear, xfar, counts[0])
    for ref, rows in ((fs, f), (cs, c)):
        for p, v in enumerate(rows):
            for n, piece in enumerate(shifted(v)):
                ref[n * v.shape[0]:(n + 1) * v.shape[0], p * Z:(p + 1) * Z] = piece
    fs[192:] = jnp.zeros((64, fs.shape[1]), BF16)
    pre[...] = jnp.dot(t1[...], stacked(fs, pre.shape[1]), preferred_element_type=F32) + b1[:, :1]
    back[...] = jnp.dot(tb[...], stacked(cs, back.shape[1]), preferred_element_type=F32)


def two_dots(v, w):
    high = v.astype(BF16)
    low = (v - high.astype(F32)).astype(BF16)
    return jnp.dot(high, w, preferred_element_type=F32) + jnp.dot(low, w, preferred_element_type=F32)


def rim_kernel(counts, rfar, rnear, fs, cs, pre_own, back_own, t1, tb, e1t, e2t, rep1, rep2, y1, y2,
               hidden_out, payload, fr, cr, taps):
    count = hidden_out.shape[0] - 4
    lanes = count * Z
    stream, radial = lax.axis_index("stream"), lax.axis_index("radial")
    at = 0
    for ref in (fr, cr):
        for p in range(ref.shape[1] // Z):
            low, high = sides(radial, counts[1], rnear[at:at + 32], rfar[at:at + 32])
            for n, piece in enumerate(shifted(jnp.concatenate([low, high], axis=0))):
                ref[n * 64:(n + 1) * 64, p * Z:(p + 1) * Z] = piece
            at += 32
        ref[192:] = jnp.zeros((64, ref.shape[1]), BF16)
    pre = pre_own[...] + jnp.dot(t1[...], stacked(fr, lanes + 4 * Z), preferred_element_type=F32)
    share = 0.5 * (1.0 + lax.erf(pre * 0.7071067811865476))
    hidden = (pre * share).astype(BF16)
    zero = jnp.zeros((), BF16)
    rims = (jnp.where(radial > 0, hidden[128:160], zero), jnp.where(radial < counts[1] - 1, hidden[160:], zero))
    for p in range(count + 4):
        at = slice(p * Z, (p + 1) * Z)
        rows = jnp.concatenate([hidden[:128, at], rims[0][:, at], rims[1][:, at]], axis=0)
        if p < 2:
            rows = jnp.where(stream > 0, rows, zero)
        elif p >= count + 2:
            rows = jnp.where(stream < counts[0] - 1, rows, zero)
        hidden_out[p] = rows
    at = slice(2 * Z, 2 * Z + lanes)
    pre, share, hidden = pre[:128, at], share[:128, at], hidden[:128, at]
    back = back_own[...] + jnp.dot(tb[...], stacked(cr, lanes), preferred_element_type=F32)
    dpre = (back * (share + pre * jnp.exp(-0.5 * pre * pre) * 0.3989422804014327)).astype(BF16)
    over_lanes = (((1,), (1,)), ((), ()))
    ones, twos = [], []
    for a in range(3):
        at = slice((a + 1) * 256, (a + 1) * 256 + lanes)
        rows = [ref[n * 64:(n + 1) * 64, at] for n in range(3) for ref in (fs, fr)]
        g1 = lax.dot_general(dpre, jnp.concatenate(rows, axis=0), over_lanes, preferred_element_type=F32)
        at = slice(a * 256, a * 256 + lanes)
        rows = jnp.concatenate([cs[:, at], cr[:, at]], axis=0)
        g2 = lax.dot_general(hidden, rows, over_lanes, preferred_element_type=F32)
        for b in range(3):
            for g, ys, out in ((g1, y1, ones), (g2, y2, twos)):
                total = jnp.zeros((CH, g.shape[1]), F32)
                for y in range(8):
                    total = jnp.where(ys[...] == float(y + 2 * (b - 1)), g[y * CH:(y + 1) * CH], total)
                out.append(total)
    taps[:, 24:] = jnp.zeros((3, 8, 128), F32)
    for parts, et, rep, at, width in ((ones, e1t, rep1, 0, 128), (twos[::-1], e2t, rep2, 1, 256)):
        sums = two_dots(jnp.concatenate(parts, axis=0), et[...])
        wide = two_dots(sums, rep[...])
        row = lax.broadcasted_iota(jnp.int32, wide.shape, 0) % CH
        lane = lax.broadcasted_iota(jnp.int32, wide.shape, 1) % width
        mine = row == (lane // CI if width == 128 else lane % CH)
        total = jnp.sum(jnp.where(mine, wide, 0.0).reshape(9, CH, 3 * width), axis=1)
        for c in range(3):
            first = c if width == 128 else 2 - c
            for n in range(width // 128):
                taps[at + n, pl.ds(first, 9, stride=3)] = total[:, c * width + n * 128:c * width + (n + 1) * 128]
    bias = jnp.sum(dpre.astype(F32), axis=1, keepdims=True)
    bias = sum(bias[y * CH:(y + 1) * CH] for y in range(8))
    row = lax.broadcasted_iota(jnp.int32, (CH, 128), 0)
    lane = lax.broadcasted_iota(jnp.int32, (CH, 128), 1)
    taps[0, 27:28] = jnp.sum(jnp.where(row == lane, bias, 0.0), axis=0, keepdims=True)
    payload[...] = jnp.concatenate([taps[n] for n in range(3)], axis=1)


def closure_kernel(hidden, t2, b2, closure, hs):
    count = closure.shape[2]
    for p in range(count + 4):
        store_wide(hs, p, hidden[p].astype(F32))
    out = (jnp.dot(t2[...], stacked(hs, count * Z), preferred_element_type=F32) + b2[:, :1]).astype(BF16)
    for x in range(count):
        closure[0, :, x] = out[:, x * Z:(x + 1) * Z].reshape(CH, 8, Z)


def add_kernel(here, there, total):
    s = here[...].astype(F32) + there[...].astype(F32)
    lost = s - s.astype(BF16).astype(F32)
    row = lax.broadcasted_iota(jnp.int32, s.shape, 0)
    total[...] = (s + jnp.where(row == 28, pltpu.roll(lost, 1, 0), 0.0)).astype(BF16)


def finish_kernel(norm, total, last, first, second, bias):
    scaled = (total[...].astype(F32) + last[...].astype(F32)) * norm
    flipped = jnp.transpose(scaled)
    first[...] = flipped[:128, :27]
    second[...] = flipped[128:, :27]
    bias[...] = scaled[27:28, :CH] + scaled[28:29, :CH]


def call(kernel, outs, name, scratch=(), flops=10_000_000, **specs):
    return pl.pallas_call(
        kernel,
        out_shape=outs,
        **specs,
        scratch_shapes=list(scratch),
        compiler_params=pltpu.CompilerParams(vmem_limit_bytes=32 * 1024 * 1024),
        cost_estimate=pl.CostEstimate(flops=flops, bytes_accessed=1_000_000, transcendentals=0),
        name=name,
    )


def shape(*dims, dtype=BF16):
    return jax.ShapeDtypeStruct(dims, dtype)


def exchange(near, far, axis):
    count = lax.axis_size(axis)
    shifted_pairs = [(i, min(max(i - 1 + 2 * (i % 2), 0), count - 1)) for i in range(count)]
    far = lax.ppermute(far, axis, shifted_pairs)
    return lax.ppermute(near, axis, [(i, i ^ 1) for i in range(count)]), far


def swap(v, axis, mask):
    return lax.ppermute(v, axis, [(i, i ^ mask) for i in range(lax.axis_size(axis))])


def add(v, w):
    return call(add_kernel, shape(*v.shape), "add_parts")(v, w)


def local(fields, first_weight, first_bias, second_weight, second_bias, cotangent):
    e1t, y1 = table(CI, 384, ((natural, 64, 0), (rim(4), 64, 64)))
    e2t, y2 = table(CH, 640, ((natural, 128, 0), (rim(2), 64, 384)))
    rep1, rep2 = np.zeros((128, 384), np.float32), np.zeros((128, 768), np.float32)
    for c in range(3):
        rep1[c * CI:(c + 1) * CI, c * 128:(c + 1) * 128] = np.tile(np.eye(CI), (1, CH))
        rep2[c * CH:(c + 1) * CH, c * 256:(c + 1) * 256] = np.repeat(np.eye(CH), CH, axis=1)

    def const(*arrays, dtype=BF16):
        return [jnp.asarray(v, dtype) for v in arrays]

    planes = fields.shape[2]
    w1 = first_weight.transpose(1, 2, 0).reshape(CH * CI, 27)
    w2 = second_weight.transpose(1, 2, 0).reshape(CH * CH, 27)
    near, far, f_rows, c_rows = call(
        pack_kernel,
        (shape(512, Z), shape(512, Z), shape(planes, CI * 8, Z), shape(planes, CH * 8, Z)),
        "pack_strips",
        flops=4_000_000_000,
    )(fields, cotangent)
    xnear, xfar = exchange(near, far, "stream")
    wide = (planes + 4) * Z
    counts = (lax.axis_size("stream"), lax.axis_size("radial"))
    t1o, t1r, tbo, tbr, b1 = call(
        band_first_kernel,
        (shape(192, 768), shape(192, 768), shape(128, 1152), shape(128, 768), shape(192, 128, dtype=F32)),
        "band_first",
        flops=4_000_000_000,
    )(w1, w2, first_bias[None])
    xfar, xnear, t1o, tbo = lax.optimization_barrier((xfar, xnear, t1o, tbo))
    near, far = call(functools.partial(join_kernel, counts), (shape((2 * planes + 12) * 32, Z),) * 2, "join_strips")(
        xfar, xnear, f_rows, c_rows)
    rnear, rfar = exchange(near, far, "radial")
    fs, cs, pre, back = call(
        functools.partial(own_kernel, counts),
        (shape(256, wide + 4 * Z), shape(384, wide), shape(192, wide, dtype=F32), shape(128, planes * Z, dtype=F32)),
        "own_rows",
        flops=1_000_000_000,
    )(xfar, xnear, f_rows, c_rows, t1o, tbo, b1)
    hidden, payload = call(
        functools.partial(rim_kernel, counts),
        (shape(planes + 4, 192, Z), shape(32, 384, dtype=F32)),
        "gradients",
        (pltpu.VMEM((256, wide + 4 * Z), BF16), pltpu.VMEM((256, wide), BF16), pltpu.VMEM((3, 32, 128), F32)),
        flops=2_000_000_000,
    )(rfar, rnear, fs, cs, pre, back, t1r, tbr, *const(e1t, e2t, rep1, rep2), *const(y1, y2, dtype=F32))

    steps = [(axis, 1 << n) for axis in ("radial", "stream", "snap") for n in range((lax.axis_size(axis) - 1).bit_length())]
    payload, w2 = lax.optimization_barrier((payload, w2))
    arrived = swap(payload, *steps[0])
    t2, b2 = call(band_second_kernel, (shape(128, 1920), shape(128, 128, dtype=F32)), "band_second")(
        w2, second_bias[None])
    payload, t2, b2 = lax.optimization_barrier((add(payload, arrived), t2, b2))
    arrived = swap(payload, *steps[1])
    closure = call(
        closure_kernel, shape(*cotangent.shape), "closure", (pltpu.VMEM((640, wide), BF16),), flops=1_000_000_000
    )(hidden, t2, b2)
    for step in steps[2:]:
        payload = add(payload, arrived)
        arrived = swap(payload, *step)

    cells = fields.shape[0] * fields.shape[2] * fields.shape[3] * fields.shape[4]
    for axis in ("stream", "radial", "snap"):
        cells *= lax.axis_size(axis)
    norm = float(1.0 / np.sqrt(np.float32(cells)))
    first, second, bias = call(
        functools.partial(finish_kernel, norm),
        (shape(CH * CI, 27, dtype=F32), shape(CH * CH, 27, dtype=F32), shape(1, CH, dtype=F32)),
        "finish",
    )(payload, arrived)
    first = first.reshape(CH, CI, 27).transpose(2, 0, 1)
    second = second.reshape(CH, CH, 27).transpose(2, 0, 1)
    return (closure, first, second, bias[0])


def solution(mesh):
    split = P("snap", None, "stream", "radial", None)
    return jax.shard_map(
        local,
        mesh=mesh,
        in_specs=(split, P(), P(), P(), P(), split),
        out_specs=(split, P(), P(), P()),
        check_vma=False,
    )
```

```python
import functools

import numpy as np
import jax
import jax.numpy as jnp
from jax import lax
from jax.experimental import pallas as pl
from jax.experimental.pallas import tpu as pltpu
from jax.sharding import PartitionSpec as P

F32 = jnp.float32
BF16 = jnp.bfloat16
Z = 128
CI = 8
CH = 16
FAR = 100


def natural(n):
    return n // 8, n % 8


def y_first(n):
    return n % CH, n // CH


def rim(channels):
    def of(n):
        side, n = n // (2 * channels), n % (2 * channels)
        return n // 2, n % 2 + 10 * side - 2
    return of


def deep_rim(n):
    part, n = n // 16, n % 16
    return n // 2, n % 2 + 10 * (part // 2) - 2 + (part % 2) * (4 * (part // 2) - 2)


def table(channels, total, places):
    e = np.zeros((total, 128), np.float32)
    ys = np.full((1, total), FAR, np.float32)
    for c in range(3):
        for of, start, step in places:
            ch, y = of(np.arange(step))
            at = start + c * step + np.arange(step)
            e[at, c * channels + ch] = 1
            ys[0, at] = y
    return e, ys


def iota(rows, columns):
    return [lax.broadcasted_iota(jnp.int32, (rows, columns), d) for d in range(2)]


def one_hot(where):
    return jnp.where(where, 1.0, 0.0).astype(BF16)


def lane_y(of, width, step):
    lane = lax.broadcasted_iota(jnp.int32, (1, width), 1)
    return jnp.where(lane < 3 * step, of(lane % step)[1], FAR)


def place(rows, wanted, of, size, slot):
    row, lane = iota(rows, 128)
    return one_hot((of(lane % size)[0] == wanted(row)) & (lane // size == slot))


def row_table(rows, own):
    row, lane = iota(rows, CH)
    own_c, own_y = own(row)
    rim_c, rim_y = rim(CH)(row - 128)
    channel, y = jnp.where(row < 128, own_c, rim_c), jnp.where(row < 128, own_y, rim_y)
    return one_hot(channel == lane), y[:, :1]


def plane(ref, x):
    v = ref[0, :, x].astype(F32)
    return v.reshape(v.shape[0] * v.shape[1], v.shape[2])


def pick_rows(channels, low, high):
    half = channels * 2
    row, col = iota(2 * half, channels * 8)
    side = row // half
    return one_hot(col == (row % half // 2) * 8 + low + (high - low) * side + row % 2)


def partners(index, count):
    return index % 2 == 0, index > 0, index < count - 1


def sides(index, count, near, far):
    near_above, below, above = partners(index, count)
    low = jnp.where(near_above, far, near).astype(F32)
    high = jnp.where(near_above, near, far).astype(F32)
    return jnp.where(below, low, 0.0), jnp.where(above, high, 0.0)


def pack_kernel(fields, cot, near, far, f_rows, c_rows):
    up_first = lax.axis_index("stream") % 2 == 0
    count, at = fields.shape[2], 0
    for ref, out, width in ((fields, f_rows, 4), (cot, c_rows, 2)):
        rows = [plane(ref, x) for x in range(count)]
        for x, v in enumerate(rows):
            out[x] = v.astype(BF16)
        for low, high in zip(rows[:width], rows[count - width:]):
            part = slice(at, at + low.shape[0])
            near[part] = jnp.where(up_first, high, low).astype(BF16)
            far[part] = jnp.where(up_first, low, high).astype(BF16)
            at += low.shape[0]


def x_planes(count, fields, cot, xnear, xfar, size):
    index = lax.axis_index("stream")
    inner = [fields[x].astype(F32) for x in range(count)]
    rims = [sides(index, size, xnear[n * 64:(n + 1) * 64], xfar[n * 64:(n + 1) * 64]) for n in range(4)]
    f = [low for low, _ in rims] + inner + [high for _, high in rims]
    inner = [cot[x].astype(F32) for x in range(count)]
    rims = [sides(index, size, xnear[256 + n * 128:384 + n * 128], xfar[256 + n * 128:384 + n * 128]) for n in range(2)]
    return f, [low for low, _ in rims] + inner + [high for _, high in rims]


def join_kernel(counts, xfar, xnear, fields, cot, near, far, near_outer, far_outer):
    up_first = lax.axis_index("radial") % 2 == 0
    f, c = x_planes(fields.shape[0], fields, cot, xnear, xfar, counts[0])
    inner, outer = pick_rows(CI, 0, 6), pick_rows(CI, 2, 4)
    ends = f[:2] + f[-2:]
    work = [(inner, f[2:-2], near, far), (pick_rows(CH, 0, 6), c, near, far)]
    work += [(inner, ends, near_outer, far_outer), (outer, ends + f[2:-2], near_outer, far_outer)]
    at = {}
    for pick, rows, near_out, far_out in work:
        half = pick.shape[0] // 2
        for v in rows:
            got = jnp.dot(pick, v.astype(BF16), preferred_element_type=F32)
            start = at.get(id(near_out), 0)
            near_out[start:start + half] = jnp.where(up_first, got[half:], got[:half]).astype(BF16)
            far_out[start:start + half] = jnp.where(up_first, got[:half], got[half:]).astype(BF16)
            at[id(near_out)] = start + half


def spread(w, by_row, flip):
    taps = jnp.transpose(w[...].astype(F32))
    width = taps.shape[1]
    row = lax.broadcasted_iota(jnp.int32, (CH, width), 0)
    lane = lax.broadcasted_iota(jnp.int32, (CH, width), 1)
    mine = row == (lane // (width // CH) if by_row else lane % CH)
    found = []
    for c in range(3):
        rows = []
        for ab in range(9):
            t = 26 - (ab * 3 + c) if flip else ab * 3 + c
            rows.append(jnp.where(mine, jnp.broadcast_to(taps[t:t + 1], (CH, width)), 0.0))
        found.append(jnp.concatenate(rows, axis=0).astype(BF16))
    return found


def dots(pairs):
    total = None
    for v, w in pairs:
        part = jnp.dot(v, w, preferred_element_type=F32)
        total = part if total is None else total + part
    return total.astype(BF16)


def packed(parts, wanted, of, size):
    per = 128 // size
    places = [place(parts[0].shape[1], wanted, of, size, slot) for slot in range(min(per, 3))]
    tiles = [range(first, min(first + per, 3)) for first in range(0, 3, per)]
    return jnp.concatenate([dots([(parts[c], places[c % per]) for c in tile]) for tile in tiles], axis=1)


def band(wide, expand, ys, rows_y, t):
    rows, width = t.shape[0], wide.shape[1]
    for a in range(3):
        total = jnp.zeros((rows, width), F32)
        for b in range(3):
            part = jnp.dot(expand[:rows], wide[(a * 3 + b) * CH:(a * 3 + b + 1) * CH], preferred_element_type=F32)
            total = jnp.where(ys == rows_y[:rows] + 2 * (b - 1), part, total)
        t[:, a * width:(a + 1) * width] = total.astype(BF16)


def repeat_bias(bias, expand, out):
    column = jnp.sum(expand.astype(F32) * bias[...], axis=1, keepdims=True)
    out[...] = jnp.broadcast_to(column, out.shape)


def band_kernel(w1, w2, first_bias, second_bias, t1o, t1r, t1d, tbo, tbr, t2, b1, b2):
    expand, rows_y = row_table(192, y_first)
    parts = spread(w1, True, False)
    for of, step, t in ((natural, 64, t1o), (rim(CI), 32, t1r), (deep_rim, 64, t1d)):
        wide = packed(parts, lambda n: n % CI, of, step)
        band(wide, expand, lane_y(of, wide.shape[1], step), rows_y, t)
    parts = spread(w2, False, True)
    for of, step, t in ((natural, 128, tbo), (rim(CH), 64, tbr)):
        wide = packed(parts, lambda n: n // CH, of, step)
        band(wide, expand, lane_y(of, wide.shape[1], step), rows_y, t)
    repeat_bias(first_bias, expand, b1)
    expand, rows_y = row_table(128, natural)
    parts = spread(w2, True, False)
    wide = [packed(parts, lambda n: n % CH, of, step) for of, step in ((y_first, 128), (rim(CH), 64))]
    ys = jnp.concatenate([lane_y(y_first, 384, 128), lane_y(rim(CH), 256, 64)], axis=1)
    band(jnp.concatenate(wide, axis=1), expand, ys, rows_y, t2)
    repeat_bias(second_bias, expand, b2)


def shifted(v):
    lane = lax.broadcasted_iota(jnp.int32, v.shape, 1)
    before = jnp.where(lane >= 2, pltpu.roll(v, 2, 1), 0.0)
    after = jnp.where(lane < Z - 2, pltpu.roll(v, Z - 2, 1), 0.0)
    return before.astype(BF16), v.astype(BF16), after.astype(BF16)


def store_wide(ref, p, v):
    at = slice(p * Z, (p + 1) * Z)
    for c, piece in enumerate(shifted(v)):
        ref[c * 128:(c + 1) * 128, at] = piece[:128]
        ref[384 + c * 64:384 + (c + 1) * 64, at] = piece[128:]
    ref[576:, at] = jnp.zeros((64, Z), BF16)


def stacked(ref, lanes):
    return jnp.concatenate([ref[:, a * 256:a * 256 + lanes] for a in range(3)], axis=0)


def own_kernel(counts, xfar, xnear, fields, cot, t1, tb, b1, fs, cs, pre, back):
    count = fields.shape[0]
    f, c = x_planes(count, fields, cot, xnear, xfar, counts[0])
    for ref, rows in ((fs, f), (cs, c)):
        for p, v in enumerate(rows):
            for n, piece in enumerate(shifted(v)):
                ref[n * v.shape[0]:(n + 1) * v.shape[0], p * Z:(p + 1) * Z] = piece
    fs[192:] = jnp.zeros((64, fs.shape[1]), BF16)
    rows = jnp.concatenate([fs[:, a * 256 + 256:a * 256 + 256 + pre.shape[1]] for a in range(3)], axis=0)
    pre[...] = jnp.dot(t1[:128], rows, preferred_element_type=F32) + b1[:128, :1]
    back[...] = jnp.dot(tb[...], stacked(cs, back.shape[1]), preferred_element_type=F32)


def two_dots(v, w):
    high = v.astype(BF16)
    low = (v - high.astype(F32)).astype(BF16)
    return jnp.dot(high, w, preferred_element_type=F32) + jnp.dot(low, w, preferred_element_type=F32)


def gelu_share(pre):
    return 0.5 * (1.0 + lax.erf(pre * 0.7071067811865476))


def rim_kernel(counts, rfar, rnear, fs, cs, pre_own, back_own, t1, tb, e1t, e2t, rep1, rep2, y1, y2,
               hidden_out, payload, fr, cr, taps):
    count = hidden_out.shape[0]
    lanes = count * Z
    radial = lax.axis_index("radial")
    at = 0
    for ref, half in ((fr, 16), (cr, 32)):
        for p in range(count + 4):
            low, high = sides(radial, counts[1], rnear[at:at + half], rfar[at:at + half])
            for n, piece in enumerate(shifted(jnp.concatenate([low, high], axis=0))):
                ref[n * 2 * half:(n + 1) * 2 * half, p * Z:(p + 1) * Z] = piece
            at += half
        ref[6 * half:] = jnp.zeros((2 * half, ref.shape[1]), BF16)
    pre = pre_own[...] + jnp.dot(t1[...], stacked(fr, lanes), preferred_element_type=F32)
    share = gelu_share(pre)
    hidden = (pre * share).astype(BF16)
    for x in range(count):
        hidden_out[x] = hidden[:, x * Z:(x + 1) * Z]
    back = back_own[...] + jnp.dot(tb[...], stacked(cr, lanes), preferred_element_type=F32)
    dpre = (back * (share + pre * jnp.exp(-0.5 * pre * pre) * 0.3989422804014327)).astype(BF16)
    over_lanes = (((1,), (1,)), ((), ()))
    ones, twos = [], []
    for a in range(3):
        at = slice((a + 1) * 256, (a + 1) * 256 + lanes)
        rows = jnp.concatenate([fs[:, at], fr[:, a * 256:a * 256 + lanes]], axis=0)
        g1 = lax.dot_general(dpre, rows, over_lanes, preferred_element_type=F32)
        at = slice(a * 256, a * 256 + lanes)
        rows = jnp.concatenate([cs[:, at], cr[:, at]], axis=0)
        g2 = lax.dot_general(hidden, rows, over_lanes, preferred_element_type=F32)
        for b in range(3):
            for g, ys, out in ((g1, y1, ones), (g2, y2, twos)):
                total = jnp.zeros((CH, g.shape[1]), F32)
                for y in range(8):
                    total = jnp.where(ys[...] == float(y + 2 * (b - 1)), g[y * CH:(y + 1) * CH], total)
                out.append(total)
    taps[:, 24:] = jnp.zeros((3, 8, 128), F32)
    for parts, et, rep, at, width in ((ones, e1t, rep1, 0, 128), (twos[::-1], e2t, rep2, 1, 256)):
        sums = two_dots(jnp.concatenate(parts, axis=0), et[...])
        wide = two_dots(sums, rep[...])
        row = lax.broadcasted_iota(jnp.int32, wide.shape, 0) % CH
        lane = lax.broadcasted_iota(jnp.int32, wide.shape, 1) % width
        mine = row == (lane // CI if width == 128 else lane % CH)
        total = jnp.sum(jnp.where(mine, wide, 0.0).reshape(9, CH, 3 * width), axis=1)
        for c in range(3):
            first = c if width == 128 else 2 - c
            for n in range(width // 128):
                taps[at + n, pl.ds(first, 9, stride=3)] = total[:, c * width + n * 128:c * width + (n + 1) * 128]
    bias = jnp.sum(dpre.astype(F32), axis=1, keepdims=True)
    bias = sum(bias[y * CH:(y + 1) * CH] for y in range(8))
    row = lax.broadcasted_iota(jnp.int32, (CH, 128), 0)
    lane = lax.broadcasted_iota(jnp.int32, (CH, 128), 1)
    taps[0, 27:28] = jnp.sum(jnp.where(row == lane, bias, 0.0), axis=0, keepdims=True)
    payload[...] = jnp.concatenate([taps[n] for n in range(3)], axis=1)


def hidden_rim_kernel(counts, rfar, rnear, rfar_outer, rnear_outer, hidden, fs, t1o, t1d, b1, hidden_out, fr):
    count = hidden.shape[0]
    stream, radial = lax.axis_index("stream"), lax.axis_index("radial")
    for p in range(count + 8):
        end = p if p < 2 else p - count - 4 if p >= count + 6 else None
        if end is None:
            near, outer = (rnear, rfar, (p - 2) * 16), (rnear_outer, rfar_outer, 128 + (p - 2) * 16)
        else:
            near, outer = (rnear_outer, rfar_outer, end * 16), (rnear_outer, rfar_outer, 64 + end * 16)
        parts = [sides(radial, counts[1], n[at:at + 16], f[at:at + 16]) for n, f, at in (near, outer)]
        rows = jnp.concatenate([part[side] for side in range(2) for part in parts], axis=0)
        for n, piece in enumerate(shifted(rows)):
            fr[n * 64:(n + 1) * 64, p * Z:(p + 1) * Z] = piece
    fr[192:] = jnp.zeros((64, fr.shape[1]), BF16)

    def gelu(rows, lanes):
        total = b1[rows, :1]
        for t, ref in ((t1o, fs), (t1d, fr)):
            cells = [jnp.concatenate([ref[:, a * 256 + at:a * 256 + at + size] for at, size in lanes], axis=1) for a in range(3)]
            total = total + jnp.dot(t[rows], jnp.concatenate(cells, axis=0), preferred_element_type=F32)
        return total * gelu_share(total)

    own = gelu(slice(0, 128), ((0, 2 * Z), ((count + 2) * Z, 2 * Z)))
    rims = gelu(slice(128, 192), ((0, (count + 4) * Z),))
    rims = jnp.concatenate([jnp.where(radial > 0, rims[:32], 0.0), jnp.where(radial < counts[1] - 1, rims[32:], 0.0)], axis=0)
    for p in range(count + 4):
        rim_rows = rims[:, p * Z:(p + 1) * Z]
        if 2 <= p < count + 2:
            hidden_out[p, :128] = hidden[p - 2]
            hidden_out[p, 128:] = rim_rows.astype(BF16)
        else:
            at = p if p < 2 else p - count
            inside = stream > 0 if p < 2 else stream < counts[0] - 1
            rows = jnp.concatenate([own[:, at * Z:(at + 1) * Z], rim_rows], axis=0)
            hidden_out[p] = jnp.where(inside, rows, 0.0).astype(BF16)


def closure_kernel(hidden, t2, b2, closure, hs):
    count = closure.shape[2]
    for p in range(count + 4):
        store_wide(hs, p, hidden[p].astype(F32))
    out = (jnp.dot(t2[...], stacked(hs, count * Z), preferred_element_type=F32) + b2[:, :1]).astype(BF16)
    for x in range(count):
        closure[0, :, x] = out[:, x * Z:(x + 1) * Z].reshape(CH, 8, Z)


def add_kernel(here, there, total):
    s = here[...].astype(F32) + there[...].astype(F32)
    lost = s - s.astype(BF16).astype(F32)
    row = lax.broadcasted_iota(jnp.int32, s.shape, 0)
    total[...] = (s + jnp.where(row == 28, pltpu.roll(lost, 1, 0), 0.0)).astype(BF16)


def finish_kernel(norm, total, last, first, second, bias):
    scaled = (total[...].astype(F32) + last[...].astype(F32)) * norm
    flipped = jnp.transpose(scaled)
    first[...] = flipped[:128, :27]
    second[...] = flipped[128:, :27]
    bias[...] = scaled[27:28, :CH] + scaled[28:29, :CH]


def call(kernel, outs, name, scratch=(), flops=10_000_000, **specs):
    return pl.pallas_call(
        kernel,
        out_shape=outs,
        **specs,
        scratch_shapes=list(scratch),
        compiler_params=pltpu.CompilerParams(vmem_limit_bytes=32 * 1024 * 1024),
        cost_estimate=pl.CostEstimate(flops=flops, bytes_accessed=1_000_000, transcendentals=0),
        name=name,
    )


def shape(*dims, dtype=BF16):
    return jax.ShapeDtypeStruct(dims, dtype)


def exchange(near, far, axis):
    count = lax.axis_size(axis)
    shifted_pairs = [(i, min(max(i - 1 + 2 * (i % 2), 0), count - 1)) for i in range(count)]
    far = lax.ppermute(far, axis, shifted_pairs)
    return lax.ppermute(near, axis, [(i, i ^ 1) for i in range(count)]), far


def swap(v, axis, mask):
    return lax.ppermute(v, axis, [(i, i ^ mask) for i in range(lax.axis_size(axis))])


def add(v, w):
    return call(add_kernel, shape(*v.shape), "add_parts")(v, w)


def local(fields, first_weight, first_bias, second_weight, second_bias, cotangent):
    e1t, y1 = table(CI, 384, ((natural, 0, 64), (rim(CI), 256, 32)))
    e2t, y2 = table(CH, 640, ((natural, 0, 128), (rim(CH), 384, 64)))
    rep1, rep2 = np.zeros((128, 384), np.float32), np.zeros((128, 768), np.float32)
    for c in range(3):
        rep1[c * CI:(c + 1) * CI, c * 128:(c + 1) * 128] = np.tile(np.eye(CI), (1, CH))
        rep2[c * CH:(c + 1) * CH, c * 256:(c + 1) * 256] = np.repeat(np.eye(CH), CH, axis=1)

    def const(*arrays, dtype=BF16):
        return [jnp.asarray(v, dtype) for v in arrays]

    planes = fields.shape[2]
    w1 = first_weight.transpose(1, 2, 0).reshape(CH * CI, 27)
    w2 = second_weight.transpose(1, 2, 0).reshape(CH * CH, 27)
    near, far, f_rows, c_rows = call(
        pack_kernel,
        (shape(512, Z), shape(512, Z), shape(planes, CI * 8, Z), shape(planes, CH * 8, Z)),
        "pack_strips",
        flops=4_000_000_000,
    )(fields, cotangent)
    xnear, xfar = exchange(near, far, "stream")
    wide = (planes + 4) * Z
    counts = (lax.axis_size("stream"), lax.axis_size("radial"))
    t1o, t1r, t1d, tbo, tbr, t2, b1, b2 = call(
        band_kernel,
        (shape(192, 768), shape(128, 384), shape(192, 768), shape(128, 1152), shape(128, 768), shape(128, 1920),
         shape(192, 128, dtype=F32), shape(128, 128, dtype=F32)),
        "band_matrices",
        flops=4_000_000_000,
    )(w1, w2, first_bias[None], second_bias[None])
    xfar, xnear, t1o, tbo = lax.optimization_barrier((xfar, xnear, t1o, tbo))
    inner, outer = (planes + 4) * 48, 128 + (planes + 4) * 16
    near, far, near_outer, far_outer = call(
        functools.partial(join_kernel, counts), (shape(inner, Z), shape(inner, Z), shape(outer, Z), shape(outer, Z)), "join_strips"
    )(xfar, xnear, f_rows, c_rows)
    rnear, rfar = exchange(near, far, "radial")
    rnear_outer, rfar_outer = exchange(near_outer, far_outer, "radial")
    fs, cs, pre, back = call(
        functools.partial(own_kernel, counts),
        (shape(256, wide + 4 * Z), shape(384, wide), shape(128, planes * Z, dtype=F32), shape(128, planes * Z, dtype=F32)),
        "own_rows",
        flops=1_000_000_000,
    )(xfar, xnear, f_rows, c_rows, t1o, tbo, b1)
    hidden, payload = call(
        functools.partial(rim_kernel, counts),
        (shape(planes, 128, Z), shape(32, 384, dtype=F32)),
        "gradients",
        (pltpu.VMEM((128, wide), BF16), pltpu.VMEM((256, wide), BF16), pltpu.VMEM((3, 32, 128), F32)),
        flops=2_000_000_000,
    )(rfar, rnear, fs, cs, pre, back, t1r, tbr, *const(e1t, e2t, rep1, rep2), *const(y1, y2, dtype=F32))

    steps = [(axis, 1 << n) for axis in ("radial", "stream", "snap") for n in range((lax.axis_size(axis) - 1).bit_length())]
    arrived = swap(payload, *steps[0])
    payload = add(payload, arrived)
    arrived = swap(payload, *steps[1])
    hidden = call(
        functools.partial(hidden_rim_kernel, counts),
        shape(planes + 4, 192, Z),
        "hidden_rim",
        (pltpu.VMEM((256, wide + 4 * Z), BF16),),
        flops=1_000_000_000,
    )(rfar, rnear, rfar_outer, rnear_outer, hidden, fs, t1o, t1d, b1)
    payload, hidden = lax.optimization_barrier((add(payload, arrived), hidden))
    arrived = swap(payload, *steps[2])
    closure = call(
        closure_kernel, shape(*cotangent.shape), "closure", (pltpu.VMEM((640, wide), BF16),), flops=1_000_000_000
    )(hidden, t2, b2)
    for step in steps[3:]:
        payload = add(payload, arrived)
        arrived = swap(payload, *step)

    cells = fields.shape[0] * fields.shape[2] * fields.shape[3] * fields.shape[4]
    for axis in ("stream", "radial", "snap"):
        cells *= lax.axis_size(axis)
    norm = float(1.0 / np.sqrt(np.float32(cells)))
    first, second, bias = call(
        functools.partial(finish_kernel, norm),
        (shape(CH * CI, 27, dtype=F32), shape(CH * CH, 27, dtype=F32), shape(1, CH, dtype=F32)),
        "finish",
    )(payload, arrived)
    first = first.reshape(CH, CI, 27).transpose(2, 0, 1)
    second = second.reshape(CH, CH, 27).transpose(2, 0, 1)
    return (closure, first, second, bias[0])


def solution(mesh):
    split = P("snap", None, "stream", "radial", None)
    return jax.shard_map(
        local,
        mesh=mesh,
        in_specs=(split, P(), P(), P(), P(), split),
        out_specs=(split, P(), P(), P()),
        check_vma=False,
    )
```

```python
import functools

import numpy as np
import jax
import jax.numpy as jnp
from jax import lax
from jax.experimental import pallas as pl
from jax.experimental.pallas import tpu as pltpu
from jax.sharding import PartitionSpec as P

F32 = jnp.float32
BF16 = jnp.bfloat16
Z = 128
CI = 8
CH = 16
FAR = 100


def natural(n):
    return n // 8, n % 8


def y_first(n):
    return n % CH, n // CH


def rim(channels):
    def of(n):
        side, n = n // (2 * channels), n % (2 * channels)
        return n // 2, n % 2 + 10 * side - 2
    return of


def deep_rim(n):
    part, n = n // 16, n % 16
    return n // 2, n % 2 + 10 * (part // 2) - 2 + (part % 2) * (4 * (part // 2) - 2)


def table(channels, total, places):
    e = np.zeros((total, 128), np.float32)
    ys = np.full((1, total), FAR, np.float32)
    for c in range(3):
        for of, start, step in places:
            ch, y = of(np.arange(step))
            at = start + c * step + np.arange(step)
            e[at, c * channels + ch] = 1
            ys[0, at] = y
    return e, ys


def iota(rows, columns):
    return [lax.broadcasted_iota(jnp.int32, (rows, columns), d) for d in range(2)]


def one_hot(where):
    return jnp.where(where, 1.0, 0.0).astype(BF16)


def lane_y(of, width, step):
    lane = lax.broadcasted_iota(jnp.int32, (1, width), 1)
    return jnp.where(lane < 3 * step, of(lane % step)[1], FAR)


def place(rows, wanted, of, size, slot):
    row, lane = iota(rows, 128)
    return one_hot((of(lane % size)[0] == wanted(row)) & (lane // size == slot))


def row_table(rows, own):
    row, lane = iota(rows, CH)
    own_c, own_y = own(row)
    rim_c, rim_y = rim(CH)(row - 128)
    channel, y = jnp.where(row < 128, own_c, rim_c), jnp.where(row < 128, own_y, rim_y)
    return one_hot(channel == lane), y[:, :1]


def plane(ref, x):
    v = ref[0, :, x].astype(F32)
    return v.reshape(v.shape[0] * v.shape[1], v.shape[2])


def pick_rows(channels, low, high):
    half = channels * 2
    row, col = iota(2 * half, channels * 8)
    side = row // half
    return one_hot(col == (row % half // 2) * 8 + low + (high - low) * side + row % 2)


def partners(index, count):
    return index % 2 == 0, index > 0, index < count - 1


def sides(index, count, near, far):
    near_above, below, above = partners(index, count)
    low = jnp.where(near_above, far, near).astype(F32)
    high = jnp.where(near_above, near, far).astype(F32)
    return jnp.where(below, low, 0.0), jnp.where(above, high, 0.0)


def pack_kernel(fields, cot, near, far, f_rows, c_rows):
    up_first = lax.axis_index("stream") % 2 == 0
    count, at = fields.shape[2], 0
    for ref, out, width in ((fields, f_rows, 4), (cot, c_rows, 2)):
        rows = [plane(ref, x) for x in range(count)]
        for x, v in enumerate(rows):
            out[x] = v.astype(BF16)
        for low, high in zip(rows[:width], rows[count - width:]):
            part = slice(at, at + low.shape[0])
            near[part] = jnp.where(up_first, high, low).astype(BF16)
            far[part] = jnp.where(up_first, low, high).astype(BF16)
            at += low.shape[0]


def x_planes(count, fields, cot, xnear, xfar, size):
    index = lax.axis_index("stream")
    inner = [fields[x].astype(F32) for x in range(count)]
    rims = [sides(index, size, xnear[n * 64:(n + 1) * 64], xfar[n * 64:(n + 1) * 64]) for n in range(4)]
    f = [low for low, _ in rims] + inner + [high for _, high in rims]
    inner = [cot[x].astype(F32) for x in range(count)]
    rims = [sides(index, size, xnear[256 + n * 128:384 + n * 128], xfar[256 + n * 128:384 + n * 128]) for n in range(2)]
    return f, [low for low, _ in rims] + inner + [high for _, high in rims]


def pick_strips(work, near, far):
    up_first = lax.axis_index("radial") % 2 == 0
    at = 0
    for pick, rows in work:
        half = pick.shape[0] // 2
        for v in rows:
            got = jnp.dot(pick, v.astype(BF16), preferred_element_type=F32)
            near[at:at + half] = jnp.where(up_first, got[half:], got[:half]).astype(BF16)
            far[at:at + half] = jnp.where(up_first, got[:half], got[half:]).astype(BF16)
            at += half


def join_kernel(counts, xfar, xnear, fields, cot, near, far):
    f, c = x_planes(fields.shape[0], fields, cot, xnear, xfar, counts[0])
    pick_strips([(pick_rows(CI, 0, 6), f[2:-2]), (pick_rows(CH, 0, 6), c)], near, far)


def join_outer_kernel(counts, xfar, xnear, fields, cot, near, far):
    f, _ = x_planes(fields.shape[0], fields, cot, xnear, xfar, counts[0])
    ends = f[:2] + f[-2:]
    pick_strips([(pick_rows(CI, 0, 6), ends), (pick_rows(CI, 2, 4), ends + f[2:-2])], near, far)


def spread(w, by_row, flip):
    taps = jnp.transpose(w[...].astype(F32))
    width = taps.shape[1]
    row = lax.broadcasted_iota(jnp.int32, (CH, width), 0)
    lane = lax.broadcasted_iota(jnp.int32, (CH, width), 1)
    mine = row == (lane // (width // CH) if by_row else lane % CH)
    found = []
    for c in range(3):
        rows = []
        for ab in range(9):
            t = 26 - (ab * 3 + c) if flip else ab * 3 + c
            rows.append(jnp.where(mine, jnp.broadcast_to(taps[t:t + 1], (CH, width)), 0.0))
        found.append(jnp.concatenate(rows, axis=0).astype(BF16))
    return found


def dots(pairs):
    total = None
    for v, w in pairs:
        part = jnp.dot(v, w, preferred_element_type=F32)
        total = part if total is None else total + part
    return total.astype(BF16)


def packed(parts, wanted, of, size):
    per = 128 // size
    places = [place(parts[0].shape[1], wanted, of, size, slot) for slot in range(min(per, 3))]
    tiles = [range(first, min(first + per, 3)) for first in range(0, 3, per)]
    return jnp.concatenate([dots([(parts[c], places[c % per]) for c in tile]) for tile in tiles], axis=1)


def band(wide, expand, ys, rows_y, t):
    rows, width = t.shape[0], wide.shape[1]
    for a in range(3):
        total = jnp.zeros((rows, width), F32)
        for b in range(3):
            part = jnp.dot(expand[:rows], wide[(a * 3 + b) * CH:(a * 3 + b + 1) * CH], preferred_element_type=F32)
            total = jnp.where(ys == rows_y[:rows] + 2 * (b - 1), part, total)
        t[:, a * width:(a + 1) * width] = total.astype(BF16)


def repeat_bias(bias, expand, out):
    column = jnp.sum(expand.astype(F32) * bias[...], axis=1, keepdims=True)
    out[...] = jnp.broadcast_to(column, out.shape)


def band_kernel(w1, w2, first_bias, second_bias, t1o, t1r, t1d, tbo, tbr, t2, b1, b2):
    expand, rows_y = row_table(192, y_first)
    parts = spread(w1, True, False)
    for of, step, t in ((natural, 64, t1o), (rim(CI), 32, t1r), (deep_rim, 64, t1d)):
        wide = packed(parts, lambda n: n % CI, of, step)
        band(wide, expand, lane_y(of, wide.shape[1], step), rows_y, t)
    parts = spread(w2, False, True)
    for of, step, t in ((natural, 128, tbo), (rim(CH), 64, tbr)):
        wide = packed(parts, lambda n: n // CH, of, step)
        band(wide, expand, lane_y(of, wide.shape[1], step), rows_y, t)
    repeat_bias(first_bias, expand, b1)
    expand, rows_y = row_table(128, natural)
    parts = spread(w2, True, False)
    wide = [packed(parts, lambda n: n % CH, of, step) for of, step in ((y_first, 128), (rim(CH), 64))]
    ys = jnp.concatenate([lane_y(y_first, 384, 128), lane_y(rim(CH), 256, 64)], axis=1)
    band(jnp.concatenate(wide, axis=1), expand, ys, rows_y, t2)
    repeat_bias(second_bias, expand, b2)


def shifted(v):
    lane = lax.broadcasted_iota(jnp.int32, v.shape, 1)
    before = jnp.where(lane >= 2, pltpu.roll(v, 2, 1), 0.0)
    after = jnp.where(lane < Z - 2, pltpu.roll(v, Z - 2, 1), 0.0)
    return before.astype(BF16), v.astype(BF16), after.astype(BF16)


def store_wide(ref, p, v):
    at = slice(p * Z, (p + 1) * Z)
    for c, piece in enumerate(shifted(v)):
        ref[c * 128:(c + 1) * 128, at] = piece[:128]
        ref[384 + c * 64:384 + (c + 1) * 64, at] = piece[128:]
    ref[576:, at] = jnp.zeros((64, Z), BF16)


def stacked(ref, lanes):
    return jnp.concatenate([ref[:, a * 256:a * 256 + lanes] for a in range(3)], axis=0)


def own_kernel(counts, xfar, xnear, fields, cot, t1, tb, b1, fs, cs, pre, back):
    count = fields.shape[0]
    f, c = x_planes(count, fields, cot, xnear, xfar, counts[0])
    for ref, rows in ((fs, f), (cs, c)):
        for p, v in enumerate(rows):
            for n, piece in enumerate(shifted(v)):
                ref[n * v.shape[0]:(n + 1) * v.shape[0], p * Z:(p + 1) * Z] = piece
    fs[192:] = jnp.zeros((64, fs.shape[1]), BF16)
    rows = jnp.concatenate([fs[:, a * 256 + 256:a * 256 + 256 + pre.shape[1]] for a in range(3)], axis=0)
    pre[...] = jnp.dot(t1[:128], rows, preferred_element_type=F32) + b1[:128, :1]
    back[...] = jnp.dot(tb[...], stacked(cs, back.shape[1]), preferred_element_type=F32)


def two_dots(v, w):
    high = v.astype(BF16)
    low = (v - high.astype(F32)).astype(BF16)
    return jnp.dot(high, w, preferred_element_type=F32) + jnp.dot(low, w, preferred_element_type=F32)


def gelu_share(pre):
    return 0.5 * (1.0 + lax.erf(pre * 0.7071067811865476))


def rim_kernel(counts, rfar, rnear, fs, cs, pre_own, back_own, t1, tb, e1t, e2t, rep1, rep2, y1, y2,
               hidden_out, payload, fr, cr, taps):
    count = hidden_out.shape[0]
    lanes = count * Z
    radial = lax.axis_index("radial")
    at = 0
    for ref, half in ((fr, 16), (cr, 32)):
        for p in range(count + 4):
            low, high = sides(radial, counts[1], rnear[at:at + half], rfar[at:at + half])
            for n, piece in enumerate(shifted(jnp.concatenate([low, high], axis=0))):
                ref[n * 2 * half:(n + 1) * 2 * half, p * Z:(p + 1) * Z] = piece
            at += half
        ref[6 * half:] = jnp.zeros((2 * half, ref.shape[1]), BF16)
    pre = pre_own[...] + jnp.dot(t1[...], stacked(fr, lanes), preferred_element_type=F32)
    share = gelu_share(pre)
    hidden = (pre * share).astype(BF16)
    for x in range(count):
        hidden_out[x] = hidden[:, x * Z:(x + 1) * Z]
    back = back_own[...] + jnp.dot(tb[...], stacked(cr, lanes), preferred_element_type=F32)
    dpre = (back * (share + pre * jnp.exp(-0.5 * pre * pre) * 0.3989422804014327)).astype(BF16)
    over_lanes = (((1,), (1,)), ((), ()))
    ones, twos = [], []
    for a in range(3):
        at = slice((a + 1) * 256, (a + 1) * 256 + lanes)
        rows = jnp.concatenate([fs[:, at], fr[:, a * 256:a * 256 + lanes]], axis=0)
        g1 = lax.dot_general(dpre, rows, over_lanes, preferred_element_type=F32)
        at = slice(a * 256, a * 256 + lanes)
        rows = jnp.concatenate([cs[:, at], cr[:, at]], axis=0)
        g2 = lax.dot_general(hidden, rows, over_lanes, preferred_element_type=F32)
        for b in range(3):
            for g, ys, out in ((g1, y1, ones), (g2, y2, twos)):
                total = jnp.zeros((CH, g.shape[1]), F32)
                for y in range(8):
                    total = jnp.where(ys[...] == float(y + 2 * (b - 1)), g[y * CH:(y + 1) * CH], total)
                out.append(total)
    taps[:, 24:] = jnp.zeros((3, 8, 128), F32)
    for parts, et, rep, at, width in ((ones, e1t, rep1, 0, 128), (twos[::-1], e2t, rep2, 1, 256)):
        sums = two_dots(jnp.concatenate(parts, axis=0), et[...])
        wide = two_dots(sums, rep[...])
        row = lax.broadcasted_iota(jnp.int32, wide.shape, 0) % CH
        lane = lax.broadcasted_iota(jnp.int32, wide.shape, 1) % width
        mine = row == (lane // CI if width == 128 else lane % CH)
        total = jnp.sum(jnp.where(mine, wide, 0.0).reshape(9, CH, 3 * width), axis=1)
        for c in range(3):
            first = c if width == 128 else 2 - c
            for n in range(width // 128):
                taps[at + n, pl.ds(first, 9, stride=3)] = total[:, c * width + n * 128:c * width + (n + 1) * 128]
    bias = jnp.sum(dpre.astype(F32), axis=1, keepdims=True)
    bias = sum(bias[y * CH:(y + 1) * CH] for y in range(8))
    row = lax.broadcasted_iota(jnp.int32, (CH, 128), 0)
    lane = lax.broadcasted_iota(jnp.int32, (CH, 128), 1)
    taps[0, 27:28] = jnp.sum(jnp.where(row == lane, bias, 0.0), axis=0, keepdims=True)
    payload[...] = jnp.concatenate([taps[n] for n in range(3)], axis=1)


def hidden_rim_kernel(counts, rfar, rnear, rfar_outer, rnear_outer, hidden, fs, t1o, t1d, b1, hidden_out, fr):
    count = hidden.shape[0]
    stream, radial = lax.axis_index("stream"), lax.axis_index("radial")
    for p in range(count + 8):
        end = p if p < 2 else p - count - 4 if p >= count + 6 else None
        if end is None:
            near, outer = (rnear, rfar, (p - 2) * 16), (rnear_outer, rfar_outer, 128 + (p - 2) * 16)
        else:
            near, outer = (rnear_outer, rfar_outer, end * 16), (rnear_outer, rfar_outer, 64 + end * 16)
        parts = [sides(radial, counts[1], n[at:at + 16], f[at:at + 16]) for n, f, at in (near, outer)]
        rows = jnp.concatenate([part[side] for side in range(2) for part in parts], axis=0)
        for n, piece in enumerate(shifted(rows)):
            fr[n * 64:(n + 1) * 64, p * Z:(p + 1) * Z] = piece
    fr[192:] = jnp.zeros((64, fr.shape[1]), BF16)

    def gelu(rows, lanes):
        total = b1[rows, :1]
        for t, ref in ((t1o, fs), (t1d, fr)):
            cells = [jnp.concatenate([ref[:, a * 256 + at:a * 256 + at + size] for at, size in lanes], axis=1) for a in range(3)]
            total = total + jnp.dot(t[rows], jnp.concatenate(cells, axis=0), preferred_element_type=F32)
        return total * gelu_share(total)

    own = gelu(slice(0, 128), ((0, 2 * Z), ((count + 2) * Z, 2 * Z)))
    rims = gelu(slice(128, 192), ((0, (count + 4) * Z),))
    rims = jnp.concatenate([jnp.where(radial > 0, rims[:32], 0.0), jnp.where(radial < counts[1] - 1, rims[32:], 0.0)], axis=0)
    for p in range(count + 4):
        rim_rows = rims[:, p * Z:(p + 1) * Z]
        if 2 <= p < count + 2:
            hidden_out[p, :128] = hidden[p - 2]
            hidden_out[p, 128:] = rim_rows.astype(BF16)
        else:
            at = p if p < 2 else p - count
            inside = stream > 0 if p < 2 else stream < counts[0] - 1
            rows = jnp.concatenate([own[:, at * Z:(at + 1) * Z], rim_rows], axis=0)
            hidden_out[p] = jnp.where(inside, rows, 0.0).astype(BF16)


def closure_kernel(hidden, t2, b2, closure, hs):
    count = closure.shape[2]
    for p in range(count + 4):
        store_wide(hs, p, hidden[p].astype(F32))
    out = (jnp.dot(t2[...], stacked(hs, count * Z), preferred_element_type=F32) + b2[:, :1]).astype(BF16)
    for x in range(count):
        closure[0, :, x] = out[:, x * Z:(x + 1) * Z].reshape(CH, 8, Z)


def summed(parts):
    parts = [part[...].astype(F32) for part in parts]
    while len(parts) > 1:
        parts = [v + w for v, w in zip(parts[::2], parts[1::2])]
    return parts[0]


def add_kernel(*refs):
    s = summed(refs[:-1])
    lost = s - s.astype(BF16).astype(F32)
    row = lax.broadcasted_iota(jnp.int32, s.shape, 0)
    refs[-1][...] = (s + jnp.where(row == 28, pltpu.roll(lost, 1, 0), 0.0)).astype(BF16)


def finish_kernel(norm, *refs):
    *parts, first, second, bias = refs
    scaled = summed(parts) * norm
    flipped = jnp.transpose(scaled)
    first[...] = flipped[:128, :27]
    second[...] = flipped[128:, :27]
    bias[...] = scaled[27:28, :CH] + scaled[28:29, :CH]


def call(kernel, outs, name, scratch=(), flops=10_000_000, **specs):
    return pl.pallas_call(
        kernel,
        out_shape=outs,
        **specs,
        scratch_shapes=list(scratch),
        compiler_params=pltpu.CompilerParams(vmem_limit_bytes=32 * 1024 * 1024),
        cost_estimate=pl.CostEstimate(flops=flops, bytes_accessed=1_000_000, transcendentals=0),
        name=name,
    )


def shape(*dims, dtype=BF16):
    return jax.ShapeDtypeStruct(dims, dtype)


def exchange(near, far, axis):
    count = lax.axis_size(axis)
    shifted_pairs = [(i, min(max(i - 1 + 2 * (i % 2), 0), count - 1)) for i in range(count)]
    far = lax.ppermute(far, axis, shifted_pairs)
    return lax.ppermute(near, axis, [(i, i ^ 1) for i in range(count)]), far


def swap(v, axis, masks):
    count = lax.axis_size(axis)
    return [lax.ppermute(v, axis, [(i, i ^ mask) for i in range(count)]) for mask in masks]


def add(v, arrived):
    return call(add_kernel, shape(*v.shape), "add_parts")(v, *arrived)


def rounds(axis, most):
    found, step = [], 1
    while step < lax.axis_size(axis):
        masks = [step * n for n in range(1, most if step * most <= lax.axis_size(axis) else 2)]
        found.append((axis, masks))
        step *= len(masks) + 1
    return found


def local(fields, first_weight, first_bias, second_weight, second_bias, cotangent):
    e1t, y1 = table(CI, 384, ((natural, 0, 64), (rim(CI), 256, 32)))
    e2t, y2 = table(CH, 640, ((natural, 0, 128), (rim(CH), 384, 64)))
    rep1, rep2 = np.zeros((128, 384), np.float32), np.zeros((128, 768), np.float32)
    for c in range(3):
        rep1[c * CI:(c + 1) * CI, c * 128:(c + 1) * 128] = np.tile(np.eye(CI), (1, CH))
        rep2[c * CH:(c + 1) * CH, c * 256:(c + 1) * 256] = np.repeat(np.eye(CH), CH, axis=1)

    def const(*arrays, dtype=BF16):
        return [jnp.asarray(v, dtype) for v in arrays]

    planes = fields.shape[2]
    w1 = first_weight.transpose(1, 2, 0).reshape(CH * CI, 27)
    w2 = second_weight.transpose(1, 2, 0).reshape(CH * CH, 27)
    near, far, f_rows, c_rows = call(
        pack_kernel,
        (shape(512, Z), shape(512, Z), shape(planes, CI * 8, Z), shape(planes, CH * 8, Z)),
        "pack_strips",
        flops=4_000_000_000,
    )(fields, cotangent)
    xnear, xfar = exchange(near, far, "stream")
    wide = (planes + 4) * Z
    counts = (lax.axis_size("stream"), lax.axis_size("radial"))
    t1o, t1r, t1d, tbo, tbr, t2, b1, b2 = call(
        band_kernel,
        (shape(192, 768), shape(128, 384), shape(192, 768), shape(128, 1152), shape(128, 768), shape(128, 1920),
         shape(192, 128, dtype=F32), shape(128, 128, dtype=F32)),
        "band_matrices",
        flops=4_000_000_000,
    )(w1, w2, first_bias[None], second_bias[None])
    xfar, xnear, t1o, tbo = lax.optimization_barrier((xfar, xnear, t1o, tbo))
    inner, outer = shape((planes + 4) * 48, Z), shape(128 + (planes + 4) * 16, Z)
    near, far = call(functools.partial(join_kernel, counts), (inner, inner), "join_strips")(xfar, xnear, f_rows, c_rows)
    rnear, rfar = exchange(near, far, "radial")
    fs, cs, pre, back = call(
        functools.partial(own_kernel, counts),
        (shape(256, wide + 4 * Z), shape(384, wide), shape(128, planes * Z, dtype=F32), shape(128, planes * Z, dtype=F32)),
        "own_rows",
        flops=1_000_000_000,
    )(xfar, xnear, f_rows, c_rows, t1o, tbo, b1)
    hidden, payload = call(
        functools.partial(rim_kernel, counts),
        (shape(planes, 128, Z), shape(32, 384, dtype=F32)),
        "gradients",
        (pltpu.VMEM((128, wide), BF16), pltpu.VMEM((256, wide), BF16), pltpu.VMEM((3, 32, 128), F32)),
        flops=2_000_000_000,
    )(rfar, rnear, fs, cs, pre, back, t1r, tbr, *const(e1t, e2t, rep1, rep2), *const(y1, y2, dtype=F32))

    steps = rounds("radial", 2) + rounds("stream", 4) + rounds("snap", 2)
    arrived = swap(payload, *steps[0])
    payload, f_rows = lax.optimization_barrier((add(payload, arrived), f_rows))
    arrived = swap(payload, *steps[1])
    near_outer, far_outer = call(
        functools.partial(join_outer_kernel, counts), (outer, outer), "join_outer", flops=1_000_000_000
    )(xfar, xnear, f_rows, c_rows)
    rnear_outer, rfar_outer = exchange(near_outer, far_outer, "radial")
    payload = add(payload, arrived)
    arrived = swap(payload, *steps[2])
    hidden = call(
        functools.partial(hidden_rim_kernel, counts),
        shape(planes + 4, 192, Z),
        "hidden_rim",
        (pltpu.VMEM((256, wide + 4 * Z), BF16),),
        flops=1_000_000_000,
    )(rfar, rnear, rfar_outer, rnear_outer, hidden, fs, t1o, t1d, b1)
    payload, hidden = lax.optimization_barrier((add(payload, arrived), hidden))
    arrived = swap(payload, *steps[3])
    closure = call(
        closure_kernel, shape(*cotangent.shape), "closure", (pltpu.VMEM((640, wide), BF16),), flops=1_000_000_000
    )(hidden, t2, b2)
    for step in steps[4:]:
        payload = add(payload, arrived)
        arrived = swap(payload, *step)

    cells = fields.shape[0] * fields.shape[2] * fields.shape[3] * fields.shape[4]
    for axis in ("stream", "radial", "snap"):
        cells *= lax.axis_size(axis)
    norm = float(1.0 / np.sqrt(np.float32(cells)))
    first, second, bias = call(
        functools.partial(finish_kernel, norm),
        (shape(CH * CI, 27, dtype=F32), shape(CH * CH, 27, dtype=F32), shape(1, CH, dtype=F32)),
        "finish",
    )(payload, *arrived)
    first = first.reshape(CH, CI, 27).transpose(2, 0, 1)
    second = second.reshape(CH, CH, 27).transpose(2, 0, 1)
    return (closure, first, second, bias[0])


def solution(mesh):
    split = P("snap", None, "stream", "radial", None)
    return jax.shard_map(
        local,
        mesh=mesh,
        in_specs=(split, P(), P(), P(), P(), split),
        out_specs=(split, P(), P(), P()),
        check_vma=False,
    )
```

```python
import functools

import numpy as np
import jax
import jax.numpy as jnp
from jax import lax
from jax.experimental import pallas as pl
from jax.experimental.pallas import tpu as pltpu
from jax.sharding import PartitionSpec as P

F32 = jnp.float32
BF16 = jnp.bfloat16
Z = 128
CI = 8
CH = 16
FAR = 100


def natural(n):
    return n // 8, n % 8


def y_first(n):
    return n % CH, n // CH


def rim(channels):
    def of(n):
        side, n = n // (2 * channels), n % (2 * channels)
        return n // 2, n % 2 + 10 * side - 2
    return of


def deep_rim(n):
    part, n = n // 16, n % 16
    return n // 2, n % 2 + 10 * (part // 2) - 2 + (part % 2) * (4 * (part // 2) - 2)


def table(channels, total, places):
    e = np.zeros((total, 128), np.float32)
    ys = np.full((1, total), FAR, np.float32)
    for c in range(3):
        for of, start, step in places:
            ch, y = of(np.arange(step))
            at = start + c * step + np.arange(step)
            e[at, c * channels + ch] = 1
            ys[0, at] = y
    return e, ys


def iota(rows, columns):
    return [lax.broadcasted_iota(jnp.int32, (rows, columns), d) for d in range(2)]


def one_hot(where):
    return jnp.where(where, 1.0, 0.0).astype(BF16)


def lane_y(of, width, step):
    lane = lax.broadcasted_iota(jnp.int32, (1, width), 1)
    return jnp.where(lane < 3 * step, of(lane % step)[1], FAR)


def place(rows, wanted, of, size, slot):
    row, lane = iota(rows, 128)
    return one_hot((of(lane % size)[0] == wanted(row)) & (lane // size == slot))


def row_table(rows, own):
    row, lane = iota(rows, CH)
    own_c, own_y = own(row)
    rim_c, rim_y = rim(CH)(row - 128)
    channel, y = jnp.where(row < 128, own_c, rim_c), jnp.where(row < 128, own_y, rim_y)
    return one_hot(channel == lane), y[:, :1]


def plane(ref, x):
    v = ref[0, :, x].astype(F32)
    return v.reshape(v.shape[0] * v.shape[1], v.shape[2])


def pick_rows(channels, low, high):
    half = channels * 2
    row, col = iota(2 * half, channels * 8)
    side = row // half
    return one_hot(col == (row % half // 2) * 8 + low + (high - low) * side + row % 2)


def partners(index, count):
    return index % 2 == 0, index > 0, index < count - 1


def sides(index, count, near, far):
    near_above, below, above = partners(index, count)
    low = jnp.where(near_above, far, near).astype(F32)
    high = jnp.where(near_above, near, far).astype(F32)
    return jnp.where(below, low, 0.0), jnp.where(above, high, 0.0)


def pack_kernel(fields, cot, near, far, f_rows, c_rows):
    up_first = lax.axis_index("stream") % 2 == 0
    count, at = fields.shape[2], 0
    for ref, out, width in ((fields, f_rows, 4), (cot, c_rows, 2)):
        rows = [plane(ref, x) for x in range(count)]
        for x, v in enumerate(rows):
            out[x] = v.astype(BF16)
        for low, high in zip(rows[:width], rows[count - width:]):
            part = slice(at, at + low.shape[0])
            near[part] = jnp.where(up_first, high, low).astype(BF16)
            far[part] = jnp.where(up_first, low, high).astype(BF16)
            at += low.shape[0]


def x_planes(count, fields, cot, xnear, xfar, size):
    index = lax.axis_index("stream")
    inner = [fields[x].astype(F32) for x in range(count)]
    rims = [sides(index, size, xnear[n * 64:(n + 1) * 64], xfar[n * 64:(n + 1) * 64]) for n in range(4)]
    f = [low for low, _ in rims] + inner + [high for _, high in rims]
    inner = [cot[x].astype(F32) for x in range(count)]
    rims = [sides(index, size, xnear[256 + n * 128:384 + n * 128], xfar[256 + n * 128:384 + n * 128]) for n in range(2)]
    return f, [low for low, _ in rims] + inner + [high for _, high in rims]


def pick_strips(work, near, far):
    up_first = lax.axis_index("radial") % 2 == 0
    at = 0
    for pick, rows in work:
        half = pick.shape[0] // 2
        for v in rows:
            got = jnp.dot(pick, v.astype(BF16), preferred_element_type=F32)
            near[at:at + half] = jnp.where(up_first, got[half:], got[:half]).astype(BF16)
            far[at:at + half] = jnp.where(up_first, got[:half], got[half:]).astype(BF16)
            at += half


def join_kernel(counts, xfar, xnear, fields, cot, near, far):
    f, c = x_planes(fields.shape[0], fields, cot, xnear, xfar, counts[0])
    pick_strips([(pick_rows(CI, 0, 6), f[2:-2]), (pick_rows(CH, 0, 6), c)], near, far)


def join_outer_kernel(counts, xfar, xnear, fields, cot, near, far):
    f, _ = x_planes(fields.shape[0], fields, cot, xnear, xfar, counts[0])
    ends = f[:2] + f[-2:]
    pick_strips([(pick_rows(CI, 0, 6), ends), (pick_rows(CI, 2, 4), ends + f[2:-2])], near, far)


def spread(w, by_row, flip):
    taps = jnp.transpose(w[...].astype(F32))
    width = taps.shape[1]
    row = lax.broadcasted_iota(jnp.int32, (CH, width), 0)
    lane = lax.broadcasted_iota(jnp.int32, (CH, width), 1)
    mine = row == (lane // (width // CH) if by_row else lane % CH)
    found = []
    for c in range(3):
        rows = []
        for ab in range(9):
            t = 26 - (ab * 3 + c) if flip else ab * 3 + c
            rows.append(jnp.where(mine, jnp.broadcast_to(taps[t:t + 1], (CH, width)), 0.0))
        found.append(jnp.concatenate(rows, axis=0).astype(BF16))
    return found


def dots(pairs):
    total = None
    for v, w in pairs:
        part = jnp.dot(v, w, preferred_element_type=F32)
        total = part if total is None else total + part
    return total.astype(BF16)


def packed(parts, wanted, of, size):
    per = 128 // size
    places = [place(parts[0].shape[1], wanted, of, size, slot) for slot in range(min(per, 3))]
    tiles = [range(first, min(first + per, 3)) for first in range(0, 3, per)]
    return jnp.concatenate([dots([(parts[c], places[c % per]) for c in tile]) for tile in tiles], axis=1)


def band(wide, expand, ys, rows_y, t):
    rows, width = t.shape[0], wide.shape[1]
    for a in range(3):
        total = jnp.zeros((rows, width), F32)
        for b in range(3):
            part = jnp.dot(expand[:rows], wide[(a * 3 + b) * CH:(a * 3 + b + 1) * CH], preferred_element_type=F32)
            total = jnp.where(ys == rows_y[:rows] + 2 * (b - 1), part, total)
        t[:, a * width:(a + 1) * width] = total.astype(BF16)


def repeat_bias(bias, expand, out):
    column = jnp.sum(expand.astype(F32) * bias[...], axis=1, keepdims=True)
    out[...] = jnp.broadcast_to(column, out.shape)


def band_kernel(w1, w2, first_bias, second_bias, t1o, t1r, t1d, tbo, tbr, t2, b1, b2):
    expand, rows_y = row_table(192, y_first)
    parts = spread(w1, True, False)
    for of, step, t in ((natural, 64, t1o), (rim(CI), 32, t1r), (deep_rim, 64, t1d)):
        wide = packed(parts, lambda n: n % CI, of, step)
        band(wide, expand, lane_y(of, wide.shape[1], step), rows_y, t)
    parts = spread(w2, False, True)
    for of, step, t in ((natural, 128, tbo), (rim(CH), 64, tbr)):
        wide = packed(parts, lambda n: n // CH, of, step)
        band(wide, expand, lane_y(of, wide.shape[1], step), rows_y, t)
    repeat_bias(first_bias, expand, b1)
    expand, rows_y = row_table(128, natural)
    parts = spread(w2, True, False)
    wide = [packed(parts, lambda n: n % CH, of, step) for of, step in ((y_first, 128), (rim(CH), 64))]
    ys = jnp.concatenate([lane_y(y_first, 384, 128), lane_y(rim(CH), 256, 64)], axis=1)
    band(jnp.concatenate(wide, axis=1), expand, ys, rows_y, t2)
    repeat_bias(second_bias, expand, b2)


def shifted(v):
    lane = lax.broadcasted_iota(jnp.int32, v.shape, 1)
    before = jnp.where(lane >= 2, pltpu.roll(v, 2, 1), 0.0)
    after = jnp.where(lane < Z - 2, pltpu.roll(v, Z - 2, 1), 0.0)
    return before.astype(BF16), v.astype(BF16), after.astype(BF16)


def store_wide(ref, p, v):
    at = slice(p * Z, (p + 1) * Z)
    for c, piece in enumerate(shifted(v)):
        ref[c * 128:(c + 1) * 128, at] = piece[:128]
        ref[384 + c * 64:384 + (c + 1) * 64, at] = piece[128:]
    ref[576:, at] = jnp.zeros((64, Z), BF16)


def stacked(ref, lanes):
    return jnp.concatenate([ref[:, a * 256:a * 256 + lanes] for a in range(3)], axis=0)


def own_kernel(counts, xfar, xnear, fields, cot, t1, tb, b1, fs, cs, pre, back):
    count = fields.shape[0]
    f, c = x_planes(count, fields, cot, xnear, xfar, counts[0])
    for ref, rows in ((fs, f), (cs, c)):
        for p, v in enumerate(rows):
            for n, piece in enumerate(shifted(v)):
                ref[n * v.shape[0]:(n + 1) * v.shape[0], p * Z:(p + 1) * Z] = piece
    fs[192:] = jnp.zeros((64, fs.shape[1]), BF16)
    rows = jnp.concatenate([fs[:, a * 256 + 256:a * 256 + 256 + pre.shape[1]] for a in range(3)], axis=0)
    pre[...] = jnp.dot(t1[:128], rows, preferred_element_type=F32) + b1[:128, :1]
    back[...] = jnp.dot(tb[...], stacked(cs, back.shape[1]), preferred_element_type=F32)


def two_dots(v, w):
    high = v.astype(BF16)
    low = (v - high.astype(F32)).astype(BF16)
    return jnp.dot(high, w, preferred_element_type=F32) + jnp.dot(low, w, preferred_element_type=F32)


def gelu_share(pre):
    return 0.5 * (1.0 + lax.erf(pre * 0.7071067811865476))


def rim_kernel(counts, rfar, rnear, fs, cs, pre_own, back_own, t1, tb, e1t, e2t, rep1, rep2, y1, y2,
               hidden_out, payload, fr, cr, taps):
    count = hidden_out.shape[0]
    lanes = count * Z
    radial = lax.axis_index("radial")
    at = 0
    for ref, half in ((fr, 16), (cr, 32)):
        for p in range(count + 4):
            low, high = sides(radial, counts[1], rnear[at:at + half], rfar[at:at + half])
            for n, piece in enumerate(shifted(jnp.concatenate([low, high], axis=0))):
                ref[n * 2 * half:(n + 1) * 2 * half, p * Z:(p + 1) * Z] = piece
            at += half
        ref[6 * half:] = jnp.zeros((2 * half, ref.shape[1]), BF16)
    pre = pre_own[...] + jnp.dot(t1[...], stacked(fr, lanes), preferred_element_type=F32)
    share = gelu_share(pre)
    hidden = (pre * share).astype(BF16)
    for x in range(count):
        hidden_out[x] = hidden[:, x * Z:(x + 1) * Z]
    back = back_own[...] + jnp.dot(tb[...], stacked(cr, lanes), preferred_element_type=F32)
    dpre = (back * (share + pre * jnp.exp(-0.5 * pre * pre) * 0.3989422804014327)).astype(BF16)
    over_lanes = (((1,), (1,)), ((), ()))
    ones, twos = [], []
    for a in range(3):
        at = slice((a + 1) * 256, (a + 1) * 256 + lanes)
        rows = jnp.concatenate([fs[:, at], fr[:, a * 256:a * 256 + lanes]], axis=0)
        g1 = lax.dot_general(dpre, rows, over_lanes, preferred_element_type=F32)
        at = slice(a * 256, a * 256 + lanes)
        rows = jnp.concatenate([cs[:, at], cr[:, at]], axis=0)
        g2 = lax.dot_general(hidden, rows, over_lanes, preferred_element_type=F32)
        for b in range(3):
            for g, ys, out in ((g1, y1, ones), (g2, y2, twos)):
                total = jnp.zeros((CH, g.shape[1]), F32)
                for y in range(8):
                    total = jnp.where(ys[...] == float(y + 2 * (b - 1)), g[y * CH:(y + 1) * CH], total)
                out.append(total)
    taps[:, 24:] = jnp.zeros((3, 8, 128), F32)
    for parts, et, rep, at, width in ((ones, e1t, rep1, 0, 128), (twos[::-1], e2t, rep2, 1, 256)):
        sums = two_dots(jnp.concatenate(parts, axis=0), et[...])
        wide = two_dots(sums, rep[...])
        row = lax.broadcasted_iota(jnp.int32, wide.shape, 0) % CH
        lane = lax.broadcasted_iota(jnp.int32, wide.shape, 1) % width
        mine = row == (lane // CI if width == 128 else lane % CH)
        total = jnp.sum(jnp.where(mine, wide, 0.0).reshape(9, CH, 3 * width), axis=1)
        for c in range(3):
            first = c if width == 128 else 2 - c
            for n in range(width // 128):
                taps[at + n, pl.ds(first, 9, stride=3)] = total[:, c * width + n * 128:c * width + (n + 1) * 128]
    bias = jnp.sum(dpre.astype(F32), axis=1, keepdims=True)
    bias = sum(bias[y * CH:(y + 1) * CH] for y in range(8))
    row = lax.broadcasted_iota(jnp.int32, (CH, 128), 0)
    lane = lax.broadcasted_iota(jnp.int32, (CH, 128), 1)
    taps[0, 27:28] = jnp.sum(jnp.where(row == lane, bias, 0.0), axis=0, keepdims=True)
    payload[...] = jnp.concatenate([taps[n] for n in range(3)], axis=1)


def hidden_rim_kernel(counts, rfar, rnear, rfar_outer, rnear_outer, hidden, fs, t1o, t1d, b1, hidden_out, fr):
    count = hidden.shape[0]
    stream, radial = lax.axis_index("stream"), lax.axis_index("radial")
    for p in range(count + 8):
        end = p if p < 2 else p - count - 4 if p >= count + 6 else None
        if end is None:
            near, outer = (rnear, rfar, (p - 2) * 16), (rnear_outer, rfar_outer, 128 + (p - 2) * 16)
        else:
            near, outer = (rnear_outer, rfar_outer, end * 16), (rnear_outer, rfar_outer, 64 + end * 16)
        parts = [sides(radial, counts[1], n[at:at + 16], f[at:at + 16]) for n, f, at in (near, outer)]
        rows = jnp.concatenate([part[side] for side in range(2) for part in parts], axis=0)
        for n, piece in enumerate(shifted(rows)):
            fr[n * 64:(n + 1) * 64, p * Z:(p + 1) * Z] = piece
    fr[192:] = jnp.zeros((64, fr.shape[1]), BF16)

    def gelu(rows, lanes):
        total = b1[rows, :1]
        for t, ref in ((t1o, fs), (t1d, fr)):
            cells = [jnp.concatenate([ref[:, a * 256 + at:a * 256 + at + size] for at, size in lanes], axis=1) for a in range(3)]
            total = total + jnp.dot(t[rows], jnp.concatenate(cells, axis=0), preferred_element_type=F32)
        return total * gelu_share(total)

    own = gelu(slice(0, 128), ((0, 2 * Z), ((count + 2) * Z, 2 * Z)))
    rims = gelu(slice(128, 192), ((0, (count + 4) * Z),))
    rims = jnp.concatenate([jnp.where(radial > 0, rims[:32], 0.0), jnp.where(radial < counts[1] - 1, rims[32:], 0.0)], axis=0)
    for p in range(count + 4):
        rim_rows = rims[:, p * Z:(p + 1) * Z]
        if 2 <= p < count + 2:
            hidden_out[p, :128] = hidden[p - 2]
            hidden_out[p, 128:] = rim_rows.astype(BF16)
        else:
            at = p if p < 2 else p - count
            inside = stream > 0 if p < 2 else stream < counts[0] - 1
            rows = jnp.concatenate([own[:, at * Z:(at + 1) * Z], rim_rows], axis=0)
            hidden_out[p] = jnp.where(inside, rows, 0.0).astype(BF16)


def closure_kernel(hidden, t2, b2, closure, hs):
    count = closure.shape[2]
    for p in range(count + 4):
        store_wide(hs, p, hidden[p].astype(F32))
    out = (jnp.dot(t2[...], stacked(hs, count * Z), preferred_element_type=F32) + b2[:, :1]).astype(BF16)
    for x in range(count):
        closure[0, :, x] = out[:, x * Z:(x + 1) * Z].reshape(CH, 8, Z)


def summed(parts):
    parts = [part[...].astype(F32) for part in parts]
    while len(parts) > 1:
        parts = [v + w for v, w in zip(parts[::2], parts[1::2])]
    return parts[0]


def add_kernel(*refs):
    s = summed(refs[:-1])
    lost = s - s.astype(BF16).astype(F32)
    row = lax.broadcasted_iota(jnp.int32, s.shape, 0)
    refs[-1][...] = (s + jnp.where(row == 28, pltpu.roll(lost, 1, 0), 0.0)).astype(BF16)


def finish_kernel(norm, *refs):
    *parts, first, second, bias = refs
    scaled = summed(parts) * norm
    flipped = jnp.transpose(scaled)
    first[...] = flipped[:128, :27]
    second[...] = flipped[128:, :27]
    bias[...] = scaled[27:28, :CH] + scaled[28:29, :CH]


def call(kernel, outs, name, scratch=(), flops=10_000_000, **specs):
    return pl.pallas_call(
        kernel,
        out_shape=outs,
        **specs,
        scratch_shapes=list(scratch),
        compiler_params=pltpu.CompilerParams(vmem_limit_bytes=32 * 1024 * 1024),
        cost_estimate=pl.CostEstimate(flops=flops, bytes_accessed=1_000_000, transcendentals=0),
        name=name,
    )


def shape(*dims, dtype=BF16):
    return jax.ShapeDtypeStruct(dims, dtype)


def exchange(near, far, axis, ends=True):
    count = lax.axis_size(axis)
    pairs = [(i, i - 1 + 2 * (i % 2)) for i in range(1, count - 1)]
    if ends:
        pairs = [(0, 0), *pairs, (count - 1, count - 1)]
    far = lax.ppermute(far, axis, pairs)
    return lax.ppermute(near, axis, [(i, i ^ 1) for i in range(count)]), far


def swap(v, axis, masks):
    count = lax.axis_size(axis)
    return [lax.ppermute(v, axis, [(i, i ^ mask) for i in range(count)]) for mask in masks]


def add(v, arrived):
    return call(add_kernel, shape(*v.shape), "add_parts")(v, *arrived)


def rounds(axis, most):
    found, step = [], 1
    while step < lax.axis_size(axis):
        masks = [step * n for n in range(1, most if step * most <= lax.axis_size(axis) else 2)]
        found.append((axis, masks))
        step *= len(masks) + 1
    return found


def local(fields, first_weight, first_bias, second_weight, second_bias, cotangent):
    e1t, y1 = table(CI, 384, ((natural, 0, 64), (rim(CI), 256, 32)))
    e2t, y2 = table(CH, 640, ((natural, 0, 128), (rim(CH), 384, 64)))
    rep1, rep2 = np.zeros((128, 384), np.float32), np.zeros((128, 768), np.float32)
    for c in range(3):
        rep1[c * CI:(c + 1) * CI, c * 128:(c + 1) * 128] = np.tile(np.eye(CI), (1, CH))
        rep2[c * CH:(c + 1) * CH, c * 256:(c + 1) * 256] = np.repeat(np.eye(CH), CH, axis=1)

    def const(*arrays, dtype=BF16):
        return [jnp.asarray(v, dtype) for v in arrays]

    planes = fields.shape[2]
    w1 = first_weight.transpose(1, 2, 0).reshape(CH * CI, 27)
    w2 = second_weight.transpose(1, 2, 0).reshape(CH * CH, 27)
    near, far, f_rows, c_rows = call(
        pack_kernel,
        (shape(512, Z), shape(512, Z), shape(planes, CI * 8, Z), shape(planes, CH * 8, Z)),
        "pack_strips",
        flops=4_000_000_000,
    )(fields, cotangent)
    xnear, xfar = exchange(near, far, "stream")
    wide = (planes + 4) * Z
    counts = (lax.axis_size("stream"), lax.axis_size("radial"))
    t1o, t1r, t1d, tbo, tbr, t2, b1, b2 = call(
        band_kernel,
        (shape(192, 768), shape(128, 384), shape(192, 768), shape(128, 1152), shape(128, 768), shape(128, 1920),
         shape(192, 128, dtype=F32), shape(128, 128, dtype=F32)),
        "band_matrices",
        flops=4_000_000_000,
    )(w1, w2, first_bias[None], second_bias[None])
    xfar, xnear, t1o, tbo = lax.optimization_barrier((xfar, xnear, t1o, tbo))
    inner, outer = shape((planes + 4) * 48, Z), shape(128 + (planes + 4) * 16, Z)
    near, far = call(functools.partial(join_kernel, counts), (inner, inner), "join_strips")(xfar, xnear, f_rows, c_rows)
    rnear, rfar = exchange(near, far, "radial", ends=False)
    near_outer, far_outer = call(functools.partial(join_outer_kernel, counts), (outer, outer), "join_outer")(
        xfar, xnear, f_rows, c_rows)
    rnear_outer, rfar_outer = exchange(near_outer, far_outer, "radial", ends=False)
    fs, cs, pre, back = call(
        functools.partial(own_kernel, counts),
        (shape(256, wide + 4 * Z), shape(384, wide), shape(128, planes * Z, dtype=F32), shape(128, planes * Z, dtype=F32)),
        "own_rows",
        flops=1_000_000_000,
    )(xfar, xnear, f_rows, c_rows, t1o, tbo, b1)
    hidden, payload = call(
        functools.partial(rim_kernel, counts),
        (shape(planes, 128, Z), shape(32, 384, dtype=F32)),
        "gradients",
        (pltpu.VMEM((128, wide), BF16), pltpu.VMEM((256, wide), BF16), pltpu.VMEM((3, 32, 128), F32)),
        flops=2_000_000_000,
    )(rfar, rnear, fs, cs, pre, back, t1r, tbr, *const(e1t, e2t, rep1, rep2), *const(y1, y2, dtype=F32))

    steps = rounds("radial", 2) + rounds("stream", 4) + rounds("snap", 2)
    arrived = swap(payload, *steps[0])
    payload = add(payload, arrived)
    arrived = swap(payload, *steps[1])
    hidden = call(
        functools.partial(hidden_rim_kernel, counts),
        shape(planes + 4, 192, Z),
        "hidden_rim",
        (pltpu.VMEM((256, wide + 4 * Z), BF16),),
        flops=1_000_000_000,
    )(rfar, rnear, rfar_outer, rnear_outer, hidden, fs, t1o, t1d, b1)
    payload, hidden = lax.optimization_barrier((add(payload, arrived), hidden))
    arrived = swap(payload, *steps[2])
    payload = add(payload, arrived)
    arrived = swap(payload, *steps[3])
    closure = call(
        closure_kernel, shape(*cotangent.shape), "closure", (pltpu.VMEM((640, wide), BF16),), flops=1_000_000_000
    )(hidden, t2, b2)
    for step in steps[4:]:
        payload = add(payload, arrived)
        arrived = swap(payload, *step)

    cells = fields.shape[0] * fields.shape[2] * fields.shape[3] * fields.shape[4]
    for axis in ("stream", "radial", "snap"):
        cells *= lax.axis_size(axis)
    norm = float(1.0 / np.sqrt(np.float32(cells)))
    first, second, bias = call(
        functools.partial(finish_kernel, norm),
        (shape(CH * CI, 27, dtype=F32), shape(CH * CH, 27, dtype=F32), shape(1, CH, dtype=F32)),
        "finish",
    )(payload, *arrived)
    first = first.reshape(CH, CI, 27).transpose(2, 0, 1)
    second = second.reshape(CH, CH, 27).transpose(2, 0, 1)
    return (closure, first, second, bias[0])


def solution(mesh):
    split = P("snap", None, "stream", "radial", None)
    return jax.shard_map(
        local,
        mesh=mesh,
        in_specs=(split, P(), P(), P(), P(), split),
        out_specs=(split, P(), P(), P()),
        check_vma=False,
    )
```

```python
import functools

import numpy as np
import jax
import jax.numpy as jnp
from jax import lax
from jax.experimental import pallas as pl
from jax.experimental.pallas import tpu as pltpu
from jax.sharding import PartitionSpec as P

F32 = jnp.float32
BF16 = jnp.bfloat16
Z = 128
CI = 8
CH = 16
FAR = 100


def natural(n):
    return n // 8, n % 8


def y_first(n):
    return n % CH, n // CH


def rim(channels):
    def of(n):
        side, n = n // (2 * channels), n % (2 * channels)
        return n // 2, n % 2 + 10 * side - 2
    return of


def deep_rim(n):
    part, n = n // 16, n % 16
    return n // 2, n % 2 + 10 * (part // 2) - 2 + (part % 2) * (4 * (part // 2) - 2)


def table(channels, total, places):
    e = np.zeros((total, 128), np.float32)
    ys = np.full((1, total), FAR, np.float32)
    for c in range(3):
        for of, start, step in places:
            ch, y = of(np.arange(step))
            at = start + c * step + np.arange(step)
            e[at, c * channels + ch] = 1
            ys[0, at] = y
    return e, ys


def iota(rows, columns):
    return [lax.broadcasted_iota(jnp.int32, (rows, columns), d) for d in range(2)]


def one_hot(where):
    return jnp.where(where, 1.0, 0.0).astype(BF16)


def lane_y(of, width, step):
    lane = lax.broadcasted_iota(jnp.int32, (1, width), 1)
    return jnp.where(lane < 3 * step, of(lane % step)[1], FAR)


def place(rows, wanted, of, size, slot):
    row, lane = iota(rows, 128)
    return one_hot((of(lane % size)[0] == wanted(row)) & (lane // size == slot))


def row_table(rows, own):
    row, lane = iota(rows, CH)
    own_c, own_y = own(row)
    rim_c, rim_y = rim(CH)(row - 128)
    channel, y = jnp.where(row < 128, own_c, rim_c), jnp.where(row < 128, own_y, rim_y)
    return one_hot(channel == lane), y[:, :1]


def plane(ref, channels, x):
    v = ref[channels, x].astype(F32)
    return v.reshape(v.shape[0] * v.shape[1], v.shape[2])


def pick_rows(channels, low, high):
    half = channels * 2
    row, col = iota(2 * half, channels * 8)
    side = row // half
    return one_hot(col == (row % half // 2) * 8 + low + (high - low) * side + row % 2)


def partners(index, count):
    return index % 2 == 0, index > 0, index < count - 1


def sides(index, count, near, far):
    near_above, below, above = partners(index, count)
    low = jnp.where(near_above, far, near).astype(F32)
    high = jnp.where(near_above, near, far).astype(F32)
    return jnp.where(below, low, 0.0), jnp.where(above, high, 0.0)


def pack_kernel(inputs, near, far, f_rows, c_rows):
    up_first = lax.axis_index("stream") % 2 == 0
    count, at = inputs.shape[1], 0
    for channels, out, width in ((slice(0, CI), f_rows, 4), (slice(CI, CI + CH), c_rows, 2)):
        rows = [plane(inputs, channels, x) for x in range(count)]
        for x, v in enumerate(rows):
            out[x] = v.astype(BF16)
        for low, high in zip(rows[:width], rows[count - width:]):
            part = slice(at, at + low.shape[0])
            near[part] = jnp.where(up_first, high, low).astype(BF16)
            far[part] = jnp.where(up_first, low, high).astype(BF16)
            at += low.shape[0]


def x_planes(count, fields, cot, xnear, xfar, size):
    index = lax.axis_index("stream")
    inner = [fields[x].astype(F32) for x in range(count)]
    rims = [sides(index, size, xnear[n * 64:(n + 1) * 64], xfar[n * 64:(n + 1) * 64]) for n in range(4)]
    f = [low for low, _ in rims] + inner + [high for _, high in rims]
    inner = [cot[x].astype(F32) for x in range(count)]
    rims = [sides(index, size, xnear[256 + n * 128:384 + n * 128], xfar[256 + n * 128:384 + n * 128]) for n in range(2)]
    return f, [low for low, _ in rims] + inner + [high for _, high in rims]


def pick_strips(work, near, far):
    up_first = lax.axis_index("radial") % 2 == 0
    at = 0
    for pick, rows in work:
        half = pick.shape[0] // 2
        for v in rows:
            got = jnp.dot(pick, v.astype(BF16), preferred_element_type=F32)
            near[at:at + half] = jnp.where(up_first, got[half:], got[:half]).astype(BF16)
            far[at:at + half] = jnp.where(up_first, got[:half], got[half:]).astype(BF16)
            at += half


def join_kernel(counts, xfar, xnear, fields, cot, near, far):
    f, c = x_planes(fields.shape[0], fields, cot, xnear, xfar, counts[0])
    pick_strips([(pick_rows(CI, 0, 6), f[2:-2]), (pick_rows(CH, 0, 6), c)], near, far)


def join_outer_kernel(counts, xfar, xnear, fields, cot, near, far):
    f, _ = x_planes(fields.shape[0], fields, cot, xnear, xfar, counts[0])
    ends = f[:2] + f[-2:]
    pick_strips([(pick_rows(CI, 0, 6), ends), (pick_rows(CI, 2, 4), ends + f[2:-2])], near, far)


def spread(w, by_row, flip):
    taps = jnp.transpose(w[...].astype(F32))
    width = taps.shape[1]
    row = lax.broadcasted_iota(jnp.int32, (CH, width), 0)
    lane = lax.broadcasted_iota(jnp.int32, (CH, width), 1)
    mine = row == (lane // (width // CH) if by_row else lane % CH)
    found = []
    for c in range(3):
        rows = []
        for ab in range(9):
            t = 26 - (ab * 3 + c) if flip else ab * 3 + c
            rows.append(jnp.where(mine, jnp.broadcast_to(taps[t:t + 1], (CH, width)), 0.0))
        found.append(jnp.concatenate(rows, axis=0).astype(BF16))
    return found


def dots(pairs):
    total = None
    for v, w in pairs:
        part = jnp.dot(v, w, preferred_element_type=F32)
        total = part if total is None else total + part
    return total.astype(BF16)


def packed(parts, wanted, of, size):
    per = 128 // size
    places = [place(parts[0].shape[1], wanted, of, size, slot) for slot in range(min(per, 3))]
    tiles = [range(first, min(first + per, 3)) for first in range(0, 3, per)]
    return jnp.concatenate([dots([(parts[c], places[c % per]) for c in tile]) for tile in tiles], axis=1)


def band(wide, expand, ys, rows_y, t):
    rows, width = t.shape[0], wide.shape[1]
    for a in range(3):
        total = jnp.zeros((rows, width), F32)
        for b in range(3):
            part = jnp.dot(expand[:rows], wide[(a * 3 + b) * CH:(a * 3 + b + 1) * CH], preferred_element_type=F32)
            total = jnp.where(ys == rows_y[:rows] + 2 * (b - 1), part, total)
        t[:, a * width:(a + 1) * width] = total.astype(BF16)


def repeat_bias(bias, expand, out):
    column = jnp.sum(expand.astype(F32) * bias[...], axis=1, keepdims=True)
    out[...] = jnp.broadcast_to(column, out.shape)


def band_kernel(w1, w2, first_bias, second_bias, t1o, t1r, t1d, tbo, tbr, t2, b1, b2):
    expand, rows_y = row_table(192, y_first)
    parts = spread(w1, True, False)
    for of, step, t in ((natural, 64, t1o), (rim(CI), 32, t1r), (deep_rim, 64, t1d)):
        wide = packed(parts, lambda n: n % CI, of, step)
        band(wide, expand, lane_y(of, wide.shape[1], step), rows_y, t)
    parts = spread(w2, False, True)
    for of, step, t in ((natural, 128, tbo), (rim(CH), 64, tbr)):
        wide = packed(parts, lambda n: n // CH, of, step)
        band(wide, expand, lane_y(of, wide.shape[1], step), rows_y, t)
    repeat_bias(first_bias, expand, b1)
    expand, rows_y = row_table(128, natural)
    parts = spread(w2, True, False)
    wide = [packed(parts, lambda n: n % CH, of, step) for of, step in ((y_first, 128), (rim(CH), 64))]
    ys = jnp.concatenate([lane_y(y_first, 384, 128), lane_y(rim(CH), 256, 64)], axis=1)
    band(jnp.concatenate(wide, axis=1), expand, ys, rows_y, t2)
    repeat_bias(second_bias, expand, b2)


def shifted(v):
    lane = lax.broadcasted_iota(jnp.int32, v.shape, 1)
    before = jnp.where(lane >= 2, pltpu.roll(v, 2, 1), 0.0)
    after = jnp.where(lane < Z - 2, pltpu.roll(v, Z - 2, 1), 0.0)
    return before.astype(BF16), v.astype(BF16), after.astype(BF16)


def store_wide(ref, p, v):
    at = slice(p * Z, (p + 1) * Z)
    for c, piece in enumerate(shifted(v)):
        ref[c * 128:(c + 1) * 128, at] = piece[:128]
        ref[384 + c * 64:384 + (c + 1) * 64, at] = piece[128:]
    ref[576:, at] = jnp.zeros((64, Z), BF16)


def stacked(ref, lanes):
    return jnp.concatenate([ref[:, a * 256:a * 256 + lanes] for a in range(3)], axis=0)


def own_kernel(counts, xfar, xnear, fields, cot, t1, tb, b1, fs, cs, pre, back):
    count = fields.shape[0]
    f, c = x_planes(count, fields, cot, xnear, xfar, counts[0])
    for ref, rows in ((fs, f), (cs, c)):
        for p, v in enumerate(rows):
            for n, piece in enumerate(shifted(v)):
                ref[n * v.shape[0]:(n + 1) * v.shape[0], p * Z:(p + 1) * Z] = piece
    fs[192:] = jnp.zeros((64, fs.shape[1]), BF16)
    rows = jnp.concatenate([fs[:, a * 256 + 256:a * 256 + 256 + pre.shape[1]] for a in range(3)], axis=0)
    pre[...] = jnp.dot(t1[:128], rows, preferred_element_type=F32) + b1[:128, :1]
    back[...] = jnp.dot(tb[...], stacked(cs, back.shape[1]), preferred_element_type=F32)


def two_dots(v, w):
    high = v.astype(BF16)
    low = (v - high.astype(F32)).astype(BF16)
    return jnp.dot(high, w, preferred_element_type=F32) + jnp.dot(low, w, preferred_element_type=F32)


def gelu_share(pre):
    return 0.5 * (1.0 + lax.erf(pre * 0.7071067811865476))


def rim_kernel(counts, rfar, rnear, fs, cs, pre_own, back_own, t1, tb, e1t, e2t, rep1, rep2, y1, y2,
               hidden_out, payload, fr, cr, taps):
    count = hidden_out.shape[0]
    lanes = count * Z
    radial = lax.axis_index("radial")
    at = 0
    for ref, half in ((fr, 16), (cr, 32)):
        for p in range(count + 4):
            low, high = sides(radial, counts[1], rnear[at:at + half], rfar[at:at + half])
            for n, piece in enumerate(shifted(jnp.concatenate([low, high], axis=0))):
                ref[n * 2 * half:(n + 1) * 2 * half, p * Z:(p + 1) * Z] = piece
            at += half
        ref[6 * half:] = jnp.zeros((2 * half, ref.shape[1]), BF16)
    pre = pre_own[...] + jnp.dot(t1[...], stacked(fr, lanes), preferred_element_type=F32)
    share = gelu_share(pre)
    hidden = (pre * share).astype(BF16)
    for x in range(count):
        hidden_out[x] = hidden[:, x * Z:(x + 1) * Z]
    back = back_own[...] + jnp.dot(tb[...], stacked(cr, lanes), preferred_element_type=F32)
    dpre = (back * (share + pre * jnp.exp(-0.5 * pre * pre) * 0.3989422804014327)).astype(BF16)
    over_lanes = (((1,), (1,)), ((), ()))
    ones, twos = [], []
    for a in range(3):
        at = slice((a + 1) * 256, (a + 1) * 256 + lanes)
        rows = jnp.concatenate([fs[:, at], fr[:, a * 256:a * 256 + lanes]], axis=0)
        g1 = lax.dot_general(dpre, rows, over_lanes, preferred_element_type=F32)
        at = slice(a * 256, a * 256 + lanes)
        rows = jnp.concatenate([cs[:, at], cr[:, at]], axis=0)
        g2 = lax.dot_general(hidden, rows, over_lanes, preferred_element_type=F32)
        for b in range(3):
            for g, ys, out in ((g1, y1, ones), (g2, y2, twos)):
                total = jnp.zeros((CH, g.shape[1]), F32)
                for y in range(8):
                    total = jnp.where(ys[...] == float(y + 2 * (b - 1)), g[y * CH:(y + 1) * CH], total)
                out.append(total)
    taps[:, 24:] = jnp.zeros((3, 8, 128), F32)
    for parts, et, rep, at, width in ((ones, e1t, rep1, 0, 128), (twos[::-1], e2t, rep2, 1, 256)):
        sums = two_dots(jnp.concatenate(parts, axis=0), et[...])
        wide = two_dots(sums, rep[...])
        row = lax.broadcasted_iota(jnp.int32, wide.shape, 0) % CH
        lane = lax.broadcasted_iota(jnp.int32, wide.shape, 1) % width
        mine = row == (lane // CI if width == 128 else lane % CH)
        total = jnp.sum(jnp.where(mine, wide, 0.0).reshape(9, CH, 3 * width), axis=1)
        for c in range(3):
            first = c if width == 128 else 2 - c
            for n in range(width // 128):
                taps[at + n, pl.ds(first, 9, stride=3)] = total[:, c * width + n * 128:c * width + (n + 1) * 128]
    bias = jnp.sum(dpre.astype(F32), axis=1, keepdims=True)
    bias = sum(bias[y * CH:(y + 1) * CH] for y in range(8))
    row = lax.broadcasted_iota(jnp.int32, (CH, 128), 0)
    lane = lax.broadcasted_iota(jnp.int32, (CH, 128), 1)
    taps[0, 27:28] = jnp.sum(jnp.where(row == lane, bias, 0.0), axis=0, keepdims=True)
    payload[...] = jnp.concatenate([taps[n] for n in range(3)], axis=1)


def hidden_rim_kernel(counts, rfar, rnear, rfar_outer, rnear_outer, hidden, fs, t1o, t1d, b1, hidden_out, fr):
    count = hidden.shape[0]
    stream, radial = lax.axis_index("stream"), lax.axis_index("radial")
    for p in range(count + 8):
        end = p if p < 2 else p - count - 4 if p >= count + 6 else None
        if end is None:
            near, outer = (rnear, rfar, (p - 2) * 16), (rnear_outer, rfar_outer, 128 + (p - 2) * 16)
        else:
            near, outer = (rnear_outer, rfar_outer, end * 16), (rnear_outer, rfar_outer, 64 + end * 16)
        parts = [sides(radial, counts[1], n[at:at + 16], f[at:at + 16]) for n, f, at in (near, outer)]
        rows = jnp.concatenate([part[side] for side in range(2) for part in parts], axis=0)
        for n, piece in enumerate(shifted(rows)):
            fr[n * 64:(n + 1) * 64, p * Z:(p + 1) * Z] = piece
    fr[192:] = jnp.zeros((64, fr.shape[1]), BF16)

    def gelu(rows, lanes):
        total = b1[rows, :1]
        for t, ref in ((t1o, fs), (t1d, fr)):
            cells = [jnp.concatenate([ref[:, a * 256 + at:a * 256 + at + size] for at, size in lanes], axis=1) for a in range(3)]
            total = total + jnp.dot(t[rows], jnp.concatenate(cells, axis=0), preferred_element_type=F32)
        return total * gelu_share(total)

    own = gelu(slice(0, 128), ((0, 2 * Z), ((count + 2) * Z, 2 * Z)))
    rims = gelu(slice(128, 192), ((0, (count + 4) * Z),))
    rims = jnp.concatenate([jnp.where(radial > 0, rims[:32], 0.0), jnp.where(radial < counts[1] - 1, rims[32:], 0.0)], axis=0)
    for p in range(count + 4):
        rim_rows = rims[:, p * Z:(p + 1) * Z]
        if 2 <= p < count + 2:
            hidden_out[p, :128] = hidden[p - 2]
            hidden_out[p, 128:] = rim_rows.astype(BF16)
        else:
            at = p if p < 2 else p - count
            inside = stream > 0 if p < 2 else stream < counts[0] - 1
            rows = jnp.concatenate([own[:, at * Z:(at + 1) * Z], rim_rows], axis=0)
            hidden_out[p] = jnp.where(inside, rows, 0.0).astype(BF16)


def closure_kernel(hidden, t2, b2, closure, hs):
    count = closure.shape[2]
    for p in range(count + 4):
        store_wide(hs, p, hidden[p].astype(F32))
    out = (jnp.dot(t2[...], stacked(hs, count * Z), preferred_element_type=F32) + b2[:, :1]).astype(BF16)
    for x in range(count):
        closure[0, :, x] = out[:, x * Z:(x + 1) * Z].reshape(CH, 8, Z)


def summed(parts):
    parts = [part[...].astype(F32) for part in parts]
    while len(parts) > 1:
        parts = [v + w for v, w in zip(parts[::2], parts[1::2])]
    return parts[0]


def add_kernel(*refs):
    s = summed(refs[:-1])
    lost = s - s.astype(BF16).astype(F32)
    row = lax.broadcasted_iota(jnp.int32, s.shape, 0)
    refs[-1][...] = (s + jnp.where(row == 28, pltpu.roll(lost, 1, 0), 0.0)).astype(BF16)


def finish_kernel(norm, *refs):
    *parts, first, second, bias = refs
    scaled = summed(parts) * norm
    flipped = jnp.transpose(scaled)
    first[...] = flipped[:128, :27]
    second[...] = flipped[128:, :27]
    bias[...] = scaled[27:28, :CH] + scaled[28:29, :CH]


def call(kernel, outs, name, scratch=(), flops=10_000_000, **specs):
    return pl.pallas_call(
        kernel,
        out_shape=outs,
        **specs,
        scratch_shapes=list(scratch),
        compiler_params=pltpu.CompilerParams(vmem_limit_bytes=32 * 1024 * 1024),
        cost_estimate=pl.CostEstimate(flops=flops, bytes_accessed=1_000_000, transcendentals=0),
        name=name,
    )


def shape(*dims, dtype=BF16):
    return jax.ShapeDtypeStruct(dims, dtype)


def exchange(near, far, axis, ends=True):
    count = lax.axis_size(axis)
    pairs = [(i, i - 1 + 2 * (i % 2)) for i in range(1, count - 1)]
    if ends:
        pairs = [(0, 0), *pairs, (count - 1, count - 1)]
    far = lax.ppermute(far, axis, pairs)
    return lax.ppermute(near, axis, [(i, i ^ 1) for i in range(count)]), far


def swap(v, axis, masks):
    count = lax.axis_size(axis)
    return [lax.ppermute(v, axis, [(i, i ^ mask) for i in range(count)]) for mask in masks]


def add(v, arrived):
    return call(add_kernel, shape(*v.shape), "add_parts")(v, *arrived)


def rounds(axis, most):
    found, step = [], 1
    while step < lax.axis_size(axis):
        masks = [step * n for n in range(1, most if step * most <= lax.axis_size(axis) else 2)]
        found.append((axis, masks))
        step *= len(masks) + 1
    return found


def local(fields, first_weight, first_bias, second_weight, second_bias, cotangent):
    e1t, y1 = table(CI, 384, ((natural, 0, 64), (rim(CI), 256, 32)))
    e2t, y2 = table(CH, 640, ((natural, 0, 128), (rim(CH), 384, 64)))
    rep1, rep2 = np.zeros((128, 384), np.float32), np.zeros((128, 768), np.float32)
    for c in range(3):
        rep1[c * CI:(c + 1) * CI, c * 128:(c + 1) * 128] = np.tile(np.eye(CI), (1, CH))
        rep2[c * CH:(c + 1) * CH, c * 256:(c + 1) * 256] = np.repeat(np.eye(CH), CH, axis=1)

    def const(*arrays, dtype=BF16):
        return [jnp.asarray(v, dtype) for v in arrays]

    planes = fields.shape[2]
    w1 = first_weight.transpose(1, 2, 0).reshape(CH * CI, 27)
    w2 = second_weight.transpose(1, 2, 0).reshape(CH * CH, 27)
    near, far, f_rows, c_rows = call(
        pack_kernel,
        (shape(512, Z), shape(512, Z), shape(planes, CI * 8, Z), shape(planes, CH * 8, Z)),
        "pack_strips",
        flops=4_000_000_000,
    )(jnp.concatenate([fields[0], cotangent[0]], axis=0))
    xnear, xfar = exchange(near, far, "stream")
    wide = (planes + 4) * Z
    counts = (lax.axis_size("stream"), lax.axis_size("radial"))
    t1o, t1r, t1d, tbo, tbr, t2, b1, b2 = call(
        band_kernel,
        (shape(192, 768), shape(128, 384), shape(192, 768), shape(128, 1152), shape(128, 768), shape(128, 1920),
         shape(192, 128, dtype=F32), shape(128, 128, dtype=F32)),
        "band_matrices",
        flops=4_000_000_000,
    )(w1, w2, first_bias[None], second_bias[None])
    xfar, xnear, t1o, tbo = lax.optimization_barrier((xfar, xnear, t1o, tbo))
    inner, outer = shape((planes + 4) * 48, Z), shape(128 + (planes + 4) * 16, Z)
    near, far = call(functools.partial(join_kernel, counts), (inner, inner), "join_strips")(xfar, xnear, f_rows, c_rows)
    rnear, rfar = exchange(near, far, "radial", ends=False)
    fs, cs, pre, back = call(
        functools.partial(own_kernel, counts),
        (shape(256, wide + 4 * Z), shape(384, wide), shape(128, planes * Z, dtype=F32), shape(128, planes * Z, dtype=F32)),
        "own_rows",
        flops=1_000_000_000,
    )(xfar, xnear, f_rows, c_rows, t1o, tbo, b1)
    f_rows, fs = lax.optimization_barrier((f_rows, fs))
    near_outer, far_outer = call(functools.partial(join_outer_kernel, counts), (outer, outer), "join_outer")(
        xfar, xnear, f_rows, c_rows)
    rnear_outer, rfar_outer = exchange(near_outer, far_outer, "radial", ends=False)
    hidden, payload = call(
        functools.partial(rim_kernel, counts),
        (shape(planes, 128, Z), shape(32, 384, dtype=F32)),
        "gradients",
        (pltpu.VMEM((128, wide), BF16), pltpu.VMEM((256, wide), BF16), pltpu.VMEM((3, 32, 128), F32)),
        flops=2_000_000_000,
    )(rfar, rnear, fs, cs, pre, back, t1r, tbr, *const(e1t, e2t, rep1, rep2), *const(y1, y2, dtype=F32))

    steps = rounds("radial", 2) + rounds("stream", 4) + rounds("snap", 2)
    arrived = swap(payload, *steps[0])
    payload = add(payload, arrived)
    arrived = swap(payload, *steps[1])
    hidden = call(
        functools.partial(hidden_rim_kernel, counts),
        shape(planes + 4, 192, Z),
        "hidden_rim",
        (pltpu.VMEM((256, wide + 4 * Z), BF16),),
        flops=1_000_000_000,
    )(rfar, rnear, rfar_outer, rnear_outer, hidden, fs, t1o, t1d, b1)
    payload, hidden = lax.optimization_barrier((add(payload, arrived), hidden))
    arrived = swap(payload, *steps[2])
    payload = add(payload, arrived)
    arrived = swap(payload, *steps[3])
    closure = call(
        closure_kernel, shape(*cotangent.shape), "closure", (pltpu.VMEM((640, wide), BF16),), flops=1_000_000_000
    )(hidden, t2, b2)
    for step in steps[4:]:
        payload = add(payload, arrived)
        arrived = swap(payload, *step)

    cells = fields.shape[0] * fields.shape[2] * fields.shape[3] * fields.shape[4]
    for axis in ("stream", "radial", "snap"):
        cells *= lax.axis_size(axis)
    norm = float(1.0 / np.sqrt(np.float32(cells)))
    first, second, bias = call(
        functools.partial(finish_kernel, norm),
        (shape(CH * CI, 27, dtype=F32), shape(CH * CH, 27, dtype=F32), shape(1, CH, dtype=F32)),
        "finish",
    )(payload, *arrived)
    first = first.reshape(CH, CI, 27).transpose(2, 0, 1)
    second = second.reshape(CH, CH, 27).transpose(2, 0, 1)
    return (closure, first, second, bias[0])


def solution(mesh):
    split = P("snap", None, "stream", "radial", None)
    return jax.shard_map(
        local,
        mesh=mesh,
        in_specs=(split, P(), P(), P(), P(), split),
        out_specs=(split, P(), P(), P()),
        check_vma=False,
    )
```

```python
import functools

import numpy as np
import jax
import jax.numpy as jnp
from jax import lax
from jax.experimental import pallas as pl
from jax.experimental.pallas import tpu as pltpu
from jax.sharding import PartitionSpec as P

F32 = jnp.float32
BF16 = jnp.bfloat16
Z = 128
CI = 8
CH = 16
FAR = 100


def natural(n):
    return n // 8, n % 8


def y_first(n):
    return n % CH, n // CH


def rim(channels):
    def of(n):
        side, n = n // (2 * channels), n % (2 * channels)
        return n // 2, n % 2 + 10 * side - 2
    return of


def deep_rim(n):
    part, n = n // 16, n % 16
    return n // 2, n % 2 + 10 * (part // 2) - 2 + (part % 2) * (4 * (part // 2) - 2)


def table(channels, total, places):
    e = np.zeros((total, 128), np.float32)
    ys = np.full((1, total), FAR, np.float32)
    for c in range(3):
        for of, start, step in places:
            ch, y = of(np.arange(step))
            at = start + c * step + np.arange(step)
            e[at, c * channels + ch] = 1
            ys[0, at] = y
    return e, ys


def iota(rows, columns):
    return [lax.broadcasted_iota(jnp.int32, (rows, columns), d) for d in range(2)]


def one_hot(where):
    return jnp.where(where, 1.0, 0.0).astype(BF16)


def lane_y(of, width, step):
    lane = lax.broadcasted_iota(jnp.int32, (1, width), 1)
    return jnp.where(lane < 3 * step, of(lane % step)[1], FAR)


def place(rows, wanted, of, size, slot):
    row, lane = iota(rows, 128)
    return one_hot((of(lane % size)[0] == wanted(row)) & (lane // size == slot))


def row_table(rows, own):
    row, lane = iota(rows, CH)
    own_c, own_y = own(row)
    rim_c, rim_y = rim(CH)(row - 128)
    channel, y = jnp.where(row < 128, own_c, rim_c), jnp.where(row < 128, own_y, rim_y)
    return one_hot(channel == lane), y[:, :1]


def plane(ref, channels, x):
    v = ref[channels, x].astype(F32)
    return v.reshape(v.shape[0] * v.shape[1], v.shape[2])


def pick_rows(channels, low, high):
    half = channels * 2
    row, col = iota(2 * half, channels * 8)
    side = row // half
    return one_hot(col == (row % half // 2) * 8 + low + (high - low) * side + row % 2)


def partners(index, count):
    return index % 2 == 0, index > 0, index < count - 1


def sides(index, count, near, far):
    near_above, below, above = partners(index, count)
    low = jnp.where(near_above, far, near).astype(F32)
    high = jnp.where(near_above, near, far).astype(F32)
    return jnp.where(below, low, 0.0), jnp.where(above, high, 0.0)


def pack_kernel(inputs, near, far, f_rows, c_rows):
    up_first = lax.axis_index("stream") % 2 == 0
    count, at = inputs.shape[1], 0
    for channels, out, width in ((slice(0, CI), f_rows, 4), (slice(CI, CI + CH), c_rows, 2)):
        rows = [plane(inputs, channels, x) for x in range(count)]
        for x, v in enumerate(rows):
            out[x] = v.astype(BF16)
        for low, high in zip(rows[:width], rows[count - width:]):
            part = slice(at, at + low.shape[0])
            near[part] = jnp.where(up_first, high, low).astype(BF16)
            far[part] = jnp.where(up_first, low, high).astype(BF16)
            at += low.shape[0]


def x_planes(count, fields, cot, xnear, xfar, size):
    index = lax.axis_index("stream")
    inner = [fields[x].astype(F32) for x in range(count)]
    rims = [sides(index, size, xnear[n * 64:(n + 1) * 64], xfar[n * 64:(n + 1) * 64]) for n in range(4)]
    f = [low for low, _ in rims] + inner + [high for _, high in rims]
    inner = [cot[x].astype(F32) for x in range(count)]
    rims = [sides(index, size, xnear[256 + n * 128:384 + n * 128], xfar[256 + n * 128:384 + n * 128]) for n in range(2)]
    return f, [low for low, _ in rims] + inner + [high for _, high in rims]


def pick_strips(work, near, far):
    up_first = lax.axis_index("radial") % 2 == 0
    at = 0
    for pick, rows in work:
        half = pick.shape[0] // 2
        for v in rows:
            got = jnp.dot(pick, v.astype(BF16), preferred_element_type=F32)
            near[at:at + half] = jnp.where(up_first, got[half:], got[:half]).astype(BF16)
            far[at:at + half] = jnp.where(up_first, got[:half], got[half:]).astype(BF16)
            at += half


def join_kernel(counts, xfar, xnear, fields, cot, near, far):
    f, c = x_planes(fields.shape[0], fields, cot, xnear, xfar, counts[0])
    pick_strips([(pick_rows(CI, 0, 6), f[2:-2]), (pick_rows(CH, 0, 6), c)], near, far)


def join_outer_kernel(counts, xfar, xnear, fields, cot, near, far):
    f, _ = x_planes(fields.shape[0], fields, cot, xnear, xfar, counts[0])
    ends = f[:2] + f[-2:]
    pick_strips([(pick_rows(CI, 0, 6), ends), (pick_rows(CI, 2, 4), ends + f[2:-2])], near, far)


def spread(w, by_row, flip):
    taps = jnp.transpose(w[...].astype(F32))
    width = taps.shape[1]
    row = lax.broadcasted_iota(jnp.int32, (CH, width), 0)
    lane = lax.broadcasted_iota(jnp.int32, (CH, width), 1)
    mine = row == (lane // (width // CH) if by_row else lane % CH)
    found = []
    for c in range(3):
        rows = []
        for ab in range(9):
            t = 26 - (ab * 3 + c) if flip else ab * 3 + c
            rows.append(jnp.where(mine, jnp.broadcast_to(taps[t:t + 1], (CH, width)), 0.0))
        found.append(jnp.concatenate(rows, axis=0).astype(BF16))
    return found


def dots(pairs):
    total = None
    for v, w in pairs:
        part = jnp.dot(v, w, preferred_element_type=F32)
        total = part if total is None else total + part
    return total.astype(BF16)


def packed(parts, wanted, of, size):
    per = 128 // size
    places = [place(parts[0].shape[1], wanted, of, size, slot) for slot in range(min(per, 3))]
    tiles = [range(first, min(first + per, 3)) for first in range(0, 3, per)]
    return jnp.concatenate([dots([(parts[c], places[c % per]) for c in tile]) for tile in tiles], axis=1)


def band(wide, expand, ys, rows_y, t):
    rows, width = t.shape[0], wide.shape[1]
    for a in range(3):
        total = jnp.zeros((rows, width), F32)
        for b in range(3):
            part = jnp.dot(expand[:rows], wide[(a * 3 + b) * CH:(a * 3 + b + 1) * CH], preferred_element_type=F32)
            total = jnp.where(ys == rows_y[:rows] + 2 * (b - 1), part, total)
        t[:, a * width:(a + 1) * width] = total.astype(BF16)


def repeat_bias(bias, expand, out):
    column = jnp.sum(expand.astype(F32) * bias[...], axis=1, keepdims=True)
    out[...] = jnp.broadcast_to(column, out.shape)


def band_kernel(w1, w2, first_bias, second_bias, t1o, t1r, t1d, tbo, tbr, t2, b1, b2):
    expand, rows_y = row_table(192, y_first)
    parts = spread(w1, True, False)
    for of, step, t in ((natural, 64, t1o), (rim(CI), 32, t1r), (deep_rim, 64, t1d)):
        wide = packed(parts, lambda n: n % CI, of, step)
        band(wide, expand, lane_y(of, wide.shape[1], step), rows_y, t)
    parts = spread(w2, False, True)
    for of, step, t in ((natural, 128, tbo), (rim(CH), 64, tbr)):
        wide = packed(parts, lambda n: n // CH, of, step)
        band(wide, expand, lane_y(of, wide.shape[1], step), rows_y, t)
    repeat_bias(first_bias, expand, b1)
    expand, rows_y = row_table(128, natural)
    parts = spread(w2, True, False)
    wide = [packed(parts, lambda n: n % CH, of, step) for of, step in ((y_first, 128), (rim(CH), 64))]
    ys = jnp.concatenate([lane_y(y_first, 384, 128), lane_y(rim(CH), 256, 64)], axis=1)
    band(jnp.concatenate(wide, axis=1), expand, ys, rows_y, t2)
    repeat_bias(second_bias, expand, b2)


def shifted(v):
    lane = lax.broadcasted_iota(jnp.int32, v.shape, 1)
    before = jnp.where(lane >= 2, pltpu.roll(v, 2, 1), 0.0)
    after = jnp.where(lane < Z - 2, pltpu.roll(v, Z - 2, 1), 0.0)
    return before.astype(BF16), v.astype(BF16), after.astype(BF16)


def store_wide(ref, p, v):
    at = slice(p * Z, (p + 1) * Z)
    for c, piece in enumerate(shifted(v)):
        ref[c * 128:(c + 1) * 128, at] = piece[:128]
        ref[384 + c * 64:384 + (c + 1) * 64, at] = piece[128:]
    ref[576:, at] = jnp.zeros((64, Z), BF16)


def stacked(ref, lanes):
    return jnp.concatenate([ref[:, a * 256:a * 256 + lanes] for a in range(3)], axis=0)


def own_kernel(counts, xfar, xnear, fields, cot, t1, tb, b1, fs, cs, pre, back):
    count = fields.shape[0]
    f, c = x_planes(count, fields, cot, xnear, xfar, counts[0])
    for ref, rows in ((fs, f), (cs, c)):
        for p, v in enumerate(rows):
            for n, piece in enumerate(shifted(v)):
                ref[n * v.shape[0]:(n + 1) * v.shape[0], p * Z:(p + 1) * Z] = piece
    fs[192:] = jnp.zeros((64, fs.shape[1]), BF16)
    rows = jnp.concatenate([fs[:, a * 256 + 256:a * 256 + 256 + pre.shape[1]] for a in range(3)], axis=0)
    pre[...] = jnp.dot(t1[:128], rows, preferred_element_type=F32) + b1[:128, :1]
    back[...] = jnp.dot(tb[...], stacked(cs, back.shape[1]), preferred_element_type=F32)


def two_dots(v, w):
    high = v.astype(BF16)
    low = (v - high.astype(F32)).astype(BF16)
    return jnp.dot(high, w, preferred_element_type=F32) + jnp.dot(low, w, preferred_element_type=F32)


def gelu_share(pre):
    return 0.5 * (1.0 + lax.erf(pre * 0.7071067811865476))


def rim_kernel(counts, rnear, rfar, fs, cs, pre_own, back_own, t1, tb, e1t, e2t, rep1, rep2, y1, y2,
               hidden_out, payload, fr, cr, taps):
    count = hidden_out.shape[0]
    lanes = count * Z
    radial = lax.axis_index("radial")
    at = 0
    for ref, half in ((fr, 16), (cr, 32)):
        for p in range(count + 4):
            low, high = sides(radial, counts[1], rnear[at:at + half], rfar[at:at + half])
            for n, piece in enumerate(shifted(jnp.concatenate([low, high], axis=0))):
                ref[n * 2 * half:(n + 1) * 2 * half, p * Z:(p + 1) * Z] = piece
            at += half
        ref[6 * half:] = jnp.zeros((2 * half, ref.shape[1]), BF16)
    pre = pre_own[...] + jnp.dot(t1[...], stacked(fr, lanes), preferred_element_type=F32)
    share = gelu_share(pre)
    hidden = (pre * share).astype(BF16)
    for x in range(count):
        hidden_out[x] = hidden[:, x * Z:(x + 1) * Z]
    back = back_own[...] + jnp.dot(tb[...], stacked(cr, lanes), preferred_element_type=F32)
    dpre = (back * (share + pre * jnp.exp(-0.5 * pre * pre) * 0.3989422804014327)).astype(BF16)
    over_lanes = (((1,), (1,)), ((), ()))
    ones, twos = [], []
    for a in range(3):
        at = slice((a + 1) * 256, (a + 1) * 256 + lanes)
        rows = jnp.concatenate([fs[:, at], fr[:, a * 256:a * 256 + lanes]], axis=0)
        g1 = lax.dot_general(dpre, rows, over_lanes, preferred_element_type=F32)
        at = slice(a * 256, a * 256 + lanes)
        rows = jnp.concatenate([cs[:, at], cr[:, at]], axis=0)
        g2 = lax.dot_general(hidden, rows, over_lanes, preferred_element_type=F32)
        for b in range(3):
            for g, ys, out in ((g1, y1, ones), (g2, y2, twos)):
                total = jnp.zeros((CH, g.shape[1]), F32)
                for y in range(8):
                    total = jnp.where(ys[...] == float(y + 2 * (b - 1)), g[y * CH:(y + 1) * CH], total)
                out.append(total)
    taps[:, 24:] = jnp.zeros((3, 8, 128), F32)
    for parts, et, rep, at, width in ((ones, e1t, rep1, 0, 128), (twos[::-1], e2t, rep2, 1, 256)):
        sums = two_dots(jnp.concatenate(parts, axis=0), et[...])
        wide = two_dots(sums, rep[...])
        row = lax.broadcasted_iota(jnp.int32, wide.shape, 0) % CH
        lane = lax.broadcasted_iota(jnp.int32, wide.shape, 1) % width
        mine = row == (lane // CI if width == 128 else lane % CH)
        total = jnp.sum(jnp.where(mine, wide, 0.0).reshape(9, CH, 3 * width), axis=1)
        for c in range(3):
            first = c if width == 128 else 2 - c
            for n in range(width // 128):
                taps[at + n, pl.ds(first, 9, stride=3)] = total[:, c * width + n * 128:c * width + (n + 1) * 128]
    bias = jnp.sum(dpre.astype(F32), axis=1, keepdims=True)
    bias = sum(bias[y * CH:(y + 1) * CH] for y in range(8))
    row = lax.broadcasted_iota(jnp.int32, (CH, 128), 0)
    lane = lax.broadcasted_iota(jnp.int32, (CH, 128), 1)
    taps[0, 27:28] = jnp.sum(jnp.where(row == lane, bias, 0.0), axis=0, keepdims=True)
    payload[...] = jnp.concatenate([taps[n] for n in range(3)], axis=1)


def hidden_rim_kernel(counts, rnear, rfar, rnear_outer, rfar_outer, hidden, fs, t1o, t1d, b1, hidden_out, fr):
    count = hidden.shape[0]
    stream, radial = lax.axis_index("stream"), lax.axis_index("radial")
    for p in range(count + 8):
        end = p if p < 2 else p - count - 4 if p >= count + 6 else None
        if end is None:
            near, outer = (rnear, rfar, (p - 2) * 16), (rnear_outer, rfar_outer, 128 + (p - 2) * 16)
        else:
            near, outer = (rnear_outer, rfar_outer, end * 16), (rnear_outer, rfar_outer, 64 + end * 16)
        parts = [sides(radial, counts[1], n[at:at + 16], f[at:at + 16]) for n, f, at in (near, outer)]
        rows = jnp.concatenate([part[side] for side in range(2) for part in parts], axis=0)
        for n, piece in enumerate(shifted(rows)):
            fr[n * 64:(n + 1) * 64, p * Z:(p + 1) * Z] = piece
    fr[192:] = jnp.zeros((64, fr.shape[1]), BF16)

    def gelu(rows, lanes):
        total = b1[rows, :1]
        for t, ref in ((t1o, fs), (t1d, fr)):
            cells = [jnp.concatenate([ref[:, a * 256 + at:a * 256 + at + size] for at, size in lanes], axis=1) for a in range(3)]
            total = total + jnp.dot(t[rows], jnp.concatenate(cells, axis=0), preferred_element_type=F32)
        return total * gelu_share(total)

    own = gelu(slice(0, 128), ((0, 2 * Z), ((count + 2) * Z, 2 * Z)))
    rims = gelu(slice(128, 192), ((0, (count + 4) * Z),))
    rims = jnp.concatenate([jnp.where(radial > 0, rims[:32], 0.0), jnp.where(radial < counts[1] - 1, rims[32:], 0.0)], axis=0)
    for p in range(count + 4):
        rim_rows = rims[:, p * Z:(p + 1) * Z]
        if 2 <= p < count + 2:
            hidden_out[p, :128] = hidden[p - 2]
            hidden_out[p, 128:] = rim_rows.astype(BF16)
        else:
            at = p if p < 2 else p - count
            inside = stream > 0 if p < 2 else stream < counts[0] - 1
            rows = jnp.concatenate([own[:, at * Z:(at + 1) * Z], rim_rows], axis=0)
            hidden_out[p] = jnp.where(inside, rows, 0.0).astype(BF16)


def closure_kernel(hidden, t2, b2, closure, hs):
    count = closure.shape[2]
    for p in range(count + 4):
        store_wide(hs, p, hidden[p].astype(F32))
    out = (jnp.dot(t2[...], stacked(hs, count * Z), preferred_element_type=F32) + b2[:, :1]).astype(BF16)
    for x in range(count):
        closure[0, :, x] = out[:, x * Z:(x + 1) * Z].reshape(CH, 8, Z)


def summed(parts):
    parts = [part[...].astype(F32) for part in parts]
    while len(parts) > 1:
        parts = [v + w for v, w in zip(parts[::2], parts[1::2])]
    return parts[0]


def add_kernel(*refs):
    s = summed(refs[:-1])
    lost = s - s.astype(BF16).astype(F32)
    row = lax.broadcasted_iota(jnp.int32, s.shape, 0)
    refs[-1][...] = (s + jnp.where(row == 28, pltpu.roll(lost, 1, 0), 0.0)).astype(BF16)


def finish_kernel(norm, *refs):
    *parts, first, second, bias = refs
    scaled = summed(parts) * norm
    flipped = jnp.transpose(scaled)
    first[...] = flipped[:128, :27]
    second[...] = flipped[128:, :27]
    bias[...] = scaled[27:28, :CH] + scaled[28:29, :CH]


def call(kernel, outs, name, scratch=(), flops=10_000_000, **specs):
    return pl.pallas_call(
        kernel,
        out_shape=outs,
        **specs,
        scratch_shapes=list(scratch),
        compiler_params=pltpu.CompilerParams(vmem_limit_bytes=32 * 1024 * 1024),
        cost_estimate=pl.CostEstimate(flops=flops, bytes_accessed=1_000_000, transcendentals=0),
        name=name,
    )


def shape(*dims, dtype=BF16):
    return jax.ShapeDtypeStruct(dims, dtype)


def exchange(near, far, axis, ends=True):
    count = lax.axis_size(axis)
    pairs = [(i, i - 1 + 2 * (i % 2)) for i in range(1, count - 1)]
    if ends:
        pairs = [(0, 0), *pairs, (count - 1, count - 1)]
    far = lax.ppermute(far, axis, pairs)
    return lax.ppermute(near, axis, [(i, i ^ 1) for i in range(count)]), far


def swap(v, axis, masks):
    count = lax.axis_size(axis)
    return [lax.ppermute(v, axis, [(i, i ^ mask) for i in range(count)]) for mask in masks]


def add(v, arrived):
    return call(add_kernel, shape(*v.shape), "add_parts")(v, *arrived)


def rounds(axis, most):
    found, step = [], 1
    while step < lax.axis_size(axis):
        masks = [step * n for n in range(1, most if step * most <= lax.axis_size(axis) else 2)]
        found.append((axis, masks))
        step *= len(masks) + 1
    return found


def local(fields, first_weight, first_bias, second_weight, second_bias, cotangent):
    e1t, y1 = table(CI, 384, ((natural, 0, 64), (rim(CI), 256, 32)))
    e2t, y2 = table(CH, 640, ((natural, 0, 128), (rim(CH), 384, 64)))
    rep1, rep2 = np.zeros((128, 384), np.float32), np.zeros((128, 768), np.float32)
    for c in range(3):
        rep1[c * CI:(c + 1) * CI, c * 128:(c + 1) * 128] = np.tile(np.eye(CI), (1, CH))
        rep2[c * CH:(c + 1) * CH, c * 256:(c + 1) * 256] = np.repeat(np.eye(CH), CH, axis=1)

    def const(*arrays, dtype=BF16):
        return [jnp.asarray(v, dtype) for v in arrays]

    planes = fields.shape[2]
    w1 = first_weight.transpose(1, 2, 0).reshape(CH * CI, 27)
    w2 = second_weight.transpose(1, 2, 0).reshape(CH * CH, 27)
    near, far, f_rows, c_rows = call(
        pack_kernel,
        (shape(512, Z), shape(512, Z), shape(planes, CI * 8, Z), shape(planes, CH * 8, Z)),
        "pack_strips",
        flops=4_000_000_000,
    )(jnp.concatenate([fields[0], cotangent[0]], axis=0))
    xnear, xfar = exchange(near, far, "stream")
    wide = (planes + 4) * Z
    counts = (lax.axis_size("stream"), lax.axis_size("radial"))
    t1o, t1r, t1d, tbo, tbr, t2, b1, b2 = call(
        band_kernel,
        (shape(192, 768), shape(128, 384), shape(192, 768), shape(128, 1152), shape(128, 768), shape(128, 1920),
         shape(192, 128, dtype=F32), shape(128, 128, dtype=F32)),
        "band_matrices",
        flops=4_000_000_000,
    )(w1, w2, first_bias[None], second_bias[None])
    xfar, xnear, t1o, tbo = lax.optimization_barrier((xfar, xnear, t1o, tbo))
    inner, outer = shape((planes + 4) * 48, Z), shape(128 + (planes + 4) * 16, Z)
    near, far = call(functools.partial(join_kernel, counts), (inner, inner), "join_strips")(xfar, xnear, f_rows, c_rows)
    rnear, rfar = exchange(near, far, "radial", ends=False)
    fs, cs, pre, back = call(
        functools.partial(own_kernel, counts),
        (shape(256, wide + 4 * Z), shape(384, wide), shape(128, planes * Z, dtype=F32), shape(128, planes * Z, dtype=F32)),
        "own_rows",
        flops=1_000_000_000,
    )(xfar, xnear, f_rows, c_rows, t1o, tbo, b1)
    f_rows, fs = lax.optimization_barrier((f_rows, fs))
    near_outer, far_outer = call(functools.partial(join_outer_kernel, counts), (outer, outer), "join_outer")(
        xfar, xnear, f_rows, c_rows)
    rnear_outer, rfar_outer = exchange(near_outer, far_outer, "radial", ends=False)
    hidden, payload = call(
        functools.partial(rim_kernel, counts),
        (shape(planes, 128, Z), shape(32, 384, dtype=F32)),
        "gradients",
        (pltpu.VMEM((128, wide), BF16), pltpu.VMEM((256, wide), BF16), pltpu.VMEM((3, 32, 128), F32)),
        flops=2_000_000_000,
    )(rnear, rfar, fs, cs, pre, back, t1r, tbr, *const(e1t, e2t, rep1, rep2), *const(y1, y2, dtype=F32))

    steps = rounds("radial", 2) + rounds("stream", 4) + rounds("snap", 2)
    arrived = swap(payload, *steps[0])
    payload = add(payload, arrived)
    arrived = swap(payload, *steps[1])
    hidden = call(
        functools.partial(hidden_rim_kernel, counts),
        shape(planes + 4, 192, Z),
        "hidden_rim",
        (pltpu.VMEM((256, wide + 4 * Z), BF16),),
        flops=1_000_000_000,
    )(rnear, rfar, rnear_outer, rfar_outer, hidden, fs, t1o, t1d, b1)
    payload, hidden = lax.optimization_barrier((add(payload, arrived), hidden))
    arrived = swap(payload, *steps[2])
    payload = add(payload, arrived)
    arrived = swap(payload, *steps[3])
    closure = call(
        closure_kernel, shape(*cotangent.shape), "closure", (pltpu.VMEM((640, wide), BF16),), flops=1_000_000_000
    )(hidden, t2, b2)
    for step in steps[4:]:
        payload = add(payload, arrived)
        arrived = swap(payload, *step)

    cells = fields.shape[0] * fields.shape[2] * fields.shape[3] * fields.shape[4]
    for axis in ("stream", "radial", "snap"):
        cells *= lax.axis_size(axis)
    norm = float(1.0 / np.sqrt(np.float32(cells)))
    first, second, bias = call(
        functools.partial(finish_kernel, norm),
        (shape(CH * CI, 27, dtype=F32), shape(CH * CH, 27, dtype=F32), shape(1, CH, dtype=F32)),
        "finish",
    )(payload, *arrived)
    first = first.reshape(CH, CI, 27).transpose(2, 0, 1)
    second = second.reshape(CH, CH, 27).transpose(2, 0, 1)
    return (closure, first, second, bias[0])


def solution(mesh):
    split = P("snap", None, "stream", "radial", None)
    return jax.shard_map(
        local,
        mesh=mesh,
        in_specs=(split, P(), P(), P(), P(), split),
        out_specs=(split, P(), P(), P()),
        check_vma=False,
    )
```

```python
import functools

import numpy as np
import jax
import jax.numpy as jnp
from jax import lax
from jax.experimental import pallas as pl
from jax.experimental.pallas import tpu as pltpu
from jax.sharding import PartitionSpec as P

F32 = jnp.float32
BF16 = jnp.bfloat16
Z = 128
CI = 8
CH = 16
FAR = 100


def natural(n):
    return n // 8, n % 8


def y_first(n):
    return n % CH, n // CH


def rim(channels):
    def of(n):
        side, n = n // (2 * channels), n % (2 * channels)
        return n // 2, n % 2 + 10 * side - 2
    return of


def deep_rim(n):
    part, n = n // 16, n % 16
    return n // 2, n % 2 + 10 * (part // 2) - 2 + (part % 2) * (4 * (part // 2) - 2)


def table(channels, total, places):
    e = np.zeros((total, 128), np.float32)
    ys = np.full((1, total), FAR, np.float32)
    for c in range(3):
        for of, start, step in places:
            ch, y = of(np.arange(step))
            at = start + c * step + np.arange(step)
            e[at, c * channels + ch] = 1
            ys[0, at] = y
    return e, ys


def iota(rows, columns):
    return [lax.broadcasted_iota(jnp.int32, (rows, columns), d) for d in range(2)]


def one_hot(where):
    return jnp.where(where, 1.0, 0.0).astype(BF16)


def lane_y(of, width, step):
    lane = lax.broadcasted_iota(jnp.int32, (1, width), 1)
    return jnp.where(lane < 3 * step, of(lane % step)[1], FAR)


def place(rows, wanted, of, size, slot):
    row, lane = iota(rows, 128)
    return one_hot((of(lane % size)[0] == wanted(row)) & (lane // size == slot))


def row_table(rows, own):
    row, lane = iota(rows, CH)
    own_c, own_y = own(row)
    rim_c, rim_y = rim(CH)(row - 128)
    channel, y = jnp.where(row < 128, own_c, rim_c), jnp.where(row < 128, own_y, rim_y)
    return one_hot(channel == lane), y[:, :1]


def plane(ref, channels, x):
    v = ref[channels, x].astype(F32)
    return v.reshape(v.shape[0] * v.shape[1], v.shape[2])


def pick_rows(channels, low, high):
    half = channels * 2
    row, col = iota(2 * half, channels * 8)
    side = row // half
    return one_hot(col == (row % half // 2) * 8 + low + (high - low) * side + row % 2)


def partners(index, count):
    return index % 2 == 0, index > 0, index < count - 1


def sides(index, count, near, far):
    near_above, below, above = partners(index, count)
    low = jnp.where(near_above, far, near).astype(F32)
    high = jnp.where(near_above, near, far).astype(F32)
    return jnp.where(below, low, 0.0), jnp.where(above, high, 0.0)


def pack_kernel(inputs, near, far, f_rows, c_rows):
    up_first = lax.axis_index("stream") % 2 == 0
    count, at = inputs.shape[1], 0
    for channels, out, width in ((slice(0, CI), f_rows, 4), (slice(CI, CI + CH), c_rows, 2)):
        rows = [plane(inputs, channels, x) for x in range(count)]
        for x, v in enumerate(rows):
            out[x] = v.astype(BF16)
        for low, high in zip(rows[:width], rows[count - width:]):
            part = slice(at, at + low.shape[0])
            near[part] = jnp.where(up_first, high, low).astype(BF16)
            far[part] = jnp.where(up_first, low, high).astype(BF16)
            at += low.shape[0]


def x_planes(count, fields, cot, xnear, xfar, size):
    index = lax.axis_index("stream")
    inner = [fields[x].astype(F32) for x in range(count)]
    rims = [sides(index, size, xnear[n * 64:(n + 1) * 64], xfar[n * 64:(n + 1) * 64]) for n in range(4)]
    f = [low for low, _ in rims] + inner + [high for _, high in rims]
    inner = [cot[x].astype(F32) for x in range(count)]
    rims = [sides(index, size, xnear[256 + n * 128:384 + n * 128], xfar[256 + n * 128:384 + n * 128]) for n in range(2)]
    return f, [low for low, _ in rims] + inner + [high for _, high in rims]


def pick_strips(work, near, far):
    up_first = lax.axis_index("radial") % 2 == 0
    at = 0
    for pick, rows in work:
        half = pick.shape[0] // 2
        for v in rows:
            got = jnp.dot(pick, v.astype(BF16), preferred_element_type=F32)
            near[at:at + half] = jnp.where(up_first, got[half:], got[:half]).astype(BF16)
            far[at:at + half] = jnp.where(up_first, got[:half], got[half:]).astype(BF16)
            at += half


def join_kernel(counts, xfar, xnear, fields, cot, near, far):
    f, c = x_planes(fields.shape[0], fields, cot, xnear, xfar, counts[0])
    pick_strips([(pick_rows(CI, 0, 6), f[2:-2]), (pick_rows(CH, 0, 6), c)], near, far)


def join_outer_kernel(counts, xfar, xnear, fields, cot, near, far):
    f, _ = x_planes(fields.shape[0], fields, cot, xnear, xfar, counts[0])
    ends = f[:2] + f[-2:]
    pick_strips([(pick_rows(CI, 0, 6), ends), (pick_rows(CI, 2, 4), ends + f[2:-2])], near, far)


def spread(w, by_row, flip):
    taps = jnp.transpose(w[...].astype(F32))
    width = taps.shape[1]
    row = lax.broadcasted_iota(jnp.int32, (CH, width), 0)
    lane = lax.broadcasted_iota(jnp.int32, (CH, width), 1)
    mine = row == (lane // (width // CH) if by_row else lane % CH)
    found = []
    for c in range(3):
        rows = []
        for ab in range(9):
            t = 26 - (ab * 3 + c) if flip else ab * 3 + c
            rows.append(jnp.where(mine, jnp.broadcast_to(taps[t:t + 1], (CH, width)), 0.0))
        found.append(jnp.concatenate(rows, axis=0).astype(BF16))
    return found


def dots(pairs):
    total = None
    for v, w in pairs:
        part = jnp.dot(v, w, preferred_element_type=F32)
        total = part if total is None else total + part
    return total.astype(BF16)


def packed(parts, wanted, of, size):
    per = 128 // size
    places = [place(parts[0].shape[1], wanted, of, size, slot) for slot in range(min(per, 3))]
    tiles = [range(first, min(first + per, 3)) for first in range(0, 3, per)]
    return jnp.concatenate([dots([(parts[c], places[c % per]) for c in tile]) for tile in tiles], axis=1)


def band(wide, expand, ys, rows_y, t):
    rows, width = t.shape[0], wide.shape[1]
    for a in range(3):
        total = jnp.zeros((rows, width), F32)
        for b in range(3):
            part = jnp.dot(expand[:rows], wide[(a * 3 + b) * CH:(a * 3 + b + 1) * CH], preferred_element_type=F32)
            total = jnp.where(ys == rows_y[:rows] + 2 * (b - 1), part, total)
        t[:, a * width:(a + 1) * width] = total.astype(BF16)


def repeat_bias(bias, expand, out):
    column = jnp.sum(expand.astype(F32) * bias[...], axis=1, keepdims=True)
    out[...] = jnp.broadcast_to(column, out.shape)


def band_kernel(w1, w2, first_bias, second_bias, t1o, t1r, t1d, tbo, tbr, t2, b1, b2):
    expand, rows_y = row_table(192, y_first)
    parts = spread(w1, True, False)
    for of, step, t in ((natural, 64, t1o), (rim(CI), 32, t1r), (deep_rim, 64, t1d)):
        wide = packed(parts, lambda n: n % CI, of, step)
        band(wide, expand, lane_y(of, wide.shape[1], step), rows_y, t)
    parts = spread(w2, False, True)
    for of, step, t in ((natural, 128, tbo), (rim(CH), 64, tbr)):
        wide = packed(parts, lambda n: n // CH, of, step)
        band(wide, expand, lane_y(of, wide.shape[1], step), rows_y, t)
    repeat_bias(first_bias, expand, b1)
    expand, rows_y = row_table(128, natural)
    parts = spread(w2, True, False)
    wide = [packed(parts, lambda n: n % CH, of, step) for of, step in ((y_first, 128), (rim(CH), 64))]
    ys = jnp.concatenate([lane_y(y_first, 384, 128), lane_y(rim(CH), 256, 64)], axis=1)
    band(jnp.concatenate(wide, axis=1), expand, ys, rows_y, t2)
    repeat_bias(second_bias, expand, b2)


def shifted(v):
    lane = lax.broadcasted_iota(jnp.int32, v.shape, 1)
    before = jnp.where(lane >= 2, pltpu.roll(v, 2, 1), 0.0)
    after = jnp.where(lane < Z - 2, pltpu.roll(v, Z - 2, 1), 0.0)
    return before.astype(BF16), v.astype(BF16), after.astype(BF16)


def store_wide(ref, p, v):
    at = slice(p * Z, (p + 1) * Z)
    for c, piece in enumerate(shifted(v)):
        ref[c * 128:(c + 1) * 128, at] = piece[:128]
        ref[384 + c * 64:384 + (c + 1) * 64, at] = piece[128:]
    ref[576:, at] = jnp.zeros((64, Z), BF16)


def stacked(ref, lanes):
    return jnp.concatenate([ref[:, a * 256:a * 256 + lanes] for a in range(3)], axis=0)


def own_kernel(counts, xfar, xnear, fields, cot, t1, tb, b1, fs, cs, pre, back):
    count = fields.shape[0]
    f, c = x_planes(count, fields, cot, xnear, xfar, counts[0])
    for ref, rows in ((fs, f), (cs, c)):
        for p, v in enumerate(rows):
            for n, piece in enumerate(shifted(v)):
                ref[n * v.shape[0]:(n + 1) * v.shape[0], p * Z:(p + 1) * Z] = piece
    fs[192:] = jnp.zeros((64, fs.shape[1]), BF16)
    rows = jnp.concatenate([fs[:, a * 256 + 256:a * 256 + 256 + pre.shape[1]] for a in range(3)], axis=0)
    pre[...] = jnp.dot(t1[:128], rows, preferred_element_type=F32) + b1[:128, :1]
    back[...] = jnp.dot(tb[...], stacked(cs, back.shape[1]), preferred_element_type=F32)


def two_dots(v, w):
    high = v.astype(BF16)
    low = (v - high.astype(F32)).astype(BF16)
    return jnp.dot(high, w, preferred_element_type=F32) + jnp.dot(low, w, preferred_element_type=F32)


def gelu_share(pre):
    return 0.5 * (1.0 + lax.erf(pre * 0.7071067811865476))


def rim_kernel(counts, rfar, rnear, fs, cs, pre_own, back_own, t1, tb, e1t, e2t, rep1, rep2, y1, y2,
               hidden_out, payload, fr, cr, taps):
    count = hidden_out.shape[0]
    lanes = count * Z
    radial = lax.axis_index("radial")
    at = 0
    for ref, half in ((fr, 16), (cr, 32)):
        for p in range(count + 4):
            low, high = sides(radial, counts[1], rnear[at:at + half], rfar[at:at + half])
            for n, piece in enumerate(shifted(jnp.concatenate([low, high], axis=0))):
                ref[n * 2 * half:(n + 1) * 2 * half, p * Z:(p + 1) * Z] = piece
            at += half
        ref[6 * half:] = jnp.zeros((2 * half, ref.shape[1]), BF16)
    pre = pre_own[...] + jnp.dot(t1[...], stacked(fr, lanes), preferred_element_type=F32)
    share = gelu_share(pre)
    hidden = (pre * share).astype(BF16)
    for x in range(count):
        hidden_out[x] = hidden[:, x * Z:(x + 1) * Z]
    back = back_own[...] + jnp.dot(tb[...], stacked(cr, lanes), preferred_element_type=F32)
    dpre = (back * (share + pre * jnp.exp(-0.5 * pre * pre) * 0.3989422804014327)).astype(BF16)
    over_lanes = (((1,), (1,)), ((), ()))
    ones, twos = [], []
    for a in range(3):
        at = slice((a + 1) * 256, (a + 1) * 256 + lanes)
        rows = jnp.concatenate([fs[:, at], fr[:, a * 256:a * 256 + lanes]], axis=0)
        g1 = lax.dot_general(dpre, rows, over_lanes, preferred_element_type=F32)
        at = slice(a * 256, a * 256 + lanes)
        rows = jnp.concatenate([cs[:, at], cr[:, at]], axis=0)
        g2 = lax.dot_general(hidden, rows, over_lanes, preferred_element_type=F32)
        for b in range(3):
            for g, ys, out in ((g1, y1, ones), (g2, y2, twos)):
                total = jnp.zeros((CH, g.shape[1]), F32)
                for y in range(8):
                    total = jnp.where(ys[...] == float(y + 2 * (b - 1)), g[y * CH:(y + 1) * CH], total)
                out.append(total)
    taps[:, 24:] = jnp.zeros((3, 8, 128), F32)
    for parts, et, rep, at, width in ((ones, e1t, rep1, 0, 128), (twos[::-1], e2t, rep2, 1, 256)):
        sums = two_dots(jnp.concatenate(parts, axis=0), et[...])
        wide = two_dots(sums, rep[...])
        row = lax.broadcasted_iota(jnp.int32, wide.shape, 0) % CH
        lane = lax.broadcasted_iota(jnp.int32, wide.shape, 1) % width
        mine = row == (lane // CI if width == 128 else lane % CH)
        total = jnp.sum(jnp.where(mine, wide, 0.0).reshape(9, CH, 3 * width), axis=1)
        for c in range(3):
            first = c if width == 128 else 2 - c
            for n in range(width // 128):
                taps[at + n, pl.ds(first, 9, stride=3)] = total[:, c * width + n * 128:c * width + (n + 1) * 128]
    bias = jnp.sum(dpre.astype(F32), axis=1, keepdims=True)
    bias = sum(bias[y * CH:(y + 1) * CH] for y in range(8))
    row = lax.broadcasted_iota(jnp.int32, (CH, 128), 0)
    lane = lax.broadcasted_iota(jnp.int32, (CH, 128), 1)
    taps[0, 27:28] = jnp.sum(jnp.where(row == lane, bias, 0.0), axis=0, keepdims=True)
    payload[...] = jnp.concatenate([taps[n] for n in range(3)], axis=1)


def hidden_rim_kernel(counts, rfar, rnear, rfar_outer, rnear_outer, hidden, fs, t1o, t1d, b1, hidden_out, fr):
    count = hidden.shape[0]
    stream, radial = lax.axis_index("stream"), lax.axis_index("radial")
    for p in range(count + 8):
        end = p if p < 2 else p - count - 4 if p >= count + 6 else None
        if end is None:
            near, outer = (rnear, rfar, (p - 2) * 16), (rnear_outer, rfar_outer, 128 + (p - 2) * 16)
        else:
            near, outer = (rnear_outer, rfar_outer, end * 16), (rnear_outer, rfar_outer, 64 + end * 16)
        parts = [sides(radial, counts[1], n[at:at + 16], f[at:at + 16]) for n, f, at in (near, outer)]
        rows = jnp.concatenate([part[side] for side in range(2) for part in parts], axis=0)
        for n, piece in enumerate(shifted(rows)):
            fr[n * 64:(n + 1) * 64, p * Z:(p + 1) * Z] = piece
    fr[192:] = jnp.zeros((64, fr.shape[1]), BF16)

    def gelu(rows, lanes):
        total = b1[rows, :1]
        for t, ref in ((t1o, fs), (t1d, fr)):
            cells = [jnp.concatenate([ref[:, a * 256 + at:a * 256 + at + size] for at, size in lanes], axis=1) for a in range(3)]
            total = total + jnp.dot(t[rows], jnp.concatenate(cells, axis=0), preferred_element_type=F32)
        return total * gelu_share(total)

    own = gelu(slice(0, 128), ((0, 2 * Z), ((count + 2) * Z, 2 * Z)))
    rims = gelu(slice(128, 192), ((0, (count + 4) * Z),))
    rims = jnp.concatenate([jnp.where(radial > 0, rims[:32], 0.0), jnp.where(radial < counts[1] - 1, rims[32:], 0.0)], axis=0)
    for p in range(count + 4):
        rim_rows = rims[:, p * Z:(p + 1) * Z]
        if 2 <= p < count + 2:
            hidden_out[p, :128] = hidden[p - 2]
            hidden_out[p, 128:] = rim_rows.astype(BF16)
        else:
            at = p if p < 2 else p - count
            inside = stream > 0 if p < 2 else stream < counts[0] - 1
            rows = jnp.concatenate([own[:, at * Z:(at + 1) * Z], rim_rows], axis=0)
            hidden_out[p] = jnp.where(inside, rows, 0.0).astype(BF16)


def closure_kernel(hidden, t2, b2, closure, hs):
    count = closure.shape[2]
    for p in range(count + 4):
        store_wide(hs, p, hidden[p].astype(F32))
    out = (jnp.dot(t2[...], stacked(hs, count * Z), preferred_element_type=F32) + b2[:, :1]).astype(BF16)
    for x in range(count):
        closure[0, :, x] = out[:, x * Z:(x + 1) * Z].reshape(CH, 8, Z)


def summed(parts):
    parts = [part[...].astype(F32) for part in parts]
    while len(parts) > 1:
        parts = [v + w for v, w in zip(parts[::2], parts[1::2])]
    return parts[0]


def add_kernel(*refs):
    s = summed(refs[:-1])
    lost = s - s.astype(BF16).astype(F32)
    row = lax.broadcasted_iota(jnp.int32, s.shape, 0)
    refs[-1][...] = (s + jnp.where(row == 28, pltpu.roll(lost, 1, 0), 0.0)).astype(BF16)


def finish_kernel(norm, *refs):
    *parts, first, second, bias = refs
    scaled = summed(parts) * norm
    flipped = jnp.transpose(scaled)
    first[...] = flipped[:128, :27]
    second[...] = flipped[128:, :27]
    bias[...] = scaled[27:28, :CH] + scaled[28:29, :CH]


def call(kernel, outs, name, scratch=(), flops=10_000_000, **specs):
    return pl.pallas_call(
        kernel,
        out_shape=outs,
        **specs,
        scratch_shapes=list(scratch),
        compiler_params=pltpu.CompilerParams(vmem_limit_bytes=32 * 1024 * 1024),
        cost_estimate=pl.CostEstimate(flops=flops, bytes_accessed=1_000_000, transcendentals=0),
        name=name,
    )


def shape(*dims, dtype=BF16):
    return jax.ShapeDtypeStruct(dims, dtype)


def exchange(near, far, axis, ends):
    count = lax.axis_size(axis)
    pairs = [(i, i - 1 + 2 * (i % 2)) for i in range(1, count - 1)]
    pairs += [(0, count - 1), (count - 1, 0)] if ends else [(0, 0), (count - 1, count - 1)]
    far = lax.ppermute(far, axis, pairs)
    return lax.ppermute(near, axis, [(i, i ^ 1) for i in range(count)]), far


def swap(v, axis, masks):
    count = lax.axis_size(axis)
    return [lax.ppermute(v, axis, [(i, i ^ mask) for i in range(count)]) for mask in masks]


def add(v, arrived):
    return call(add_kernel, shape(*v.shape), "add_parts")(v, *arrived)


def rounds(axis, most):
    found, step = [], 1
    while step < lax.axis_size(axis):
        masks = [step * n for n in range(1, most if step * most <= lax.axis_size(axis) else 2)]
        found.append((axis, masks))
        step *= len(masks) + 1
    return found


def local(fields, first_weight, first_bias, second_weight, second_bias, cotangent):
    e1t, y1 = table(CI, 384, ((natural, 0, 64), (rim(CI), 256, 32)))
    e2t, y2 = table(CH, 640, ((natural, 0, 128), (rim(CH), 384, 64)))
    rep1, rep2 = np.zeros((128, 384), np.float32), np.zeros((128, 768), np.float32)
    for c in range(3):
        rep1[c * CI:(c + 1) * CI, c * 128:(c + 1) * 128] = np.tile(np.eye(CI), (1, CH))
        rep2[c * CH:(c + 1) * CH, c * 256:(c + 1) * 256] = np.repeat(np.eye(CH), CH, axis=1)

    def const(*arrays, dtype=BF16):
        return [jnp.asarray(v, dtype) for v in arrays]

    planes = fields.shape[2]
    w1 = first_weight.transpose(1, 2, 0).reshape(CH * CI, 27)
    w2 = second_weight.transpose(1, 2, 0).reshape(CH * CH, 27)
    near, far, f_rows, c_rows = call(
        pack_kernel,
        (shape(512, Z), shape(512, Z), shape(planes, CI * 8, Z), shape(planes, CH * 8, Z)),
        "pack_strips",
        flops=4_000_000_000,
    )(jnp.concatenate([fields[0], cotangent[0]], axis=0))
    xnear, xfar = exchange(near, far, "stream", False)
    wide = (planes + 4) * Z
    counts = (lax.axis_size("stream"), lax.axis_size("radial"))
    t1o, t1r, t1d, tbo, tbr, t2, b1, b2 = call(
        band_kernel,
        (shape(192, 768), shape(128, 384), shape(192, 768), shape(128, 1152), shape(128, 768), shape(128, 1920),
         shape(192, 128, dtype=F32), shape(128, 128, dtype=F32)),
        "band_matrices",
        flops=4_000_000_000,
    )(w1, w2, first_bias[None], second_bias[None])
    xfar, xnear, t1o, tbo = lax.optimization_barrier((xfar, xnear, t1o, tbo))
    inner, outer = shape((planes + 4) * 48, Z), shape(128 + (planes + 4) * 16, Z)
    near, far = call(functools.partial(join_kernel, counts), (inner, inner), "join_strips")(xfar, xnear, f_rows, c_rows)
    rnear, rfar = exchange(near, far, "radial", True)
    fs, cs, pre, back = call(
        functools.partial(own_kernel, counts),
        (shape(256, wide + 4 * Z), shape(384, wide), shape(128, planes * Z, dtype=F32), shape(128, planes * Z, dtype=F32)),
        "own_rows",
        flops=1_000_000_000,
    )(xfar, xnear, f_rows, c_rows, t1o, tbo, b1)
    f_rows, fs = lax.optimization_barrier((f_rows, fs))
    near_outer, far_outer = call(functools.partial(join_outer_kernel, counts), (outer, outer), "join_outer")(
        xfar, xnear, f_rows, c_rows)
    rnear_outer, rfar_outer = exchange(near_outer, far_outer, "radial", True)
    hidden, payload = call(
        functools.partial(rim_kernel, counts),
        (shape(planes, 128, Z), shape(32, 384, dtype=F32)),
        "gradients",
        (pltpu.VMEM((128, wide), BF16), pltpu.VMEM((256, wide), BF16), pltpu.VMEM((3, 32, 128), F32)),
        flops=2_000_000_000,
    )(rfar, rnear, fs, cs, pre, back, t1r, tbr, *const(e1t, e2t, rep1, rep2), *const(y1, y2, dtype=F32))

    steps = rounds("radial", 2) + rounds("stream", 4) + rounds("snap", 2)
    arrived = swap(payload, *steps[0])
    payload = add(payload, arrived)
    arrived = swap(payload, *steps[1])
    hidden = call(
        functools.partial(hidden_rim_kernel, counts),
        shape(planes + 4, 192, Z),
        "hidden_rim",
        (pltpu.VMEM((256, wide + 4 * Z), BF16),),
        flops=1_000_000_000,
    )(rfar, rnear, rfar_outer, rnear_outer, hidden, fs, t1o, t1d, b1)
    payload, hidden = lax.optimization_barrier((add(payload, arrived), hidden))
    arrived = swap(payload, *steps[2])
    payload = add(payload, arrived)
    arrived = swap(payload, *steps[3])
    closure = call(
        closure_kernel, shape(*cotangent.shape), "closure", (pltpu.VMEM((640, wide), BF16),), flops=1_000_000_000
    )(hidden, t2, b2)
    for step in steps[4:]:
        payload = add(payload, arrived)
        arrived = swap(payload, *step)

    cells = fields.shape[0] * fields.shape[2] * fields.shape[3] * fields.shape[4]
    for axis in ("stream", "radial", "snap"):
        cells *= lax.axis_size(axis)
    norm = float(1.0 / np.sqrt(np.float32(cells)))
    first, second, bias = call(
        functools.partial(finish_kernel, norm),
        (shape(CH * CI, 27, dtype=F32), shape(CH * CH, 27, dtype=F32), shape(1, CH, dtype=F32)),
        "finish",
    )(payload, *arrived)
    first = first.reshape(CH, CI, 27).transpose(2, 0, 1)
    second = second.reshape(CH, CH, 27).transpose(2, 0, 1)
    return (closure, first, second, bias[0])


def solution(mesh):
    split = P("snap", None, "stream", "radial", None)
    return jax.shard_map(
        local,
        mesh=mesh,
        in_specs=(split, P(), P(), P(), P(), split),
        out_specs=(split, P(), P(), P()),
        check_vma=False,
    )
```

```python
import functools

import numpy as np
import jax
import jax.numpy as jnp
from jax import lax
from jax.experimental import pallas as pl
from jax.experimental.pallas import tpu as pltpu
from jax.sharding import PartitionSpec as P

F32 = jnp.float32
BF16 = jnp.bfloat16
Z = 128
CI = 8
CH = 16
FAR = 100


def natural(n):
    return n // 8, n % 8


def y_first(n):
    return n % CH, n // CH


def rim(channels):
    def of(n):
        side, n = n // (2 * channels), n % (2 * channels)
        return n // 2, n % 2 + 10 * side - 2
    return of


def deep_rim(n):
    part, n = n // 16, n % 16
    return n // 2, n % 2 + 10 * (part // 2) - 2 + (part % 2) * (4 * (part // 2) - 2)


def table(channels, total, places):
    e = np.zeros((total, 128), np.float32)
    ys = np.full((1, total), FAR, np.float32)
    for c in range(3):
        for of, start, step in places:
            ch, y = of(np.arange(step))
            at = start + c * step + np.arange(step)
            e[at, c * channels + ch] = 1
            ys[0, at] = y
    return e, ys


def iota(rows, columns):
    return [lax.broadcasted_iota(jnp.int32, (rows, columns), d) for d in range(2)]


def one_hot(where):
    return jnp.where(where, 1.0, 0.0).astype(BF16)


def lane_y(of, width, step):
    lane = lax.broadcasted_iota(jnp.int32, (1, width), 1)
    return jnp.where(lane < 3 * step, of(lane % step)[1], FAR)


def place(rows, wanted, of, size, slot):
    row, lane = iota(rows, 128)
    return one_hot((of(lane % size)[0] == wanted(row)) & (lane // size == slot))


def row_table(rows, own):
    row, lane = iota(rows, CH)
    own_c, own_y = own(row)
    rim_c, rim_y = rim(CH)(row - 128)
    channel, y = jnp.where(row < 128, own_c, rim_c), jnp.where(row < 128, own_y, rim_y)
    return one_hot(channel == lane), y[:, :1]


def plane(ref, channels, x):
    v = ref[channels, x].astype(F32)
    return v.reshape(v.shape[0] * v.shape[1], v.shape[2])


def pick_rows(channels, low, high):
    half = channels * 2
    row, col = iota(2 * half, channels * 8)
    side = row // half
    return one_hot(col == (row % half // 2) * 8 + low + (high - low) * side + row % 2)


def partners(index, count):
    return index % 2 == 0, index > 0, index < count - 1


def sides(index, count, near, far):
    near_above, below, above = partners(index, count)
    low = jnp.where(near_above, far, near).astype(F32)
    high = jnp.where(near_above, near, far).astype(F32)
    return jnp.where(below, low, 0.0), jnp.where(above, high, 0.0)


def pack_kernel(inputs, near, far, f_rows, c_rows):
    up_first = lax.axis_index("stream") % 2 == 0
    count, at = inputs.shape[1], 0
    for channels, out, width in ((slice(0, CI), f_rows, 4), (slice(CI, CI + CH), c_rows, 2)):
        rows = [plane(inputs, channels, x) for x in range(count)]
        for x, v in enumerate(rows):
            out[x] = v.astype(BF16)
        for low, high in zip(rows[:width], rows[count - width:]):
            part = slice(at, at + low.shape[0])
            near[part] = jnp.where(up_first, high, low).astype(BF16)
            far[part] = jnp.where(up_first, low, high).astype(BF16)
            at += low.shape[0]


def x_planes(count, fields, cot, xnear, xfar, size):
    index = lax.axis_index("stream")
    inner = [fields[x].astype(F32) for x in range(count)]
    rims = [sides(index, size, xnear[n * 64:(n + 1) * 64], xfar[n * 64:(n + 1) * 64]) for n in range(4)]
    f = [low for low, _ in rims] + inner + [high for _, high in rims]
    inner = [cot[x].astype(F32) for x in range(count)]
    rims = [sides(index, size, xnear[256 + n * 128:384 + n * 128], xfar[256 + n * 128:384 + n * 128]) for n in range(2)]
    return f, [low for low, _ in rims] + inner + [high for _, high in rims]


def pick_strips(work, near, far):
    up_first = lax.axis_index("radial") % 2 == 0
    at = 0
    for pick, rows in work:
        half = pick.shape[0] // 2
        for v in rows:
            got = jnp.dot(pick, v.astype(BF16), preferred_element_type=F32)
            near[at:at + half] = jnp.where(up_first, got[half:], got[:half]).astype(BF16)
            far[at:at + half] = jnp.where(up_first, got[:half], got[half:]).astype(BF16)
            at += half


def join_kernel(counts, xfar, xnear, fields, cot, near, far):
    f, c = x_planes(fields.shape[0], fields, cot, xnear, xfar, counts[0])
    pick_strips([(pick_rows(CI, 0, 6), f[2:-2]), (pick_rows(CH, 0, 6), c)], near, far)


def join_outer_kernel(counts, xfar, xnear, fields, cot, near, far):
    f, _ = x_planes(fields.shape[0], fields, cot, xnear, xfar, counts[0])
    ends = f[:2] + f[-2:]
    pick_strips([(pick_rows(CI, 0, 6), ends), (pick_rows(CI, 2, 4), ends + f[2:-2])], near, far)


def spread(w, by_row, flip):
    taps = jnp.transpose(w[...].astype(F32))
    width = taps.shape[1]
    row = lax.broadcasted_iota(jnp.int32, (CH, width), 0)
    lane = lax.broadcasted_iota(jnp.int32, (CH, width), 1)
    mine = row == (lane // (width // CH) if by_row else lane % CH)
    found = []
    for c in range(3):
        rows = []
        for ab in range(9):
            t = 26 - (ab * 3 + c) if flip else ab * 3 + c
            rows.append(jnp.where(mine, jnp.broadcast_to(taps[t:t + 1], (CH, width)), 0.0))
        found.append(jnp.concatenate(rows, axis=0).astype(BF16))
    return found


def dots(pairs):
    total = None
    for v, w in pairs:
        part = jnp.dot(v, w, preferred_element_type=F32)
        total = part if total is None else total + part
    return total.astype(BF16)


def packed(parts, wanted, of, size):
    per = 128 // size
    places = [place(parts[0].shape[1], wanted, of, size, slot) for slot in range(min(per, 3))]
    tiles = [range(first, min(first + per, 3)) for first in range(0, 3, per)]
    return jnp.concatenate([dots([(parts[c], places[c % per]) for c in tile]) for tile in tiles], axis=1)


def band(wide, expand, ys, rows_y, t):
    rows, width = t.shape[0], wide.shape[1]
    for a in range(3):
        total = jnp.zeros((rows, width), F32)
        for b in range(3):
            part = jnp.dot(expand[:rows], wide[(a * 3 + b) * CH:(a * 3 + b + 1) * CH], preferred_element_type=F32)
            total = jnp.where(ys == rows_y[:rows] + 2 * (b - 1), part, total)
        t[:, a * width:(a + 1) * width] = total.astype(BF16)


def repeat_bias(bias, expand, out):
    column = jnp.sum(expand.astype(F32) * bias[...], axis=1, keepdims=True)
    out[...] = jnp.broadcast_to(column, out.shape)


def band_kernel(w1, w2, first_bias, second_bias, t1o, t1r, t1d, tbo, tbr, t2, b1, b2):
    expand, rows_y = row_table(192, y_first)
    parts = spread(w1, True, False)
    for of, step, t in ((natural, 64, t1o), (rim(CI), 32, t1r), (deep_rim, 64, t1d)):
        wide = packed(parts, lambda n: n % CI, of, step)
        band(wide, expand, lane_y(of, wide.shape[1], step), rows_y, t)
    parts = spread(w2, False, True)
    for of, step, t in ((natural, 128, tbo), (rim(CH), 64, tbr)):
        wide = packed(parts, lambda n: n // CH, of, step)
        band(wide, expand, lane_y(of, wide.shape[1], step), rows_y, t)
    repeat_bias(first_bias, expand, b1)
    expand, rows_y = row_table(128, natural)
    parts = spread(w2, True, False)
    wide = [packed(parts, lambda n: n % CH, of, step) for of, step in ((y_first, 128), (rim(CH), 64))]
    ys = jnp.concatenate([lane_y(y_first, 384, 128), lane_y(rim(CH), 256, 64)], axis=1)
    band(jnp.concatenate(wide, axis=1), expand, ys, rows_y, t2)
    repeat_bias(second_bias, expand, b2)


def shifted(v):
    lane = lax.broadcasted_iota(jnp.int32, v.shape, 1)
    before = jnp.where(lane >= 2, pltpu.roll(v, 2, 1), 0.0)
    after = jnp.where(lane < Z - 2, pltpu.roll(v, Z - 2, 1), 0.0)
    return before.astype(BF16), v.astype(BF16), after.astype(BF16)


def store_wide(ref, p, v):
    at = slice(p * Z, (p + 1) * Z)
    for c, piece in enumerate(shifted(v)):
        ref[c * 128:(c + 1) * 128, at] = piece[:128]
        ref[384 + c * 64:384 + (c + 1) * 64, at] = piece[128:]
    ref[576:, at] = jnp.zeros((64, Z), BF16)


def stacked(ref, lanes):
    return jnp.concatenate([ref[:, a * 256:a * 256 + lanes] for a in range(3)], axis=0)


def own_kernel(counts, xfar, xnear, fields, cot, t1, tb, b1, fs, cs, pre, back):
    count = fields.shape[0]
    f, c = x_planes(count, fields, cot, xnear, xfar, counts[0])
    for ref, rows in ((fs, f), (cs, c)):
        for p, v in enumerate(rows):
            for n, piece in enumerate(shifted(v)):
                ref[n * v.shape[0]:(n + 1) * v.shape[0], p * Z:(p + 1) * Z] = piece
    fs[192:] = jnp.zeros((64, fs.shape[1]), BF16)
    rows = jnp.concatenate([fs[:, a * 256 + 256:a * 256 + 256 + pre.shape[1]] for a in range(3)], axis=0)
    pre[...] = jnp.dot(t1[:128], rows, preferred_element_type=F32) + b1[:128, :1]
    back[...] = jnp.dot(tb[...], stacked(cs, back.shape[1]), preferred_element_type=F32)


def two_dots(v, w):
    high = v.astype(BF16)
    low = (v - high.astype(F32)).astype(BF16)
    return jnp.dot(high, w, preferred_element_type=F32) + jnp.dot(low, w, preferred_element_type=F32)


def gelu_share(pre):
    return 0.5 * (1.0 + lax.erf(pre * 0.7071067811865476))


def rim_kernel(counts, rfar, rnear, fs, cs, pre_own, back_own, t1, tb, e1t, e2t, rep1, rep2, y1, y2,
               hidden_out, payload, fr, cr, taps):
    count = hidden_out.shape[0]
    lanes = count * Z
    radial = lax.axis_index("radial")
    at = 0
    for ref, half in ((fr, 16), (cr, 32)):
        for p in range(count + 4):
            low, high = sides(radial, counts[1], rnear[at:at + half], rfar[at:at + half])
            for n, piece in enumerate(shifted(jnp.concatenate([low, high], axis=0))):
                ref[n * 2 * half:(n + 1) * 2 * half, p * Z:(p + 1) * Z] = piece
            at += half
        ref[6 * half:] = jnp.zeros((2 * half, ref.shape[1]), BF16)
    pre = pre_own[...] + jnp.dot(t1[...], stacked(fr, lanes), preferred_element_type=F32)
    share = gelu_share(pre)
    hidden = (pre * share).astype(BF16)
    for x in range(count):
        hidden_out[x] = hidden[:, x * Z:(x + 1) * Z]
    back = back_own[...] + jnp.dot(tb[...], stacked(cr, lanes), preferred_element_type=F32)
    dpre = (back * (share + pre * jnp.exp(-0.5 * pre * pre) * 0.3989422804014327)).astype(BF16)
    over_lanes = (((1,), (1,)), ((), ()))
    ones, twos = [], []
    for a in range(3):
        at = slice((a + 1) * 256, (a + 1) * 256 + lanes)
        rows = jnp.concatenate([fs[:, at], fr[:, a * 256:a * 256 + lanes]], axis=0)
        g1 = lax.dot_general(dpre, rows, over_lanes, preferred_element_type=F32)
        at = slice(a * 256, a * 256 + lanes)
        rows = jnp.concatenate([cs[:, at], cr[:, at]], axis=0)
        g2 = lax.dot_general(hidden, rows, over_lanes, preferred_element_type=F32)
        for b in range(3):
            for g, ys, out in ((g1, y1, ones), (g2, y2, twos)):
                total = jnp.zeros((CH, g.shape[1]), F32)
                for y in range(8):
                    total = jnp.where(ys[...] == float(y + 2 * (b - 1)), g[y * CH:(y + 1) * CH], total)
                out.append(total)
    taps[:, 24:] = jnp.zeros((3, 8, 128), F32)
    for parts, et, rep, at, width in ((ones, e1t, rep1, 0, 128), (twos[::-1], e2t, rep2, 1, 256)):
        sums = two_dots(jnp.concatenate(parts, axis=0), et[...])
        wide = two_dots(sums, rep[...])
        row = lax.broadcasted_iota(jnp.int32, wide.shape, 0) % CH
        lane = lax.broadcasted_iota(jnp.int32, wide.shape, 1) % width
        mine = row == (lane // CI if width == 128 else lane % CH)
        total = jnp.sum(jnp.where(mine, wide, 0.0).reshape(9, CH, 3 * width), axis=1)
        for c in range(3):
            first = c if width == 128 else 2 - c
            for n in range(width // 128):
                taps[at + n, pl.ds(first, 9, stride=3)] = total[:, c * width + n * 128:c * width + (n + 1) * 128]
    bias = jnp.sum(dpre.astype(F32), axis=1, keepdims=True)
    bias = sum(bias[y * CH:(y + 1) * CH] for y in range(8))
    row = lax.broadcasted_iota(jnp.int32, (CH, 128), 0)
    lane = lax.broadcasted_iota(jnp.int32, (CH, 128), 1)
    taps[0, 27:28] = jnp.sum(jnp.where(row == lane, bias, 0.0), axis=0, keepdims=True)
    payload[...] = jnp.concatenate([taps[n] for n in range(3)], axis=1)


def hidden_rim_kernel(counts, rfar, rnear, rfar_outer, rnear_outer, hidden, fs, t1o, t1d, b1, hidden_out, fr):
    count = hidden.shape[0]
    stream, radial = lax.axis_index("stream"), lax.axis_index("radial")
    for p in range(count + 8):
        end = p if p < 2 else p - count - 4 if p >= count + 6 else None
        if end is None:
            near, outer = (rnear, rfar, (p - 2) * 16), (rnear_outer, rfar_outer, 128 + (p - 2) * 16)
        else:
            near, outer = (rnear_outer, rfar_outer, end * 16), (rnear_outer, rfar_outer, 64 + end * 16)
        parts = [sides(radial, counts[1], n[at:at + 16], f[at:at + 16]) for n, f, at in (near, outer)]
        rows = jnp.concatenate([part[side] for side in range(2) for part in parts], axis=0)
        for n, piece in enumerate(shifted(rows)):
            fr[n * 64:(n + 1) * 64, p * Z:(p + 1) * Z] = piece
    fr[192:] = jnp.zeros((64, fr.shape[1]), BF16)

    def gelu(rows, lanes):
        total = b1[rows, :1]
        for t, ref in ((t1o, fs), (t1d, fr)):
            cells = [jnp.concatenate([ref[:, a * 256 + at:a * 256 + at + size] for at, size in lanes], axis=1) for a in range(3)]
            total = total + jnp.dot(t[rows], jnp.concatenate(cells, axis=0), preferred_element_type=F32)
        return total * gelu_share(total)

    own = gelu(slice(0, 128), ((0, 2 * Z), ((count + 2) * Z, 2 * Z)))
    rims = gelu(slice(128, 192), ((0, (count + 4) * Z),))
    rims = jnp.concatenate([jnp.where(radial > 0, rims[:32], 0.0), jnp.where(radial < counts[1] - 1, rims[32:], 0.0)], axis=0)
    for p in range(count + 4):
        rim_rows = rims[:, p * Z:(p + 1) * Z]
        if 2 <= p < count + 2:
            hidden_out[p, :128] = hidden[p - 2]
            hidden_out[p, 128:] = rim_rows.astype(BF16)
        else:
            at = p if p < 2 else p - count
            inside = stream > 0 if p < 2 else stream < counts[0] - 1
            rows = jnp.concatenate([own[:, at * Z:(at + 1) * Z], rim_rows], axis=0)
            hidden_out[p] = jnp.where(inside, rows, 0.0).astype(BF16)


def closure_kernel(hidden, t2, b2, closure, hs):
    count = closure.shape[2]
    for p in range(count + 4):
        store_wide(hs, p, hidden[p].astype(F32))
    out = (jnp.dot(t2[...], stacked(hs, count * Z), preferred_element_type=F32) + b2[:, :1]).astype(BF16)
    for x in range(count):
        closure[0, :, x] = out[:, x * Z:(x + 1) * Z].reshape(CH, 8, Z)


def summed(parts):
    parts = [part[...].astype(F32) for part in parts]
    while len(parts) > 1:
        parts = [v + w for v, w in zip(parts[::2], parts[1::2])]
    return parts[0]


def add_kernel(*refs):
    s = summed(refs[:-1])
    lost = s - s.astype(BF16).astype(F32)
    row = lax.broadcasted_iota(jnp.int32, s.shape, 0)
    refs[-1][...] = (s + jnp.where(row == 28, pltpu.roll(lost, 1, 0), 0.0)).astype(BF16)


def finish_kernel(norm, *refs):
    *parts, first, second, bias = refs
    scaled = summed(parts) * norm
    flipped = jnp.transpose(scaled)
    first[...] = flipped[:128, :27]
    second[...] = flipped[128:, :27]
    bias[...] = scaled[27:28, :CH] + scaled[28:29, :CH]


def call(kernel, outs, name, scratch=(), flops=10_000_000, **specs):
    return pl.pallas_call(
        kernel,
        out_shape=outs,
        **specs,
        scratch_shapes=list(scratch),
        compiler_params=pltpu.CompilerParams(vmem_limit_bytes=32 * 1024 * 1024),
        cost_estimate=pl.CostEstimate(flops=flops, bytes_accessed=1_000_000, transcendentals=0),
        name=name,
    )


def shape(*dims, dtype=BF16):
    return jax.ShapeDtypeStruct(dims, dtype)


def exchange(near, far, axis, other):
    count, others = lax.axis_size(axis), lax.axis_size(other)
    pairs = []
    for i in range(count):
        for j in range(others):
            end = i in (0, count - 1)
            to = (i, j ^ 1 if others % 2 == 0 else j) if end else (i - 1 + 2 * (i % 2), j)
            pairs.append((i * others + j, to[0] * others + to[1]))
    far = lax.ppermute(far, (axis, other), pairs)
    return lax.ppermute(near, axis, [(i, i ^ 1) for i in range(count)]), far


def swap(v, axis, masks):
    count = lax.axis_size(axis)
    return [lax.ppermute(v, axis, [(i, i ^ mask) for i in range(count)]) for mask in masks]


def add(v, arrived):
    return call(add_kernel, shape(*v.shape), "add_parts")(v, *arrived)


def rounds(axis, most):
    found, step = [], 1
    while step < lax.axis_size(axis):
        masks = [step * n for n in range(1, most if step * most <= lax.axis_size(axis) else 2)]
        found.append((axis, masks))
        step *= len(masks) + 1
    return found


def local(fields, first_weight, first_bias, second_weight, second_bias, cotangent):
    e1t, y1 = table(CI, 384, ((natural, 0, 64), (rim(CI), 256, 32)))
    e2t, y2 = table(CH, 640, ((natural, 0, 128), (rim(CH), 384, 64)))
    rep1, rep2 = np.zeros((128, 384), np.float32), np.zeros((128, 768), np.float32)
    for c in range(3):
        rep1[c * CI:(c + 1) * CI, c * 128:(c + 1) * 128] = np.tile(np.eye(CI), (1, CH))
        rep2[c * CH:(c + 1) * CH, c * 256:(c + 1) * 256] = np.repeat(np.eye(CH), CH, axis=1)

    def const(*arrays, dtype=BF16):
        return [jnp.asarray(v, dtype) for v in arrays]

    planes = fields.shape[2]
    w1 = first_weight.transpose(1, 2, 0).reshape(CH * CI, 27)
    w2 = second_weight.transpose(1, 2, 0).reshape(CH * CH, 27)
    near, far, f_rows, c_rows = call(
        pack_kernel,
        (shape(512, Z), shape(512, Z), shape(planes, CI * 8, Z), shape(planes, CH * 8, Z)),
        "pack_strips",
        flops=4_000_000_000,
    )(jnp.concatenate([fields[0], cotangent[0]], axis=0))
    xnear, xfar = exchange(near, far, "stream", "radial")
    wide = (planes + 4) * Z
    counts = (lax.axis_size("stream"), lax.axis_size("radial"))
    t1o, t1r, t1d, tbo, tbr, t2, b1, b2 = call(
        band_kernel,
        (shape(192, 768), shape(128, 384), shape(192, 768), shape(128, 1152), shape(128, 768), shape(128, 1920),
         shape(192, 128, dtype=F32), shape(128, 128, dtype=F32)),
        "band_matrices",
        flops=4_000_000_000,
    )(w1, w2, first_bias[None], second_bias[None])
    xfar, xnear, t1o, tbo = lax.optimization_barrier((xfar, xnear, t1o, tbo))
    inner, outer = shape((planes + 4) * 48, Z), shape(128 + (planes + 4) * 16, Z)
    near, far = call(functools.partial(join_kernel, counts), (inner, inner), "join_strips")(xfar, xnear, f_rows, c_rows)
    rnear, rfar = exchange(near, far, "radial", "snap")
    fs, cs, pre, back = call(
        functools.partial(own_kernel, counts),
        (shape(256, wide + 4 * Z), shape(384, wide), shape(128, planes * Z, dtype=F32), shape(128, planes * Z, dtype=F32)),
        "own_rows",
        flops=1_000_000_000,
    )(xfar, xnear, f_rows, c_rows, t1o, tbo, b1)
    f_rows, fs = lax.optimization_barrier((f_rows, fs))
    near_outer, far_outer = call(functools.partial(join_outer_kernel, counts), (outer, outer), "join_outer")(
        xfar, xnear, f_rows, c_rows)
    rnear_outer, rfar_outer = exchange(near_outer, far_outer, "radial", "snap")
    hidden, payload = call(
        functools.partial(rim_kernel, counts),
        (shape(planes, 128, Z), shape(32, 384, dtype=F32)),
        "gradients",
        (pltpu.VMEM((128, wide), BF16), pltpu.VMEM((256, wide), BF16), pltpu.VMEM((3, 32, 128), F32)),
        flops=2_000_000_000,
    )(rfar, rnear, fs, cs, pre, back, t1r, tbr, *const(e1t, e2t, rep1, rep2), *const(y1, y2, dtype=F32))

    steps = rounds("radial", 2) + rounds("stream", 4) + rounds("snap", 2)
    arrived = swap(payload, *steps[0])
    payload = add(payload, arrived)
    arrived = swap(payload, *steps[1])
    hidden = call(
        functools.partial(hidden_rim_kernel, counts),
        shape(planes + 4, 192, Z),
        "hidden_rim",
        (pltpu.VMEM((256, wide + 4 * Z), BF16),),
        flops=1_000_000_000,
    )(rfar, rnear, rfar_outer, rnear_outer, hidden, fs, t1o, t1d, b1)
    payload, hidden = lax.optimization_barrier((add(payload, arrived), hidden))
    arrived = swap(payload, *steps[2])
    payload = add(payload, arrived)
    arrived = swap(payload, *steps[3])
    closure = call(
        closure_kernel, shape(*cotangent.shape), "closure", (pltpu.VMEM((640, wide), BF16),), flops=1_000_000_000
    )(hidden, t2, b2)
    for step in steps[4:]:
        payload = add(payload, arrived)
        arrived = swap(payload, *step)

    cells = fields.shape[0] * fields.shape[2] * fields.shape[3] * fields.shape[4]
    for axis in ("stream", "radial", "snap"):
        cells *= lax.axis_size(axis)
    norm = float(1.0 / np.sqrt(np.float32(cells)))
    first, second, bias = call(
        functools.partial(finish_kernel, norm),
        (shape(CH * CI, 27, dtype=F32), shape(CH * CH, 27, dtype=F32), shape(1, CH, dtype=F32)),
        "finish",
    )(payload, *arrived)
    first = first.reshape(CH, CI, 27).transpose(2, 0, 1)
    second = second.reshape(CH, CH, 27).transpose(2, 0, 1)
    return (closure, first, second, bias[0])


def solution(mesh):
    split = P("snap", None, "stream", "radial", None)
    return jax.shard_map(
        local,
        mesh=mesh,
        in_specs=(split, P(), P(), P(), P(), split),
        out_specs=(split, P(), P(), P()),
        check_vma=False,
    )
```

```python
import functools

import numpy as np
import jax
import jax.numpy as jnp
from jax import lax
from jax.experimental import pallas as pl
from jax.experimental.pallas import tpu as pltpu
from jax.sharding import PartitionSpec as P

F32 = jnp.float32
BF16 = jnp.bfloat16
Z = 128
CI = 8
CH = 16
FAR = 100


def natural(n):
    return n // 8, n % 8


def y_first(n):
    return n % CH, n // CH


def rim(channels):
    def of(n):
        side, n = n // (2 * channels), n % (2 * channels)
        return n // 2, n % 2 + 10 * side - 2
    return of


def deep_rim(n):
    part, n = n // 16, n % 16
    return n // 2, n % 2 + 10 * (part // 2) - 2 + (part % 2) * (4 * (part // 2) - 2)


def table(channels, total, places):
    e = np.zeros((total, 128), np.float32)
    ys = np.full((1, total), FAR, np.float32)
    for c in range(3):
        for of, start, step in places:
            ch, y = of(np.arange(step))
            at = start + c * step + np.arange(step)
            e[at, c * channels + ch] = 1
            ys[0, at] = y
    return e, ys


def iota(rows, columns):
    return [lax.broadcasted_iota(jnp.int32, (rows, columns), d) for d in range(2)]


def one_hot(where):
    return jnp.where(where, 1.0, 0.0).astype(BF16)


def lane_y(of, width, step):
    lane = lax.broadcasted_iota(jnp.int32, (1, width), 1)
    return jnp.where(lane < 3 * step, of(lane % step)[1], FAR)


def place(rows, wanted, of, size, slot):
    row, lane = iota(rows, 128)
    return one_hot((of(lane % size)[0] == wanted(row)) & (lane // size == slot))


def row_table(rows, own):
    row, lane = iota(rows, CH)
    own_c, own_y = own(row)
    rim_c, rim_y = rim(CH)(row - 128)
    channel, y = jnp.where(row < 128, own_c, rim_c), jnp.where(row < 128, own_y, rim_y)
    return one_hot(channel == lane), y[:, :1]


def plane(ref, channels, x):
    v = ref[channels, x].astype(F32)
    return v.reshape(v.shape[0] * v.shape[1], v.shape[2])


def pick_rows(channels, low, high):
    half = channels * 2
    row, col = iota(2 * half, channels * 8)
    side = row // half
    return one_hot(col == (row % half // 2) * 8 + low + (high - low) * side + row % 2)


def partners(index, count):
    return index % 2 == 0, index > 0, index < count - 1


def sides(index, count, near, far):
    near_above, below, above = partners(index, count)
    low = jnp.where(near_above, far, near).astype(F32)
    high = jnp.where(near_above, near, far).astype(F32)
    return jnp.where(below, low, 0.0), jnp.where(above, high, 0.0)


def pack_kernel(inputs, near, far, f_rows, c_rows):
    up_first = lax.axis_index("stream") % 2 == 0
    count, at = inputs.shape[1], 0
    for channels, out, width in ((slice(0, CI), f_rows, 4), (slice(CI, CI + CH), c_rows, 2)):
        rows = [plane(inputs, channels, x) for x in range(count)]
        for x, v in enumerate(rows):
            out[x] = v.astype(BF16)
        for low, high in zip(rows[:width], rows[count - width:]):
            part = slice(at, at + low.shape[0])
            near[part] = jnp.where(up_first, high, low).astype(BF16)
            far[part] = jnp.where(up_first, low, high).astype(BF16)
            at += low.shape[0]


def x_planes(count, fields, cot, xnear, xfar, size):
    index = lax.axis_index("stream")
    inner = [fields[x].astype(F32) for x in range(count)]
    rims = [sides(index, size, xnear[n * 64:(n + 1) * 64], xfar[n * 64:(n + 1) * 64]) for n in range(4)]
    f = [low for low, _ in rims] + inner + [high for _, high in rims]
    inner = [cot[x].astype(F32) for x in range(count)]
    rims = [sides(index, size, xnear[256 + n * 128:384 + n * 128], xfar[256 + n * 128:384 + n * 128]) for n in range(2)]
    return f, [low for low, _ in rims] + inner + [high for _, high in rims]


def pick_strips(work, near, far):
    up_first = lax.axis_index("radial") % 2 == 0
    at = 0
    for pick, rows in work:
        half = pick.shape[0] // 2
        for v in rows:
            got = jnp.dot(pick, v.astype(BF16), preferred_element_type=F32)
            near[at:at + half] = jnp.where(up_first, got[half:], got[:half]).astype(BF16)
            far[at:at + half] = jnp.where(up_first, got[:half], got[half:]).astype(BF16)
            at += half


def join_kernel(counts, xfar, xnear, fields, cot, near, far):
    f, c = x_planes(fields.shape[0], fields, cot, xnear, xfar, counts[0])
    pick_strips([(pick_rows(CI, 0, 6), f[2:-2]), (pick_rows(CH, 0, 6), c)], near, far)


def join_outer_kernel(counts, xfar, xnear, fields, cot, near, far):
    f, _ = x_planes(fields.shape[0], fields, cot, xnear, xfar, counts[0])
    ends = f[:2] + f[-2:]
    pick_strips([(pick_rows(CI, 0, 6), ends), (pick_rows(CI, 2, 4), ends + f[2:-2])], near, far)


def spread(w, by_row, flip):
    taps = jnp.transpose(w[...].astype(F32))
    width = taps.shape[1]
    row = lax.broadcasted_iota(jnp.int32, (CH, width), 0)
    lane = lax.broadcasted_iota(jnp.int32, (CH, width), 1)
    mine = row == (lane // (width // CH) if by_row else lane % CH)
    found = []
    for c in range(3):
        rows = []
        for ab in range(9):
            t = 26 - (ab * 3 + c) if flip else ab * 3 + c
            rows.append(jnp.where(mine, jnp.broadcast_to(taps[t:t + 1], (CH, width)), 0.0))
        found.append(jnp.concatenate(rows, axis=0).astype(BF16))
    return found


def dots(pairs):
    total = None
    for v, w in pairs:
        part = jnp.dot(v, w, preferred_element_type=F32)
        total = part if total is None else total + part
    return total.astype(BF16)


def packed(parts, wanted, of, size):
    per = 128 // size
    places = [place(parts[0].shape[1], wanted, of, size, slot) for slot in range(min(per, 3))]
    tiles = [range(first, min(first + per, 3)) for first in range(0, 3, per)]
    return jnp.concatenate([dots([(parts[c], places[c % per]) for c in tile]) for tile in tiles], axis=1)


def band(wide, expand, ys, rows_y, t):
    rows, width = t.shape[0], wide.shape[1]
    for a in range(3):
        total = jnp.zeros((rows, width), F32)
        for b in range(3):
            part = jnp.dot(expand[:rows], wide[(a * 3 + b) * CH:(a * 3 + b + 1) * CH], preferred_element_type=F32)
            total = jnp.where(ys == rows_y[:rows] + 2 * (b - 1), part, total)
        t[:, a * width:(a + 1) * width] = total.astype(BF16)


def repeat_bias(bias, expand, out):
    column = jnp.sum(expand.astype(F32) * bias[...], axis=1, keepdims=True)
    out[...] = jnp.broadcast_to(column, out.shape)


def band_first_kernel(w1, w2, first_bias, t1o, t1r, tbo, tbr, b1):
    expand, rows_y = row_table(192, y_first)
    parts = spread(w1, True, False)
    for of, step, t in ((natural, 64, t1o), (rim(CI), 32, t1r)):
        wide = packed(parts, lambda n: n % CI, of, step)
        band(wide, expand, lane_y(of, wide.shape[1], step), rows_y, t)
    parts = spread(w2, False, True)
    for of, step, t in ((natural, 128, tbo), (rim(CH), 64, tbr)):
        wide = packed(parts, lambda n: n // CH, of, step)
        band(wide, expand, lane_y(of, wide.shape[1], step), rows_y, t)
    repeat_bias(first_bias, expand, b1)


def band_second_kernel(w1, w2, second_bias, t1d, t2, b2):
    expand, rows_y = row_table(192, y_first)
    wide = packed(spread(w1, True, False), lambda n: n % CI, deep_rim, 64)
    band(wide, expand, lane_y(deep_rim, wide.shape[1], 64), rows_y, t1d)
    expand, rows_y = row_table(128, natural)
    parts = spread(w2, True, False)
    wide = [packed(parts, lambda n: n % CH, of, step) for of, step in ((y_first, 128), (rim(CH), 64))]
    ys = jnp.concatenate([lane_y(y_first, 384, 128), lane_y(rim(CH), 256, 64)], axis=1)
    band(jnp.concatenate(wide, axis=1), expand, ys, rows_y, t2)
    repeat_bias(second_bias, expand, b2)


def shifted(v):
    lane = lax.broadcasted_iota(jnp.int32, v.shape, 1)
    before = jnp.where(lane >= 2, pltpu.roll(v, 2, 1), 0.0)
    after = jnp.where(lane < Z - 2, pltpu.roll(v, Z - 2, 1), 0.0)
    return before.astype(BF16), v.astype(BF16), after.astype(BF16)


def store_wide(ref, p, v):
    at = slice(p * Z, (p + 1) * Z)
    for c, piece in enumerate(shifted(v)):
        ref[c * 128:(c + 1) * 128, at] = piece[:128]
        ref[384 + c * 64:384 + (c + 1) * 64, at] = piece[128:]
    ref[576:, at] = jnp.zeros((64, Z), BF16)


def stacked(ref, lanes):
    return jnp.concatenate([ref[:, a * 256:a * 256 + lanes] for a in range(3)], axis=0)


def own_kernel(counts, xfar, xnear, fields, cot, t1, tb, b1, fs, cs, pre, back):
    count = fields.shape[0]
    f, c = x_planes(count, fields, cot, xnear, xfar, counts[0])
    for ref, rows in ((fs, f), (cs, c)):
        for p, v in enumerate(rows):
            for n, piece in enumerate(shifted(v)):
                ref[n * v.shape[0]:(n + 1) * v.shape[0], p * Z:(p + 1) * Z] = piece
    fs[192:] = jnp.zeros((64, fs.shape[1]), BF16)
    rows = jnp.concatenate([fs[:, a * 256 + 256:a * 256 + 256 + pre.shape[1]] for a in range(3)], axis=0)
    pre[...] = jnp.dot(t1[:128], rows, preferred_element_type=F32) + b1[:128, :1]
    back[...] = jnp.dot(tb[...], stacked(cs, back.shape[1]), preferred_element_type=F32)


def two_dots(v, w):
    high = v.astype(BF16)
    low = (v - high.astype(F32)).astype(BF16)
    return jnp.dot(high, w, preferred_element_type=F32) + jnp.dot(low, w, preferred_element_type=F32)


def gelu_share(pre):
    return 0.5 * (1.0 + lax.erf(pre * 0.7071067811865476))


def rim_kernel(counts, rfar, rnear, fs, cs, pre_own, back_own, t1, tb, e1t, e2t, rep1, rep2, y1, y2,
               hidden_out, payload, fr, cr, taps):
    count = hidden_out.shape[0]
    lanes = count * Z
    radial = lax.axis_index("radial")
    at = 0
    for ref, half in ((fr, 16), (cr, 32)):
        for p in range(count + 4):
            low, high = sides(radial, counts[1], rnear[at:at + half], rfar[at:at + half])
            for n, piece in enumerate(shifted(jnp.concatenate([low, high], axis=0))):
                ref[n * 2 * half:(n + 1) * 2 * half, p * Z:(p + 1) * Z] = piece
            at += half
        ref[6 * half:] = jnp.zeros((2 * half, ref.shape[1]), BF16)
    pre = pre_own[...] + jnp.dot(t1[...], stacked(fr, lanes), preferred_element_type=F32)
    share = gelu_share(pre)
    hidden = (pre * share).astype(BF16)
    for x in range(count):
        hidden_out[x] = hidden[:, x * Z:(x + 1) * Z]
    back = back_own[...] + jnp.dot(tb[...], stacked(cr, lanes), preferred_element_type=F32)
    dpre = (back * (share + pre * jnp.exp(-0.5 * pre * pre) * 0.3989422804014327)).astype(BF16)
    over_lanes = (((1,), (1,)), ((), ()))
    ones, twos = [], []
    for a in range(3):
        at = slice((a + 1) * 256, (a + 1) * 256 + lanes)
        rows = jnp.concatenate([fs[:, at], fr[:, a * 256:a * 256 + lanes]], axis=0)
        g1 = lax.dot_general(dpre, rows, over_lanes, preferred_element_type=F32)
        at = slice(a * 256, a * 256 + lanes)
        rows = jnp.concatenate([cs[:, at], cr[:, at]], axis=0)
        g2 = lax.dot_general(hidden, rows, over_lanes, preferred_element_type=F32)
        for b in range(3):
            for g, ys, out in ((g1, y1, ones), (g2, y2, twos)):
                total = jnp.zeros((CH, g.shape[1]), F32)
                for y in range(8):
                    total = jnp.where(ys[...] == float(y + 2 * (b - 1)), g[y * CH:(y + 1) * CH], total)
                out.append(total)
    taps[:, 24:] = jnp.zeros((3, 8, 128), F32)
    for parts, et, rep, at, width in ((ones, e1t, rep1, 0, 128), (twos[::-1], e2t, rep2, 1, 256)):
        sums = two_dots(jnp.concatenate(parts, axis=0), et[...])
        wide = two_dots(sums, rep[...])
        row = lax.broadcasted_iota(jnp.int32, wide.shape, 0) % CH
        lane = lax.broadcasted_iota(jnp.int32, wide.shape, 1) % width
        mine = row == (lane // CI if width == 128 else lane % CH)
        total = jnp.sum(jnp.where(mine, wide, 0.0).reshape(9, CH, 3 * width), axis=1)
        for c in range(3):
            first = c if width == 128 else 2 - c
            for n in range(width // 128):
                taps[at + n, pl.ds(first, 9, stride=3)] = total[:, c * width + n * 128:c * width + (n + 1) * 128]
    bias = jnp.sum(dpre.astype(F32), axis=1, keepdims=True)
    bias = sum(bias[y * CH:(y + 1) * CH] for y in range(8))
    row = lax.broadcasted_iota(jnp.int32, (CH, 128), 0)
    lane = lax.broadcasted_iota(jnp.int32, (CH, 128), 1)
    taps[0, 27:28] = jnp.sum(jnp.where(row == lane, bias, 0.0), axis=0, keepdims=True)
    payload[...] = jnp.concatenate([taps[n] for n in range(3)], axis=1)


def hidden_rim_kernel(counts, rfar, rnear, rfar_outer, rnear_outer, hidden, fs, t1o, t1d, b1, hidden_out, fr):
    count = hidden.shape[0]
    stream, radial = lax.axis_index("stream"), lax.axis_index("radial")
    for p in range(count + 8):
        end = p if p < 2 else p - count - 4 if p >= count + 6 else None
        if end is None:
            near, outer = (rnear, rfar, (p - 2) * 16), (rnear_outer, rfar_outer, 128 + (p - 2) * 16)
        else:
            near, outer = (rnear_outer, rfar_outer, end * 16), (rnear_outer, rfar_outer, 64 + end * 16)
        parts = [sides(radial, counts[1], n[at:at + 16], f[at:at + 16]) for n, f, at in (near, outer)]
        rows = jnp.concatenate([part[side] for side in range(2) for part in parts], axis=0)
        for n, piece in enumerate(shifted(rows)):
            fr[n * 64:(n + 1) * 64, p * Z:(p + 1) * Z] = piece
    fr[192:] = jnp.zeros((64, fr.shape[1]), BF16)

    def gelu(rows, lanes):
        total = b1[rows, :1]
        for t, ref in ((t1o, fs), (t1d, fr)):
            cells = [jnp.concatenate([ref[:, a * 256 + at:a * 256 + at + size] for at, size in lanes], axis=1) for a in range(3)]
            total = total + jnp.dot(t[rows], jnp.concatenate(cells, axis=0), preferred_element_type=F32)
        return total * gelu_share(total)

    own = gelu(slice(0, 128), ((0, 2 * Z), ((count + 2) * Z, 2 * Z)))
    rims = gelu(slice(128, 192), ((0, (count + 4) * Z),))
    rims = jnp.concatenate([jnp.where(radial > 0, rims[:32], 0.0), jnp.where(radial < counts[1] - 1, rims[32:], 0.0)], axis=0)
    for p in range(count + 4):
        rim_rows = rims[:, p * Z:(p + 1) * Z]
        if 2 <= p < count + 2:
            hidden_out[p, :128] = hidden[p - 2]
            hidden_out[p, 128:] = rim_rows.astype(BF16)
        else:
            at = p if p < 2 else p - count
            inside = stream > 0 if p < 2 else stream < counts[0] - 1
            rows = jnp.concatenate([own[:, at * Z:(at + 1) * Z], rim_rows], axis=0)
            hidden_out[p] = jnp.where(inside, rows, 0.0).astype(BF16)


def closure_kernel(hidden, t2, b2, closure, hs):
    count = closure.shape[2]
    for p in range(count + 4):
        store_wide(hs, p, hidden[p].astype(F32))
    out = (jnp.dot(t2[...], stacked(hs, count * Z), preferred_element_type=F32) + b2[:, :1]).astype(BF16)
    for x in range(count):
        closure[0, :, x] = out[:, x * Z:(x + 1) * Z].reshape(CH, 8, Z)


def summed(parts):
    parts = [part[...].astype(F32) for part in parts]
    while len(parts) > 1:
        parts = [v + w for v, w in zip(parts[::2], parts[1::2])]
    return parts[0]


def add_kernel(*refs):
    s = summed(refs[:-1])
    lost = s - s.astype(BF16).astype(F32)
    row = lax.broadcasted_iota(jnp.int32, s.shape, 0)
    refs[-1][...] = (s + jnp.where(row == 28, pltpu.roll(lost, 1, 0), 0.0)).astype(BF16)


def finish_kernel(norm, *refs):
    *parts, first, second, bias = refs
    scaled = summed(parts) * norm
    flipped = jnp.transpose(scaled)
    first[...] = flipped[:128, :27]
    second[...] = flipped[128:, :27]
    bias[...] = scaled[27:28, :CH] + scaled[28:29, :CH]


def call(kernel, outs, name, scratch=(), flops=10_000_000, **specs):
    return pl.pallas_call(
        kernel,
        out_shape=outs,
        **specs,
        scratch_shapes=list(scratch),
        compiler_params=pltpu.CompilerParams(vmem_limit_bytes=32 * 1024 * 1024),
        cost_estimate=pl.CostEstimate(flops=flops, bytes_accessed=1_000_000, transcendentals=0),
        name=name,
    )


def shape(*dims, dtype=BF16):
    return jax.ShapeDtypeStruct(dims, dtype)


def exchange(near, far, axis, other):
    count, others = lax.axis_size(axis), lax.axis_size(other)
    pairs = []
    for i in range(count):
        for j in range(others):
            end = i in (0, count - 1)
            to = (i, j ^ 1 if others % 2 == 0 else j) if end else (i - 1 + 2 * (i % 2), j)
            pairs.append((i * others + j, to[0] * others + to[1]))
    far = lax.ppermute(far, (axis, other), pairs)
    return lax.ppermute(near, axis, [(i, i ^ 1) for i in range(count)]), far


def swap(v, axis, masks):
    count = lax.axis_size(axis)
    return [lax.ppermute(v, axis, [(i, i ^ mask) for i in range(count)]) for mask in masks]


def add(v, arrived):
    return call(add_kernel, shape(*v.shape), "add_parts")(v, *arrived)


def rounds(axis, most):
    found, step = [], 1
    while step < lax.axis_size(axis):
        masks = [step * n for n in range(1, most if step * most <= lax.axis_size(axis) else 2)]
        found.append((axis, masks))
        step *= len(masks) + 1
    return found


def local(fields, first_weight, first_bias, second_weight, second_bias, cotangent):
    e1t, y1 = table(CI, 384, ((natural, 0, 64), (rim(CI), 256, 32)))
    e2t, y2 = table(CH, 640, ((natural, 0, 128), (rim(CH), 384, 64)))
    rep1, rep2 = np.zeros((128, 384), np.float32), np.zeros((128, 768), np.float32)
    for c in range(3):
        rep1[c * CI:(c + 1) * CI, c * 128:(c + 1) * 128] = np.tile(np.eye(CI), (1, CH))
        rep2[c * CH:(c + 1) * CH, c * 256:(c + 1) * 256] = np.repeat(np.eye(CH), CH, axis=1)

    def const(*arrays, dtype=BF16):
        return [jnp.asarray(v, dtype) for v in arrays]

    planes = fields.shape[2]
    w1 = first_weight.transpose(1, 2, 0).reshape(CH * CI, 27)
    w2 = second_weight.transpose(1, 2, 0).reshape(CH * CH, 27)
    near, far, f_rows, c_rows = call(
        pack_kernel,
        (shape(512, Z), shape(512, Z), shape(planes, CI * 8, Z), shape(planes, CH * 8, Z)),
        "pack_strips",
        flops=4_000_000_000,
    )(jnp.concatenate([fields[0], cotangent[0]], axis=0))
    xnear, xfar = exchange(near, far, "stream", "radial")
    wide = (planes + 4) * Z
    counts = (lax.axis_size("stream"), lax.axis_size("radial"))
    t1o, t1r, tbo, tbr, b1 = call(
        band_first_kernel,
        (shape(192, 768), shape(128, 384), shape(128, 1152), shape(128, 768), shape(192, 128, dtype=F32)),
        "band_first",
        flops=4_000_000_000,
    )(w1, w2, first_bias[None])
    xfar, xnear, t1o, tbo = lax.optimization_barrier((xfar, xnear, t1o, tbo))
    inner, outer = shape((planes + 4) * 48, Z), shape(128 + (planes + 4) * 16, Z)
    near, far = call(functools.partial(join_kernel, counts), (inner, inner), "join_strips")(xfar, xnear, f_rows, c_rows)
    rnear, rfar = exchange(near, far, "radial", "snap")
    fs, cs, pre, back = call(
        functools.partial(own_kernel, counts),
        (shape(256, wide + 4 * Z), shape(384, wide), shape(128, planes * Z, dtype=F32), shape(128, planes * Z, dtype=F32)),
        "own_rows",
        flops=1_000_000_000,
    )(xfar, xnear, f_rows, c_rows, t1o, tbo, b1)
    f_rows, fs = lax.optimization_barrier((f_rows, fs))
    near_outer, far_outer = call(functools.partial(join_outer_kernel, counts), (outer, outer), "join_outer")(
        xfar, xnear, f_rows, c_rows)
    rnear_outer, rfar_outer = exchange(near_outer, far_outer, "radial", "snap")
    hidden, payload = call(
        functools.partial(rim_kernel, counts),
        (shape(planes, 128, Z), shape(32, 384, dtype=F32)),
        "gradients",
        (pltpu.VMEM((128, wide), BF16), pltpu.VMEM((256, wide), BF16), pltpu.VMEM((3, 32, 128), F32)),
        flops=2_000_000_000,
    )(rfar, rnear, fs, cs, pre, back, t1r, tbr, *const(e1t, e2t, rep1, rep2), *const(y1, y2, dtype=F32))

    steps = rounds("radial", 2) + rounds("stream", 4) + rounds("snap", 2)
    arrived = swap(payload, *steps[0])
    payload, w2 = lax.optimization_barrier((add(payload, arrived), w2))
    arrived = swap(payload, *steps[1])
    t1d, t2, b2 = call(
        band_second_kernel,
        (shape(192, 768), shape(128, 1920), shape(128, 128, dtype=F32)),
        "band_second",
        flops=1_000_000_000,
    )(w1, w2, second_bias[None])
    payload, t1d, t2, b2 = lax.optimization_barrier((add(payload, arrived), t1d, t2, b2))
    arrived = swap(payload, *steps[2])
    hidden = call(
        functools.partial(hidden_rim_kernel, counts),
        shape(planes + 4, 192, Z),
        "hidden_rim",
        (pltpu.VMEM((256, wide + 4 * Z), BF16),),
        flops=1_000_000_000,
    )(rfar, rnear, rfar_outer, rnear_outer, hidden, fs, t1o, t1d, b1)
    payload, hidden = lax.optimization_barrier((add(payload, arrived), hidden))
    arrived = swap(payload, *steps[3])
    closure = call(
        closure_kernel, shape(*cotangent.shape), "closure", (pltpu.VMEM((640, wide), BF16),), flops=1_000_000_000
    )(hidden, t2, b2)
    for step in steps[4:]:
        payload = add(payload, arrived)
        arrived = swap(payload, *step)

    cells = fields.shape[0] * fields.shape[2] * fields.shape[3] * fields.shape[4]
    for axis in ("stream", "radial", "snap"):
        cells *= lax.axis_size(axis)
    norm = float(1.0 / np.sqrt(np.float32(cells)))
    first, second, bias = call(
        functools.partial(finish_kernel, norm),
        (shape(CH * CI, 27, dtype=F32), shape(CH * CH, 27, dtype=F32), shape(1, CH, dtype=F32)),
        "finish",
    )(payload, *arrived)
    first = first.reshape(CH, CI, 27).transpose(2, 0, 1)
    second = second.reshape(CH, CH, 27).transpose(2, 0, 1)
    return (closure, first, second, bias[0])


def solution(mesh):
    split = P("snap", None, "stream", "radial", None)
    return jax.shard_map(
        local,
        mesh=mesh,
        in_specs=(split, P(), P(), P(), P(), split),
        out_specs=(split, P(), P(), P()),
        check_vma=False,
    )
```

```python
import functools

import numpy as np
import jax
import jax.numpy as jnp
from jax import lax
from jax.experimental import pallas as pl
from jax.experimental.pallas import tpu as pltpu
from jax.sharding import PartitionSpec as P

F32 = jnp.float32
BF16 = jnp.bfloat16
Z = 128
CI = 8
CH = 16
FAR = 100


def natural(n):
    return n // 8, n % 8


def y_first(n):
    return n % CH, n // CH


def rim(channels):
    def of(n):
        side, n = n // (2 * channels), n % (2 * channels)
        return n // 2, n % 2 + 10 * side - 2
    return of


def deep_rim(n):
    part, n = n // 16, n % 16
    return n // 2, n % 2 + 10 * (part // 2) - 2 + (part % 2) * (4 * (part // 2) - 2)


def table(channels, total, places):
    e = np.zeros((total, 128), np.float32)
    ys = np.full((1, total), FAR, np.float32)
    for c in range(3):
        for of, start, step in places:
            ch, y = of(np.arange(step))
            at = start + c * step + np.arange(step)
            e[at, c * channels + ch] = 1
            ys[0, at] = y
    return e, ys


def iota(rows, columns):
    return [lax.broadcasted_iota(jnp.int32, (rows, columns), d) for d in range(2)]


def one_hot(where):
    return jnp.where(where, 1.0, 0.0).astype(BF16)


def lane_y(of, width, step):
    lane = lax.broadcasted_iota(jnp.int32, (1, width), 1)
    return jnp.where(lane < 3 * step, of(lane % step)[1], FAR)


def place(rows, wanted, of, size, slot):
    row, lane = iota(rows, 128)
    return one_hot((of(lane % size)[0] == wanted(row)) & (lane // size == slot))


def row_table(rows, own):
    row, lane = iota(rows, CH)
    own_c, own_y = own(row)
    rim_c, rim_y = rim(CH)(row - 128)
    channel, y = jnp.where(row < 128, own_c, rim_c), jnp.where(row < 128, own_y, rim_y)
    return one_hot(channel == lane), y[:, :1]


def plane(ref, channels, x):
    v = ref[channels, x].astype(F32)
    return v.reshape(v.shape[0] * v.shape[1], v.shape[2])


def pick_rows(channels, low, high):
    half = channels * 2
    row, col = iota(2 * half, channels * 8)
    side = row // half
    return one_hot(col == (row % half // 2) * 8 + low + (high - low) * side + row % 2)


def partners(index, count):
    return index % 2 == 0, index > 0, index < count - 1


def sides(index, count, near, far):
    near_above, below, above = partners(index, count)
    low = jnp.where(near_above, far, near).astype(F32)
    high = jnp.where(near_above, near, far).astype(F32)
    return jnp.where(below, low, 0.0), jnp.where(above, high, 0.0)


def pack_kernel(inputs, near, far, f_rows, c_rows):
    up_first = lax.axis_index("stream") % 2 == 0
    count, at = inputs.shape[1], 0
    for channels, out, width in ((slice(0, CI), f_rows, 4), (slice(CI, CI + CH), c_rows, 2)):
        rows = [plane(inputs, channels, x) for x in range(count)]
        for x, v in enumerate(rows):
            out[x] = v.astype(BF16)
        for low, high in zip(rows[:width], rows[count - width:]):
            part = slice(at, at + low.shape[0])
            near[part] = jnp.where(up_first, high, low).astype(BF16)
            far[part] = jnp.where(up_first, low, high).astype(BF16)
            at += low.shape[0]


def x_planes(count, fields, cot, xnear, xfar, size):
    index = lax.axis_index("stream")
    inner = [fields[x].astype(F32) for x in range(count)]
    rims = [sides(index, size, xnear[n * 64:(n + 1) * 64], xfar[n * 64:(n + 1) * 64]) for n in range(4)]
    f = [low for low, _ in rims] + inner + [high for _, high in rims]
    inner = [cot[x].astype(F32) for x in range(count)]
    rims = [sides(index, size, xnear[256 + n * 128:384 + n * 128], xfar[256 + n * 128:384 + n * 128]) for n in range(2)]
    return f, [low for low, _ in rims] + inner + [high for _, high in rims]


def pick_strips(work, near, far):
    up_first = lax.axis_index("radial") % 2 == 0
    at = 0
    for pick, rows in work:
        half = pick.shape[0] // 2
        for v in rows:
            got = jnp.dot(pick, v.astype(BF16), preferred_element_type=F32)
            near[at:at + half] = jnp.where(up_first, got[half:], got[:half]).astype(BF16)
            far[at:at + half] = jnp.where(up_first, got[:half], got[half:]).astype(BF16)
            at += half


def join_kernel(counts, xfar, xnear, fields, cot, near, far):
    f, c = x_planes(fields.shape[0], fields, cot, xnear, xfar, counts[0])
    pick_strips([(pick_rows(CI, 0, 6), f[2:-2]), (pick_rows(CH, 0, 6), c)], near, far)


def join_outer_kernel(counts, xfar, xnear, fields, cot, near, far):
    f, _ = x_planes(fields.shape[0], fields, cot, xnear, xfar, counts[0])
    ends = f[:2] + f[-2:]
    pick_strips([(pick_rows(CI, 0, 6), ends), (pick_rows(CI, 2, 4), ends + f[2:-2])], near, far)


def spread(w, by_row, flip):
    taps = jnp.transpose(w[...].astype(F32))
    width = taps.shape[1]
    row = lax.broadcasted_iota(jnp.int32, (CH, width), 0)
    lane = lax.broadcasted_iota(jnp.int32, (CH, width), 1)
    mine = row == (lane // (width // CH) if by_row else lane % CH)
    found = []
    for c in range(3):
        rows = []
        for ab in range(9):
            t = 26 - (ab * 3 + c) if flip else ab * 3 + c
            rows.append(jnp.where(mine, jnp.broadcast_to(taps[t:t + 1], (CH, width)), 0.0))
        found.append(jnp.concatenate(rows, axis=0).astype(BF16))
    return found


def dots(pairs):
    total = None
    for v, w in pairs:
        part = jnp.dot(v, w, preferred_element_type=F32)
        total = part if total is None else total + part
    return total.astype(BF16)


def packed(parts, wanted, of, size):
    per = 128 // size
    places = [place(parts[0].shape[1], wanted, of, size, slot) for slot in range(min(per, 3))]
    tiles = [range(first, min(first + per, 3)) for first in range(0, 3, per)]
    return jnp.concatenate([dots([(parts[c], places[c % per]) for c in tile]) for tile in tiles], axis=1)


def band(wide, expand, ys, rows_y, t):
    rows, width = t.shape[0], wide.shape[1]
    for a in range(3):
        total = jnp.zeros((rows, width), F32)
        for b in range(3):
            part = jnp.dot(expand[:rows], wide[(a * 3 + b) * CH:(a * 3 + b + 1) * CH], preferred_element_type=F32)
            total = jnp.where(ys == rows_y[:rows] + 2 * (b - 1), part, total)
        t[:, a * width:(a + 1) * width] = total.astype(BF16)


def repeat_bias(bias, expand, out):
    column = jnp.sum(expand.astype(F32) * bias[...], axis=1, keepdims=True)
    out[...] = jnp.broadcast_to(column, out.shape)


def band_kernel(w1, w2, first_bias, second_bias, t1o, t1r, t1d, tbo, tbr, t2, b1, b2):
    expand, rows_y = row_table(192, y_first)
    parts = spread(w1, True, False)
    for of, step, t in ((natural, 64, t1o), (rim(CI), 32, t1r), (deep_rim, 64, t1d)):
        wide = packed(parts, lambda n: n % CI, of, step)
        band(wide, expand, lane_y(of, wide.shape[1], step), rows_y, t)
    parts = spread(w2, False, True)
    for of, step, t in ((natural, 128, tbo), (rim(CH), 64, tbr)):
        wide = packed(parts, lambda n: n // CH, of, step)
        band(wide, expand, lane_y(of, wide.shape[1], step), rows_y, t)
    repeat_bias(first_bias, expand, b1)
    expand, rows_y = row_table(128, natural)
    parts = spread(w2, True, False)
    wide = [packed(parts, lambda n: n % CH, of, step) for of, step in ((y_first, 128), (rim(CH), 64))]
    ys = jnp.concatenate([lane_y(y_first, 384, 128), lane_y(rim(CH), 256, 64)], axis=1)
    band(jnp.concatenate(wide, axis=1), expand, ys, rows_y, t2)
    repeat_bias(second_bias, expand, b2)


def shifted(v):
    lane = lax.broadcasted_iota(jnp.int32, v.shape, 1)
    before = jnp.where(lane >= 2, pltpu.roll(v, 2, 1), 0.0)
    after = jnp.where(lane < Z - 2, pltpu.roll(v, Z - 2, 1), 0.0)
    return before.astype(BF16), v.astype(BF16), after.astype(BF16)


def store_wide(ref, p, v):
    at = slice(p * Z, (p + 1) * Z)
    for c, piece in enumerate(shifted(v)):
        ref[c * 128:(c + 1) * 128, at] = piece[:128]
        ref[384 + c * 64:384 + (c + 1) * 64, at] = piece[128:]
    ref[576:, at] = jnp.zeros((64, Z), BF16)


def stacked(ref, lanes):
    return jnp.concatenate([ref[:, a * 256:a * 256 + lanes] for a in range(3)], axis=0)


def own_kernel(counts, xfar, xnear, fields, cot, t1, tb, b1, fs, cs, pre, back):
    count = fields.shape[0]
    f, c = x_planes(count, fields, cot, xnear, xfar, counts[0])
    for ref, rows in ((fs, f), (cs, c)):
        for p, v in enumerate(rows):
            for n, piece in enumerate(shifted(v)):
                ref[n * v.shape[0]:(n + 1) * v.shape[0], p * Z:(p + 1) * Z] = piece
    fs[192:] = jnp.zeros((64, fs.shape[1]), BF16)
    rows = jnp.concatenate([fs[:, a * 256 + 256:a * 256 + 256 + pre.shape[1]] for a in range(3)], axis=0)
    pre[...] = jnp.dot(t1[:128], rows, preferred_element_type=F32) + b1[:128, :1]
    back[...] = jnp.dot(tb[...], stacked(cs, back.shape[1]), preferred_element_type=F32)


def rounded(s):
    lost = s - s.astype(BF16).astype(F32)
    row = lax.broadcasted_iota(jnp.int32, s.shape, 0)
    return (s + jnp.where(row == 28, pltpu.roll(lost, 1, 0), 0.0)).astype(BF16)


def two_dots(v, w):
    high = v.astype(BF16)
    low = (v - high.astype(F32)).astype(BF16)
    return jnp.dot(high, w, preferred_element_type=F32) + jnp.dot(low, w, preferred_element_type=F32)


def gelu_share(pre):
    return 0.5 * (1.0 + lax.erf(pre * 0.7071067811865476))


def rim_kernel(counts, rfar, rnear, fs, cs, pre_own, back_own, t1, tb, e1t, e2t, rep1, rep2, y1, y2,
               hidden_out, payload, fr, cr, taps):
    count = hidden_out.shape[0]
    lanes = count * Z
    radial = lax.axis_index("radial")
    at = 0
    for ref, half in ((fr, 16), (cr, 32)):
        for p in range(count + 4):
            low, high = sides(radial, counts[1], rnear[at:at + half], rfar[at:at + half])
            for n, piece in enumerate(shifted(jnp.concatenate([low, high], axis=0))):
                ref[n * 2 * half:(n + 1) * 2 * half, p * Z:(p + 1) * Z] = piece
            at += half
        ref[6 * half:] = jnp.zeros((2 * half, ref.shape[1]), BF16)
    pre = pre_own[...] + jnp.dot(t1[...], stacked(fr, lanes), preferred_element_type=F32)
    share = gelu_share(pre)
    hidden = (pre * share).astype(BF16)
    for x in range(count):
        hidden_out[x] = hidden[:, x * Z:(x + 1) * Z]
    back = back_own[...] + jnp.dot(tb[...], stacked(cr, lanes), preferred_element_type=F32)
    dpre = (back * (share + pre * jnp.exp(-0.5 * pre * pre) * 0.3989422804014327)).astype(BF16)
    over_lanes = (((1,), (1,)), ((), ()))
    ones, twos = [], []
    for a in range(3):
        at = slice((a + 1) * 256, (a + 1) * 256 + lanes)
        rows = jnp.concatenate([fs[:, at], fr[:, a * 256:a * 256 + lanes]], axis=0)
        g1 = lax.dot_general(dpre, rows, over_lanes, preferred_element_type=F32)
        at = slice(a * 256, a * 256 + lanes)
        rows = jnp.concatenate([cs[:, at], cr[:, at]], axis=0)
        g2 = lax.dot_general(hidden, rows, over_lanes, preferred_element_type=F32)
        for b in range(3):
            for g, ys, out in ((g1, y1, ones), (g2, y2, twos)):
                total = jnp.zeros((CH, g.shape[1]), F32)
                for y in range(8):
                    total = jnp.where(ys[...] == float(y + 2 * (b - 1)), g[y * CH:(y + 1) * CH], total)
                out.append(total)
    taps[:, 24:] = jnp.zeros((3, 8, 128), F32)
    for parts, et, rep, at, width in ((ones, e1t, rep1, 0, 128), (twos[::-1], e2t, rep2, 1, 256)):
        sums = two_dots(jnp.concatenate(parts, axis=0), et[...])
        wide = two_dots(sums, rep[...])
        row = lax.broadcasted_iota(jnp.int32, wide.shape, 0) % CH
        lane = lax.broadcasted_iota(jnp.int32, wide.shape, 1) % width
        mine = row == (lane // CI if width == 128 else lane % CH)
        total = jnp.sum(jnp.where(mine, wide, 0.0).reshape(9, CH, 3 * width), axis=1)
        for c in range(3):
            first = c if width == 128 else 2 - c
            for n in range(width // 128):
                taps[at + n, pl.ds(first, 9, stride=3)] = total[:, c * width + n * 128:c * width + (n + 1) * 128]
    bias = jnp.sum(dpre.astype(F32), axis=1, keepdims=True)
    bias = sum(bias[y * CH:(y + 1) * CH] for y in range(8))
    row = lax.broadcasted_iota(jnp.int32, (CH, 128), 0)
    lane = lax.broadcasted_iota(jnp.int32, (CH, 128), 1)
    taps[0, 27:28] = jnp.sum(jnp.where(row == lane, bias, 0.0), axis=0, keepdims=True)
    payload[...] = rounded(jnp.concatenate([taps[n] for n in range(3)], axis=1))


def hidden_rim_kernel(counts, rfar, rnear, rfar_outer, rnear_outer, hidden, fs, t1o, t1d, b1, hidden_out, fr):
    count = hidden.shape[0]
    stream, radial = lax.axis_index("stream"), lax.axis_index("radial")
    for p in range(count + 8):
        end = p if p < 2 else p - count - 4 if p >= count + 6 else None
        if end is None:
            near, outer = (rnear, rfar, (p - 2) * 16), (rnear_outer, rfar_outer, 128 + (p - 2) * 16)
        else:
            near, outer = (rnear_outer, rfar_outer, end * 16), (rnear_outer, rfar_outer, 64 + end * 16)
        parts = [sides(radial, counts[1], n[at:at + 16], f[at:at + 16]) for n, f, at in (near, outer)]
        rows = jnp.concatenate([part[side] for side in range(2) for part in parts], axis=0)
        for n, piece in enumerate(shifted(rows)):
            fr[n * 64:(n + 1) * 64, p * Z:(p + 1) * Z] = piece
    fr[192:] = jnp.zeros((64, fr.shape[1]), BF16)

    def gelu(rows, lanes):
        total = b1[rows, :1]
        for t, ref in ((t1o, fs), (t1d, fr)):
            cells = [jnp.concatenate([ref[:, a * 256 + at:a * 256 + at + size] for at, size in lanes], axis=1) for a in range(3)]
            total = total + jnp.dot(t[rows], jnp.concatenate(cells, axis=0), preferred_element_type=F32)
        return total * gelu_share(total)

    own = gelu(slice(0, 128), ((0, 2 * Z), ((count + 2) * Z, 2 * Z)))
    rims = gelu(slice(128, 192), ((0, (count + 4) * Z),))
    rims = jnp.concatenate([jnp.where(radial > 0, rims[:32], 0.0), jnp.where(radial < counts[1] - 1, rims[32:], 0.0)], axis=0)
    for p in range(count + 4):
        rim_rows = rims[:, p * Z:(p + 1) * Z]
        if 2 <= p < count + 2:
            hidden_out[p, :128] = hidden[p - 2]
            hidden_out[p, 128:] = rim_rows.astype(BF16)
        else:
            at = p if p < 2 else p - count
            inside = stream > 0 if p < 2 else stream < counts[0] - 1
            rows = jnp.concatenate([own[:, at * Z:(at + 1) * Z], rim_rows], axis=0)
            hidden_out[p] = jnp.where(inside, rows, 0.0).astype(BF16)


def closure_kernel(hidden, t2, b2, closure, hs):
    count = closure.shape[2]
    for p in range(count + 4):
        store_wide(hs, p, hidden[p].astype(F32))
    out = (jnp.dot(t2[...], stacked(hs, count * Z), preferred_element_type=F32) + b2[:, :1]).astype(BF16)
    for x in range(count):
        closure[0, :, x] = out[:, x * Z:(x + 1) * Z].reshape(CH, 8, Z)


def summed(parts):
    parts = [part[...].astype(F32) for part in parts]
    while len(parts) > 1:
        parts = [v + w for v, w in zip(parts[::2], parts[1::2])]
    return parts[0]


def add_kernel(*refs):
    refs[-1][...] = rounded(summed(refs[:-1]))


def finish_kernel(norm, *refs):
    *parts, first, second, bias = refs
    scaled = summed(parts) * norm
    flipped = jnp.transpose(scaled)
    first[...] = flipped[:128, :27]
    second[...] = flipped[128:, :27]
    bias[...] = scaled[27:28, :CH] + scaled[28:29, :CH]


def call(kernel, outs, name, scratch=(), flops=10_000_000, **specs):
    return pl.pallas_call(
        kernel,
        out_shape=outs,
        **specs,
        scratch_shapes=list(scratch),
        compiler_params=pltpu.CompilerParams(vmem_limit_bytes=32 * 1024 * 1024),
        cost_estimate=pl.CostEstimate(flops=flops, bytes_accessed=1_000_000, transcendentals=0),
        name=name,
    )


def shape(*dims, dtype=BF16):
    return jax.ShapeDtypeStruct(dims, dtype)


def exchange(near, far, axis, other):
    count, others = lax.axis_size(axis), lax.axis_size(other)
    axes = tuple(name for name in ("stream", "radial", "snap") if name in (axis, other))
    flat = (others, 1) if axes[0] == axis else (1, count)
    pairs = []
    for i in range(count):
        for j in range(others):
            end = i in (0, count - 1)
            to = (i, j ^ 1 if others % 2 == 0 else j) if end else (i - 1 + 2 * (i % 2), j)
            pairs.append((i * flat[0] + j * flat[1], to[0] * flat[0] + to[1] * flat[1]))
    far = lax.ppermute(far, axes, pairs)
    return lax.ppermute(near, axis, [(i, i ^ 1) for i in range(count)]), far


def swap(v, axis, masks):
    count = lax.axis_size(axis)
    return [lax.ppermute(v, axis, [(i, i ^ mask) for i in range(count)]) for mask in masks]


def add(v, arrived):
    return call(add_kernel, shape(*v.shape), "add_parts")(v, *arrived)


def rounds(axis, most):
    found, step = [], 1
    while step < lax.axis_size(axis):
        masks = [step * n for n in range(1, most if step * most <= lax.axis_size(axis) else 2)]
        found.append((axis, masks))
        step *= len(masks) + 1
    return found


def local(fields, first_weight, first_bias, second_weight, second_bias, cotangent):
    e1t, y1 = table(CI, 384, ((natural, 0, 64), (rim(CI), 256, 32)))
    e2t, y2 = table(CH, 640, ((natural, 0, 128), (rim(CH), 384, 64)))
    rep1, rep2 = np.zeros((128, 384), np.float32), np.zeros((128, 768), np.float32)
    for c in range(3):
        rep1[c * CI:(c + 1) * CI, c * 128:(c + 1) * 128] = np.tile(np.eye(CI), (1, CH))
        rep2[c * CH:(c + 1) * CH, c * 256:(c + 1) * 256] = np.repeat(np.eye(CH), CH, axis=1)

    def const(*arrays, dtype=BF16):
        return [jnp.asarray(v, dtype) for v in arrays]

    planes = fields.shape[2]
    w1 = first_weight.transpose(1, 2, 0).reshape(CH * CI, 27)
    w2 = second_weight.transpose(1, 2, 0).reshape(CH * CH, 27)
    near, far, f_rows, c_rows = call(
        pack_kernel,
        (shape(512, Z), shape(512, Z), shape(planes, CI * 8, Z), shape(planes, CH * 8, Z)),
        "pack_strips",
        flops=4_000_000_000,
    )(jnp.concatenate([fields[0], cotangent[0]], axis=0))
    xnear, xfar = exchange(near, far, "stream", "radial")
    wide = (planes + 4) * Z
    counts = (lax.axis_size("stream"), lax.axis_size("radial"))
    t1o, t1r, t1d, tbo, tbr, t2, b1, b2 = call(
        band_kernel,
        (shape(192, 768), shape(128, 384), shape(192, 768), shape(128, 1152), shape(128, 768), shape(128, 1920),
         shape(192, 128, dtype=F32), shape(128, 128, dtype=F32)),
        "band_matrices",
        flops=4_000_000_000,
    )(w1, w2, first_bias[None], second_bias[None])
    xfar, xnear, t1o, tbo = lax.optimization_barrier((xfar, xnear, t1o, tbo))
    inner, outer = shape((planes + 4) * 48, Z), shape(128 + (planes + 4) * 16, Z)
    near, far = call(functools.partial(join_kernel, counts), (inner, inner), "join_strips")(xfar, xnear, f_rows, c_rows)
    rnear, rfar = exchange(near, far, "radial", "stream")
    fs, cs, pre, back = call(
        functools.partial(own_kernel, counts),
        (shape(256, wide + 4 * Z), shape(384, wide), shape(128, planes * Z, dtype=F32), shape(128, planes * Z, dtype=F32)),
        "own_rows",
        flops=1_000_000_000,
    )(xfar, xnear, f_rows, c_rows, t1o, tbo, b1)
    f_rows, fs = lax.optimization_barrier((f_rows, fs))
    near_outer, far_outer = call(functools.partial(join_outer_kernel, counts), (outer, outer), "join_outer")(
        xfar, xnear, f_rows, c_rows)
    rnear_outer, rfar_outer = exchange(near_outer, far_outer, "radial", "stream")
    hidden, payload = call(
        functools.partial(rim_kernel, counts),
        (shape(planes, 128, Z), shape(32, 384)),
        "gradients",
        (pltpu.VMEM((128, wide), BF16), pltpu.VMEM((256, wide), BF16), pltpu.VMEM((3, 32, 128), F32)),
        flops=2_000_000_000,
    )(rfar, rnear, fs, cs, pre, back, t1r, tbr, *const(e1t, e2t, rep1, rep2), *const(y1, y2, dtype=F32))

    steps = rounds("radial", 4) + rounds("stream", 4) + rounds("snap", 2)
    arrived = swap(payload, *steps[0])
    hidden = call(
        functools.partial(hidden_rim_kernel, counts),
        shape(planes + 4, 192, Z),
        "hidden_rim",
        (pltpu.VMEM((256, wide + 4 * Z), BF16),),
        flops=1_000_000_000,
    )(rfar, rnear, rfar_outer, rnear_outer, hidden, fs, t1o, t1d, b1)
    payload, hidden = lax.optimization_barrier((add(payload, arrived), hidden))
    arrived = swap(payload, *steps[1])
    payload = add(payload, arrived)
    arrived = swap(payload, *steps[2])
    closure = call(
        closure_kernel, shape(*cotangent.shape), "closure", (pltpu.VMEM((640, wide), BF16),), flops=1_000_000_000
    )(hidden, t2, b2)
    for step in steps[3:]:
        payload = add(payload, arrived)
        arrived = swap(payload, *step)

    cells = fields.shape[0] * fields.shape[2] * fields.shape[3] * fields.shape[4]
    for axis in ("stream", "radial", "snap"):
        cells *= lax.axis_size(axis)
    norm = float(1.0 / np.sqrt(np.float32(cells)))
    first, second, bias = call(
        functools.partial(finish_kernel, norm),
        (shape(CH * CI, 27, dtype=F32), shape(CH * CH, 27, dtype=F32), shape(1, CH, dtype=F32)),
        "finish",
    )(payload, *arrived)
    first = first.reshape(CH, CI, 27).transpose(2, 0, 1)
    second = second.reshape(CH, CH, 27).transpose(2, 0, 1)
    return (closure, first, second, bias[0])


def solution(mesh):
    split = P("snap", None, "stream", "radial", None)
    return jax.shard_map(
        local,
        mesh=mesh,
        in_specs=(split, P(), P(), P(), P(), split),
        out_specs=(split, P(), P(), P()),
        check_vma=False,
    )
```

```python
import functools

import numpy as np
import jax
import jax.numpy as jnp
from jax import lax
from jax.experimental import pallas as pl
from jax.experimental.pallas import tpu as pltpu
from jax.sharding import PartitionSpec as P

F32 = jnp.float32
BF16 = jnp.bfloat16
Z = 128
CI = 8
CH = 16
FAR = 100


def natural(n):
    return n // 8, n % 8


def y_first(n):
    return n % CH, n // CH


def rim(channels):
    def of(n):
        side, n = n // (2 * channels), n % (2 * channels)
        return n // 2, n % 2 + 10 * side - 2
    return of


def deep_rim(n):
    part, n = n // 16, n % 16
    return n // 2, n % 2 + 10 * (part // 2) - 2 + (part % 2) * (4 * (part // 2) - 2)


def table(channels, total, places):
    e = np.zeros((total, 128), np.float32)
    ys = np.full((1, total), FAR, np.float32)
    for c in range(3):
        for of, start, step in places:
            ch, y = of(np.arange(step))
            at = start + c * step + np.arange(step)
            e[at, c * channels + ch] = 1
            ys[0, at] = y
    return e, ys


def iota(rows, columns):
    return [lax.broadcasted_iota(jnp.int32, (rows, columns), d) for d in range(2)]


def one_hot(where):
    return jnp.where(where, 1.0, 0.0).astype(BF16)


def lane_y(of, width, step):
    lane = lax.broadcasted_iota(jnp.int32, (1, width), 1)
    return jnp.where(lane < 3 * step, of(lane % step)[1], FAR)


def place(rows, wanted, of, size, slot):
    row, lane = iota(rows, 128)
    return one_hot((of(lane % size)[0] == wanted(row)) & (lane // size == slot))


def row_table(rows, own):
    row, lane = iota(rows, CH)
    own_c, own_y = own(row)
    rim_c, rim_y = rim(CH)(row - 128)
    channel, y = jnp.where(row < 128, own_c, rim_c), jnp.where(row < 128, own_y, rim_y)
    return one_hot(channel == lane), y[:, :1]


def plane(ref, channels, x):
    v = ref[channels, x].astype(F32)
    return v.reshape(v.shape[0] * v.shape[1], v.shape[2])


def pick_rows(channels, low, high):
    half = channels * 2
    row, col = iota(2 * half, channels * 8)
    side = row // half
    return one_hot(col == (row % half // 2) * 8 + low + (high - low) * side + row % 2)


def partners(index, count):
    return index % 2 == 0, index > 0, index < count - 1


def sides(index, count, near, far):
    near_above, below, above = partners(index, count)
    low = jnp.where(near_above, far, near).astype(F32)
    high = jnp.where(near_above, near, far).astype(F32)
    return jnp.where(below, low, 0.0), jnp.where(above, high, 0.0)


def pack_kernel(inputs, near, far, f_rows, c_rows):
    up_first = lax.axis_index("stream") % 2 == 0
    count, at = inputs.shape[1], 0
    for channels, out, width in ((slice(0, CI), f_rows, 4), (slice(CI, CI + CH), c_rows, 2)):
        rows = [plane(inputs, channels, x) for x in range(count)]
        for x, v in enumerate(rows):
            out[x] = v.astype(BF16)
        for low, high in zip(rows[:width], rows[count - width:]):
            part = slice(at, at + low.shape[0])
            near[part] = jnp.where(up_first, high, low).astype(BF16)
            far[part] = jnp.where(up_first, low, high).astype(BF16)
            at += low.shape[0]


def x_planes(count, fields, cot, xnear, xfar, size):
    index = lax.axis_index("stream")
    inner = [fields[x].astype(F32) for x in range(count)]
    rims = [sides(index, size, xnear[n * 64:(n + 1) * 64], xfar[n * 64:(n + 1) * 64]) for n in range(4)]
    f = [low for low, _ in rims] + inner + [high for _, high in rims]
    inner = [cot[x].astype(F32) for x in range(count)]
    rims = [sides(index, size, xnear[256 + n * 128:384 + n * 128], xfar[256 + n * 128:384 + n * 128]) for n in range(2)]
    return f, [low for low, _ in rims] + inner + [high for _, high in rims]


def pick_strips(work, near, far):
    up_first = lax.axis_index("radial") % 2 == 0
    at = 0
    for pick, rows in work:
        half = pick.shape[0] // 2
        for v in rows:
            got = jnp.dot(pick, v.astype(BF16), preferred_element_type=F32)
            near[at:at + half] = jnp.where(up_first, got[half:], got[:half]).astype(BF16)
            far[at:at + half] = jnp.where(up_first, got[:half], got[half:]).astype(BF16)
            at += half


def join_kernel(counts, xfar, xnear, fields, cot, near, far):
    f, c = x_planes(fields.shape[0], fields, cot, xnear, xfar, counts[0])
    pick_strips([(pick_rows(CI, 0, 6), f[2:-2]), (pick_rows(CH, 0, 6), c)], near, far)


def join_outer_kernel(counts, xfar, xnear, fields, cot, near, far):
    f, _ = x_planes(fields.shape[0], fields, cot, xnear, xfar, counts[0])
    ends = f[:2] + f[-2:]
    pick_strips([(pick_rows(CI, 0, 6), ends), (pick_rows(CI, 2, 4), ends + f[2:-2])], near, far)


def spread(w, by_row, flip):
    taps = jnp.transpose(w[...].astype(F32))
    width = taps.shape[1]
    row = lax.broadcasted_iota(jnp.int32, (CH, width), 0)
    lane = lax.broadcasted_iota(jnp.int32, (CH, width), 1)
    mine = row == (lane // (width // CH) if by_row else lane % CH)
    found = []
    for c in range(3):
        rows = []
        for ab in range(9):
            t = 26 - (ab * 3 + c) if flip else ab * 3 + c
            rows.append(jnp.where(mine, jnp.broadcast_to(taps[t:t + 1], (CH, width)), 0.0))
        found.append(jnp.concatenate(rows, axis=0).astype(BF16))
    return found


def dots(pairs):
    total = None
    for v, w in pairs:
        part = jnp.dot(v, w, preferred_element_type=F32)
        total = part if total is None else total + part
    return total.astype(BF16)


def packed(parts, wanted, of, size):
    per = 128 // size
    places = [place(parts[0].shape[1], wanted, of, size, slot) for slot in range(min(per, 3))]
    tiles = [range(first, min(first + per, 3)) for first in range(0, 3, per)]
    return jnp.concatenate([dots([(parts[c], places[c % per]) for c in tile]) for tile in tiles], axis=1)


def band(wide, expand, ys, rows_y, t):
    rows, width = t.shape[0], wide.shape[1]
    for a in range(3):
        total = jnp.zeros((rows, width), F32)
        for b in range(3):
            part = jnp.dot(expand[:rows], wide[(a * 3 + b) * CH:(a * 3 + b + 1) * CH], preferred_element_type=F32)
            total = jnp.where(ys == rows_y[:rows] + 2 * (b - 1), part, total)
        t[:, a * width:(a + 1) * width] = total.astype(BF16)


def repeat_bias(bias, expand, out):
    column = jnp.sum(expand.astype(F32) * bias[...], axis=1, keepdims=True)
    out[...] = jnp.broadcast_to(column, out.shape)


def band_kernel(w1, w2, first_bias, second_bias, t1o, t1r, t1d, tbo, tbr, t2, b1, b2):
    expand, rows_y = row_table(192, y_first)
    parts = spread(w1, True, False)
    for of, step, t in ((natural, 64, t1o), (rim(CI), 32, t1r), (deep_rim, 64, t1d)):
        wide = packed(parts, lambda n: n % CI, of, step)
        band(wide, expand, lane_y(of, wide.shape[1], step), rows_y, t)
    parts = spread(w2, False, True)
    for of, step, t in ((natural, 128, tbo), (rim(CH), 64, tbr)):
        wide = packed(parts, lambda n: n // CH, of, step)
        band(wide, expand, lane_y(of, wide.shape[1], step), rows_y, t)
    repeat_bias(first_bias, expand, b1)
    expand, rows_y = row_table(128, natural)
    parts = spread(w2, True, False)
    wide = [packed(parts, lambda n: n % CH, of, step) for of, step in ((y_first, 128), (rim(CH), 64))]
    ys = jnp.concatenate([lane_y(y_first, 384, 128), lane_y(rim(CH), 256, 64)], axis=1)
    band(jnp.concatenate(wide, axis=1), expand, ys, rows_y, t2)
    repeat_bias(second_bias, expand, b2)


def shifted(v):
    lane = lax.broadcasted_iota(jnp.int32, v.shape, 1)
    before = jnp.where(lane >= 2, pltpu.roll(v, 2, 1), 0.0)
    after = jnp.where(lane < Z - 2, pltpu.roll(v, Z - 2, 1), 0.0)
    return before.astype(BF16), v.astype(BF16), after.astype(BF16)


def store_wide(ref, p, v):
    at = slice(p * Z, (p + 1) * Z)
    for c, piece in enumerate(shifted(v)):
        ref[c * 128:(c + 1) * 128, at] = piece[:128]
        ref[384 + c * 64:384 + (c + 1) * 64, at] = piece[128:]
    ref[576:, at] = jnp.zeros((64, Z), BF16)


def stacked(ref, lanes):
    return jnp.concatenate([ref[:, a * 256:a * 256 + lanes] for a in range(3)], axis=0)


def gelu_share(pre):
    return 0.5 * (1.0 + lax.erf(pre * 0.7071067811865476))


def gelu_slope(pre, share):
    return share + pre * jnp.exp(-0.5 * pre * pre) * 0.3989422804014327


def edges(v):
    return jnp.concatenate([v[:32], v[96:128]], axis=0)


def whole(edge, middle):
    return jnp.concatenate([edge[:32], middle, edge[32:]], axis=0)


def own_kernel(counts, xfar, xnear, fields, cot, t1, tb, b1, fs, cs, pre, back, hidden, dpre):
    count, lanes = fields.shape[0], pre.shape[1]
    f, c = x_planes(count, fields, cot, xnear, xfar, counts[0])
    for ref, rows in ((fs, f), (cs, c)):
        for p, v in enumerate(rows):
            for n, piece in enumerate(shifted(v)):
                ref[n * v.shape[0]:(n + 1) * v.shape[0], p * Z:(p + 1) * Z] = piece
    fs[192:] = jnp.zeros((64, fs.shape[1]), BF16)
    rows = jnp.concatenate([fs[:, a * 256 + 256:a * 256 + 256 + lanes] for a in range(3)], axis=0)
    first = jnp.dot(t1[:128], rows, preferred_element_type=F32) + b1[:128, :1]
    second = jnp.dot(tb[...], stacked(cs, lanes), preferred_element_type=F32)
    pre[...] = edges(first)
    back[...] = edges(second)
    first, second = first[32:96], second[32:96]
    share = gelu_share(first)
    hidden[...] = (first * share).astype(BF16)
    dpre[...] = (second * gelu_slope(first, share)).astype(BF16)


def rounded(s):
    lost = s - s.astype(BF16).astype(F32)
    row = lax.broadcasted_iota(jnp.int32, s.shape, 0)
    return (s + jnp.where(row == 28, pltpu.roll(lost, 1, 0), 0.0)).astype(BF16)


def two_dots(v, w):
    high = v.astype(BF16)
    low = (v - high.astype(F32)).astype(BF16)
    return jnp.dot(high, w, preferred_element_type=F32) + jnp.dot(low, w, preferred_element_type=F32)


def rim_kernel(counts, rfar, rnear, fs, cs, pre_own, back_own, hidden_own, dpre_own, t1, tb, e1t, e2t, rep1, rep2, y1, y2,
               hidden_out, payload, fr, cr, taps):
    count = hidden_out.shape[0]
    lanes = count * Z
    radial = lax.axis_index("radial")
    at = 0
    for ref, half in ((fr, 16), (cr, 32)):
        for p in range(count + 4):
            low, high = sides(radial, counts[1], rnear[at:at + half], rfar[at:at + half])
            for n, piece in enumerate(shifted(jnp.concatenate([low, high], axis=0))):
                ref[n * 2 * half:(n + 1) * 2 * half, p * Z:(p + 1) * Z] = piece
            at += half
        ref[6 * half:] = jnp.zeros((2 * half, ref.shape[1]), BF16)
    pre = pre_own[...] + jnp.dot(edges(t1), stacked(fr, lanes), preferred_element_type=F32)
    share = gelu_share(pre)
    hidden = whole((pre * share).astype(BF16), hidden_own[...])
    for x in range(count):
        hidden_out[x] = hidden[:, x * Z:(x + 1) * Z]
    back = back_own[...] + jnp.dot(edges(tb), stacked(cr, lanes), preferred_element_type=F32)
    dpre = whole((back * gelu_slope(pre, share)).astype(BF16), dpre_own[...])
    over_lanes = (((1,), (1,)), ((), ()))
    ones, twos = [], []
    for a in range(3):
        at = slice((a + 1) * 256, (a + 1) * 256 + lanes)
        rows = jnp.concatenate([fs[:, at], fr[:, a * 256:a * 256 + lanes]], axis=0)
        g1 = lax.dot_general(dpre, rows, over_lanes, preferred_element_type=F32)
        at = slice(a * 256, a * 256 + lanes)
        rows = jnp.concatenate([cs[:, at], cr[:, at]], axis=0)
        g2 = lax.dot_general(hidden, rows, over_lanes, preferred_element_type=F32)
        for b in range(3):
            for g, ys, out in ((g1, y1, ones), (g2, y2, twos)):
                total = jnp.zeros((CH, g.shape[1]), F32)
                for y in range(8):
                    total = jnp.where(ys[...] == float(y + 2 * (b - 1)), g[y * CH:(y + 1) * CH], total)
                out.append(total)
    taps[:, 24:] = jnp.zeros((3, 8, 128), F32)
    for parts, et, rep, at, width in ((ones, e1t, rep1, 0, 128), (twos[::-1], e2t, rep2, 1, 256)):
        sums = two_dots(jnp.concatenate(parts, axis=0), et[...])
        wide = two_dots(sums, rep[...])
        row = lax.broadcasted_iota(jnp.int32, wide.shape, 0) % CH
        lane = lax.broadcasted_iota(jnp.int32, wide.shape, 1) % width
        mine = row == (lane // CI if width == 128 else lane % CH)
        total = jnp.sum(jnp.where(mine, wide, 0.0).reshape(9, CH, 3 * width), axis=1)
        for c in range(3):
            first = c if width == 128 else 2 - c
            for n in range(width // 128):
                taps[at + n, pl.ds(first, 9, stride=3)] = total[:, c * width + n * 128:c * width + (n + 1) * 128]
    bias = jnp.sum(dpre.astype(F32), axis=1, keepdims=True)
    bias = sum(bias[y * CH:(y + 1) * CH] for y in range(8))
    row = lax.broadcasted_iota(jnp.int32, (CH, 128), 0)
    lane = lax.broadcasted_iota(jnp.int32, (CH, 128), 1)
    taps[0, 27:28] = jnp.sum(jnp.where(row == lane, bias, 0.0), axis=0, keepdims=True)
    payload[...] = rounded(jnp.concatenate([taps[n] for n in range(3)], axis=1))


def hidden_rim_kernel(counts, rfar, rnear, rfar_outer, rnear_outer, hidden, fs, t1o, t1d, b1, hidden_out, fr):
    count = hidden.shape[0]
    stream, radial = lax.axis_index("stream"), lax.axis_index("radial")
    for p in range(count + 8):
        end = p if p < 2 else p - count - 4 if p >= count + 6 else None
        if end is None:
            near, outer = (rnear, rfar, (p - 2) * 16), (rnear_outer, rfar_outer, 128 + (p - 2) * 16)
        else:
            near, outer = (rnear_outer, rfar_outer, end * 16), (rnear_outer, rfar_outer, 64 + end * 16)
        parts = [sides(radial, counts[1], n[at:at + 16], f[at:at + 16]) for n, f, at in (near, outer)]
        rows = jnp.concatenate([part[side] for side in range(2) for part in parts], axis=0)
        for n, piece in enumerate(shifted(rows)):
            fr[n * 64:(n + 1) * 64, p * Z:(p + 1) * Z] = piece
    fr[192:] = jnp.zeros((64, fr.shape[1]), BF16)

    def gelu(rows, lanes):
        total = b1[rows, :1]
        for t, ref in ((t1o, fs), (t1d, fr)):
            cells = [jnp.concatenate([ref[:, a * 256 + at:a * 256 + at + size] for at, size in lanes], axis=1) for a in range(3)]
            total = total + jnp.dot(t[rows], jnp.concatenate(cells, axis=0), preferred_element_type=F32)
        return total * gelu_share(total)

    own = gelu(slice(0, 128), ((0, 2 * Z), ((count + 2) * Z, 2 * Z)))
    rims = gelu(slice(128, 192), ((0, (count + 4) * Z),))
    rims = jnp.concatenate([jnp.where(radial > 0, rims[:32], 0.0), jnp.where(radial < counts[1] - 1, rims[32:], 0.0)], axis=0)
    for p in range(count + 4):
        rim_rows = rims[:, p * Z:(p + 1) * Z]
        if 2 <= p < count + 2:
            hidden_out[p, :128] = hidden[p - 2]
            hidden_out[p, 128:] = rim_rows.astype(BF16)
        else:
            at = p if p < 2 else p - count
            inside = stream > 0 if p < 2 else stream < counts[0] - 1
            rows = jnp.concatenate([own[:, at * Z:(at + 1) * Z], rim_rows], axis=0)
            hidden_out[p] = jnp.where(inside, rows, 0.0).astype(BF16)


def closure_kernel(hidden, t2, b2, closure, hs):
    count = closure.shape[2]
    for p in range(count + 4):
        store_wide(hs, p, hidden[p].astype(F32))
    out = (jnp.dot(t2[...], stacked(hs, count * Z), preferred_element_type=F32) + b2[:, :1]).astype(BF16)
    for x in range(count):
        closure[0, :, x] = out[:, x * Z:(x + 1) * Z].reshape(CH, 8, Z)


def summed(parts):
    parts = [part[...].astype(F32) for part in parts]
    while len(parts) > 1:
        parts = [v + w for v, w in zip(parts[::2], parts[1::2])]
    return parts[0]


def add_kernel(*refs):
    refs[-1][...] = rounded(summed(refs[:-1]))


def finish_kernel(norm, *refs):
    *parts, first, second, bias = refs
    scaled = summed(parts) * norm
    flipped = jnp.transpose(scaled)
    first[...] = flipped[:128, :27]
    second[...] = flipped[128:, :27]
    bias[...] = scaled[27:28, :CH] + scaled[28:29, :CH]


def call(kernel, outs, name, scratch=(), flops=10_000_000, **specs):
    return pl.pallas_call(
        kernel,
        out_shape=outs,
        **specs,
        scratch_shapes=list(scratch),
        compiler_params=pltpu.CompilerParams(vmem_limit_bytes=32 * 1024 * 1024),
        cost_estimate=pl.CostEstimate(flops=flops, bytes_accessed=1_000_000, transcendentals=0),
        name=name,
    )


def shape(*dims, dtype=BF16):
    return jax.ShapeDtypeStruct(dims, dtype)


def exchange(near, far, axis, other):
    count, others = lax.axis_size(axis), lax.axis_size(other)
    axes = tuple(name for name in ("stream", "radial", "snap") if name in (axis, other))
    flat = (others, 1) if axes[0] == axis else (1, count)
    pairs = []
    for i in range(count):
        for j in range(others):
            end = i in (0, count - 1)
            to = (i, j ^ 1 if others % 2 == 0 else j) if end else (i - 1 + 2 * (i % 2), j)
            pairs.append((i * flat[0] + j * flat[1], to[0] * flat[0] + to[1] * flat[1]))
    far = lax.ppermute(far, axes, pairs)
    return lax.ppermute(near, axis, [(i, i ^ 1) for i in range(count)]), far


def swap(v, axis, masks):
    count = lax.axis_size(axis)
    return [lax.ppermute(v, axis, [(i, i ^ mask) for i in range(count)]) for mask in masks]


def add(v, arrived):
    return call(add_kernel, shape(*v.shape), "add_parts")(v, *arrived)


def rounds(axis, most):
    found, step = [], 1
    while step < lax.axis_size(axis):
        masks = [step * n for n in range(1, most if step * most <= lax.axis_size(axis) else 2)]
        found.append((axis, masks))
        step *= len(masks) + 1
    return found


def local(fields, first_weight, first_bias, second_weight, second_bias, cotangent):
    e1t, y1 = table(CI, 384, ((natural, 0, 64), (rim(CI), 256, 32)))
    e2t, y2 = table(CH, 640, ((natural, 0, 128), (rim(CH), 384, 64)))
    rep1, rep2 = np.zeros((128, 384), np.float32), np.zeros((128, 768), np.float32)
    for c in range(3):
        rep1[c * CI:(c + 1) * CI, c * 128:(c + 1) * 128] = np.tile(np.eye(CI), (1, CH))
        rep2[c * CH:(c + 1) * CH, c * 256:(c + 1) * 256] = np.repeat(np.eye(CH), CH, axis=1)

    def const(*arrays, dtype=BF16):
        return [jnp.asarray(v, dtype) for v in arrays]

    planes = fields.shape[2]
    w1 = first_weight.transpose(1, 2, 0).reshape(CH * CI, 27)
    w2 = second_weight.transpose(1, 2, 0).reshape(CH * CH, 27)
    near, far, f_rows, c_rows = call(
        pack_kernel,
        (shape(512, Z), shape(512, Z), shape(planes, CI * 8, Z), shape(planes, CH * 8, Z)),
        "pack_strips",
        flops=4_000_000_000,
    )(jnp.concatenate([fields[0], cotangent[0]], axis=0))
    xnear, xfar = exchange(near, far, "stream", "radial")
    wide = (planes + 4) * Z
    counts = (lax.axis_size("stream"), lax.axis_size("radial"))
    t1o, t1r, t1d, tbo, tbr, t2, b1, b2 = call(
        band_kernel,
        (shape(192, 768), shape(128, 384), shape(192, 768), shape(128, 1152), shape(128, 768), shape(128, 1920),
         shape(192, 128, dtype=F32), shape(128, 128, dtype=F32)),
        "band_matrices",
        flops=4_000_000_000,
    )(w1, w2, first_bias[None], second_bias[None])
    xfar, xnear, t1o, tbo = lax.optimization_barrier((xfar, xnear, t1o, tbo))
    inner, outer = shape((planes + 4) * 48, Z), shape(128 + (planes + 4) * 16, Z)
    near, far = call(functools.partial(join_kernel, counts), (inner, inner), "join_strips")(xfar, xnear, f_rows, c_rows)
    rnear, rfar = exchange(near, far, "radial", "stream")
    half, half_f32 = shape(64, planes * Z), shape(64, planes * Z, dtype=F32)
    fs, cs, pre, back, hidden, dpre = call(
        functools.partial(own_kernel, counts),
        (shape(256, wide + 4 * Z), shape(384, wide), half_f32, half_f32, half, half),
        "own_rows",
        flops=1_000_000_000,
    )(xfar, xnear, f_rows, c_rows, t1o, tbo, b1)
    f_rows, fs = lax.optimization_barrier((f_rows, fs))
    near_outer, far_outer = call(functools.partial(join_outer_kernel, counts), (outer, outer), "join_outer")(
        xfar, xnear, f_rows, c_rows)
    rnear_outer, rfar_outer = exchange(near_outer, far_outer, "radial", "stream")
    hidden, payload = call(
        functools.partial(rim_kernel, counts),
        (shape(planes, 128, Z), shape(32, 384)),
        "gradients",
        (pltpu.VMEM((128, wide), BF16), pltpu.VMEM((256, wide), BF16), pltpu.VMEM((3, 32, 128), F32)),
        flops=2_000_000_000,
    )(rfar, rnear, fs, cs, pre, back, hidden, dpre, t1r, tbr, *const(e1t, e2t, rep1, rep2), *const(y1, y2, dtype=F32))

    steps = rounds("radial", 4) + rounds("stream", 4) + rounds("snap", 2)
    arrived = swap(payload, *steps[0])
    hidden = call(
        functools.partial(hidden_rim_kernel, counts),
        shape(planes + 4, 192, Z),
        "hidden_rim",
        (pltpu.VMEM((256, wide + 4 * Z), BF16),),
        flops=1_000_000_000,
    )(rfar, rnear, rfar_outer, rnear_outer, hidden, fs, t1o, t1d, b1)
    payload, hidden = lax.optimization_barrier((add(payload, arrived), hidden))
    arrived = swap(payload, *steps[1])
    payload = add(payload, arrived)
    arrived = swap(payload, *steps[2])
    closure = call(
        closure_kernel, shape(*cotangent.shape), "closure", (pltpu.VMEM((640, wide), BF16),), flops=1_000_000_000
    )(hidden, t2, b2)
    for step in steps[3:]:
        payload = add(payload, arrived)
        arrived = swap(payload, *step)

    cells = fields.shape[0] * fields.shape[2] * fields.shape[3] * fields.shape[4]
    for axis in ("stream", "radial", "snap"):
        cells *= lax.axis_size(axis)
    norm = float(1.0 / np.sqrt(np.float32(cells)))
    first, second, bias = call(
        functools.partial(finish_kernel, norm),
        (shape(CH * CI, 27, dtype=F32), shape(CH * CH, 27, dtype=F32), shape(1, CH, dtype=F32)),
        "finish",
    )(payload, *arrived)
    first = first.reshape(CH, CI, 27).transpose(2, 0, 1)
    second = second.reshape(CH, CH, 27).transpose(2, 0, 1)
    return (closure, first, second, bias[0])


def solution(mesh):
    split = P("snap", None, "stream", "radial", None)
    return jax.shard_map(
        local,
        mesh=mesh,
        in_specs=(split, P(), P(), P(), P(), split),
        out_specs=(split, P(), P(), P()),
        check_vma=False,
    )
```

```python
import functools

import numpy as np
import jax
import jax.numpy as jnp
from jax import lax
from jax.experimental import pallas as pl
from jax.experimental.pallas import tpu as pltpu
from jax.sharding import PartitionSpec as P

F32 = jnp.float32
BF16 = jnp.bfloat16
Z = 128
CI = 8
CH = 16
FAR = 100


def natural(n):
    return n // 8, n % 8


def y_first(n):
    return n % CH, n // CH


def rim(channels):
    def of(n):
        side, n = n // (2 * channels), n % (2 * channels)
        return n // 2, n % 2 + 10 * side - 2
    return of


def deep_rim(n):
    part, n = n // 16, n % 16
    return n // 2, n % 2 + 10 * (part // 2) - 2 + (part % 2) * (4 * (part // 2) - 2)


def table(channels, total, places):
    e = np.zeros((total, 128), np.float32)
    ys = np.full((1, total), FAR, np.float32)
    for c in range(3):
        for of, start, step in places:
            ch, y = of(np.arange(step))
            at = start + c * step + np.arange(step)
            e[at, c * channels + ch] = 1
            ys[0, at] = y
    return e, ys


def iota(rows, columns):
    return [lax.broadcasted_iota(jnp.int32, (rows, columns), d) for d in range(2)]


def one_hot(where):
    return jnp.where(where, 1.0, 0.0).astype(BF16)


def lane_y(of, width, step):
    lane = lax.broadcasted_iota(jnp.int32, (1, width), 1)
    return jnp.where(lane < 3 * step, of(lane % step)[1], FAR)


def place(rows, wanted, of, size, slot):
    row, lane = iota(rows, 128)
    return one_hot((of(lane % size)[0] == wanted(row)) & (lane // size == slot))


def row_table(rows, own):
    row, lane = iota(rows, CH)
    own_c, own_y = own(row)
    rim_c, rim_y = rim(CH)(row - 128)
    channel, y = jnp.where(row < 128, own_c, rim_c), jnp.where(row < 128, own_y, rim_y)
    return one_hot(channel == lane), y[:, :1]


def plane(ref, channels, x):
    v = ref[channels, x].astype(F32)
    return v.reshape(v.shape[0] * v.shape[1], v.shape[2])


def pick_rows(channels, low, high):
    half = channels * 2
    row, col = iota(2 * half, channels * 8)
    side = row // half
    return one_hot(col == (row % half // 2) * 8 + low + (high - low) * side + row % 2)


def partners(index, count):
    return index % 2 == 0, index > 0, index < count - 1


def sides(index, count, near, far):
    near_above, below, above = partners(index, count)
    low = jnp.where(near_above, far, near).astype(F32)
    high = jnp.where(near_above, near, far).astype(F32)
    return jnp.where(below, low, 0.0), jnp.where(above, high, 0.0)


def pack_kernel(inputs, near, far, f_rows, c_rows):
    up_first = lax.axis_index("stream") % 2 == 0
    count, at = inputs.shape[1], 0
    for channels, out, width in ((slice(0, CI), f_rows, 4), (slice(CI, CI + CH), c_rows, 2)):
        rows = [plane(inputs, channels, x) for x in range(count)]
        for x, v in enumerate(rows):
            out[x] = v.astype(BF16)
        for low, high in zip(rows[:width], rows[count - width:]):
            part = slice(at, at + low.shape[0])
            near[part] = jnp.where(up_first, high, low).astype(BF16)
            far[part] = jnp.where(up_first, low, high).astype(BF16)
            at += low.shape[0]


def x_planes(count, fields, cot, xnear, xfar, size):
    index = lax.axis_index("stream")
    inner = [fields[x].astype(F32) for x in range(count)]
    rims = [sides(index, size, xnear[n * 64:(n + 1) * 64], xfar[n * 64:(n + 1) * 64]) for n in range(4)]
    f = [low for low, _ in rims] + inner + [high for _, high in rims]
    inner = [cot[x].astype(F32) for x in range(count)]
    rims = [sides(index, size, xnear[256 + n * 128:384 + n * 128], xfar[256 + n * 128:384 + n * 128]) for n in range(2)]
    return f, [low for low, _ in rims] + inner + [high for _, high in rims]


def pick_strips(work, near, far):
    up_first = lax.axis_index("radial") % 2 == 0
    at = 0
    for pick, rows in work:
        half = pick.shape[0] // 2
        for v in rows:
            got = jnp.dot(pick, v.astype(BF16), preferred_element_type=F32)
            near[at:at + half] = jnp.where(up_first, got[half:], got[:half]).astype(BF16)
            far[at:at + half] = jnp.where(up_first, got[:half], got[half:]).astype(BF16)
            at += half


def join_kernel(counts, xfar, xnear, fields, cot, near, far):
    f, c = x_planes(fields.shape[0], fields, cot, xnear, xfar, counts[0])
    pick_strips([(pick_rows(CI, 0, 6), f[2:-2]), (pick_rows(CH, 0, 6), c)], near, far)


def join_outer_kernel(counts, xfar, xnear, fields, cot, near, far):
    f, _ = x_planes(fields.shape[0], fields, cot, xnear, xfar, counts[0])
    ends = f[:2] + f[-2:]
    pick_strips([(pick_rows(CI, 0, 6), ends), (pick_rows(CI, 2, 4), ends + f[2:-2])], near, far)


def spread(w, by_row, flip):
    taps = jnp.transpose(w[...].astype(F32))
    width = taps.shape[1]
    row = lax.broadcasted_iota(jnp.int32, (CH, width), 0)
    lane = lax.broadcasted_iota(jnp.int32, (CH, width), 1)
    mine = row == (lane // (width // CH) if by_row else lane % CH)
    found = []
    for c in range(3):
        rows = []
        for ab in range(9):
            t = 26 - (ab * 3 + c) if flip else ab * 3 + c
            rows.append(jnp.where(mine, jnp.broadcast_to(taps[t:t + 1], (CH, width)), 0.0))
        found.append(jnp.concatenate(rows, axis=0).astype(BF16))
    return found


def dots(pairs):
    total = None
    for v, w in pairs:
        part = jnp.dot(v, w, preferred_element_type=F32)
        total = part if total is None else total + part
    return total.astype(BF16)


def packed(parts, wanted, of, size):
    per = 128 // size
    places = [place(parts[0].shape[1], wanted, of, size, slot) for slot in range(min(per, 3))]
    tiles = [range(first, min(first + per, 3)) for first in range(0, 3, per)]
    return jnp.concatenate([dots([(parts[c], places[c % per]) for c in tile]) for tile in tiles], axis=1)


def band(wide, expand, ys, rows_y, t):
    rows, width = t.shape[0], wide.shape[1]
    for a in range(3):
        total = jnp.zeros((rows, width), F32)
        for b in range(3):
            part = jnp.dot(expand[:rows], wide[(a * 3 + b) * CH:(a * 3 + b + 1) * CH], preferred_element_type=F32)
            total = jnp.where(ys == rows_y[:rows] + 2 * (b - 1), part, total)
        t[:, a * width:(a + 1) * width] = total.astype(BF16)


def repeat_bias(bias, expand, out):
    column = jnp.sum(expand.astype(F32) * bias[...], axis=1, keepdims=True)
    out[...] = jnp.broadcast_to(column, out.shape)


def band_kernel(w1, w2, first_bias, second_bias, t1o, t1r, t1d, tbo, tbr, t2, b1, b2):
    expand, rows_y = row_table(192, y_first)
    parts = spread(w1, True, False)
    for of, step, t in ((natural, 64, t1o), (rim(CI), 32, t1r), (deep_rim, 64, t1d)):
        wide = packed(parts, lambda n: n % CI, of, step)
        band(wide, expand, lane_y(of, wide.shape[1], step), rows_y, t)
    parts = spread(w2, False, True)
    for of, step, t in ((natural, 128, tbo), (rim(CH), 64, tbr)):
        wide = packed(parts, lambda n: n // CH, of, step)
        band(wide, expand, lane_y(of, wide.shape[1], step), rows_y, t)
    repeat_bias(first_bias, expand, b1)
    expand, rows_y = row_table(128, natural)
    parts = spread(w2, True, False)
    wide = [packed(parts, lambda n: n % CH, of, step) for of, step in ((y_first, 128), (rim(CH), 64))]
    ys = jnp.concatenate([lane_y(y_first, 384, 128), lane_y(rim(CH), 256, 64)], axis=1)
    band(jnp.concatenate(wide, axis=1), expand, ys, rows_y, t2)
    repeat_bias(second_bias, expand, b2)


def shifted(v):
    lane = lax.broadcasted_iota(jnp.int32, v.shape, 1)
    before = jnp.where(lane >= 2, pltpu.roll(v, 2, 1), 0.0)
    after = jnp.where(lane < Z - 2, pltpu.roll(v, Z - 2, 1), 0.0)
    return before.astype(BF16), v.astype(BF16), after.astype(BF16)


def store_wide(ref, p, v):
    at = slice(p * Z, (p + 1) * Z)
    for c, piece in enumerate(shifted(v)):
        ref[c * 128:(c + 1) * 128, at] = piece[:128]
        ref[384 + c * 64:384 + (c + 1) * 64, at] = piece[128:]
    ref[576:, at] = jnp.zeros((64, Z), BF16)


def stacked(ref, lanes):
    return jnp.concatenate([ref[:, a * 256:a * 256 + lanes] for a in range(3)], axis=0)


def gelu_share(pre):
    return 0.5 * (1.0 + lax.erf(pre * 0.7071067811865476))


def gelu_slope(pre, share):
    return share + pre * jnp.exp(-0.5 * pre * pre) * 0.3989422804014327


def edges(v):
    return jnp.concatenate([v[:32], v[96:128]], axis=0)


def whole(edge, middle):
    return jnp.concatenate([edge[:32], middle, edge[32:]], axis=0)


def own_kernel(counts, xfar, xnear, fields, cot, t1, tb, b1, fs, cs, pre, back, hidden, dpre):
    count, lanes = fields.shape[0], pre.shape[1]
    f, c = x_planes(count, fields, cot, xnear, xfar, counts[0])
    for ref, rows in ((fs, f), (cs, c)):
        for p, v in enumerate(rows):
            for n, piece in enumerate(shifted(v)):
                ref[n * v.shape[0]:(n + 1) * v.shape[0], p * Z:(p + 1) * Z] = piece
    fs[192:] = jnp.zeros((64, fs.shape[1]), BF16)
    rows = jnp.concatenate([fs[:, a * 256 + 256:a * 256 + 256 + lanes] for a in range(3)], axis=0)
    first = jnp.dot(t1[:128], rows, preferred_element_type=F32) + b1[:128, :1]
    second = jnp.dot(tb[...], stacked(cs, lanes), preferred_element_type=F32)
    pre[...] = edges(first)
    back[...] = edges(second)
    first, second = first[32:96], second[32:96]
    share = gelu_share(first)
    hidden[...] = (first * share).astype(BF16)
    dpre[...] = (second * gelu_slope(first, share)).astype(BF16)


def rounded(s):
    lost = s - s.astype(BF16).astype(F32)
    row = lax.broadcasted_iota(jnp.int32, s.shape, 0)
    return (s + jnp.where(row == 28, pltpu.roll(lost, 1, 0), 0.0)).astype(BF16)


def two_dots(v, w):
    high = v.astype(BF16)
    low = (v - high.astype(F32)).astype(BF16)
    return jnp.dot(high, w, preferred_element_type=F32) + jnp.dot(low, w, preferred_element_type=F32)


def rim_kernel(counts, rfar, rnear, fs, cs, pre_own, back_own, hidden_own, dpre_own, t1, tb, e1t, e2t, rep1, rep2, y1, y2,
               hidden_out, payload, fr, cr, taps):
    count = hidden_out.shape[0]
    lanes = count * Z
    radial = lax.axis_index("radial")
    at = 0
    for ref, half in ((fr, 16), (cr, 32)):
        for p in range(count + 4):
            low, high = sides(radial, counts[1], rnear[at:at + half], rfar[at:at + half])
            for n, piece in enumerate(shifted(jnp.concatenate([low, high], axis=0))):
                ref[n * 2 * half:(n + 1) * 2 * half, p * Z:(p + 1) * Z] = piece
            at += half
        ref[6 * half:] = jnp.zeros((2 * half, ref.shape[1]), BF16)
    pre = pre_own[...] + jnp.dot(edges(t1), stacked(fr, lanes), preferred_element_type=F32)
    share = gelu_share(pre)
    hidden = whole((pre * share).astype(BF16), hidden_own[...])
    for x in range(count):
        hidden_out[x] = hidden[:, x * Z:(x + 1) * Z]
    back = back_own[...] + jnp.dot(edges(tb), stacked(cr, lanes), preferred_element_type=F32)
    dpre = whole((back * gelu_slope(pre, share)).astype(BF16), dpre_own[...])
    over_lanes = (((1,), (1,)), ((), ()))
    ones, twos = [], []
    sums = [[None] * 3, [None] * 3]
    for pair in range(count // 2 + 2):
        taps_here = [a for a in range(3) if 0 <= pair - a < count // 2]
        at = slice(pair * 256, (pair + 1) * 256)
        shifted_rows = (
            jnp.concatenate([fs[:, (pair + 1) * 256:(pair + 2) * 256], fr[:, at]], axis=0),
            jnp.concatenate([cs[:, at], cr[:, at]], axis=0),
        )
        for here, rows, total in zip((dpre, hidden), shifted_rows, sums):
            here = jnp.concatenate([here[:, (pair - a) * 256:(pair - a + 1) * 256] for a in taps_here], axis=0)
            got = lax.dot_general(here, rows, over_lanes, preferred_element_type=F32)
            for n, a in enumerate(taps_here):
                part = got[n * 128:(n + 1) * 128]
                total[a] = part if total[a] is None else total[a] + part
    for a in range(3):
        g1, g2 = sums[0][a], sums[1][a]
        for b in range(3):
            for g, ys, out in ((g1, y1, ones), (g2, y2, twos)):
                total = jnp.zeros((CH, g.shape[1]), F32)
                for y in range(8):
                    total = jnp.where(ys[...] == float(y + 2 * (b - 1)), g[y * CH:(y + 1) * CH], total)
                out.append(total)
    taps[:, 24:] = jnp.zeros((3, 8, 128), F32)
    for parts, et, rep, at, width in ((ones, e1t, rep1, 0, 128), (twos[::-1], e2t, rep2, 1, 256)):
        sums = two_dots(jnp.concatenate(parts, axis=0), et[...])
        wide = two_dots(sums, rep[...])
        row = lax.broadcasted_iota(jnp.int32, wide.shape, 0) % CH
        lane = lax.broadcasted_iota(jnp.int32, wide.shape, 1) % width
        mine = row == (lane // CI if width == 128 else lane % CH)
        total = jnp.sum(jnp.where(mine, wide, 0.0).reshape(9, CH, 3 * width), axis=1)
        for c in range(3):
            first = c if width == 128 else 2 - c
            for n in range(width // 128):
                taps[at + n, pl.ds(first, 9, stride=3)] = total[:, c * width + n * 128:c * width + (n + 1) * 128]
    bias = jnp.sum(dpre.astype(F32), axis=1, keepdims=True)
    bias = sum(bias[y * CH:(y + 1) * CH] for y in range(8))
    row = lax.broadcasted_iota(jnp.int32, (CH, 128), 0)
    lane = lax.broadcasted_iota(jnp.int32, (CH, 128), 1)
    taps[0, 27:28] = jnp.sum(jnp.where(row == lane, bias, 0.0), axis=0, keepdims=True)
    payload[...] = rounded(jnp.concatenate([taps[n] for n in range(3)], axis=1))


def hidden_rim_kernel(counts, rfar, rnear, rfar_outer, rnear_outer, hidden, fs, t1o, t1d, b1, hidden_out, fr):
    count = hidden.shape[0]
    stream, radial = lax.axis_index("stream"), lax.axis_index("radial")
    for p in range(count + 8):
        end = p if p < 2 else p - count - 4 if p >= count + 6 else None
        if end is None:
            near, outer = (rnear, rfar, (p - 2) * 16), (rnear_outer, rfar_outer, 128 + (p - 2) * 16)
        else:
            near, outer = (rnear_outer, rfar_outer, end * 16), (rnear_outer, rfar_outer, 64 + end * 16)
        parts = [sides(radial, counts[1], n[at:at + 16], f[at:at + 16]) for n, f, at in (near, outer)]
        rows = jnp.concatenate([part[side] for side in range(2) for part in parts], axis=0)
        for n, piece in enumerate(shifted(rows)):
            fr[n * 64:(n + 1) * 64, p * Z:(p + 1) * Z] = piece
    fr[192:] = jnp.zeros((64, fr.shape[1]), BF16)

    def gelu(rows, lanes):
        total = b1[rows, :1]
        for t, ref in ((t1o, fs), (t1d, fr)):
            cells = [jnp.concatenate([ref[:, a * 256 + at:a * 256 + at + size] for at, size in lanes], axis=1) for a in range(3)]
            total = total + jnp.dot(t[rows], jnp.concatenate(cells, axis=0), preferred_element_type=F32)
        return total * gelu_share(total)

    own = gelu(slice(0, 128), ((0, 2 * Z), ((count + 2) * Z, 2 * Z)))
    rims = gelu(slice(128, 192), ((0, (count + 4) * Z),))
    rims = jnp.concatenate([jnp.where(radial > 0, rims[:32], 0.0), jnp.where(radial < counts[1] - 1, rims[32:], 0.0)], axis=0)
    for p in range(count + 4):
        rim_rows = rims[:, p * Z:(p + 1) * Z]
        if 2 <= p < count + 2:
            hidden_out[p, :128] = hidden[p - 2]
            hidden_out[p, 128:] = rim_rows.astype(BF16)
        else:
            at = p if p < 2 else p - count
            inside = stream > 0 if p < 2 else stream < counts[0] - 1
            rows = jnp.concatenate([own[:, at * Z:(at + 1) * Z], rim_rows], axis=0)
            hidden_out[p] = jnp.where(inside, rows, 0.0).astype(BF16)


def closure_kernel(hidden, t2, b2, closure, hs):
    count = closure.shape[2]
    for p in range(count + 4):
        store_wide(hs, p, hidden[p].astype(F32))
    out = (jnp.dot(t2[...], stacked(hs, count * Z), preferred_element_type=F32) + b2[:, :1]).astype(BF16)
    for x in range(count):
        closure[0, :, x] = out[:, x * Z:(x + 1) * Z].reshape(CH, 8, Z)


def summed(parts):
    parts = [part[...].astype(F32) for part in parts]
    while len(parts) > 1:
        parts = [v + w for v, w in zip(parts[::2], parts[1::2])]
    return parts[0]


def add_kernel(*refs):
    refs[-1][...] = rounded(summed(refs[:-1]))


def finish_kernel(norm, *refs):
    *parts, first, second, bias = refs
    scaled = summed(parts) * norm
    flipped = jnp.transpose(scaled)
    first[...] = flipped[:128, :27]
    second[...] = flipped[128:, :27]
    bias[...] = scaled[27:28, :CH] + scaled[28:29, :CH]


def call(kernel, outs, name, scratch=(), flops=10_000_000, **specs):
    return pl.pallas_call(
        kernel,
        out_shape=outs,
        **specs,
        scratch_shapes=list(scratch),
        compiler_params=pltpu.CompilerParams(vmem_limit_bytes=32 * 1024 * 1024),
        cost_estimate=pl.CostEstimate(flops=flops, bytes_accessed=1_000_000, transcendentals=0),
        name=name,
    )


def shape(*dims, dtype=BF16):
    return jax.ShapeDtypeStruct(dims, dtype)


def exchange(near, far, axis, other):
    count, others = lax.axis_size(axis), lax.axis_size(other)
    axes = tuple(name for name in ("stream", "radial", "snap") if name in (axis, other))
    flat = (others, 1) if axes[0] == axis else (1, count)
    pairs = []
    for i in range(count):
        for j in range(others):
            end = i in (0, count - 1)
            to = (i, j ^ 1 if others % 2 == 0 else j) if end else (i - 1 + 2 * (i % 2), j)
            pairs.append((i * flat[0] + j * flat[1], to[0] * flat[0] + to[1] * flat[1]))
    far = lax.ppermute(far, axes, pairs)
    return lax.ppermute(near, axis, [(i, i ^ 1) for i in range(count)]), far


def swap(v, axis, masks):
    count = lax.axis_size(axis)
    return [lax.ppermute(v, axis, [(i, i ^ mask) for i in range(count)]) for mask in masks]


def add(v, arrived):
    return call(add_kernel, shape(*v.shape), "add_parts")(v, *arrived)


def rounds(axis, most):
    found, step = [], 1
    while step < lax.axis_size(axis):
        masks = [step * n for n in range(1, most if step * most <= lax.axis_size(axis) else 2)]
        found.append((axis, masks))
        step *= len(masks) + 1
    return found


def local(fields, first_weight, first_bias, second_weight, second_bias, cotangent):
    e1t, y1 = table(CI, 384, ((natural, 0, 64), (rim(CI), 256, 32)))
    e2t, y2 = table(CH, 640, ((natural, 0, 128), (rim(CH), 384, 64)))
    rep1, rep2 = np.zeros((128, 384), np.float32), np.zeros((128, 768), np.float32)
    for c in range(3):
        rep1[c * CI:(c + 1) * CI, c * 128:(c + 1) * 128] = np.tile(np.eye(CI), (1, CH))
        rep2[c * CH:(c + 1) * CH, c * 256:(c + 1) * 256] = np.repeat(np.eye(CH), CH, axis=1)

    def const(*arrays, dtype=BF16):
        return [jnp.asarray(v, dtype) for v in arrays]

    planes = fields.shape[2]
    w1 = first_weight.transpose(1, 2, 0).reshape(CH * CI, 27)
    w2 = second_weight.transpose(1, 2, 0).reshape(CH * CH, 27)
    near, far, f_rows, c_rows = call(
        pack_kernel,
        (shape(512, Z), shape(512, Z), shape(planes, CI * 8, Z), shape(planes, CH * 8, Z)),
        "pack_strips",
        flops=4_000_000_000,
    )(jnp.concatenate([fields[0], cotangent[0]], axis=0))
    xnear, xfar = exchange(near, far, "stream", "radial")
    wide = (planes + 4) * Z
    counts = (lax.axis_size("stream"), lax.axis_size("radial"))
    t1o, t1r, t1d, tbo, tbr, t2, b1, b2 = call(
        band_kernel,
        (shape(192, 768), shape(128, 384), shape(192, 768), shape(128, 1152), shape(128, 768), shape(128, 1920),
         shape(192, 128, dtype=F32), shape(128, 128, dtype=F32)),
        "band_matrices",
        flops=4_000_000_000,
    )(w1, w2, first_bias[None], second_bias[None])
    xfar, xnear, t1o, tbo = lax.optimization_barrier((xfar, xnear, t1o, tbo))
    inner, outer = shape((planes + 4) * 48, Z), shape(128 + (planes + 4) * 16, Z)
    near, far = call(functools.partial(join_kernel, counts), (inner, inner), "join_strips")(xfar, xnear, f_rows, c_rows)
    rnear, rfar = exchange(near, far, "radial", "stream")
    half, half_f32 = shape(64, planes * Z), shape(64, planes * Z, dtype=F32)
    fs, cs, pre, back, hidden, dpre = call(
        functools.partial(own_kernel, counts),
        (shape(256, wide + 4 * Z), shape(384, wide), half_f32, half_f32, half, half),
        "own_rows",
        flops=1_000_000_000,
    )(xfar, xnear, f_rows, c_rows, t1o, tbo, b1)
    f_rows, fs = lax.optimization_barrier((f_rows, fs))
    near_outer, far_outer = call(functools.partial(join_outer_kernel, counts), (outer, outer), "join_outer")(
        xfar, xnear, f_rows, c_rows)
    rnear_outer, rfar_outer = exchange(near_outer, far_outer, "radial", "stream")
    hidden, payload = call(
        functools.partial(rim_kernel, counts),
        (shape(planes, 128, Z), shape(32, 384)),
        "gradients",
        (pltpu.VMEM((128, wide), BF16), pltpu.VMEM((256, wide), BF16), pltpu.VMEM((3, 32, 128), F32)),
        flops=2_000_000_000,
    )(rfar, rnear, fs, cs, pre, back, hidden, dpre, t1r, tbr, *const(e1t, e2t, rep1, rep2), *const(y1, y2, dtype=F32))

    steps = rounds("radial", 4) + rounds("stream", 4) + rounds("snap", 2)
    arrived = swap(payload, *steps[0])
    hidden = call(
        functools.partial(hidden_rim_kernel, counts),
        shape(planes + 4, 192, Z),
        "hidden_rim",
        (pltpu.VMEM((256, wide + 4 * Z), BF16),),
        flops=1_000_000_000,
    )(rfar, rnear, rfar_outer, rnear_outer, hidden, fs, t1o, t1d, b1)
    payload, hidden = lax.optimization_barrier((add(payload, arrived), hidden))
    arrived = swap(payload, *steps[1])
    payload = add(payload, arrived)
    arrived = swap(payload, *steps[2])
    closure = call(
        closure_kernel, shape(*cotangent.shape), "closure", (pltpu.VMEM((640, wide), BF16),), flops=1_000_000_000
    )(hidden, t2, b2)
    for step in steps[3:]:
        payload = add(payload, arrived)
        arrived = swap(payload, *step)

    cells = fields.shape[0] * fields.shape[2] * fields.shape[3] * fields.shape[4]
    for axis in ("stream", "radial", "snap"):
        cells *= lax.axis_size(axis)
    norm = float(1.0 / np.sqrt(np.float32(cells)))
    first, second, bias = call(
        functools.partial(finish_kernel, norm),
        (shape(CH * CI, 27, dtype=F32), shape(CH * CH, 27, dtype=F32), shape(1, CH, dtype=F32)),
        "finish",
    )(payload, *arrived)
    first = first.reshape(CH, CI, 27).transpose(2, 0, 1)
    second = second.reshape(CH, CH, 27).transpose(2, 0, 1)
    return (closure, first, second, bias[0])


def solution(mesh):
    split = P("snap", None, "stream", "radial", None)
    return jax.shard_map(
        local,
        mesh=mesh,
        in_specs=(split, P(), P(), P(), P(), split),
        out_specs=(split, P(), P(), P()),
        check_vma=False,
    )
```

```python
import functools

import numpy as np
import jax
import jax.numpy as jnp
from jax import lax
from jax.experimental import pallas as pl
from jax.experimental.pallas import tpu as pltpu
from jax.sharding import PartitionSpec as P

F32 = jnp.float32
BF16 = jnp.bfloat16
Z = 128
CI = 8
CH = 16
FAR = 100


def natural(n):
    return n // 8, n % 8


def y_first(n):
    return n % CH, n // CH


def rim(channels):
    def of(n):
        side, n = n // (2 * channels), n % (2 * channels)
        return n // 2, n % 2 + 10 * side - 2
    return of


def deep_rim(n):
    part, n = n // 16, n % 16
    return n // 2, n % 2 + 10 * (part // 2) - 2 + (part % 2) * (4 * (part // 2) - 2)


def table(channels, total, places):
    e = np.zeros((total, 128), np.float32)
    ys = np.full((1, total), FAR, np.float32)
    for c in range(3):
        for of, start, step in places:
            ch, y = of(np.arange(step))
            at = start + c * step + np.arange(step)
            e[at, c * channels + ch] = 1
            ys[0, at] = y
    return e, ys


def iota(rows, columns):
    return [lax.broadcasted_iota(jnp.int32, (rows, columns), d) for d in range(2)]


def one_hot(where):
    return jnp.where(where, 1.0, 0.0).astype(BF16)


def lane_y(of, width, step):
    lane = lax.broadcasted_iota(jnp.int32, (1, width), 1)
    return jnp.where(lane < 3 * step, of(lane % step)[1], FAR)


def place(rows, wanted, of, size, slot):
    row, lane = iota(rows, 128)
    return one_hot((of(lane % size)[0] == wanted(row)) & (lane // size == slot))


def row_table(rows, own):
    row, lane = iota(rows, CH)
    own_c, own_y = own(row)
    rim_c, rim_y = rim(CH)(row - 128)
    channel, y = jnp.where(row < 128, own_c, rim_c), jnp.where(row < 128, own_y, rim_y)
    return one_hot(channel == lane), y[:, :1]


def plane(ref, channels, x):
    v = ref[channels, x].astype(F32)
    return v.reshape(v.shape[0] * v.shape[1], v.shape[2])


def pick_rows(channels, low, high):
    half = channels * 2
    row, col = iota(2 * half, channels * 8)
    side = row // half
    return one_hot(col == (row % half // 2) * 8 + low + (high - low) * side + row % 2)


def partners(index, count):
    return index % 2 == 0, index > 0, index < count - 1


def sides(index, count, near, far):
    near_above, below, above = partners(index, count)
    low = jnp.where(near_above, far, near).astype(F32)
    high = jnp.where(near_above, near, far).astype(F32)
    return jnp.where(below, low, 0.0), jnp.where(above, high, 0.0)


def pack_kernel(inputs, near, far, f_rows, c_rows):
    up_first = lax.axis_index("stream") % 2 == 0
    count, at = inputs.shape[1], 0
    for channels, out, width in ((slice(0, CI), f_rows, 4), (slice(CI, CI + CH), c_rows, 2)):
        rows = [plane(inputs, channels, x) for x in range(count)]
        for x, v in enumerate(rows):
            out[x] = v.astype(BF16)
        for low, high in zip(rows[:width], rows[count - width:]):
            part = slice(at, at + low.shape[0])
            near[part] = jnp.where(up_first, high, low).astype(BF16)
            far[part] = jnp.where(up_first, low, high).astype(BF16)
            at += low.shape[0]


def x_planes(count, fields, cot, xnear, xfar, size):
    index = lax.axis_index("stream")
    inner = [fields[x].astype(F32) for x in range(count)]
    rims = [sides(index, size, xnear[n * 64:(n + 1) * 64], xfar[n * 64:(n + 1) * 64]) for n in range(4)]
    f = [low for low, _ in rims] + inner + [high for _, high in rims]
    inner = [cot[x].astype(F32) for x in range(count)]
    rims = [sides(index, size, xnear[256 + n * 128:384 + n * 128], xfar[256 + n * 128:384 + n * 128]) for n in range(2)]
    return f, [low for low, _ in rims] + inner + [high for _, high in rims]


def pick_strips(work, near, far, near_at=0):
    up_first = lax.axis_index("radial") % 2 == 0
    at = 0
    for pick, rows in work:
        half = pick.shape[0] // 2
        for v in rows:
            got = jnp.dot(pick, v.astype(BF16), preferred_element_type=F32)
            if near is not None:
                start = near_at + at
                near[start:start + half] = jnp.where(up_first, got[half:], got[:half]).astype(BF16)
            if far is not None:
                far[at:at + half] = jnp.where(up_first, got[:half], got[half:]).astype(BF16)
            at += half


def outer_strips(f):
    ends = f[:2] + f[-2:]
    return [(pick_rows(CI, 0, 6), ends), (pick_rows(CI, 2, 4), ends + f[2:-2])]


def join_kernel(counts, xfar, xnear, fields, cot, near, far):
    f, c = x_planes(fields.shape[0], fields, cot, xnear, xfar, counts[0])
    pick_strips([(pick_rows(CI, 0, 6), f[2:-2]), (pick_rows(CH, 0, 6), c)], near, far)
    pick_strips(outer_strips(f), near, None, far.shape[0])


def join_outer_kernel(counts, xfar, xnear, fields, cot, far):
    f, _ = x_planes(fields.shape[0], fields, cot, xnear, xfar, counts[0])
    pick_strips(outer_strips(f), None, far)


def spread(w, by_row, flip):
    taps = jnp.transpose(w[...].astype(F32))
    width = taps.shape[1]
    row = lax.broadcasted_iota(jnp.int32, (CH, width), 0)
    lane = lax.broadcasted_iota(jnp.int32, (CH, width), 1)
    mine = row == (lane // (width // CH) if by_row else lane % CH)
    found = []
    for c in range(3):
        rows = []
        for ab in range(9):
            t = 26 - (ab * 3 + c) if flip else ab * 3 + c
            rows.append(jnp.where(mine, jnp.broadcast_to(taps[t:t + 1], (CH, width)), 0.0))
        found.append(jnp.concatenate(rows, axis=0).astype(BF16))
    return found


def dots(pairs):
    total = None
    for v, w in pairs:
        part = jnp.dot(v, w, preferred_element_type=F32)
        total = part if total is None else total + part
    return total.astype(BF16)


def packed(parts, wanted, of, size):
    per = 128 // size
    places = [place(parts[0].shape[1], wanted, of, size, slot) for slot in range(min(per, 3))]
    tiles = [range(first, min(first + per, 3)) for first in range(0, 3, per)]
    return jnp.concatenate([dots([(parts[c], places[c % per]) for c in tile]) for tile in tiles], axis=1)


def band(wide, expand, ys, rows_y, t):
    rows, width = t.shape[0], wide.shape[1]
    for a in range(3):
        total = jnp.zeros((rows, width), F32)
        for b in range(3):
            part = jnp.dot(expand[:rows], wide[(a * 3 + b) * CH:(a * 3 + b + 1) * CH], preferred_element_type=F32)
            total = jnp.where(ys == rows_y[:rows] + 2 * (b - 1), part, total)
        t[:, a * width:(a + 1) * width] = total.astype(BF16)


def repeat_bias(bias, expand, out):
    column = jnp.sum(expand.astype(F32) * bias[...], axis=1, keepdims=True)
    out[...] = jnp.broadcast_to(column, out.shape)


def band_kernel(w1, w2, first_bias, second_bias, t1o, t1r, t1d, tbo, tbr, t2, b1, b2):
    expand, rows_y = row_table(192, y_first)
    parts = spread(w1, True, False)
    for of, step, t in ((natural, 64, t1o), (rim(CI), 32, t1r), (deep_rim, 64, t1d)):
        wide = packed(parts, lambda n: n % CI, of, step)
        band(wide, expand, lane_y(of, wide.shape[1], step), rows_y, t)
    parts = spread(w2, False, True)
    for of, step, t in ((natural, 128, tbo), (rim(CH), 64, tbr)):
        wide = packed(parts, lambda n: n // CH, of, step)
        band(wide, expand, lane_y(of, wide.shape[1], step), rows_y, t)
    repeat_bias(first_bias, expand, b1)
    expand, rows_y = row_table(128, natural)
    parts = spread(w2, True, False)
    wide = [packed(parts, lambda n: n % CH, of, step) for of, step in ((y_first, 128), (rim(CH), 64))]
    ys = jnp.concatenate([lane_y(y_first, 384, 128), lane_y(rim(CH), 256, 64)], axis=1)
    band(jnp.concatenate(wide, axis=1), expand, ys, rows_y, t2)
    repeat_bias(second_bias, expand, b2)


def shifted(v):
    lane = lax.broadcasted_iota(jnp.int32, v.shape, 1)
    before = jnp.where(lane >= 2, pltpu.roll(v, 2, 1), 0.0)
    after = jnp.where(lane < Z - 2, pltpu.roll(v, Z - 2, 1), 0.0)
    return before.astype(BF16), v.astype(BF16), after.astype(BF16)


def store_wide(ref, p, v):
    at = slice(p * Z, (p + 1) * Z)
    for c, piece in enumerate(shifted(v)):
        ref[c * 128:(c + 1) * 128, at] = piece[:128]
        ref[384 + c * 64:384 + (c + 1) * 64, at] = piece[128:]
    ref[576:, at] = jnp.zeros((64, Z), BF16)


def stacked(ref, lanes):
    return jnp.concatenate([ref[:, a * 256:a * 256 + lanes] for a in range(3)], axis=0)


def gelu_share(pre):
    return 0.5 * (1.0 + lax.erf(pre * 0.7071067811865476))


def gelu_slope(pre, share):
    return share + pre * jnp.exp(-0.5 * pre * pre) * 0.3989422804014327


def edges(v):
    return jnp.concatenate([v[:32], v[96:128]], axis=0)


def whole(edge, middle):
    return jnp.concatenate([edge[:32], middle, edge[32:]], axis=0)


def own_kernel(counts, xfar, xnear, fields, cot, t1, tb, b1, fs, cs, pre, back, hidden, dpre):
    count, lanes = fields.shape[0], pre.shape[1]
    f, c = x_planes(count, fields, cot, xnear, xfar, counts[0])
    for ref, rows in ((fs, f), (cs, c)):
        for p, v in enumerate(rows):
            for n, piece in enumerate(shifted(v)):
                ref[n * v.shape[0]:(n + 1) * v.shape[0], p * Z:(p + 1) * Z] = piece
    fs[192:] = jnp.zeros((64, fs.shape[1]), BF16)
    rows = jnp.concatenate([fs[:, a * 256 + 256:a * 256 + 256 + lanes] for a in range(3)], axis=0)
    first = jnp.dot(t1[:128], rows, preferred_element_type=F32) + b1[:128, :1]
    second = jnp.dot(tb[...], stacked(cs, lanes), preferred_element_type=F32)
    pre[...] = edges(first)
    back[...] = edges(second)
    first, second = first[32:96], second[32:96]
    share = gelu_share(first)
    hidden[...] = (first * share).astype(BF16)
    dpre[...] = (second * gelu_slope(first, share)).astype(BF16)


def rounded(s):
    lost = s - s.astype(BF16).astype(F32)
    row = lax.broadcasted_iota(jnp.int32, s.shape, 0)
    return (s + jnp.where(row == 28, pltpu.roll(lost, 1, 0), 0.0)).astype(BF16)


def two_dots(v, w):
    high = v.astype(BF16)
    low = (v - high.astype(F32)).astype(BF16)
    return jnp.dot(high, w, preferred_element_type=F32) + jnp.dot(low, w, preferred_element_type=F32)


def rim_kernel(counts, rfar, rnear, fs, cs, pre_own, back_own, hidden_own, dpre_own, t1, tb, e1t, e2t, rep1, rep2, y1, y2,
               hidden_out, payload, fr, cr, taps):
    count = hidden_out.shape[0]
    lanes = count * Z
    radial = lax.axis_index("radial")
    at = 0
    for ref, half in ((fr, 16), (cr, 32)):
        for p in range(count + 4):
            low, high = sides(radial, counts[1], rnear[at:at + half], rfar[at:at + half])
            for n, piece in enumerate(shifted(jnp.concatenate([low, high], axis=0))):
                ref[n * 2 * half:(n + 1) * 2 * half, p * Z:(p + 1) * Z] = piece
            at += half
        ref[6 * half:] = jnp.zeros((2 * half, ref.shape[1]), BF16)
    pre = pre_own[...] + jnp.dot(edges(t1), stacked(fr, lanes), preferred_element_type=F32)
    share = gelu_share(pre)
    hidden = whole((pre * share).astype(BF16), hidden_own[...])
    for x in range(count):
        hidden_out[x] = hidden[:, x * Z:(x + 1) * Z]
    back = back_own[...] + jnp.dot(edges(tb), stacked(cr, lanes), preferred_element_type=F32)
    dpre = whole((back * gelu_slope(pre, share)).astype(BF16), dpre_own[...])
    over_lanes = (((1,), (1,)), ((), ()))
    ones, twos = [], []
    sums = [[None] * 3, [None] * 3]
    for pair in range(count // 2 + 2):
        taps_here = [a for a in range(3) if 0 <= pair - a < count // 2]
        at = slice(pair * 256, (pair + 1) * 256)
        shifted_rows = (
            jnp.concatenate([fs[:, (pair + 1) * 256:(pair + 2) * 256], fr[:, at]], axis=0),
            jnp.concatenate([cs[:, at], cr[:, at]], axis=0),
        )
        for here, rows, total in zip((dpre, hidden), shifted_rows, sums):
            here = jnp.concatenate([here[:, (pair - a) * 256:(pair - a + 1) * 256] for a in taps_here], axis=0)
            got = lax.dot_general(here, rows, over_lanes, preferred_element_type=F32)
            for n, a in enumerate(taps_here):
                part = got[n * 128:(n + 1) * 128]
                total[a] = part if total[a] is None else total[a] + part
    for a in range(3):
        g1, g2 = sums[0][a], sums[1][a]
        for b in range(3):
            for g, ys, out in ((g1, y1, ones), (g2, y2, twos)):
                total = jnp.zeros((CH, g.shape[1]), F32)
                for y in range(8):
                    total = jnp.where(ys[...] == float(y + 2 * (b - 1)), g[y * CH:(y + 1) * CH], total)
                out.append(total)
    taps[:, 24:] = jnp.zeros((3, 8, 128), F32)
    for parts, et, rep, at, width in ((ones, e1t, rep1, 0, 128), (twos[::-1], e2t, rep2, 1, 256)):
        sums = two_dots(jnp.concatenate(parts, axis=0), et[...])
        wide = two_dots(sums, rep[...])
        row = lax.broadcasted_iota(jnp.int32, wide.shape, 0) % CH
        lane = lax.broadcasted_iota(jnp.int32, wide.shape, 1) % width
        mine = row == (lane // CI if width == 128 else lane % CH)
        total = jnp.sum(jnp.where(mine, wide, 0.0).reshape(9, CH, 3 * width), axis=1)
        for c in range(3):
            first = c if width == 128 else 2 - c
            for n in range(width // 128):
                taps[at + n, pl.ds(first, 9, stride=3)] = total[:, c * width + n * 128:c * width + (n + 1) * 128]
    bias = jnp.sum(dpre.astype(F32), axis=1, keepdims=True)
    bias = sum(bias[y * CH:(y + 1) * CH] for y in range(8))
    row = lax.broadcasted_iota(jnp.int32, (CH, 128), 0)
    lane = lax.broadcasted_iota(jnp.int32, (CH, 128), 1)
    taps[0, 27:28] = jnp.sum(jnp.where(row == lane, bias, 0.0), axis=0, keepdims=True)
    payload[...] = rounded(jnp.concatenate([taps[n] for n in range(3)], axis=1))


def hidden_rim_kernel(counts, rfar, rnear, rfar_outer, hidden, fs, t1o, t1d, b1, hidden_out, fr):
    count, inner = hidden.shape[0], rfar.shape[0]
    stream, radial = lax.axis_index("stream"), lax.axis_index("radial")
    for p in range(count + 8):
        end = p if p < 2 else p - count - 4 if p >= count + 6 else None
        if end is None:
            near, outer = (0, rfar, (p - 2) * 16), (inner, rfar_outer, 128 + (p - 2) * 16)
        else:
            near, outer = (inner, rfar_outer, end * 16), (inner, rfar_outer, 64 + end * 16)
        parts = [sides(radial, counts[1], rnear[n + at:n + at + 16], f[at:at + 16]) for n, f, at in (near, outer)]
        rows = jnp.concatenate([part[side] for side in range(2) for part in parts], axis=0)
        for n, piece in enumerate(shifted(rows)):
            fr[n * 64:(n + 1) * 64, p * Z:(p + 1) * Z] = piece
    fr[192:] = jnp.zeros((64, fr.shape[1]), BF16)

    def gelu(rows, lanes):
        total = b1[rows, :1]
        for t, ref in ((t1o, fs), (t1d, fr)):
            cells = [jnp.concatenate([ref[:, a * 256 + at:a * 256 + at + size] for at, size in lanes], axis=1) for a in range(3)]
            total = total + jnp.dot(t[rows], jnp.concatenate(cells, axis=0), preferred_element_type=F32)
        return total * gelu_share(total)

    own = gelu(slice(0, 128), ((0, 2 * Z), ((count + 2) * Z, 2 * Z)))
    rims = gelu(slice(128, 192), ((0, (count + 4) * Z),))
    rims = jnp.concatenate([jnp.where(radial > 0, rims[:32], 0.0), jnp.where(radial < counts[1] - 1, rims[32:], 0.0)], axis=0)
    for p in range(count + 4):
        rim_rows = rims[:, p * Z:(p + 1) * Z]
        if 2 <= p < count + 2:
            hidden_out[p, :128] = hidden[p - 2]
            hidden_out[p, 128:] = rim_rows.astype(BF16)
        else:
            at = p if p < 2 else p - count
            inside = stream > 0 if p < 2 else stream < counts[0] - 1
            rows = jnp.concatenate([own[:, at * Z:(at + 1) * Z], rim_rows], axis=0)
            hidden_out[p] = jnp.where(inside, rows, 0.0).astype(BF16)


def closure_kernel(hidden, t2, b2, closure, hs):
    count = closure.shape[2]
    for p in range(count + 4):
        store_wide(hs, p, hidden[p].astype(F32))
    out = (jnp.dot(t2[...], stacked(hs, count * Z), preferred_element_type=F32) + b2[:, :1]).astype(BF16)
    for x in range(count):
        closure[0, :, x] = out[:, x * Z:(x + 1) * Z].reshape(CH, 8, Z)


def summed(parts):
    parts = [part[...].astype(F32) for part in parts]
    while len(parts) > 1:
        parts = [v + w for v, w in zip(parts[::2], parts[1::2])]
    return parts[0]


def add_kernel(*refs):
    refs[-1][...] = rounded(summed(refs[:-1]))


def finish_kernel(norm, *refs):
    *parts, first, second, bias = refs
    scaled = summed(parts) * norm
    flipped = jnp.transpose(scaled)
    first[...] = flipped[:128, :27]
    second[...] = flipped[128:, :27]
    bias[...] = scaled[27:28, :CH] + scaled[28:29, :CH]


def call(kernel, outs, name, scratch=(), flops=10_000_000, **specs):
    return pl.pallas_call(
        kernel,
        out_shape=outs,
        **specs,
        scratch_shapes=list(scratch),
        compiler_params=pltpu.CompilerParams(vmem_limit_bytes=32 * 1024 * 1024),
        cost_estimate=pl.CostEstimate(flops=flops, bytes_accessed=1_000_000, transcendentals=0),
        name=name,
    )


def shape(*dims, dtype=BF16):
    return jax.ShapeDtypeStruct(dims, dtype)


def send_far(far, axis, other):
    count, others = lax.axis_size(axis), lax.axis_size(other)
    axes = tuple(name for name in ("stream", "radial", "snap") if name in (axis, other))
    flat = (others, 1) if axes[0] == axis else (1, count)
    pairs = []
    for i in range(count):
        for j in range(others):
            end = i in (0, count - 1)
            to = (i, j ^ 1 if others % 2 == 0 else j) if end else (i - 1 + 2 * (i % 2), j)
            pairs.append((i * flat[0] + j * flat[1], to[0] * flat[0] + to[1] * flat[1]))
    return lax.ppermute(far, axes, pairs)


def exchange(near, far, axis, other):
    far = send_far(far, axis, other)
    return lax.ppermute(near, axis, [(i, i ^ 1) for i in range(lax.axis_size(axis))]), far


def swap(v, axis, masks):
    count = lax.axis_size(axis)
    return [lax.ppermute(v, axis, [(i, i ^ mask) for i in range(count)]) for mask in masks]


def add(v, arrived):
    return call(add_kernel, shape(*v.shape), "add_parts")(v, *arrived)


def rounds(axis, most):
    found, step = [], 1
    while step < lax.axis_size(axis):
        masks = [step * n for n in range(1, most if step * most <= lax.axis_size(axis) else 2)]
        found.append((axis, masks))
        step *= len(masks) + 1
    return found


def local(fields, first_weight, first_bias, second_weight, second_bias, cotangent):
    e1t, y1 = table(CI, 384, ((natural, 0, 64), (rim(CI), 256, 32)))
    e2t, y2 = table(CH, 640, ((natural, 0, 128), (rim(CH), 384, 64)))
    rep1, rep2 = np.zeros((128, 384), np.float32), np.zeros((128, 768), np.float32)
    for c in range(3):
        rep1[c * CI:(c + 1) * CI, c * 128:(c + 1) * 128] = np.tile(np.eye(CI), (1, CH))
        rep2[c * CH:(c + 1) * CH, c * 256:(c + 1) * 256] = np.repeat(np.eye(CH), CH, axis=1)

    def const(*arrays, dtype=BF16):
        return [jnp.asarray(v, dtype) for v in arrays]

    planes = fields.shape[2]
    w1 = first_weight.transpose(1, 2, 0).reshape(CH * CI, 27)
    w2 = second_weight.transpose(1, 2, 0).reshape(CH * CH, 27)
    near, far, f_rows, c_rows = call(
        pack_kernel,
        (shape(512, Z), shape(512, Z), shape(planes, CI * 8, Z), shape(planes, CH * 8, Z)),
        "pack_strips",
        flops=4_000_000_000,
    )(jnp.concatenate([fields[0], cotangent[0]], axis=0))
    xnear, xfar = exchange(near, far, "stream", "radial")
    wide = (planes + 4) * Z
    counts = (lax.axis_size("stream"), lax.axis_size("radial"))
    t1o, t1r, t1d, tbo, tbr, t2, b1, b2 = call(
        band_kernel,
        (shape(192, 768), shape(128, 384), shape(192, 768), shape(128, 1152), shape(128, 768), shape(128, 1920),
         shape(192, 128, dtype=F32), shape(128, 128, dtype=F32)),
        "band_matrices",
        flops=4_000_000_000,
    )(w1, w2, first_bias[None], second_bias[None])
    xfar, xnear, t1o, tbo = lax.optimization_barrier((xfar, xnear, t1o, tbo))
    inner, outer = (planes + 4) * 48, 128 + (planes + 4) * 16
    near, far = call(
        functools.partial(join_kernel, counts), (shape(inner + outer, Z), shape(inner, Z)), "join_strips"
    )(xfar, xnear, f_rows, c_rows)
    rnear, rfar = exchange(near, far, "radial", "stream")
    half, half_f32 = shape(64, planes * Z), shape(64, planes * Z, dtype=F32)
    fs, cs, pre, back, hidden, dpre = call(
        functools.partial(own_kernel, counts),
        (shape(256, wide + 4 * Z), shape(384, wide), half_f32, half_f32, half, half),
        "own_rows",
        flops=1_000_000_000,
    )(xfar, xnear, f_rows, c_rows, t1o, tbo, b1)
    f_rows, fs = lax.optimization_barrier((f_rows, fs))
    far_outer = call(functools.partial(join_outer_kernel, counts), shape(outer, Z), "join_outer")(
        xfar, xnear, f_rows, c_rows)
    rfar_outer = send_far(far_outer, "radial", "stream")
    hidden, payload = call(
        functools.partial(rim_kernel, counts),
        (shape(planes, 128, Z), shape(32, 384)),
        "gradients",
        (pltpu.VMEM((128, wide), BF16), pltpu.VMEM((256, wide), BF16), pltpu.VMEM((3, 32, 128), F32)),
        flops=2_000_000_000,
    )(rfar, rnear, fs, cs, pre, back, hidden, dpre, t1r, tbr, *const(e1t, e2t, rep1, rep2), *const(y1, y2, dtype=F32))

    steps = rounds("radial", 4) + rounds("stream", 4) + rounds("snap", 2)
    arrived = swap(payload, *steps[0])
    hidden = call(
        functools.partial(hidden_rim_kernel, counts),
        shape(planes + 4, 192, Z),
        "hidden_rim",
        (pltpu.VMEM((256, wide + 4 * Z), BF16),),
        flops=1_000_000_000,
    )(rfar, rnear, rfar_outer, hidden, fs, t1o, t1d, b1)
    payload, hidden = lax.optimization_barrier((add(payload, arrived), hidden))
    arrived = swap(payload, *steps[1])
    payload = add(payload, arrived)
    arrived = swap(payload, *steps[2])
    closure = call(
        closure_kernel, shape(*cotangent.shape), "closure", (pltpu.VMEM((640, wide), BF16),), flops=1_000_000_000
    )(hidden, t2, b2)
    for step in steps[3:]:
        payload = add(payload, arrived)
        arrived = swap(payload, *step)

    cells = fields.shape[0] * fields.shape[2] * fields.shape[3] * fields.shape[4]
    for axis in ("stream", "radial", "snap"):
        cells *= lax.axis_size(axis)
    norm = float(1.0 / np.sqrt(np.float32(cells)))
    first, second, bias = call(
        functools.partial(finish_kernel, norm),
        (shape(CH * CI, 27, dtype=F32), shape(CH * CH, 27, dtype=F32), shape(1, CH, dtype=F32)),
        "finish",
    )(payload, *arrived)
    first = first.reshape(CH, CI, 27).transpose(2, 0, 1)
    second = second.reshape(CH, CH, 27).transpose(2, 0, 1)
    return (closure, first, second, bias[0])


def solution(mesh):
    split = P("snap", None, "stream", "radial", None)
    return jax.shard_map(
        local,
        mesh=mesh,
        in_specs=(split, P(), P(), P(), P(), split),
        out_specs=(split, P(), P(), P()),
        check_vma=False,
    )
```

```python
import functools

import numpy as np
import jax
import jax.numpy as jnp
from jax import lax
from jax.experimental import pallas as pl
from jax.experimental.pallas import tpu as pltpu
from jax.sharding import PartitionSpec as P

F32 = jnp.float32
BF16 = jnp.bfloat16
Z = 128
CI = 8
CH = 16
FAR = 100


def natural(n):
    return n // 8, n % 8


def y_first(n):
    return n % CH, n // CH


def rim(channels):
    def of(n):
        side, n = n // (2 * channels), n % (2 * channels)
        return n // 2, n % 2 + 10 * side - 2
    return of


def deep_rim(n):
    part, n = n // 16, n % 16
    return n // 2, n % 2 + 10 * (part // 2) - 2 + (part % 2) * (4 * (part // 2) - 2)


def table(channels, total, places):
    e = np.zeros((total, 128), np.float32)
    ys = np.full((1, total), FAR, np.float32)
    for c in range(3):
        for of, start, step in places:
            ch, y = of(np.arange(step))
            at = start + c * step + np.arange(step)
            e[at, c * channels + ch] = 1
            ys[0, at] = y
    return e, ys


def iota(rows, columns):
    return [lax.broadcasted_iota(jnp.int32, (rows, columns), d) for d in range(2)]


def one_hot(where):
    return jnp.where(where, 1.0, 0.0).astype(BF16)


def lane_y(of, width, step):
    lane = lax.broadcasted_iota(jnp.int32, (1, width), 1)
    return jnp.where(lane < 3 * step, of(lane % step)[1], FAR)


def place(rows, wanted, of, size, slot):
    row, lane = iota(rows, 128)
    return one_hot((of(lane % size)[0] == wanted(row)) & (lane // size == slot))


def row_table(rows, own):
    row, lane = iota(rows, CH)
    own_c, own_y = own(row)
    rim_c, rim_y = rim(CH)(row - 128)
    channel, y = jnp.where(row < 128, own_c, rim_c), jnp.where(row < 128, own_y, rim_y)
    return one_hot(channel == lane), y[:, :1]


def plane(ref, channels, x):
    v = ref[channels, x].astype(F32)
    return v.reshape(v.shape[0] * v.shape[1], v.shape[2])


def pick_rows(channels, low, high):
    half = channels * 2
    row, col = iota(2 * half, channels * 8)
    side = row // half
    return one_hot(col == (row % half // 2) * 8 + low + (high - low) * side + row % 2)


def partners(index, count):
    return index % 2 == 0, index > 0, index < count - 1


def sides(index, count, near, far):
    near_above, below, above = partners(index, count)
    low = jnp.where(near_above, far, near).astype(F32)
    high = jnp.where(near_above, near, far).astype(F32)
    return jnp.where(below, low, 0.0), jnp.where(above, high, 0.0)


def pack_kernel(inputs, near, far, f_rows, c_rows):
    up_first = lax.axis_index("stream") % 2 == 0
    count, at = inputs.shape[1], 0
    for channels, out, width in ((slice(0, CI), f_rows, 4), (slice(CI, CI + CH), c_rows, 2)):
        rows = [plane(inputs, channels, x) for x in range(count)]
        for x, v in enumerate(rows):
            out[x] = v.astype(BF16)
        for low, high in zip(rows[:width], rows[count - width:]):
            part = slice(at, at + low.shape[0])
            near[part] = jnp.where(up_first, high, low).astype(BF16)
            far[part] = jnp.where(up_first, low, high).astype(BF16)
            at += low.shape[0]


def x_planes(count, fields, cot, xnear, xfar, size):
    index = lax.axis_index("stream")
    inner = [fields[x].astype(F32) for x in range(count)]
    rims = [sides(index, size, xnear[n * 64:(n + 1) * 64], xfar[n * 64:(n + 1) * 64]) for n in range(4)]
    f = [low for low, _ in rims] + inner + [high for _, high in rims]
    inner = [cot[x].astype(F32) for x in range(count)]
    rims = [sides(index, size, xnear[256 + n * 128:384 + n * 128], xfar[256 + n * 128:384 + n * 128]) for n in range(2)]
    return f, [low for low, _ in rims] + inner + [high for _, high in rims]


def pick_strips(work, near, far):
    up_first = lax.axis_index("radial") % 2 == 0
    at = 0
    for pick, rows in work:
        half = pick.shape[0] // 2
        for v in rows:
            got = jnp.dot(pick, v.astype(BF16), preferred_element_type=F32)
            near[at:at + half] = jnp.where(up_first, got[half:], got[:half]).astype(BF16)
            far[at:at + half] = jnp.where(up_first, got[:half], got[half:]).astype(BF16)
            at += half


def join_kernel(counts, xfar, xnear, fields, cot, near, far):
    f, c = x_planes(fields.shape[0], fields, cot, xnear, xfar, counts[0])
    pick_strips([(pick_rows(CI, 0, 6), f[2:-2]), (pick_rows(CH, 0, 6), c)], near, far)


def join_outer_kernel(counts, xfar, xnear, fields, cot, near, far):
    f, _ = x_planes(fields.shape[0], fields, cot, xnear, xfar, counts[0])
    ends = f[:2] + f[-2:]
    pick_strips([(pick_rows(CI, 0, 6), ends), (pick_rows(CI, 2, 4), ends + f[2:-2])], near, far)


def spread(w, by_row, flip):
    taps = jnp.transpose(w[...].astype(F32))
    width = taps.shape[1]
    row = lax.broadcasted_iota(jnp.int32, (CH, width), 0)
    lane = lax.broadcasted_iota(jnp.int32, (CH, width), 1)
    mine = row == (lane // (width // CH) if by_row else lane % CH)
    found = []
    for c in range(3):
        rows = []
        for ab in range(9):
            t = 26 - (ab * 3 + c) if flip else ab * 3 + c
            rows.append(jnp.where(mine, jnp.broadcast_to(taps[t:t + 1], (CH, width)), 0.0))
        found.append(jnp.concatenate(rows, axis=0).astype(BF16))
    return found


def dots(pairs):
    total = None
    for v, w in pairs:
        part = jnp.dot(v, w, preferred_element_type=F32)
        total = part if total is None else total + part
    return total.astype(BF16)


def packed(parts, wanted, of, size):
    per = 128 // size
    places = [place(parts[0].shape[1], wanted, of, size, slot) for slot in range(min(per, 3))]
    tiles = [range(first, min(first + per, 3)) for first in range(0, 3, per)]
    return jnp.concatenate([dots([(parts[c], places[c % per]) for c in tile]) for tile in tiles], axis=1)


def band(wide, expand, ys, rows_y, t):
    rows, width = t.shape[0], wide.shape[1]
    for a in range(3):
        total = jnp.zeros((rows, width), F32)
        for b in range(3):
            part = jnp.dot(expand[:rows], wide[(a * 3 + b) * CH:(a * 3 + b + 1) * CH], preferred_element_type=F32)
            total = jnp.where(ys == rows_y[:rows] + 2 * (b - 1), part, total)
        t[:, a * width:(a + 1) * width] = total.astype(BF16)


def repeat_bias(bias, expand, out):
    column = jnp.sum(expand.astype(F32) * bias[...], axis=1, keepdims=True)
    out[...] = jnp.broadcast_to(column, out.shape)


def band_kernel(w1, w2, first_bias, second_bias, t1o, t1r, t1d, tbo, tbr, t2, b1, b2):
    expand, rows_y = row_table(192, y_first)
    parts = spread(w1, True, False)
    for of, step, t in ((natural, 64, t1o), (rim(CI), 32, t1r), (deep_rim, 64, t1d)):
        wide = packed(parts, lambda n: n % CI, of, step)
        band(wide, expand, lane_y(of, wide.shape[1], step), rows_y, t)
    parts = spread(w2, False, True)
    for of, step, t in ((natural, 128, tbo), (rim(CH), 64, tbr)):
        wide = packed(parts, lambda n: n // CH, of, step)
        band(wide, expand, lane_y(of, wide.shape[1], step), rows_y, t)
    repeat_bias(first_bias, expand, b1)
    expand, rows_y = row_table(128, natural)
    parts = spread(w2, True, False)
    wide = [packed(parts, lambda n: n % CH, of, step) for of, step in ((y_first, 128), (rim(CH), 64))]
    ys = jnp.concatenate([lane_y(y_first, 384, 128), lane_y(rim(CH), 256, 64)], axis=1)
    band(jnp.concatenate(wide, axis=1), expand, ys, rows_y, t2)
    repeat_bias(second_bias, expand, b2)


def shifted(v):
    lane = lax.broadcasted_iota(jnp.int32, v.shape, 1)
    before = jnp.where(lane >= 2, pltpu.roll(v, 2, 1), 0.0)
    after = jnp.where(lane < Z - 2, pltpu.roll(v, Z - 2, 1), 0.0)
    return before.astype(BF16), v.astype(BF16), after.astype(BF16)


def store_wide(ref, p, v):
    at = slice(p * Z, (p + 1) * Z)
    for c, piece in enumerate(shifted(v)):
        ref[c * 128:(c + 1) * 128, at] = piece[:128]
        ref[384 + c * 64:384 + (c + 1) * 64, at] = piece[128:]
    ref[576:, at] = jnp.zeros((64, Z), BF16)


def stacked(ref, lanes):
    return jnp.concatenate([ref[:, a * 256:a * 256 + lanes] for a in range(3)], axis=0)


def gelu_share(pre):
    return 0.5 * (1.0 + lax.erf(pre * 0.7071067811865476))


def gelu_slope(pre, share):
    return share + pre * jnp.exp(-0.5 * pre * pre) * 0.3989422804014327


def edges(v):
    return jnp.concatenate([v[:32], v[96:128]], axis=0)


def whole(edge, middle):
    return jnp.concatenate([edge[:32], middle, edge[32:]], axis=0)


def own_kernel(counts, xfar, xnear, fields, cot, t1, tb, b1, fs, cs, pre, back, hidden, dpre):
    count, lanes = fields.shape[0], pre.shape[1]
    f, c = x_planes(count, fields, cot, xnear, xfar, counts[0])
    for ref, rows in ((fs, f), (cs, c)):
        for p, v in enumerate(rows):
            for n, piece in enumerate(shifted(v)):
                ref[n * v.shape[0]:(n + 1) * v.shape[0], p * Z:(p + 1) * Z] = piece
    fs[192:] = jnp.zeros((64, fs.shape[1]), BF16)
    rows = jnp.concatenate([fs[:, a * 256 + 256:a * 256 + 256 + lanes] for a in range(3)], axis=0)
    first = jnp.dot(t1[:128], rows, preferred_element_type=F32) + b1[:128, :1]
    second = jnp.dot(tb[...], stacked(cs, lanes), preferred_element_type=F32)
    pre[...] = edges(first)
    back[...] = edges(second)
    first, second = first[32:96], second[32:96]
    share = gelu_share(first)
    hidden[...] = (first * share).astype(BF16)
    dpre[...] = (second * gelu_slope(first, share)).astype(BF16)


def rounded(s):
    lost = s - s.astype(BF16).astype(F32)
    row = lax.broadcasted_iota(jnp.int32, s.shape, 0)
    return (s + jnp.where(row == 28, pltpu.roll(lost, 1, 0), 0.0)).astype(BF16)


def two_dots(v, w):
    high = v.astype(BF16)
    low = (v - high.astype(F32)).astype(BF16)
    return jnp.dot(high, w, preferred_element_type=F32) + jnp.dot(low, w, preferred_element_type=F32)


def rim_kernel(counts, rfar, rnear, fs, cs, pre_own, back_own, hidden_own, dpre_own, t1, tb, e1t, e2t, rep1, rep2, y1, y2,
               hidden_out, payload, fr, cr, taps):
    count = hidden_out.shape[0]
    lanes = count * Z
    radial = lax.axis_index("radial")
    at = 0
    for ref, half in ((fr, 16), (cr, 32)):
        for p in range(count + 4):
            low, high = sides(radial, counts[1], rnear[at:at + half], rfar[at:at + half])
            for n, piece in enumerate(shifted(jnp.concatenate([low, high], axis=0))):
                ref[n * 2 * half:(n + 1) * 2 * half, p * Z:(p + 1) * Z] = piece
            at += half
        ref[6 * half:] = jnp.zeros((2 * half, ref.shape[1]), BF16)
    pre = pre_own[...] + jnp.dot(edges(t1), stacked(fr, lanes), preferred_element_type=F32)
    share = gelu_share(pre)
    hidden = whole((pre * share).astype(BF16), hidden_own[...])
    for x in range(count):
        hidden_out[x] = hidden[:, x * Z:(x + 1) * Z]
    back = back_own[...] + jnp.dot(edges(tb), stacked(cr, lanes), preferred_element_type=F32)
    dpre = whole((back * gelu_slope(pre, share)).astype(BF16), dpre_own[...])
    over_lanes = (((1,), (1,)), ((), ()))
    ones, twos = [], []
    sums = [[None] * 3, [None] * 3]
    for pair in range(count // 2 + 2):
        taps_here = [a for a in range(3) if 0 <= pair - a < count // 2]
        at = slice(pair * 256, (pair + 1) * 256)
        shifted_rows = (
            jnp.concatenate([fs[:, (pair + 1) * 256:(pair + 2) * 256], fr[:, at]], axis=0),
            jnp.concatenate([cs[:, at], cr[:, at]], axis=0),
        )
        for here, rows, total in zip((dpre, hidden), shifted_rows, sums):
            here = jnp.concatenate([here[:, (pair - a) * 256:(pair - a + 1) * 256] for a in taps_here], axis=0)
            got = lax.dot_general(here, rows, over_lanes, preferred_element_type=F32)
            for n, a in enumerate(taps_here):
                part = got[n * 128:(n + 1) * 128]
                total[a] = part if total[a] is None else total[a] + part
    for a in range(3):
        g1, g2 = sums[0][a], sums[1][a]
        for b in range(3):
            for g, ys, out in ((g1, y1, ones), (g2, y2, twos)):
                total = jnp.zeros((CH, g.shape[1]), F32)
                for y in range(8):
                    total = jnp.where(ys[...] == float(y + 2 * (b - 1)), g[y * CH:(y + 1) * CH], total)
                out.append(total)
    taps[:, 24:] = jnp.zeros((3, 8, 128), F32)
    for parts, et, rep, at, width in ((ones, e1t, rep1, 0, 128), (twos[::-1], e2t, rep2, 1, 256)):
        sums = two_dots(jnp.concatenate(parts, axis=0), et[...])
        wide = two_dots(sums, rep[...])
        row = lax.broadcasted_iota(jnp.int32, wide.shape, 0) % CH
        lane = lax.broadcasted_iota(jnp.int32, wide.shape, 1) % width
        mine = row == (lane // CI if width == 128 else lane % CH)
        total = jnp.sum(jnp.where(mine, wide, 0.0).reshape(9, CH, 3 * width), axis=1)
        for c in range(3):
            first = c if width == 128 else 2 - c
            for n in range(width // 128):
                taps[at + n, pl.ds(first, 9, stride=3)] = total[:, c * width + n * 128:c * width + (n + 1) * 128]
    bias = jnp.sum(dpre.astype(F32), axis=1, keepdims=True)
    bias = sum(bias[y * CH:(y + 1) * CH] for y in range(8))
    row = lax.broadcasted_iota(jnp.int32, (CH, 128), 0)
    lane = lax.broadcasted_iota(jnp.int32, (CH, 128), 1)
    taps[0, 27:28] = jnp.sum(jnp.where(row == lane, bias, 0.0), axis=0, keepdims=True)
    payload[...] = rounded(jnp.concatenate([taps[n] for n in range(3)], axis=1))


def hidden_rim_kernel(counts, rfar, rnear, rfar_outer, rnear_outer, hidden, fs, t1o, t1d, b1, hidden_out, fr):
    count = hidden.shape[0]
    stream, radial = lax.axis_index("stream"), lax.axis_index("radial")
    for p in range(count + 8):
        end = p if p < 2 else p - count - 4 if p >= count + 6 else None
        if end is None:
            near, outer = (rnear, rfar, (p - 2) * 16), (rnear_outer, rfar_outer, 128 + (p - 2) * 16)
        else:
            near, outer = (rnear_outer, rfar_outer, end * 16), (rnear_outer, rfar_outer, 64 + end * 16)
        parts = [sides(radial, counts[1], n[at:at + 16], f[at:at + 16]) for n, f, at in (near, outer)]
        rows = jnp.concatenate([part[side] for side in range(2) for part in parts], axis=0)
        for n, piece in enumerate(shifted(rows)):
            fr[n * 64:(n + 1) * 64, p * Z:(p + 1) * Z] = piece
    fr[192:] = jnp.zeros((64, fr.shape[1]), BF16)

    def gelu(rows, lanes):
        total = b1[rows, :1]
        for t, ref in ((t1o, fs), (t1d, fr)):
            cells = [jnp.concatenate([ref[:, a * 256 + at:a * 256 + at + size] for at, size in lanes], axis=1) for a in range(3)]
            total = total + jnp.dot(t[rows], jnp.concatenate(cells, axis=0), preferred_element_type=F32)
        return total * gelu_share(total)

    own = gelu(slice(0, 128), ((0, 2 * Z), ((count + 2) * Z, 2 * Z)))
    rims = gelu(slice(128, 192), ((0, (count + 4) * Z),))
    rims = jnp.concatenate([jnp.where(radial > 0, rims[:32], 0.0), jnp.where(radial < counts[1] - 1, rims[32:], 0.0)], axis=0)
    for p in range(count + 4):
        rim_rows = rims[:, p * Z:(p + 1) * Z]
        if 2 <= p < count + 2:
            hidden_out[p, :128] = hidden[p - 2]
            hidden_out[p, 128:] = rim_rows.astype(BF16)
        else:
            at = p if p < 2 else p - count
            inside = stream > 0 if p < 2 else stream < counts[0] - 1
            rows = jnp.concatenate([own[:, at * Z:(at + 1) * Z], rim_rows], axis=0)
            hidden_out[p] = jnp.where(inside, rows, 0.0).astype(BF16)


def closure_kernel(hidden, t2, b2, closure, hs):
    count = closure.shape[2]
    for p in range(count + 4):
        store_wide(hs, p, hidden[p].astype(F32))
    out = (jnp.dot(t2[...], stacked(hs, count * Z), preferred_element_type=F32) + b2[:, :1]).astype(BF16)
    for x in range(count):
        closure[0, :, x] = out[:, x * Z:(x + 1) * Z].reshape(CH, 8, Z)


def summed(parts):
    parts = [part[...].astype(F32) for part in parts]
    while len(parts) > 1:
        parts = [v + w for v, w in zip(parts[::2], parts[1::2])]
    return parts[0]


def add_kernel(*refs):
    refs[-1][...] = rounded(summed(refs[:-1]))


def finish_kernel(norm, *refs):
    *parts, first, second, bias = refs
    scaled = summed(parts) * norm
    flipped = jnp.transpose(scaled)
    first[...] = flipped[:128, :27]
    second[...] = flipped[128:, :27]
    bias[...] = scaled[27:28, :CH] + scaled[28:29, :CH]


def call(kernel, outs, name, scratch=(), flops=10_000_000, **specs):
    return pl.pallas_call(
        kernel,
        out_shape=outs,
        **specs,
        scratch_shapes=list(scratch),
        compiler_params=pltpu.CompilerParams(vmem_limit_bytes=32 * 1024 * 1024),
        cost_estimate=pl.CostEstimate(flops=flops, bytes_accessed=1_000_000, transcendentals=0),
        name=name,
    )


def shape(*dims, dtype=BF16):
    return jax.ShapeDtypeStruct(dims, dtype)


def exchange(near, far, axis, other):
    count, others = lax.axis_size(axis), lax.axis_size(other)
    axes = tuple(name for name in ("stream", "radial", "snap") if name in (axis, other))
    flat = (others, 1) if axes[0] == axis else (1, count)
    pairs = []
    for i in range(count):
        for j in range(others):
            end = i in (0, count - 1)
            to = (i, j ^ 1 if others % 2 == 0 else j) if end else (i - 1 + 2 * (i % 2), j)
            pairs.append((i * flat[0] + j * flat[1], to[0] * flat[0] + to[1] * flat[1]))
    far = lax.ppermute(far, axes, pairs)
    return lax.ppermute(near, axis, [(i, i ^ 1) for i in range(count)]), far


def swap(v, axis, masks):
    count = lax.axis_size(axis)
    return [lax.ppermute(v, axis, [(i, i ^ mask) for i in range(count)]) for mask in masks]


def stream_round(v):
    count, others = lax.axis_size("stream"), lax.axis_size("radial")
    pairs = [(i * others + j, (i ^ (2 + (j + 1) % 2)) * others + j) for i in range(count) for j in range(others)]
    apart = lax.ppermute(v, ("stream", "radial"), pairs)
    return [*swap(v, "stream", [1]), apart, *swap(apart, "radial", [1])]


def add(v, arrived):
    return call(add_kernel, shape(*v.shape), "add_parts")(v, *arrived)


def rounds(axis, most):
    found, step = [], 1
    while step < lax.axis_size(axis):
        masks = [step * n for n in range(1, most if step * most <= lax.axis_size(axis) else 2)]
        found.append((axis, masks))
        step *= len(masks) + 1
    return found


def local(fields, first_weight, first_bias, second_weight, second_bias, cotangent):
    e1t, y1 = table(CI, 384, ((natural, 0, 64), (rim(CI), 256, 32)))
    e2t, y2 = table(CH, 640, ((natural, 0, 128), (rim(CH), 384, 64)))
    rep1, rep2 = np.zeros((128, 384), np.float32), np.zeros((128, 768), np.float32)
    for c in range(3):
        rep1[c * CI:(c + 1) * CI, c * 128:(c + 1) * 128] = np.tile(np.eye(CI), (1, CH))
        rep2[c * CH:(c + 1) * CH, c * 256:(c + 1) * 256] = np.repeat(np.eye(CH), CH, axis=1)

    def const(*arrays, dtype=BF16):
        return [jnp.asarray(v, dtype) for v in arrays]

    planes = fields.shape[2]
    w1 = first_weight.transpose(1, 2, 0).reshape(CH * CI, 27)
    w2 = second_weight.transpose(1, 2, 0).reshape(CH * CH, 27)
    near, far, f_rows, c_rows = call(
        pack_kernel,
        (shape(512, Z), shape(512, Z), shape(planes, CI * 8, Z), shape(planes, CH * 8, Z)),
        "pack_strips",
        flops=4_000_000_000,
    )(jnp.concatenate([fields[0], cotangent[0]], axis=0))
    xnear, xfar = exchange(near, far, "stream", "radial")
    wide = (planes + 4) * Z
    counts = (lax.axis_size("stream"), lax.axis_size("radial"))
    t1o, t1r, t1d, tbo, tbr, t2, b1, b2 = call(
        band_kernel,
        (shape(192, 768), shape(128, 384), shape(192, 768), shape(128, 1152), shape(128, 768), shape(128, 1920),
         shape(192, 128, dtype=F32), shape(128, 128, dtype=F32)),
        "band_matrices",
        flops=4_000_000_000,
    )(w1, w2, first_bias[None], second_bias[None])
    xfar, xnear, t1o, tbo = lax.optimization_barrier((xfar, xnear, t1o, tbo))
    inner, outer = shape((planes + 4) * 48, Z), shape(128 + (planes + 4) * 16, Z)
    near, far = call(functools.partial(join_kernel, counts), (inner, inner), "join_strips")(xfar, xnear, f_rows, c_rows)
    rnear, rfar = exchange(near, far, "radial", "stream")
    half, half_f32 = shape(64, planes * Z), shape(64, planes * Z, dtype=F32)
    fs, cs, pre, back, hidden, dpre = call(
        functools.partial(own_kernel, counts),
        (shape(256, wide + 4 * Z), shape(384, wide), half_f32, half_f32, half, half),
        "own_rows",
        flops=1_000_000_000,
    )(xfar, xnear, f_rows, c_rows, t1o, tbo, b1)
    f_rows, fs = lax.optimization_barrier((f_rows, fs))
    near_outer, far_outer = call(functools.partial(join_outer_kernel, counts), (outer, outer), "join_outer")(
        xfar, xnear, f_rows, c_rows)
    rnear_outer, rfar_outer = exchange(near_outer, far_outer, "radial", "stream")
    hidden, payload = call(
        functools.partial(rim_kernel, counts),
        (shape(planes, 128, Z), shape(32, 384)),
        "gradients",
        (pltpu.VMEM((128, wide), BF16), pltpu.VMEM((256, wide), BF16), pltpu.VMEM((3, 32, 128), F32)),
        flops=2_000_000_000,
    )(rfar, rnear, fs, cs, pre, back, hidden, dpre, t1r, tbr, *const(e1t, e2t, rep1, rep2), *const(y1, y2, dtype=F32))

    steps = rounds("radial", 4) + rounds("stream", 4)[1:] + rounds("snap", 2)
    arrived = swap(payload, *steps[0])
    hidden = call(
        functools.partial(hidden_rim_kernel, counts),
        shape(planes + 4, 192, Z),
        "hidden_rim",
        (pltpu.VMEM((256, wide + 4 * Z), BF16),),
        flops=1_000_000_000,
    )(rfar, rnear, rfar_outer, rnear_outer, hidden, fs, t1o, t1d, b1)
    payload, hidden = lax.optimization_barrier((add(payload, arrived), hidden))
    payload = add(payload, stream_round(payload))
    arrived = swap(payload, *steps[1])
    closure = call(
        closure_kernel, shape(*cotangent.shape), "closure", (pltpu.VMEM((640, wide), BF16),), flops=1_000_000_000
    )(hidden, t2, b2)
    for step in steps[2:]:
        payload = add(payload, arrived)
        arrived = swap(payload, *step)

    cells = fields.shape[0] * fields.shape[2] * fields.shape[3] * fields.shape[4]
    for axis in ("stream", "radial", "snap"):
        cells *= lax.axis_size(axis)
    norm = float(1.0 / np.sqrt(np.float32(cells)))
    first, second, bias = call(
        functools.partial(finish_kernel, norm),
        (shape(CH * CI, 27, dtype=F32), shape(CH * CH, 27, dtype=F32), shape(1, CH, dtype=F32)),
        "finish",
    )(payload, *arrived)
    first = first.reshape(CH, CI, 27).transpose(2, 0, 1)
    second = second.reshape(CH, CH, 27).transpose(2, 0, 1)
    return (closure, first, second, bias[0])


def solution(mesh):
    split = P("snap", None, "stream", "radial", None)
    return jax.shard_map(
        local,
        mesh=mesh,
        in_specs=(split, P(), P(), P(), P(), split),
        out_specs=(split, P(), P(), P()),
        check_vma=False,
    )
```

```python
import functools

import numpy as np
import jax
import jax.numpy as jnp
from jax import lax
from jax.experimental import pallas as pl
from jax.experimental.pallas import tpu as pltpu
from jax.sharding import PartitionSpec as P

F32 = jnp.float32
BF16 = jnp.bfloat16
Z = 128
CI = 8
CH = 16
FAR = 100


def natural(n):
    return n // 8, n % 8


def y_first(n):
    return n % CH, n // CH


def rim(channels):
    def of(n):
        side, n = n // (2 * channels), n % (2 * channels)
        return n // 2, n % 2 + 10 * side - 2
    return of


def deep_rim(n):
    part, n = n // 16, n % 16
    return n // 2, n % 2 + 10 * (part // 2) - 2 + (part % 2) * (4 * (part // 2) - 2)


def table(channels, total, places):
    e = np.zeros((total, 128), np.float32)
    ys = np.full((1, total), FAR, np.float32)
    for c in range(3):
        for of, start, step in places:
            ch, y = of(np.arange(step))
            at = start + c * step + np.arange(step)
            e[at, c * channels + ch] = 1
            ys[0, at] = y
    return e, ys


def iota(rows, columns):
    return [lax.broadcasted_iota(jnp.int32, (rows, columns), d) for d in range(2)]


def one_hot(where):
    return jnp.where(where, 1.0, 0.0).astype(BF16)


def lane_y(of, width, step):
    lane = lax.broadcasted_iota(jnp.int32, (1, width), 1)
    return jnp.where(lane < 3 * step, of(lane % step)[1], FAR)


def place(rows, wanted, of, size, slot):
    row, lane = iota(rows, 128)
    return one_hot((of(lane % size)[0] == wanted(row)) & (lane // size == slot))


def row_table(rows, own):
    row, lane = iota(rows, CH)
    own_c, own_y = own(row)
    rim_c, rim_y = rim(CH)(row - 128)
    channel, y = jnp.where(row < 128, own_c, rim_c), jnp.where(row < 128, own_y, rim_y)
    return one_hot(channel == lane), y[:, :1]


def plane(ref, channels, x):
    v = ref[channels, x].astype(F32)
    return v.reshape(v.shape[0] * v.shape[1], v.shape[2])


def pick_rows(channels, low, high):
    half = channels * 2
    row, col = iota(2 * half, channels * 8)
    side = row // half
    return one_hot(col == (row % half // 2) * 8 + low + (high - low) * side + row % 2)


def partners(index, count):
    return index % 2 == 0, index > 0, index < count - 1


def sides(index, count, near, far):
    near_above, below, above = partners(index, count)
    low = jnp.where(near_above, far, near).astype(F32)
    high = jnp.where(near_above, near, far).astype(F32)
    return jnp.where(below, low, 0.0), jnp.where(above, high, 0.0)


def pack_kernel(inputs, near, far, f_rows, c_rows):
    up_first = lax.axis_index("stream") % 2 == 0
    count, at = inputs.shape[1], 0
    for channels, out, width in ((slice(0, CI), f_rows, 4), (slice(CI, CI + CH), c_rows, 2)):
        rows = [plane(inputs, channels, x) for x in range(count)]
        for x, v in enumerate(rows):
            out[x] = v.astype(BF16)
        for low, high in zip(rows[:width], rows[count - width:]):
            part = slice(at, at + low.shape[0])
            near[part] = jnp.where(up_first, high, low).astype(BF16)
            far[part] = jnp.where(up_first, low, high).astype(BF16)
            at += low.shape[0]


def x_planes(count, fields, cot, xnear, xfar, size):
    index = lax.axis_index("stream")
    inner = [fields[x].astype(F32) for x in range(count)]
    rims = [sides(index, size, xnear[n * 64:(n + 1) * 64], xfar[n * 64:(n + 1) * 64]) for n in range(4)]
    f = [low for low, _ in rims] + inner + [high for _, high in rims]
    inner = [cot[x].astype(F32) for x in range(count)]
    rims = [sides(index, size, xnear[256 + n * 128:384 + n * 128], xfar[256 + n * 128:384 + n * 128]) for n in range(2)]
    return f, [low for low, _ in rims] + inner + [high for _, high in rims]


def pick_strips(work, near, far):
    up_first = lax.axis_index("radial") % 2 == 0
    at = 0
    for pick, rows in work:
        half = pick.shape[0] // 2
        for v in rows:
            got = jnp.dot(pick, v.astype(BF16), preferred_element_type=F32)
            near[at:at + half] = jnp.where(up_first, got[half:], got[:half]).astype(BF16)
            far[at:at + half] = jnp.where(up_first, got[:half], got[half:]).astype(BF16)
            at += half


def join_kernel(counts, xfar, xnear, fields, cot, near, far):
    f, c = x_planes(fields.shape[0], fields, cot, xnear, xfar, counts[0])
    pick_strips([(pick_rows(CI, 0, 6), f[2:-2]), (pick_rows(CH, 0, 6), c)], near, far)


def join_outer_kernel(counts, xfar, xnear, fields, cot, near, far):
    f, _ = x_planes(fields.shape[0], fields, cot, xnear, xfar, counts[0])
    ends = f[:2] + f[-2:]
    pick_strips([(pick_rows(CI, 0, 6), ends), (pick_rows(CI, 2, 4), ends + f[2:-2])], near, far)


def spread(w, by_row, flip):
    taps = jnp.transpose(w[...].astype(F32))
    width = taps.shape[1]
    row = lax.broadcasted_iota(jnp.int32, (CH, width), 0)
    lane = lax.broadcasted_iota(jnp.int32, (CH, width), 1)
    mine = row == (lane // (width // CH) if by_row else lane % CH)
    found = []
    for c in range(3):
        rows = []
        for ab in range(9):
            t = 26 - (ab * 3 + c) if flip else ab * 3 + c
            rows.append(jnp.where(mine, jnp.broadcast_to(taps[t:t + 1], (CH, width)), 0.0))
        found.append(jnp.concatenate(rows, axis=0).astype(BF16))
    return found


def dots(pairs):
    total = None
    for v, w in pairs:
        part = jnp.dot(v, w, preferred_element_type=F32)
        total = part if total is None else total + part
    return total.astype(BF16)


def packed(parts, wanted, of, size):
    per = 128 // size
    places = [place(parts[0].shape[1], wanted, of, size, slot) for slot in range(min(per, 3))]
    tiles = [range(first, min(first + per, 3)) for first in range(0, 3, per)]
    return jnp.concatenate([dots([(parts[c], places[c % per]) for c in tile]) for tile in tiles], axis=1)


def band(wide, expand, ys, rows_y, t):
    rows, width = t.shape[0], wide.shape[1]
    for a in range(3):
        total = jnp.zeros((rows, width), F32)
        for b in range(3):
            part = jnp.dot(expand[:rows], wide[(a * 3 + b) * CH:(a * 3 + b + 1) * CH], preferred_element_type=F32)
            total = jnp.where(ys == rows_y[:rows] + 2 * (b - 1), part, total)
        t[:, a * width:(a + 1) * width] = total.astype(BF16)


def repeat_bias(bias, expand, out):
    column = jnp.sum(expand.astype(F32) * bias[...], axis=1, keepdims=True)
    out[...] = jnp.broadcast_to(column, out.shape)


def band_kernel(w1, w2, first_bias, second_bias, t1o, t1r, t1d, tbo, tbr, t2, b1, b2):
    expand, rows_y = row_table(192, y_first)
    parts = spread(w1, True, False)
    for of, step, t in ((natural, 64, t1o), (rim(CI), 32, t1r), (deep_rim, 64, t1d)):
        wide = packed(parts, lambda n: n % CI, of, step)
        band(wide, expand, lane_y(of, wide.shape[1], step), rows_y, t)
    parts = spread(w2, False, True)
    for of, step, t in ((natural, 128, tbo), (rim(CH), 64, tbr)):
        wide = packed(parts, lambda n: n // CH, of, step)
        band(wide, expand, lane_y(of, wide.shape[1], step), rows_y, t)
    repeat_bias(first_bias, expand, b1)
    expand, rows_y = row_table(128, natural)
    parts = spread(w2, True, False)
    wide = [packed(parts, lambda n: n % CH, of, step) for of, step in ((y_first, 128), (rim(CH), 64))]
    ys = jnp.concatenate([lane_y(y_first, 384, 128), lane_y(rim(CH), 256, 64)], axis=1)
    band(jnp.concatenate(wide, axis=1), expand, ys, rows_y, t2)
    repeat_bias(second_bias, expand, b2)


def shifted(v):
    lane = lax.broadcasted_iota(jnp.int32, v.shape, 1)
    before = jnp.where(lane >= 2, pltpu.roll(v, 2, 1), 0.0)
    after = jnp.where(lane < Z - 2, pltpu.roll(v, Z - 2, 1), 0.0)
    return before.astype(BF16), v.astype(BF16), after.astype(BF16)


def store_wide(ref, p, v):
    at = slice(p * Z, (p + 1) * Z)
    for c, piece in enumerate(shifted(v)):
        ref[c * 128:(c + 1) * 128, at] = piece[:128]
        ref[384 + c * 64:384 + (c + 1) * 64, at] = piece[128:]
    ref[576:, at] = jnp.zeros((64, Z), BF16)


def stacked(ref, lanes):
    return jnp.concatenate([ref[:, a * 256:a * 256 + lanes] for a in range(3)], axis=0)


def gelu_share(pre):
    return 0.5 * (1.0 + lax.erf(pre * 0.7071067811865476))


def gelu_slope(pre, share):
    return share + pre * jnp.exp(-0.5 * pre * pre) * 0.3989422804014327


def edges(v):
    return jnp.concatenate([v[:32], v[96:128]], axis=0)


def whole(edge, middle):
    return jnp.concatenate([edge[:32], middle, edge[32:]], axis=0)


def own_kernel(counts, xfar, xnear, fields, cot, t1, tb, b1, fs, cs, pre, back, hidden, dpre):
    count, lanes = fields.shape[0], pre.shape[1]
    f, c = x_planes(count, fields, cot, xnear, xfar, counts[0])
    for ref, rows in ((fs, f), (cs, c)):
        for p, v in enumerate(rows):
            for n, piece in enumerate(shifted(v)):
                ref[n * v.shape[0]:(n + 1) * v.shape[0], p * Z:(p + 1) * Z] = piece
    fs[192:] = jnp.zeros((64, fs.shape[1]), BF16)
    rows = jnp.concatenate([fs[:, a * 256 + 256:a * 256 + 256 + lanes] for a in range(3)], axis=0)
    first = jnp.dot(t1[:128], rows, preferred_element_type=F32) + b1[:128, :1]
    second = jnp.dot(tb[...], stacked(cs, lanes), preferred_element_type=F32)
    pre[...] = edges(first)
    back[...] = edges(second)
    first, second = first[32:96], second[32:96]
    share = gelu_share(first)
    hidden[...] = (first * share).astype(BF16)
    dpre[...] = (second * gelu_slope(first, share)).astype(BF16)


def rounded(s):
    lost = s - s.astype(BF16).astype(F32)
    row = lax.broadcasted_iota(jnp.int32, s.shape, 0)
    return (s + jnp.where(row == 28, pltpu.roll(lost, 1, 0), 0.0)).astype(BF16)


def two_dots(v, w):
    high = v.astype(BF16)
    low = (v - high.astype(F32)).astype(BF16)
    return jnp.dot(high, w, preferred_element_type=F32) + jnp.dot(low, w, preferred_element_type=F32)


def rim_kernel(counts, rfar, rnear, fs, cs, pre_own, back_own, hidden_own, dpre_own, t1, tb, e1t, e2t, rep1, rep2, y1, y2,
               hidden_out, payload, fr, cr, taps):
    count = hidden_out.shape[0]
    lanes = count * Z
    radial = lax.axis_index("radial")
    at = 0
    for ref, half in ((fr, 16), (cr, 32)):
        for p in range(count + 4):
            low, high = sides(radial, counts[1], rnear[at:at + half], rfar[at:at + half])
            for n, piece in enumerate(shifted(jnp.concatenate([low, high], axis=0))):
                ref[n * 2 * half:(n + 1) * 2 * half, p * Z:(p + 1) * Z] = piece
            at += half
        ref[6 * half:] = jnp.zeros((2 * half, ref.shape[1]), BF16)
    pre = pre_own[...] + jnp.dot(edges(t1), stacked(fr, lanes), preferred_element_type=F32)
    share = gelu_share(pre)
    hidden = whole((pre * share).astype(BF16), hidden_own[...])
    for x in range(count):
        hidden_out[x] = hidden[:, x * Z:(x + 1) * Z]
    back = back_own[...] + jnp.dot(edges(tb), stacked(cr, lanes), preferred_element_type=F32)
    dpre = whole((back * gelu_slope(pre, share)).astype(BF16), dpre_own[...])
    over_lanes = (((1,), (1,)), ((), ()))
    ones, twos = [], []
    sums = [[None] * 3, [None] * 3]
    for pair in range(count // 2 + 2):
        taps_here = [a for a in range(3) if 0 <= pair - a < count // 2]
        at = slice(pair * 256, (pair + 1) * 256)
        shifted_rows = (
            jnp.concatenate([fs[:, (pair + 1) * 256:(pair + 2) * 256], fr[:, at]], axis=0),
            jnp.concatenate([cs[:, at], cr[:, at]], axis=0),
        )
        for here, rows, total in zip((dpre, hidden), shifted_rows, sums):
            here = jnp.concatenate([here[:, (pair - a) * 256:(pair - a + 1) * 256] for a in taps_here], axis=0)
            got = lax.dot_general(here, rows, over_lanes, preferred_element_type=F32)
            for n, a in enumerate(taps_here):
                part = got[n * 128:(n + 1) * 128]
                total[a] = part if total[a] is None else total[a] + part
    for a in range(3):
        g1, g2 = sums[0][a], sums[1][a]
        for b in range(3):
            for g, ys, out in ((g1, y1, ones), (g2, y2, twos)):
                total = jnp.zeros((CH, g.shape[1]), F32)
                for y in range(8):
                    total = jnp.where(ys[...] == float(y + 2 * (b - 1)), g[y * CH:(y + 1) * CH], total)
                out.append(total)
    taps[:, 24:] = jnp.zeros((3, 8, 128), F32)
    for parts, et, rep, at, width in ((ones, e1t, rep1, 0, 128), (twos[::-1], e2t, rep2, 1, 256)):
        sums = two_dots(jnp.concatenate(parts, axis=0), et[...])
        wide = two_dots(sums, rep[...])
        row = lax.broadcasted_iota(jnp.int32, wide.shape, 0) % CH
        lane = lax.broadcasted_iota(jnp.int32, wide.shape, 1) % width
        mine = row == (lane // CI if width == 128 else lane % CH)
        total = jnp.sum(jnp.where(mine, wide, 0.0).reshape(9, CH, 3 * width), axis=1)
        for c in range(3):
            first = c if width == 128 else 2 - c
            for n in range(width // 128):
                taps[at + n, pl.ds(first, 9, stride=3)] = total[:, c * width + n * 128:c * width + (n + 1) * 128]
    bias = jnp.sum(dpre.astype(F32), axis=1, keepdims=True)
    bias = sum(bias[y * CH:(y + 1) * CH] for y in range(8))
    row = lax.broadcasted_iota(jnp.int32, (CH, 128), 0)
    lane = lax.broadcasted_iota(jnp.int32, (CH, 128), 1)
    taps[0, 27:28] = jnp.sum(jnp.where(row == lane, bias, 0.0), axis=0, keepdims=True)
    payload[...] = rounded(jnp.concatenate([taps[n] for n in range(3)], axis=1))


def hidden_rim_kernel(counts, rfar, rnear, rfar_outer, rnear_outer, hidden, fs, t1o, t1d, b1, hidden_out, fr):
    count = hidden.shape[0]
    stream, radial = lax.axis_index("stream"), lax.axis_index("radial")
    for p in range(count + 8):
        end = p if p < 2 else p - count - 4 if p >= count + 6 else None
        if end is None:
            near, outer = (rnear, rfar, (p - 2) * 16), (rnear_outer, rfar_outer, 128 + (p - 2) * 16)
        else:
            near, outer = (rnear_outer, rfar_outer, end * 16), (rnear_outer, rfar_outer, 64 + end * 16)
        parts = [sides(radial, counts[1], n[at:at + 16], f[at:at + 16]) for n, f, at in (near, outer)]
        rows = jnp.concatenate([part[side] for side in range(2) for part in parts], axis=0)
        for n, piece in enumerate(shifted(rows)):
            fr[n * 64:(n + 1) * 64, p * Z:(p + 1) * Z] = piece
    fr[192:] = jnp.zeros((64, fr.shape[1]), BF16)

    def gelu(rows, lanes):
        total = b1[rows, :1]
        for t, ref in ((t1o, fs), (t1d, fr)):
            cells = [jnp.concatenate([ref[:, a * 256 + at:a * 256 + at + size] for at, size in lanes], axis=1) for a in range(3)]
            total = total + jnp.dot(t[rows], jnp.concatenate(cells, axis=0), preferred_element_type=F32)
        return total * gelu_share(total)

    own = gelu(slice(0, 128), ((0, 2 * Z), ((count + 2) * Z, 2 * Z)))
    rims = gelu(slice(128, 192), ((0, (count + 4) * Z),))
    rims = jnp.concatenate([jnp.where(radial > 0, rims[:32], 0.0), jnp.where(radial < counts[1] - 1, rims[32:], 0.0)], axis=0)
    for p in range(count + 4):
        rim_rows = rims[:, p * Z:(p + 1) * Z]
        if 2 <= p < count + 2:
            hidden_out[p, :128] = hidden[p - 2]
            hidden_out[p, 128:] = rim_rows.astype(BF16)
        else:
            at = p if p < 2 else p - count
            inside = stream > 0 if p < 2 else stream < counts[0] - 1
            rows = jnp.concatenate([own[:, at * Z:(at + 1) * Z], rim_rows], axis=0)
            hidden_out[p] = jnp.where(inside, rows, 0.0).astype(BF16)


def closure_kernel(hidden, t2, b2, closure, hs):
    count = closure.shape[2]
    for p in range(count + 4):
        store_wide(hs, p, hidden[p].astype(F32))
    out = (jnp.dot(t2[...], stacked(hs, count * Z), preferred_element_type=F32) + b2[:, :1]).astype(BF16)
    for x in range(count):
        closure[0, :, x] = out[:, x * Z:(x + 1) * Z].reshape(CH, 8, Z)


def summed(parts):
    parts = [part[...].astype(F32) for part in parts]
    while len(parts) > 1:
        parts = [v + w for v, w in zip(parts[::2], parts[1::2])]
    return parts[0]


def add_kernel(*refs):
    refs[-1][...] = rounded(summed(refs[:-1]))


def finish_kernel(norm, *refs):
    *parts, first, second, bias = refs
    scaled = summed(parts) * norm
    flipped = jnp.transpose(scaled)
    first[...] = flipped[:128, :27]
    second[...] = flipped[128:, :27]
    bias[...] = scaled[27:28, :CH] + scaled[28:29, :CH]


def call(kernel, outs, name, scratch=(), flops=10_000_000, **specs):
    return pl.pallas_call(
        kernel,
        out_shape=outs,
        **specs,
        scratch_shapes=list(scratch),
        compiler_params=pltpu.CompilerParams(vmem_limit_bytes=32 * 1024 * 1024),
        cost_estimate=pl.CostEstimate(flops=flops, bytes_accessed=1_000_000, transcendentals=0),
        name=name,
    )


def shape(*dims, dtype=BF16):
    return jax.ShapeDtypeStruct(dims, dtype)


def exchange(near, far, axis, other):
    count, others = lax.axis_size(axis), lax.axis_size(other)
    axes = tuple(name for name in ("stream", "radial", "snap") if name in (axis, other))
    flat = (others, 1) if axes[0] == axis else (1, count)
    pairs = []
    for i in range(count):
        for j in range(others):
            end = i in (0, count - 1)
            to = (i, j ^ 1 if others % 2 == 0 else j) if end else (i - 1 + 2 * (i % 2), j)
            pairs.append((i * flat[0] + j * flat[1], to[0] * flat[0] + to[1] * flat[1]))
    far = lax.ppermute(far, axes, pairs)
    return lax.ppermute(near, axis, [(i, i ^ 1) for i in range(count)]), far


def swap(v, axis, masks):
    count = lax.axis_size(axis)
    return [lax.ppermute(v, axis, [(i, i ^ mask) for i in range(count)]) for mask in masks]


def stream_round(v):
    count, others = lax.axis_size("stream"), lax.axis_size("radial")
    pairs = [(i * others + j, (i ^ (1 + j % 2)) * others + j) for i in range(count) for j in range(others)]
    apart = lax.ppermute(v, ("stream", "radial"), pairs)
    return [*swap(v, "stream", [3]), apart, *swap(apart, "radial", [1])]


def add(v, arrived):
    return call(add_kernel, shape(*v.shape), "add_parts")(v, *arrived)


def rounds(axis, most):
    found, step = [], 1
    while step < lax.axis_size(axis):
        masks = [step * n for n in range(1, most if step * most <= lax.axis_size(axis) else 2)]
        found.append((axis, masks))
        step *= len(masks) + 1
    return found


def local(fields, first_weight, first_bias, second_weight, second_bias, cotangent):
    e1t, y1 = table(CI, 384, ((natural, 0, 64), (rim(CI), 256, 32)))
    e2t, y2 = table(CH, 640, ((natural, 0, 128), (rim(CH), 384, 64)))
    rep1, rep2 = np.zeros((128, 384), np.float32), np.zeros((128, 768), np.float32)
    for c in range(3):
        rep1[c * CI:(c + 1) * CI, c * 128:(c + 1) * 128] = np.tile(np.eye(CI), (1, CH))
        rep2[c * CH:(c + 1) * CH, c * 256:(c + 1) * 256] = np.repeat(np.eye(CH), CH, axis=1)

    def const(*arrays, dtype=BF16):
        return [jnp.asarray(v, dtype) for v in arrays]

    planes = fields.shape[2]
    w1 = first_weight.transpose(1, 2, 0).reshape(CH * CI, 27)
    w2 = second_weight.transpose(1, 2, 0).reshape(CH * CH, 27)
    near, far, f_rows, c_rows = call(
        pack_kernel,
        (shape(512, Z), shape(512, Z), shape(planes, CI * 8, Z), shape(planes, CH * 8, Z)),
        "pack_strips",
        flops=4_000_000_000,
    )(jnp.concatenate([fields[0], cotangent[0]], axis=0))
    xnear, xfar = exchange(near, far, "stream", "radial")
    wide = (planes + 4) * Z
    counts = (lax.axis_size("stream"), lax.axis_size("radial"))
    t1o, t1r, t1d, tbo, tbr, t2, b1, b2 = call(
        band_kernel,
        (shape(192, 768), shape(128, 384), shape(192, 768), shape(128, 1152), shape(128, 768), shape(128, 1920),
         shape(192, 128, dtype=F32), shape(128, 128, dtype=F32)),
        "band_matrices",
        flops=4_000_000_000,
    )(w1, w2, first_bias[None], second_bias[None])
    xfar, xnear, t1o, tbo = lax.optimization_barrier((xfar, xnear, t1o, tbo))
    inner, outer = shape((planes + 4) * 48, Z), shape(128 + (planes + 4) * 16, Z)
    near, far = call(functools.partial(join_kernel, counts), (inner, inner), "join_strips")(xfar, xnear, f_rows, c_rows)
    rnear, rfar = exchange(near, far, "radial", "stream")
    half, half_f32 = shape(64, planes * Z), shape(64, planes * Z, dtype=F32)
    fs, cs, pre, back, hidden, dpre = call(
        functools.partial(own_kernel, counts),
        (shape(256, wide + 4 * Z), shape(384, wide), half_f32, half_f32, half, half),
        "own_rows",
        flops=1_000_000_000,
    )(xfar, xnear, f_rows, c_rows, t1o, tbo, b1)
    f_rows, fs = lax.optimization_barrier((f_rows, fs))
    near_outer, far_outer = call(functools.partial(join_outer_kernel, counts), (outer, outer), "join_outer")(
        xfar, xnear, f_rows, c_rows)
    rnear_outer, rfar_outer = exchange(near_outer, far_outer, "radial", "stream")
    hidden, payload = call(
        functools.partial(rim_kernel, counts),
        (shape(planes, 128, Z), shape(32, 384)),
        "gradients",
        (pltpu.VMEM((128, wide), BF16), pltpu.VMEM((256, wide), BF16), pltpu.VMEM((3, 32, 128), F32)),
        flops=2_000_000_000,
    )(rfar, rnear, fs, cs, pre, back, hidden, dpre, t1r, tbr, *const(e1t, e2t, rep1, rep2), *const(y1, y2, dtype=F32))

    steps = rounds("radial", 4) + rounds("stream", 4)[1:] + rounds("snap", 2)
    arrived = swap(payload, *steps[0])
    hidden = call(
        functools.partial(hidden_rim_kernel, counts),
        shape(planes + 4, 192, Z),
        "hidden_rim",
        (pltpu.VMEM((256, wide + 4 * Z), BF16),),
        flops=1_000_000_000,
    )(rfar, rnear, rfar_outer, rnear_outer, hidden, fs, t1o, t1d, b1)
    payload, hidden = lax.optimization_barrier((add(payload, arrived), hidden))
    payload = add(payload, stream_round(payload))
    arrived = swap(payload, *steps[1])
    closure = call(
        closure_kernel, shape(*cotangent.shape), "closure", (pltpu.VMEM((640, wide), BF16),), flops=1_000_000_000
    )(hidden, t2, b2)
    for step in steps[2:]:
        payload = add(payload, arrived)
        arrived = swap(payload, *step)

    cells = fields.shape[0] * fields.shape[2] * fields.shape[3] * fields.shape[4]
    for axis in ("stream", "radial", "snap"):
        cells *= lax.axis_size(axis)
    norm = float(1.0 / np.sqrt(np.float32(cells)))
    first, second, bias = call(
        functools.partial(finish_kernel, norm),
        (shape(CH * CI, 27, dtype=F32), shape(CH * CH, 27, dtype=F32), shape(1, CH, dtype=F32)),
        "finish",
    )(payload, *arrived)
    first = first.reshape(CH, CI, 27).transpose(2, 0, 1)
    second = second.reshape(CH, CH, 27).transpose(2, 0, 1)
    return (closure, first, second, bias[0])


def solution(mesh):
    split = P("snap", None, "stream", "radial", None)
    return jax.shard_map(
        local,
        mesh=mesh,
        in_specs=(split, P(), P(), P(), P(), split),
        out_specs=(split, P(), P(), P()),
        check_vma=False,
    )
```

```python
import functools

import numpy as np
import jax
import jax.numpy as jnp
from jax import lax
from jax.experimental import pallas as pl
from jax.experimental.pallas import tpu as pltpu
from jax.sharding import PartitionSpec as P

F32 = jnp.float32
BF16 = jnp.bfloat16
Z = 128
CI = 8
CH = 16
FAR = 100


def natural(n):
    return n // 8, n % 8


def y_first(n):
    return n % CH, n // CH


def rim(channels):
    def of(n):
        side, n = n // (2 * channels), n % (2 * channels)
        return n // 2, n % 2 + 10 * side - 2
    return of


def deep_rim(n):
    part, n = n // 16, n % 16
    return n // 2, n % 2 + 10 * (part // 2) - 2 + (part % 2) * (4 * (part // 2) - 2)


def table(channels, total, places):
    e = np.zeros((total, 128), np.float32)
    ys = np.full((1, total), FAR, np.float32)
    for c in range(3):
        for of, start, step in places:
            ch, y = of(np.arange(step))
            at = start + c * step + np.arange(step)
            e[at, c * channels + ch] = 1
            ys[0, at] = y
    return e, ys


def iota(rows, columns):
    return [lax.broadcasted_iota(jnp.int32, (rows, columns), d) for d in range(2)]


def one_hot(where):
    return jnp.where(where, 1.0, 0.0).astype(BF16)


def lane_y(of, width, step):
    lane = lax.broadcasted_iota(jnp.int32, (1, width), 1)
    return jnp.where(lane < 3 * step, of(lane % step)[1], FAR)


def place(rows, wanted, of, size, slot):
    row, lane = iota(rows, 128)
    return one_hot((of(lane % size)[0] == wanted(row)) & (lane // size == slot))


def row_table(rows, own):
    row, lane = iota(rows, CH)
    own_c, own_y = own(row)
    rim_c, rim_y = rim(CH)(row - 128)
    channel, y = jnp.where(row < 128, own_c, rim_c), jnp.where(row < 128, own_y, rim_y)
    return one_hot(channel == lane), y[:, :1]


def plane(ref, channels, x):
    v = ref[channels, x].astype(F32)
    return v.reshape(v.shape[0] * v.shape[1], v.shape[2])


def pick_rows(channels, low, high):
    half = channels * 2
    row, col = iota(2 * half, channels * 8)
    side = row // half
    return one_hot(col == (row % half // 2) * 8 + low + (high - low) * side + row % 2)


def partners(index, count):
    return index % 2 == 0, index > 0, index < count - 1


def sides(index, count, near, far):
    near_above, below, above = partners(index, count)
    low = jnp.where(near_above, far, near).astype(F32)
    high = jnp.where(near_above, near, far).astype(F32)
    return jnp.where(below, low, 0.0), jnp.where(above, high, 0.0)


def pack_kernel(inputs, near, far, f_rows, c_rows):
    up_first = lax.axis_index("stream") % 2 == 0
    count, at = inputs.shape[1], 0
    for channels, out, width in ((slice(0, CI), f_rows, 4), (slice(CI, CI + CH), c_rows, 2)):
        rows = [plane(inputs, channels, x) for x in range(count)]
        for x, v in enumerate(rows):
            out[x] = v.astype(BF16)
        for low, high in zip(rows[:width], rows[count - width:]):
            part = slice(at, at + low.shape[0])
            near[part] = jnp.where(up_first, high, low).astype(BF16)
            far[part] = jnp.where(up_first, low, high).astype(BF16)
            at += low.shape[0]


def x_planes(count, fields, cot, xnear, xfar, size):
    index = lax.axis_index("stream")
    inner = [fields[x].astype(F32) for x in range(count)]
    rims = [sides(index, size, xnear[n * 64:(n + 1) * 64], xfar[n * 64:(n + 1) * 64]) for n in range(4)]
    f = [low for low, _ in rims] + inner + [high for _, high in rims]
    inner = [cot[x].astype(F32) for x in range(count)]
    rims = [sides(index, size, xnear[256 + n * 128:384 + n * 128], xfar[256 + n * 128:384 + n * 128]) for n in range(2)]
    return f, [low for low, _ in rims] + inner + [high for _, high in rims]


def pick_strips(work, near, far):
    up_first = lax.axis_index("radial") % 2 == 0
    at = 0
    for pick, rows in work:
        half = pick.shape[0] // 2
        for v in rows:
            got = jnp.dot(pick, v.astype(BF16), preferred_element_type=F32)
            near[at:at + half] = jnp.where(up_first, got[half:], got[:half]).astype(BF16)
            far[at:at + half] = jnp.where(up_first, got[:half], got[half:]).astype(BF16)
            at += half


def own_strips_kernel(fields, cot, near, far):
    planes = range(fields.shape[0])
    pick_strips([(pick_rows(CI, 0, 6), [fields[x] for x in planes]), (pick_rows(CH, 0, 6), [cot[x] for x in planes])], near, far)


def join_kernel(counts, xfar, xnear, near_own, far_own, near, far):
    up_first = lax.axis_index("radial") % 2 == 0
    index, count = lax.axis_index("stream"), near_own.shape[0] // 48
    at = own_at = 0
    for pick, rows, start, skip, half in ((pick_rows(CI, 0, 6), 64, 0, 2, 16), (pick_rows(CH, 0, 6), 128, 256, 0, 32)):
        places = [slice(start + n * rows, start + (n + 1) * rows) for n in range(4 if skip else 2)]
        rims = [sides(index, counts[0], xnear[place], xfar[place]) for place in places]
        below, above = [low for low, _ in rims[skip:]], [high for _, high in rims[:2]]
        for offset, part in ((0, below), (count + 2, above)):
            for n, v in enumerate(part):
                got = jnp.dot(pick, v.astype(BF16), preferred_element_type=F32)
                place = slice(at + (offset + n) * half, at + (offset + n + 1) * half)
                near[place] = jnp.where(up_first, got[half:], got[:half]).astype(BF16)
                far[place] = jnp.where(up_first, got[:half], got[half:]).astype(BF16)
        inside = slice(at + 2 * half, at + (2 + count) * half)
        near[inside] = near_own[own_at:own_at + count * half]
        far[inside] = far_own[own_at:own_at + count * half]
        at += (count + 4) * half
        own_at += count * half


def join_outer_kernel(counts, xfar, xnear, fields, cot, near, far):
    f, _ = x_planes(fields.shape[0], fields, cot, xnear, xfar, counts[0])
    ends = f[:2] + f[-2:]
    pick_strips([(pick_rows(CI, 0, 6), ends), (pick_rows(CI, 2, 4), ends + f[2:-2])], near, far)


def spread(w, by_row, flip):
    taps = jnp.transpose(w[...].astype(F32))
    width = taps.shape[1]
    row = lax.broadcasted_iota(jnp.int32, (CH, width), 0)
    lane = lax.broadcasted_iota(jnp.int32, (CH, width), 1)
    mine = row == (lane // (width // CH) if by_row else lane % CH)
    found = []
    for c in range(3):
        rows = []
        for ab in range(9):
            t = 26 - (ab * 3 + c) if flip else ab * 3 + c
            rows.append(jnp.where(mine, jnp.broadcast_to(taps[t:t + 1], (CH, width)), 0.0))
        found.append(jnp.concatenate(rows, axis=0).astype(BF16))
    return found


def dots(pairs):
    total = None
    for v, w in pairs:
        part = jnp.dot(v, w, preferred_element_type=F32)
        total = part if total is None else total + part
    return total.astype(BF16)


def packed(parts, wanted, of, size):
    per = 128 // size
    places = [place(parts[0].shape[1], wanted, of, size, slot) for slot in range(min(per, 3))]
    tiles = [range(first, min(first + per, 3)) for first in range(0, 3, per)]
    return jnp.concatenate([dots([(parts[c], places[c % per]) for c in tile]) for tile in tiles], axis=1)


def band(wide, expand, ys, rows_y, t):
    rows, width = t.shape[0], wide.shape[1]
    for a in range(3):
        total = jnp.zeros((rows, width), F32)
        for b in range(3):
            part = jnp.dot(expand[:rows], wide[(a * 3 + b) * CH:(a * 3 + b + 1) * CH], preferred_element_type=F32)
            total = jnp.where(ys == rows_y[:rows] + 2 * (b - 1), part, total)
        t[:, a * width:(a + 1) * width] = total.astype(BF16)


def repeat_bias(bias, expand, out):
    column = jnp.sum(expand.astype(F32) * bias[...], axis=1, keepdims=True)
    out[...] = jnp.broadcast_to(column, out.shape)


def band_kernel(w1, w2, first_bias, second_bias, t1o, t1r, t1d, tbo, tbr, t2, b1, b2):
    expand, rows_y = row_table(192, y_first)
    parts = spread(w1, True, False)
    for of, step, t in ((natural, 64, t1o), (rim(CI), 32, t1r), (deep_rim, 64, t1d)):
        wide = packed(parts, lambda n: n % CI, of, step)
        band(wide, expand, lane_y(of, wide.shape[1], step), rows_y, t)
    parts = spread(w2, False, True)
    for of, step, t in ((natural, 128, tbo), (rim(CH), 64, tbr)):
        wide = packed(parts, lambda n: n // CH, of, step)
        band(wide, expand, lane_y(of, wide.shape[1], step), rows_y, t)
    repeat_bias(first_bias, expand, b1)
    expand, rows_y = row_table(128, natural)
    parts = spread(w2, True, False)
    wide = [packed(parts, lambda n: n % CH, of, step) for of, step in ((y_first, 128), (rim(CH), 64))]
    ys = jnp.concatenate([lane_y(y_first, 384, 128), lane_y(rim(CH), 256, 64)], axis=1)
    band(jnp.concatenate(wide, axis=1), expand, ys, rows_y, t2)
    repeat_bias(second_bias, expand, b2)


def shifted(v):
    lane = lax.broadcasted_iota(jnp.int32, v.shape, 1)
    before = jnp.where(lane >= 2, pltpu.roll(v, 2, 1), 0.0)
    after = jnp.where(lane < Z - 2, pltpu.roll(v, Z - 2, 1), 0.0)
    return before.astype(BF16), v.astype(BF16), after.astype(BF16)


def store_wide(ref, p, v):
    at = slice(p * Z, (p + 1) * Z)
    for c, piece in enumerate(shifted(v)):
        ref[c * 128:(c + 1) * 128, at] = piece[:128]
        ref[384 + c * 64:384 + (c + 1) * 64, at] = piece[128:]
    ref[576:, at] = jnp.zeros((64, Z), BF16)


def stacked(ref, lanes):
    return jnp.concatenate([ref[:, a * 256:a * 256 + lanes] for a in range(3)], axis=0)


def gelu_share(pre):
    return 0.5 * (1.0 + lax.erf(pre * 0.7071067811865476))


def gelu_slope(pre, share):
    return share + pre * jnp.exp(-0.5 * pre * pre) * 0.3989422804014327


def edges(v):
    return jnp.concatenate([v[:32], v[96:128]], axis=0)


def whole(edge, middle):
    return jnp.concatenate([edge[:32], middle, edge[32:]], axis=0)


def own_kernel(counts, xfar, xnear, fields, cot, t1, tb, b1, fs, cs, pre, back, hidden, dpre):
    count, lanes = fields.shape[0], pre.shape[1]
    f, c = x_planes(count, fields, cot, xnear, xfar, counts[0])
    for ref, rows in ((fs, f), (cs, c)):
        for p, v in enumerate(rows):
            for n, piece in enumerate(shifted(v)):
                ref[n * v.shape[0]:(n + 1) * v.shape[0], p * Z:(p + 1) * Z] = piece
    fs[192:] = jnp.zeros((64, fs.shape[1]), BF16)
    rows = jnp.concatenate([fs[:, a * 256 + 256:a * 256 + 256 + lanes] for a in range(3)], axis=0)
    first = jnp.dot(t1[:128], rows, preferred_element_type=F32) + b1[:128, :1]
    second = jnp.dot(tb[...], stacked(cs, lanes), preferred_element_type=F32)
    pre[...] = edges(first)
    back[...] = edges(second)
    first, second = first[32:96], second[32:96]
    share = gelu_share(first)
    hidden[...] = (first * share).astype(BF16)
    dpre[...] = (second * gelu_slope(first, share)).astype(BF16)


def rounded(s):
    lost = s - s.astype(BF16).astype(F32)
    row = lax.broadcasted_iota(jnp.int32, s.shape, 0)
    return (s + jnp.where(row == 28, pltpu.roll(lost, 1, 0), 0.0)).astype(BF16)


def two_dots(v, w):
    high = v.astype(BF16)
    low = (v - high.astype(F32)).astype(BF16)
    return jnp.dot(high, w, preferred_element_type=F32) + jnp.dot(low, w, preferred_element_type=F32)


def rim_kernel(counts, rfar, rnear, fs, cs, pre_own, back_own, hidden_own, dpre_own, t1, tb, e1t, e2t, rep1, rep2, y1, y2,
               hidden_out, payload, fr, cr, taps):
    count = hidden_out.shape[0]
    lanes = count * Z
    radial = lax.axis_index("radial")
    at = 0
    for ref, half in ((fr, 16), (cr, 32)):
        for p in range(count + 4):
            low, high = sides(radial, counts[1], rnear[at:at + half], rfar[at:at + half])
            for n, piece in enumerate(shifted(jnp.concatenate([low, high], axis=0))):
                ref[n * 2 * half:(n + 1) * 2 * half, p * Z:(p + 1) * Z] = piece
            at += half
        ref[6 * half:] = jnp.zeros((2 * half, ref.shape[1]), BF16)
    pre = pre_own[...] + jnp.dot(edges(t1), stacked(fr, lanes), preferred_element_type=F32)
    share = gelu_share(pre)
    hidden = whole((pre * share).astype(BF16), hidden_own[...])
    for x in range(count):
        hidden_out[x] = hidden[:, x * Z:(x + 1) * Z]
    back = back_own[...] + jnp.dot(edges(tb), stacked(cr, lanes), preferred_element_type=F32)
    dpre = whole((back * gelu_slope(pre, share)).astype(BF16), dpre_own[...])
    over_lanes = (((1,), (1,)), ((), ()))
    ones, twos = [], []
    sums = [[None] * 3, [None] * 3]
    for pair in range(count // 2 + 2):
        taps_here = [a for a in range(3) if 0 <= pair - a < count // 2]
        at = slice(pair * 256, (pair + 1) * 256)
        shifted_rows = (
            jnp.concatenate([fs[:, (pair + 1) * 256:(pair + 2) * 256], fr[:, at]], axis=0),
            jnp.concatenate([cs[:, at], cr[:, at]], axis=0),
        )
        for here, rows, total in zip((dpre, hidden), shifted_rows, sums):
            here = jnp.concatenate([here[:, (pair - a) * 256:(pair - a + 1) * 256] for a in taps_here], axis=0)
            got = lax.dot_general(here, rows, over_lanes, preferred_element_type=F32)
            for n, a in enumerate(taps_here):
                part = got[n * 128:(n + 1) * 128]
                total[a] = part if total[a] is None else total[a] + part
    for a in range(3):
        g1, g2 = sums[0][a], sums[1][a]
        for b in range(3):
            for g, ys, out in ((g1, y1, ones), (g2, y2, twos)):
                total = jnp.zeros((CH, g.shape[1]), F32)
                for y in range(8):
                    total = jnp.where(ys[...] == float(y + 2 * (b - 1)), g[y * CH:(y + 1) * CH], total)
                out.append(total)
    taps[:, 24:] = jnp.zeros((3, 8, 128), F32)
    for parts, et, rep, at, width in ((ones, e1t, rep1, 0, 128), (twos[::-1], e2t, rep2, 1, 256)):
        sums = two_dots(jnp.concatenate(parts, axis=0), et[...])
        wide = two_dots(sums, rep[...])
        row = lax.broadcasted_iota(jnp.int32, wide.shape, 0) % CH
        lane = lax.broadcasted_iota(jnp.int32, wide.shape, 1) % width
        mine = row == (lane // CI if width == 128 else lane % CH)
        total = jnp.sum(jnp.where(mine, wide, 0.0).reshape(9, CH, 3 * width), axis=1)
        for c in range(3):
            first = c if width == 128 else 2 - c
            for n in range(width // 128):
                taps[at + n, pl.ds(first, 9, stride=3)] = total[:, c * width + n * 128:c * width + (n + 1) * 128]
    bias = jnp.sum(dpre.astype(F32), axis=1, keepdims=True)
    bias = sum(bias[y * CH:(y + 1) * CH] for y in range(8))
    row = lax.broadcasted_iota(jnp.int32, (CH, 128), 0)
    lane = lax.broadcasted_iota(jnp.int32, (CH, 128), 1)
    taps[0, 27:28] = jnp.sum(jnp.where(row == lane, bias, 0.0), axis=0, keepdims=True)
    payload[...] = rounded(jnp.concatenate([taps[n] for n in range(3)], axis=1))


def hidden_rim_kernel(counts, rfar, rnear, rfar_outer, rnear_outer, hidden, fs, t1o, t1d, b1, hidden_out, fr):
    count = hidden.shape[0]
    stream, radial = lax.axis_index("stream"), lax.axis_index("radial")
    for p in range(count + 8):
        end = p if p < 2 else p - count - 4 if p >= count + 6 else None
        if end is None:
            near, outer = (rnear, rfar, (p - 2) * 16), (rnear_outer, rfar_outer, 128 + (p - 2) * 16)
        else:
            near, outer = (rnear_outer, rfar_outer, end * 16), (rnear_outer, rfar_outer, 64 + end * 16)
        parts = [sides(radial, counts[1], n[at:at + 16], f[at:at + 16]) for n, f, at in (near, outer)]
        rows = jnp.concatenate([part[side] for side in range(2) for part in parts], axis=0)
        for n, piece in enumerate(shifted(rows)):
            fr[n * 64:(n + 1) * 64, p * Z:(p + 1) * Z] = piece
    fr[192:] = jnp.zeros((64, fr.shape[1]), BF16)

    def gelu(rows, lanes):
        total = b1[rows, :1]
        for t, ref in ((t1o, fs), (t1d, fr)):
            cells = [jnp.concatenate([ref[:, a * 256 + at:a * 256 + at + size] for at, size in lanes], axis=1) for a in range(3)]
            total = total + jnp.dot(t[rows], jnp.concatenate(cells, axis=0), preferred_element_type=F32)
        return total * gelu_share(total)

    own = gelu(slice(0, 128), ((0, 2 * Z), ((count + 2) * Z, 2 * Z)))
    rims = gelu(slice(128, 192), ((0, (count + 4) * Z),))
    rims = jnp.concatenate([jnp.where(radial > 0, rims[:32], 0.0), jnp.where(radial < counts[1] - 1, rims[32:], 0.0)], axis=0)
    for p in range(count + 4):
        rim_rows = rims[:, p * Z:(p + 1) * Z]
        if 2 <= p < count + 2:
            hidden_out[p, :128] = hidden[p - 2]
            hidden_out[p, 128:] = rim_rows.astype(BF16)
        else:
            at = p if p < 2 else p - count
            inside = stream > 0 if p < 2 else stream < counts[0] - 1
            rows = jnp.concatenate([own[:, at * Z:(at + 1) * Z], rim_rows], axis=0)
            hidden_out[p] = jnp.where(inside, rows, 0.0).astype(BF16)


def closure_kernel(hidden, t2, b2, closure, hs):
    count = closure.shape[2]
    for p in range(count + 4):
        store_wide(hs, p, hidden[p].astype(F32))
    out = (jnp.dot(t2[...], stacked(hs, count * Z), preferred_element_type=F32) + b2[:, :1]).astype(BF16)
    for x in range(count):
        closure[0, :, x] = out[:, x * Z:(x + 1) * Z].reshape(CH, 8, Z)


def summed(parts):
    parts = [part[...].astype(F32) for part in parts]
    while len(parts) > 1:
        parts = [v + w for v, w in zip(parts[::2], parts[1::2])]
    return parts[0]


def add_kernel(*refs):
    refs[-1][...] = rounded(summed(refs[:-1]))


def finish_kernel(norm, *refs):
    *parts, first, second, bias = refs
    scaled = summed(parts) * norm
    flipped = jnp.transpose(scaled)
    first[...] = flipped[:128, :27]
    second[...] = flipped[128:, :27]
    bias[...] = scaled[27:28, :CH] + scaled[28:29, :CH]


def call(kernel, outs, name, scratch=(), flops=10_000_000, **specs):
    return pl.pallas_call(
        kernel,
        out_shape=outs,
        **specs,
        scratch_shapes=list(scratch),
        compiler_params=pltpu.CompilerParams(vmem_limit_bytes=32 * 1024 * 1024),
        cost_estimate=pl.CostEstimate(flops=flops, bytes_accessed=1_000_000, transcendentals=0),
        name=name,
    )


def shape(*dims, dtype=BF16):
    return jax.ShapeDtypeStruct(dims, dtype)


def exchange(near, far, axis, other):
    count, others = lax.axis_size(axis), lax.axis_size(other)
    axes = tuple(name for name in ("stream", "radial", "snap") if name in (axis, other))
    flat = (others, 1) if axes[0] == axis else (1, count)
    pairs = []
    for i in range(count):
        for j in range(others):
            end = i in (0, count - 1)
            to = (i, j ^ 1 if others % 2 == 0 else j) if end else (i - 1 + 2 * (i % 2), j)
            pairs.append((i * flat[0] + j * flat[1], to[0] * flat[0] + to[1] * flat[1]))
    far = lax.ppermute(far, axes, pairs)
    return lax.ppermute(near, axis, [(i, i ^ 1) for i in range(count)]), far


def swap(v, axis, masks):
    count = lax.axis_size(axis)
    return [lax.ppermute(v, axis, [(i, i ^ mask) for i in range(count)]) for mask in masks]


def stream_round(v):
    count, others = lax.axis_size("stream"), lax.axis_size("radial")
    pairs = [(i * others + j, (i ^ (2 + (j + 1) % 2)) * others + j) for i in range(count) for j in range(others)]
    apart = lax.ppermute(v, ("stream", "radial"), pairs)
    return [*swap(v, "stream", [1]), apart, *swap(apart, "radial", [1])]


def add(v, arrived):
    return call(add_kernel, shape(*v.shape), "add_parts")(v, *arrived)


def rounds(axis, most):
    found, step = [], 1
    while step < lax.axis_size(axis):
        masks = [step * n for n in range(1, most if step * most <= lax.axis_size(axis) else 2)]
        found.append((axis, masks))
        step *= len(masks) + 1
    return found


def local(fields, first_weight, first_bias, second_weight, second_bias, cotangent):
    e1t, y1 = table(CI, 384, ((natural, 0, 64), (rim(CI), 256, 32)))
    e2t, y2 = table(CH, 640, ((natural, 0, 128), (rim(CH), 384, 64)))
    rep1, rep2 = np.zeros((128, 384), np.float32), np.zeros((128, 768), np.float32)
    for c in range(3):
        rep1[c * CI:(c + 1) * CI, c * 128:(c + 1) * 128] = np.tile(np.eye(CI), (1, CH))
        rep2[c * CH:(c + 1) * CH, c * 256:(c + 1) * 256] = np.repeat(np.eye(CH), CH, axis=1)

    def const(*arrays, dtype=BF16):
        return [jnp.asarray(v, dtype) for v in arrays]

    planes = fields.shape[2]
    w1 = first_weight.transpose(1, 2, 0).reshape(CH * CI, 27)
    w2 = second_weight.transpose(1, 2, 0).reshape(CH * CH, 27)
    near, far, f_rows, c_rows = call(
        pack_kernel,
        (shape(512, Z), shape(512, Z), shape(planes, CI * 8, Z), shape(planes, CH * 8, Z)),
        "pack_strips",
        flops=4_000_000_000,
    )(jnp.concatenate([fields[0], cotangent[0]], axis=0))
    xnear, xfar = exchange(near, far, "stream", "radial")
    wide = (planes + 4) * Z
    counts = (lax.axis_size("stream"), lax.axis_size("radial"))
    t1o, t1r, t1d, tbo, tbr, t2, b1, b2 = call(
        band_kernel,
        (shape(192, 768), shape(128, 384), shape(192, 768), shape(128, 1152), shape(128, 768), shape(128, 1920),
         shape(192, 128, dtype=F32), shape(128, 128, dtype=F32)),
        "band_matrices",
        flops=4_000_000_000,
    )(w1, w2, first_bias[None], second_bias[None])
    near_own, far_own = call(own_strips_kernel, (shape(planes * 48, Z),) * 2, "own_strips")(f_rows, c_rows)
    xfar, xnear, t1o, tbo = lax.optimization_barrier((xfar, xnear, t1o, tbo))
    inner, outer = shape((planes + 4) * 48, Z), shape(128 + (planes + 4) * 16, Z)
    near, far = call(functools.partial(join_kernel, counts), (inner, inner), "join_strips")(xfar, xnear, near_own, far_own)
    rnear, rfar = exchange(near, far, "radial", "stream")
    half, half_f32 = shape(64, planes * Z), shape(64, planes * Z, dtype=F32)
    fs, cs, pre, back, hidden, dpre = call(
        functools.partial(own_kernel, counts),
        (shape(256, wide + 4 * Z), shape(384, wide), half_f32, half_f32, half, half),
        "own_rows",
        flops=1_000_000_000,
    )(xfar, xnear, f_rows, c_rows, t1o, tbo, b1)
    f_rows, fs = lax.optimization_barrier((f_rows, fs))
    near_outer, far_outer = call(functools.partial(join_outer_kernel, counts), (outer, outer), "join_outer")(
        xfar, xnear, f_rows, c_rows)
    rnear_outer, rfar_outer = exchange(near_outer, far_outer, "radial", "stream")
    hidden, payload = call(
        functools.partial(rim_kernel, counts),
        (shape(planes, 128, Z), shape(32, 384)),
        "gradients",
        (pltpu.VMEM((128, wide), BF16), pltpu.VMEM((256, wide), BF16), pltpu.VMEM((3, 32, 128), F32)),
        flops=2_000_000_000,
    )(rfar, rnear, fs, cs, pre, back, hidden, dpre, t1r, tbr, *const(e1t, e2t, rep1, rep2), *const(y1, y2, dtype=F32))

    steps = rounds("radial", 4) + rounds("stream", 4)[1:] + rounds("snap", 2)
    arrived = swap(payload, *steps[0])
    hidden = call(
        functools.partial(hidden_rim_kernel, counts),
        shape(planes + 4, 192, Z),
        "hidden_rim",
        (pltpu.VMEM((256, wide + 4 * Z), BF16),),
        flops=1_000_000_000,
    )(rfar, rnear, rfar_outer, rnear_outer, hidden, fs, t1o, t1d, b1)
    payload, hidden = lax.optimization_barrier((add(payload, arrived), hidden))
    payload = add(payload, stream_round(payload))
    arrived = swap(payload, *steps[1])
    closure = call(
        closure_kernel, shape(*cotangent.shape), "closure", (pltpu.VMEM((640, wide), BF16),), flops=1_000_000_000
    )(hidden, t2, b2)
    for step in steps[2:]:
        payload = add(payload, arrived)
        arrived = swap(payload, *step)

    cells = fields.shape[0] * fields.shape[2] * fields.shape[3] * fields.shape[4]
    for axis in ("stream", "radial", "snap"):
        cells *= lax.axis_size(axis)
    norm = float(1.0 / np.sqrt(np.float32(cells)))
    first, second, bias = call(
        functools.partial(finish_kernel, norm),
        (shape(CH * CI, 27, dtype=F32), shape(CH * CH, 27, dtype=F32), shape(1, CH, dtype=F32)),
        "finish",
    )(payload, *arrived)
    first = first.reshape(CH, CI, 27).transpose(2, 0, 1)
    second = second.reshape(CH, CH, 27).transpose(2, 0, 1)
    return (closure, first, second, bias[0])


def solution(mesh):
    split = P("snap", None, "stream", "radial", None)
    return jax.shard_map(
        local,
        mesh=mesh,
        in_specs=(split, P(), P(), P(), P(), split),
        out_specs=(split, P(), P(), P()),
        check_vma=False,
    )
```

```python
import functools

import numpy as np
import jax
import jax.numpy as jnp
from jax import lax
from jax.experimental import pallas as pl
from jax.experimental.pallas import tpu as pltpu
from jax.sharding import PartitionSpec as P

F32 = jnp.float32
BF16 = jnp.bfloat16
Z = 128
CI = 8
CH = 16
FAR = 100


def natural(n):
    return n // 8, n % 8


def y_first(n):
    return n % CH, n // CH


def rim(channels):
    def of(n):
        side, n = n // (2 * channels), n % (2 * channels)
        return n // 2, n % 2 + 10 * side - 2
    return of


def deep_rim(n):
    part, n = n // 16, n % 16
    return n // 2, n % 2 + 10 * (part // 2) - 2 + (part % 2) * (4 * (part // 2) - 2)


def table(channels, total, places):
    e = np.zeros((total, 128), np.float32)
    ys = np.full((1, total), FAR, np.float32)
    for c in range(3):
        for of, start, step in places:
            ch, y = of(np.arange(step))
            at = start + c * step + np.arange(step)
            e[at, c * channels + ch] = 1
            ys[0, at] = y
    return e, ys


def iota(rows, columns):
    return [lax.broadcasted_iota(jnp.int32, (rows, columns), d) for d in range(2)]


def one_hot(where):
    return jnp.where(where, 1.0, 0.0).astype(BF16)


def lane_y(of, width, step):
    lane = lax.broadcasted_iota(jnp.int32, (1, width), 1)
    return jnp.where(lane < 3 * step, of(lane % step)[1], FAR)


def place(rows, wanted, of, size, slot):
    row, lane = iota(rows, 128)
    return one_hot((of(lane % size)[0] == wanted(row)) & (lane // size == slot))


def row_table(rows, own):
    row, lane = iota(rows, CH)
    own_c, own_y = own(row)
    rim_c, rim_y = rim(CH)(row - 128)
    channel, y = jnp.where(row < 128, own_c, rim_c), jnp.where(row < 128, own_y, rim_y)
    return one_hot(channel == lane), y[:, :1]


def plane(ref, channels, x):
    v = ref[channels, x].astype(F32)
    return v.reshape(v.shape[0] * v.shape[1], v.shape[2])


def pick_rows(channels, low, high):
    half = channels * 2
    row, col = iota(2 * half, channels * 8)
    side = row // half
    return one_hot(col == (row % half // 2) * 8 + low + (high - low) * side + row % 2)


def partners(index, count):
    return index % 2 == 0, index > 0, index < count - 1


def sides(index, count, near, far):
    near_above, below, above = partners(index, count)
    low = jnp.where(near_above, far, near).astype(F32)
    high = jnp.where(near_above, near, far).astype(F32)
    return jnp.where(below, low, 0.0), jnp.where(above, high, 0.0)


def pack_kernel(inputs, near, far, f_rows, c_rows):
    up_first = lax.axis_index("stream") % 2 == 0
    count, at = inputs.shape[1], 0
    for channels, out, width in ((slice(0, CI), f_rows, 4), (slice(CI, CI + CH), c_rows, 2)):
        rows = [plane(inputs, channels, x) for x in range(count)]
        for x, v in enumerate(rows):
            out[x] = v.astype(BF16)
        for low, high in zip(rows[:width], rows[count - width:]):
            part = slice(at, at + low.shape[0])
            near[part] = jnp.where(up_first, high, low).astype(BF16)
            far[part] = jnp.where(up_first, low, high).astype(BF16)
            at += low.shape[0]


def x_planes(count, fields, cot, xnear, xfar, size):
    index = lax.axis_index("stream")
    inner = [fields[x].astype(F32) for x in range(count)]
    rims = [sides(index, size, xnear[n * 64:(n + 1) * 64], xfar[n * 64:(n + 1) * 64]) for n in range(4)]
    f = [low for low, _ in rims] + inner + [high for _, high in rims]
    inner = [cot[x].astype(F32) for x in range(count)]
    rims = [sides(index, size, xnear[256 + n * 128:384 + n * 128], xfar[256 + n * 128:384 + n * 128]) for n in range(2)]
    return f, [low for low, _ in rims] + inner + [high for _, high in rims]


def pick_strips(work, near, far):
    up_first = lax.axis_index("radial") % 2 == 0
    at = 0
    for pick, rows in work:
        half = pick.shape[0] // 2
        for v in rows:
            got = jnp.dot(pick, v.astype(BF16), preferred_element_type=F32)
            near[at:at + half] = jnp.where(up_first, got[half:], got[:half]).astype(BF16)
            far[at:at + half] = jnp.where(up_first, got[:half], got[half:]).astype(BF16)
            at += half


def join_kernel(counts, xnear, xfar, fields, cot, near, far):
    f, c = x_planes(fields.shape[0], fields, cot, xnear, xfar, counts[0])
    pick_strips([(pick_rows(CI, 0, 6), f[2:-2]), (pick_rows(CH, 0, 6), c)], near, far)


def join_outer_kernel(counts, xnear, xfar, fields, cot, near, far):
    f, _ = x_planes(fields.shape[0], fields, cot, xnear, xfar, counts[0])
    ends = f[:2] + f[-2:]
    pick_strips([(pick_rows(CI, 0, 6), ends), (pick_rows(CI, 2, 4), ends + f[2:-2])], near, far)


def spread(w, by_row, flip):
    taps = jnp.transpose(w[...].astype(F32))
    width = taps.shape[1]
    row = lax.broadcasted_iota(jnp.int32, (CH, width), 0)
    lane = lax.broadcasted_iota(jnp.int32, (CH, width), 1)
    mine = row == (lane // (width // CH) if by_row else lane % CH)
    found = []
    for c in range(3):
        rows = []
        for ab in range(9):
            t = 26 - (ab * 3 + c) if flip else ab * 3 + c
            rows.append(jnp.where(mine, jnp.broadcast_to(taps[t:t + 1], (CH, width)), 0.0))
        found.append(jnp.concatenate(rows, axis=0).astype(BF16))
    return found


def dots(pairs):
    total = None
    for v, w in pairs:
        part = jnp.dot(v, w, preferred_element_type=F32)
        total = part if total is None else total + part
    return total.astype(BF16)


def packed(parts, wanted, of, size):
    per = 128 // size
    places = [place(parts[0].shape[1], wanted, of, size, slot) for slot in range(min(per, 3))]
    tiles = [range(first, min(first + per, 3)) for first in range(0, 3, per)]
    return jnp.concatenate([dots([(parts[c], places[c % per]) for c in tile]) for tile in tiles], axis=1)


def band(wide, expand, ys, rows_y, t):
    rows, width = t.shape[0], wide.shape[1]
    for a in range(3):
        total = jnp.zeros((rows, width), F32)
        for b in range(3):
            part = jnp.dot(expand[:rows], wide[(a * 3 + b) * CH:(a * 3 + b + 1) * CH], preferred_element_type=F32)
            total = jnp.where(ys == rows_y[:rows] + 2 * (b - 1), part, total)
        t[:, a * width:(a + 1) * width] = total.astype(BF16)


def repeat_bias(bias, expand, out):
    column = jnp.sum(expand.astype(F32) * bias[...], axis=1, keepdims=True)
    out[...] = jnp.broadcast_to(column, out.shape)


def band_kernel(w1, w2, first_bias, second_bias, t1o, t1r, t1d, tbo, tbr, t2, b1, b2):
    expand, rows_y = row_table(192, y_first)
    parts = spread(w1, True, False)
    for of, step, t in ((natural, 64, t1o), (rim(CI), 32, t1r), (deep_rim, 64, t1d)):
        wide = packed(parts, lambda n: n % CI, of, step)
        band(wide, expand, lane_y(of, wide.shape[1], step), rows_y, t)
    parts = spread(w2, False, True)
    for of, step, t in ((natural, 128, tbo), (rim(CH), 64, tbr)):
        wide = packed(parts, lambda n: n // CH, of, step)
        band(wide, expand, lane_y(of, wide.shape[1], step), rows_y, t)
    repeat_bias(first_bias, expand, b1)
    expand, rows_y = row_table(128, natural)
    parts = spread(w2, True, False)
    wide = [packed(parts, lambda n: n % CH, of, step) for of, step in ((y_first, 128), (rim(CH), 64))]
    ys = jnp.concatenate([lane_y(y_first, 384, 128), lane_y(rim(CH), 256, 64)], axis=1)
    band(jnp.concatenate(wide, axis=1), expand, ys, rows_y, t2)
    repeat_bias(second_bias, expand, b2)


def shifted(v):
    lane = lax.broadcasted_iota(jnp.int32, v.shape, 1)
    before = jnp.where(lane >= 2, pltpu.roll(v, 2, 1), 0.0)
    after = jnp.where(lane < Z - 2, pltpu.roll(v, Z - 2, 1), 0.0)
    return before.astype(BF16), v.astype(BF16), after.astype(BF16)


def store_wide(ref, p, v):
    at = slice(p * Z, (p + 1) * Z)
    for c, piece in enumerate(shifted(v)):
        ref[c * 128:(c + 1) * 128, at] = piece[:128]
        ref[384 + c * 64:384 + (c + 1) * 64, at] = piece[128:]
    ref[576:, at] = jnp.zeros((64, Z), BF16)


def stacked(ref, lanes):
    return jnp.concatenate([ref[:, a * 256:a * 256 + lanes] for a in range(3)], axis=0)


def gelu_share(pre):
    return 0.5 * (1.0 + lax.erf(pre * 0.7071067811865476))


def gelu_slope(pre, share):
    return share + pre * jnp.exp(-0.5 * pre * pre) * 0.3989422804014327


def edges(v):
    return jnp.concatenate([v[:32], v[96:128]], axis=0)


def whole(edge, middle):
    return jnp.concatenate([edge[:32], middle, edge[32:]], axis=0)


def own_kernel(counts, xnear, xfar, fields, cot, t1, tb, b1, fs, cs, pre, back, hidden, dpre):
    count, lanes = fields.shape[0], pre.shape[1]
    f, c = x_planes(count, fields, cot, xnear, xfar, counts[0])
    for ref, rows in ((fs, f), (cs, c)):
        for p, v in enumerate(rows):
            for n, piece in enumerate(shifted(v)):
                ref[n * v.shape[0]:(n + 1) * v.shape[0], p * Z:(p + 1) * Z] = piece
    fs[192:] = jnp.zeros((64, fs.shape[1]), BF16)
    rows = jnp.concatenate([fs[:, a * 256 + 256:a * 256 + 256 + lanes] for a in range(3)], axis=0)
    first = jnp.dot(t1[:128], rows, preferred_element_type=F32) + b1[:128, :1]
    second = jnp.dot(tb[...], stacked(cs, lanes), preferred_element_type=F32)
    pre[...] = edges(first)
    back[...] = edges(second)
    first, second = first[32:96], second[32:96]
    share = gelu_share(first)
    hidden[...] = (first * share).astype(BF16)
    dpre[...] = (second * gelu_slope(first, share)).astype(BF16)


def rounded(s):
    lost = s - s.astype(BF16).astype(F32)
    row = lax.broadcasted_iota(jnp.int32, s.shape, 0)
    return (s + jnp.where(row == 28, pltpu.roll(lost, 1, 0), 0.0)).astype(BF16)


def two_dots(v, w):
    high = v.astype(BF16)
    low = (v - high.astype(F32)).astype(BF16)
    return jnp.dot(high, w, preferred_element_type=F32) + jnp.dot(low, w, preferred_element_type=F32)


def rim_kernel(counts, rfar, rnear, fs, cs, pre_own, back_own, hidden_own, dpre_own, t1, tb, e1t, e2t, rep1, rep2, y1, y2,
               hidden_out, payload, fr, cr, taps):
    count = hidden_out.shape[0]
    lanes = count * Z
    radial = lax.axis_index("radial")
    at = 0
    for ref, half in ((fr, 16), (cr, 32)):
        for p in range(count + 4):
            low, high = sides(radial, counts[1], rnear[at:at + half], rfar[at:at + half])
            for n, piece in enumerate(shifted(jnp.concatenate([low, high], axis=0))):
                ref[n * 2 * half:(n + 1) * 2 * half, p * Z:(p + 1) * Z] = piece
            at += half
        ref[6 * half:] = jnp.zeros((2 * half, ref.shape[1]), BF16)
    pre = pre_own[...] + jnp.dot(edges(t1), stacked(fr, lanes), preferred_element_type=F32)
    share = gelu_share(pre)
    hidden = whole((pre * share).astype(BF16), hidden_own[...])
    for x in range(count):
        hidden_out[x] = hidden[:, x * Z:(x + 1) * Z]
    back = back_own[...] + jnp.dot(edges(tb), stacked(cr, lanes), preferred_element_type=F32)
    dpre = whole((back * gelu_slope(pre, share)).astype(BF16), dpre_own[...])
    over_lanes = (((1,), (1,)), ((), ()))
    ones, twos = [], []
    sums = [[None] * 3, [None] * 3]
    for pair in range(count // 2 + 2):
        taps_here = [a for a in range(3) if 0 <= pair - a < count // 2]
        at = slice(pair * 256, (pair + 1) * 256)
        shifted_rows = (
            jnp.concatenate([fs[:, (pair + 1) * 256:(pair + 2) * 256], fr[:, at]], axis=0),
            jnp.concatenate([cs[:, at], cr[:, at]], axis=0),
        )
        for here, rows, total in zip((dpre, hidden), shifted_rows, sums):
            here = jnp.concatenate([here[:, (pair - a) * 256:(pair - a + 1) * 256] for a in taps_here], axis=0)
            got = lax.dot_general(here, rows, over_lanes, preferred_element_type=F32)
            for n, a in enumerate(taps_here):
                part = got[n * 128:(n + 1) * 128]
                total[a] = part if total[a] is None else total[a] + part
    for a in range(3):
        g1, g2 = sums[0][a], sums[1][a]
        for b in range(3):
            for g, ys, out in ((g1, y1, ones), (g2, y2, twos)):
                total = jnp.zeros((CH, g.shape[1]), F32)
                for y in range(8):
                    total = jnp.where(ys[...] == float(y + 2 * (b - 1)), g[y * CH:(y + 1) * CH], total)
                out.append(total)
    taps[:, 24:] = jnp.zeros((3, 8, 128), F32)
    for parts, et, rep, at, width in ((ones, e1t, rep1, 0, 128), (twos[::-1], e2t, rep2, 1, 256)):
        sums = two_dots(jnp.concatenate(parts, axis=0), et[...])
        wide = two_dots(sums, rep[...])
        row = lax.broadcasted_iota(jnp.int32, wide.shape, 0) % CH
        lane = lax.broadcasted_iota(jnp.int32, wide.shape, 1) % width
        mine = row == (lane // CI if width == 128 else lane % CH)
        total = jnp.sum(jnp.where(mine, wide, 0.0).reshape(9, CH, 3 * width), axis=1)
        for c in range(3):
            first = c if width == 128 else 2 - c
            for n in range(width // 128):
                taps[at + n, pl.ds(first, 9, stride=3)] = total[:, c * width + n * 128:c * width + (n + 1) * 128]
    bias = jnp.sum(dpre.astype(F32), axis=1, keepdims=True)
    bias = sum(bias[y * CH:(y + 1) * CH] for y in range(8))
    row = lax.broadcasted_iota(jnp.int32, (CH, 128), 0)
    lane = lax.broadcasted_iota(jnp.int32, (CH, 128), 1)
    taps[0, 27:28] = jnp.sum(jnp.where(row == lane, bias, 0.0), axis=0, keepdims=True)
    payload[...] = rounded(jnp.concatenate([taps[n] for n in range(3)], axis=1))


def hidden_rim_kernel(counts, rfar, rnear, rfar_outer, rnear_outer, hidden, fs, t1o, t1d, b1, hidden_out, fr):
    count = hidden.shape[0]
    stream, radial = lax.axis_index("stream"), lax.axis_index("radial")
    for p in range(count + 8):
        end = p if p < 2 else p - count - 4 if p >= count + 6 else None
        if end is None:
            near, outer = (rnear, rfar, (p - 2) * 16), (rnear_outer, rfar_outer, 128 + (p - 2) * 16)
        else:
            near, outer = (rnear_outer, rfar_outer, end * 16), (rnear_outer, rfar_outer, 64 + end * 16)
        parts = [sides(radial, counts[1], n[at:at + 16], f[at:at + 16]) for n, f, at in (near, outer)]
        rows = jnp.concatenate([part[side] for side in range(2) for part in parts], axis=0)
        for n, piece in enumerate(shifted(rows)):
            fr[n * 64:(n + 1) * 64, p * Z:(p + 1) * Z] = piece
    fr[192:] = jnp.zeros((64, fr.shape[1]), BF16)

    def gelu(rows, lanes):
        total = b1[rows, :1]
        for t, ref in ((t1o, fs), (t1d, fr)):
            cells = [jnp.concatenate([ref[:, a * 256 + at:a * 256 + at + size] for at, size in lanes], axis=1) for a in range(3)]
            total = total + jnp.dot(t[rows], jnp.concatenate(cells, axis=0), preferred_element_type=F32)
        return total * gelu_share(total)

    own = gelu(slice(0, 128), ((0, 2 * Z), ((count + 2) * Z, 2 * Z)))
    rims = gelu(slice(128, 192), ((0, (count + 4) * Z),))
    rims = jnp.concatenate([jnp.where(radial > 0, rims[:32], 0.0), jnp.where(radial < counts[1] - 1, rims[32:], 0.0)], axis=0)
    for p in range(count + 4):
        rim_rows = rims[:, p * Z:(p + 1) * Z]
        if 2 <= p < count + 2:
            hidden_out[p, :128] = hidden[p - 2]
            hidden_out[p, 128:] = rim_rows.astype(BF16)
        else:
            at = p if p < 2 else p - count
            inside = stream > 0 if p < 2 else stream < counts[0] - 1
            rows = jnp.concatenate([own[:, at * Z:(at + 1) * Z], rim_rows], axis=0)
            hidden_out[p] = jnp.where(inside, rows, 0.0).astype(BF16)


def closure_kernel(hidden, t2, b2, closure, hs):
    count = closure.shape[2]
    for p in range(count + 4):
        store_wide(hs, p, hidden[p].astype(F32))
    out = (jnp.dot(t2[...], stacked(hs, count * Z), preferred_element_type=F32) + b2[:, :1]).astype(BF16)
    for x in range(count):
        closure[0, :, x] = out[:, x * Z:(x + 1) * Z].reshape(CH, 8, Z)


def summed(parts):
    parts = [part[...].astype(F32) for part in parts]
    while len(parts) > 1:
        parts = [v + w for v, w in zip(parts[::2], parts[1::2])]
    return parts[0]


def add_kernel(*refs):
    refs[-1][...] = rounded(summed(refs[:-1]))


def finish_kernel(norm, *refs):
    *parts, first, second, bias = refs
    scaled = summed(parts) * norm
    flipped = jnp.transpose(scaled)
    first[...] = flipped[:128, :27]
    second[...] = flipped[128:, :27]
    bias[...] = scaled[27:28, :CH] + scaled[28:29, :CH]


def call(kernel, outs, name, scratch=(), flops=10_000_000, **specs):
    return pl.pallas_call(
        kernel,
        out_shape=outs,
        **specs,
        scratch_shapes=list(scratch),
        compiler_params=pltpu.CompilerParams(vmem_limit_bytes=32 * 1024 * 1024),
        cost_estimate=pl.CostEstimate(flops=flops, bytes_accessed=1_000_000, transcendentals=0),
        name=name,
    )


def shape(*dims, dtype=BF16):
    return jax.ShapeDtypeStruct(dims, dtype)


def exchange(near, far, axis, other):
    count, others = lax.axis_size(axis), lax.axis_size(other)
    axes = tuple(name for name in ("stream", "radial", "snap") if name in (axis, other))
    flat = (others, 1) if axes[0] == axis else (1, count)
    pairs = []
    for i in range(count):
        for j in range(others):
            end = i in (0, count - 1)
            to = (i, j ^ 1 if others % 2 == 0 else j) if end else (i - 1 + 2 * (i % 2), j)
            pairs.append((i * flat[0] + j * flat[1], to[0] * flat[0] + to[1] * flat[1]))
    far = lax.ppermute(far, axes, pairs)
    return lax.ppermute(near, axis, [(i, i ^ 1) for i in range(count)]), far


def swap(v, axis, masks):
    count = lax.axis_size(axis)
    return [lax.ppermute(v, axis, [(i, i ^ mask) for i in range(count)]) for mask in masks]


def stream_round(v):
    count, others = lax.axis_size("stream"), lax.axis_size("radial")
    pairs = [(i * others + j, (i ^ (2 + (j + 1) % 2)) * others + j) for i in range(count) for j in range(others)]
    apart = lax.ppermute(v, ("stream", "radial"), pairs)
    return [*swap(v, "stream", [1]), apart, *swap(apart, "radial", [1])]


def add(v, arrived):
    return call(add_kernel, shape(*v.shape), "add_parts")(v, *arrived)


def rounds(axis, most):
    found, step = [], 1
    while step < lax.axis_size(axis):
        masks = [step * n for n in range(1, most if step * most <= lax.axis_size(axis) else 2)]
        found.append((axis, masks))
        step *= len(masks) + 1
    return found


def local(fields, first_weight, first_bias, second_weight, second_bias, cotangent):
    e1t, y1 = table(CI, 384, ((natural, 0, 64), (rim(CI), 256, 32)))
    e2t, y2 = table(CH, 640, ((natural, 0, 128), (rim(CH), 384, 64)))
    rep1, rep2 = np.zeros((128, 384), np.float32), np.zeros((128, 768), np.float32)
    for c in range(3):
        rep1[c * CI:(c + 1) * CI, c * 128:(c + 1) * 128] = np.tile(np.eye(CI), (1, CH))
        rep2[c * CH:(c + 1) * CH, c * 256:(c + 1) * 256] = np.repeat(np.eye(CH), CH, axis=1)

    def const(*arrays, dtype=BF16):
        return [jnp.asarray(v, dtype) for v in arrays]

    planes = fields.shape[2]
    w1 = first_weight.transpose(1, 2, 0).reshape(CH * CI, 27)
    w2 = second_weight.transpose(1, 2, 0).reshape(CH * CH, 27)
    near, far, f_rows, c_rows = call(
        pack_kernel,
        (shape(512, Z), shape(512, Z), shape(planes, CI * 8, Z), shape(planes, CH * 8, Z)),
        "pack_strips",
        flops=4_000_000_000,
    )(jnp.concatenate([fields[0], cotangent[0]], axis=0))
    xnear, xfar = exchange(near, far, "stream", "radial")
    wide = (planes + 4) * Z
    counts = (lax.axis_size("stream"), lax.axis_size("radial"))
    t1o, t1r, t1d, tbo, tbr, t2, b1, b2 = call(
        band_kernel,
        (shape(192, 768), shape(128, 384), shape(192, 768), shape(128, 1152), shape(128, 768), shape(128, 1920),
         shape(192, 128, dtype=F32), shape(128, 128, dtype=F32)),
        "band_matrices",
        flops=4_000_000_000,
    )(w1, w2, first_bias[None], second_bias[None])
    xnear, xfar, t1o, tbo = lax.optimization_barrier((xnear, xfar, t1o, tbo))
    inner, outer = shape((planes + 4) * 48, Z), shape(128 + (planes + 4) * 16, Z)
    near, far = call(functools.partial(join_kernel, counts), (inner, inner), "join_strips")(xnear, xfar, f_rows, c_rows)
    rnear, rfar = exchange(near, far, "radial", "stream")
    half, half_f32 = shape(64, planes * Z), shape(64, planes * Z, dtype=F32)
    fs, cs, pre, back, hidden, dpre = call(
        functools.partial(own_kernel, counts),
        (shape(256, wide + 4 * Z), shape(384, wide), half_f32, half_f32, half, half),
        "own_rows",
        flops=1_000_000_000,
    )(xnear, xfar, f_rows, c_rows, t1o, tbo, b1)
    f_rows, fs = lax.optimization_barrier((f_rows, fs))
    near_outer, far_outer = call(functools.partial(join_outer_kernel, counts), (outer, outer), "join_outer")(
        xnear, xfar, f_rows, c_rows)
    rnear_outer, rfar_outer = exchange(near_outer, far_outer, "radial", "stream")
    hidden, payload = call(
        functools.partial(rim_kernel, counts),
        (shape(planes, 128, Z), shape(32, 384)),
        "gradients",
        (pltpu.VMEM((128, wide), BF16), pltpu.VMEM((256, wide), BF16), pltpu.VMEM((3, 32, 128), F32)),
        flops=2_000_000_000,
    )(rfar, rnear, fs, cs, pre, back, hidden, dpre, t1r, tbr, *const(e1t, e2t, rep1, rep2), *const(y1, y2, dtype=F32))

    steps = rounds("radial", 4) + rounds("stream", 4)[1:] + rounds("snap", 2)
    arrived = swap(payload, *steps[0])
    hidden = call(
        functools.partial(hidden_rim_kernel, counts),
        shape(planes + 4, 192, Z),
        "hidden_rim",
        (pltpu.VMEM((256, wide + 4 * Z), BF16),),
        flops=1_000_000_000,
    )(rfar, rnear, rfar_outer, rnear_outer, hidden, fs, t1o, t1d, b1)
    payload, hidden = lax.optimization_barrier((add(payload, arrived), hidden))
    payload = add(payload, stream_round(payload))
    arrived = swap(payload, *steps[1])
    closure = call(
        closure_kernel, shape(*cotangent.shape), "closure", (pltpu.VMEM((640, wide), BF16),), flops=1_000_000_000
    )(hidden, t2, b2)
    for step in steps[2:]:
        payload = add(payload, arrived)
        arrived = swap(payload, *step)

    cells = fields.shape[0] * fields.shape[2] * fields.shape[3] * fields.shape[4]
    for axis in ("stream", "radial", "snap"):
        cells *= lax.axis_size(axis)
    norm = float(1.0 / np.sqrt(np.float32(cells)))
    first, second, bias = call(
        functools.partial(finish_kernel, norm),
        (shape(CH * CI, 27, dtype=F32), shape(CH * CH, 27, dtype=F32), shape(1, CH, dtype=F32)),
        "finish",
    )(payload, *arrived)
    first = first.reshape(CH, CI, 27).transpose(2, 0, 1)
    second = second.reshape(CH, CH, 27).transpose(2, 0, 1)
    return (closure, first, second, bias[0])


def solution(mesh):
    split = P("snap", None, "stream", "radial", None)
    return jax.shard_map(
        local,
        mesh=mesh,
        in_specs=(split, P(), P(), P(), P(), split),
        out_specs=(split, P(), P(), P()),
        check_vma=False,
    )
```

```python
import functools

import numpy as np
import jax
import jax.numpy as jnp
from jax import lax
from jax.experimental import pallas as pl
from jax.experimental.pallas import tpu as pltpu
from jax.sharding import PartitionSpec as P

F32 = jnp.float32
BF16 = jnp.bfloat16
Z = 128
CI = 8
CH = 16
FAR = 100


def natural(n):
    return n // 8, n % 8


def y_first(n):
    return n % CH, n // CH


def rim(channels):
    def of(n):
        side, n = n // (2 * channels), n % (2 * channels)
        return n // 2, n % 2 + 10 * side - 2
    return of


def deep_rim(n):
    part, n = n // 16, n % 16
    return n // 2, n % 2 + 10 * (part // 2) - 2 + (part % 2) * (4 * (part // 2) - 2)


def table(channels, total, places):
    e = np.zeros((total, 128), np.float32)
    ys = np.full((1, total), FAR, np.float32)
    for c in range(3):
        for of, start, step in places:
            ch, y = of(np.arange(step))
            at = start + c * step + np.arange(step)
            e[at, c * channels + ch] = 1
            ys[0, at] = y
    return e, ys


def iota(rows, columns):
    return [lax.broadcasted_iota(jnp.int32, (rows, columns), d) for d in range(2)]


def one_hot(where):
    return jnp.where(where, 1.0, 0.0).astype(BF16)


def lane_y(of, width, step):
    lane = lax.broadcasted_iota(jnp.int32, (1, width), 1)
    return jnp.where(lane < 3 * step, of(lane % step)[1], FAR)


def place(rows, wanted, of, size, slot):
    row, lane = iota(rows, 128)
    return one_hot((of(lane % size)[0] == wanted(row)) & (lane // size == slot))


def row_table(rows, own):
    row, lane = iota(rows, CH)
    own_c, own_y = own(row)
    rim_c, rim_y = rim(CH)(row - 128)
    channel, y = jnp.where(row < 128, own_c, rim_c), jnp.where(row < 128, own_y, rim_y)
    return one_hot(channel == lane), y[:, :1]


def plane(ref, channels, x):
    v = ref[channels, x].astype(F32)
    return v.reshape(v.shape[0] * v.shape[1], v.shape[2])


def pick_rows(channels, low, high):
    half = channels * 2
    row, col = iota(2 * half, channels * 8)
    side = row // half
    return one_hot(col == (row % half // 2) * 8 + low + (high - low) * side + row % 2)


def partners(index, count):
    return index % 2 == 0, index > 0, index < count - 1


def sides(index, count, near, far):
    near_above, below, above = partners(index, count)
    low = jnp.where(near_above, far, near).astype(F32)
    high = jnp.where(near_above, near, far).astype(F32)
    return jnp.where(below, low, 0.0), jnp.where(above, high, 0.0)


def pack_kernel(inputs, near, far, f_rows, c_rows):
    up_first = lax.axis_index("stream") % 2 == 0
    count, at = inputs.shape[1], 0
    for channels, out, width in ((slice(0, CI), f_rows, 4), (slice(CI, CI + CH), c_rows, 2)):
        rows = [plane(inputs, channels, x) for x in range(count)]
        for x, v in enumerate(rows):
            out[x] = v.astype(BF16)
        for low, high in zip(rows[:width], rows[count - width:]):
            part = slice(at, at + low.shape[0])
            near[part] = jnp.where(up_first, high, low).astype(BF16)
            far[part] = jnp.where(up_first, low, high).astype(BF16)
            at += low.shape[0]


def x_planes(count, fields, cot, xnear, xfar, size):
    index = lax.axis_index("stream")
    inner = [fields[x].astype(F32) for x in range(count)]
    rims = [sides(index, size, xnear[n * 64:(n + 1) * 64], xfar[n * 64:(n + 1) * 64]) for n in range(4)]
    f = [low for low, _ in rims] + inner + [high for _, high in rims]
    inner = [cot[x].astype(F32) for x in range(count)]
    rims = [sides(index, size, xnear[256 + n * 128:384 + n * 128], xfar[256 + n * 128:384 + n * 128]) for n in range(2)]
    return f, [low for low, _ in rims] + inner + [high for _, high in rims]


def pick_strips(work, near, far):
    up_first = lax.axis_index("radial") % 2 == 0
    at = 0
    for pick, rows in work:
        half = pick.shape[0] // 2
        for v in rows:
            got = jnp.dot(pick, v.astype(BF16), preferred_element_type=F32)
            near[at:at + half] = jnp.where(up_first, got[half:], got[:half]).astype(BF16)
            far[at:at + half] = jnp.where(up_first, got[:half], got[half:]).astype(BF16)
            at += half


def own_strips_kernel(fields, cot, near, far):
    planes = range(fields.shape[0])
    pick_strips([(pick_rows(CI, 0, 6), [fields[x] for x in planes]), (pick_rows(CH, 0, 6), [cot[x] for x in planes])], near, far)


def join_kernel(counts, xnear, xfar, near_own, far_own, near, far):
    up_first = lax.axis_index("radial") % 2 == 0
    index, count = lax.axis_index("stream"), near_own.shape[0] // 48
    at = own_at = 0
    for pick, rows, start, skip, half in ((pick_rows(CI, 0, 6), 64, 0, 2, 16), (pick_rows(CH, 0, 6), 128, 256, 0, 32)):
        places = [slice(start + n * rows, start + (n + 1) * rows) for n in range(4 if skip else 2)]
        rims = [sides(index, counts[0], xnear[place], xfar[place]) for place in places]
        below, above = [low for low, _ in rims[skip:]], [high for _, high in rims[:2]]
        for offset, part in ((0, below), (count + 2, above)):
            for n, v in enumerate(part):
                got = jnp.dot(pick, v.astype(BF16), preferred_element_type=F32)
                place = slice(at + (offset + n) * half, at + (offset + n + 1) * half)
                near[place] = jnp.where(up_first, got[half:], got[:half]).astype(BF16)
                far[place] = jnp.where(up_first, got[:half], got[half:]).astype(BF16)
        inside = slice(at + 2 * half, at + (2 + count) * half)
        near[inside] = near_own[own_at:own_at + count * half]
        far[inside] = far_own[own_at:own_at + count * half]
        at += (count + 4) * half
        own_at += count * half


def join_outer_kernel(counts, xnear, xfar, fields, cot, near, far):
    f, _ = x_planes(fields.shape[0], fields, cot, xnear, xfar, counts[0])
    ends = f[:2] + f[-2:]
    pick_strips([(pick_rows(CI, 0, 6), ends), (pick_rows(CI, 2, 4), ends + f[2:-2])], near, far)


def spread(w, by_row, flip):
    taps = jnp.transpose(w[...].astype(F32))
    width = taps.shape[1]
    row = lax.broadcasted_iota(jnp.int32, (CH, width), 0)
    lane = lax.broadcasted_iota(jnp.int32, (CH, width), 1)
    mine = row == (lane // (width // CH) if by_row else lane % CH)
    found = []
    for c in range(3):
        rows = []
        for ab in range(9):
            t = 26 - (ab * 3 + c) if flip else ab * 3 + c
            rows.append(jnp.where(mine, jnp.broadcast_to(taps[t:t + 1], (CH, width)), 0.0))
        found.append(jnp.concatenate(rows, axis=0).astype(BF16))
    return found


def dots(pairs):
    total = None
    for v, w in pairs:
        part = jnp.dot(v, w, preferred_element_type=F32)
        total = part if total is None else total + part
    return total.astype(BF16)


def packed(parts, wanted, of, size):
    per = 128 // size
    places = [place(parts[0].shape[1], wanted, of, size, slot) for slot in range(min(per, 3))]
    tiles = [range(first, min(first + per, 3)) for first in range(0, 3, per)]
    return jnp.concatenate([dots([(parts[c], places[c % per]) for c in tile]) for tile in tiles], axis=1)


def band(wide, expand, ys, rows_y, t):
    rows, width = t.shape[0], wide.shape[1]
    for a in range(3):
        total = jnp.zeros((rows, width), F32)
        for b in range(3):
            part = jnp.dot(expand[:rows], wide[(a * 3 + b) * CH:(a * 3 + b + 1) * CH], preferred_element_type=F32)
            total = jnp.where(ys == rows_y[:rows] + 2 * (b - 1), part, total)
        t[:, a * width:(a + 1) * width] = total.astype(BF16)


def repeat_bias(bias, expand, out):
    column = jnp.sum(expand.astype(F32) * bias[...], axis=1, keepdims=True)
    out[...] = jnp.broadcast_to(column, out.shape)


def band_kernel(w1, w2, first_bias, second_bias, t1o, t1r, t1d, tbo, tbr, t2, b1, b2):
    expand, rows_y = row_table(192, y_first)
    parts = spread(w1, True, False)
    for of, step, t in ((natural, 64, t1o), (rim(CI), 32, t1r), (deep_rim, 64, t1d)):
        wide = packed(parts, lambda n: n % CI, of, step)
        band(wide, expand, lane_y(of, wide.shape[1], step), rows_y, t)
    parts = spread(w2, False, True)
    for of, step, t in ((natural, 128, tbo), (rim(CH), 64, tbr)):
        wide = packed(parts, lambda n: n // CH, of, step)
        band(wide, expand, lane_y(of, wide.shape[1], step), rows_y, t)
    repeat_bias(first_bias, expand, b1)
    expand, rows_y = row_table(128, natural)
    parts = spread(w2, True, False)
    wide = [packed(parts, lambda n: n % CH, of, step) for of, step in ((y_first, 128), (rim(CH), 64))]
    ys = jnp.concatenate([lane_y(y_first, 384, 128), lane_y(rim(CH), 256, 64)], axis=1)
    band(jnp.concatenate(wide, axis=1), expand, ys, rows_y, t2)
    repeat_bias(second_bias, expand, b2)


def shifted(v):
    lane = lax.broadcasted_iota(jnp.int32, v.shape, 1)
    before = jnp.where(lane >= 2, pltpu.roll(v, 2, 1), 0.0)
    after = jnp.where(lane < Z - 2, pltpu.roll(v, Z - 2, 1), 0.0)
    return before.astype(BF16), v.astype(BF16), after.astype(BF16)


def store_wide(ref, p, v):
    at = slice(p * Z, (p + 1) * Z)
    for c, piece in enumerate(shifted(v)):
        ref[c * 128:(c + 1) * 128, at] = piece[:128]
        ref[384 + c * 64:384 + (c + 1) * 64, at] = piece[128:]
    ref[576:, at] = jnp.zeros((64, Z), BF16)


def stacked(ref, lanes):
    return jnp.concatenate([ref[:, a * 256:a * 256 + lanes] for a in range(3)], axis=0)


def gelu_share(pre):
    return 0.5 * (1.0 + lax.erf(pre * 0.7071067811865476))


def gelu_slope(pre, share):
    return share + pre * jnp.exp(-0.5 * pre * pre) * 0.3989422804014327


def edges(v):
    return jnp.concatenate([v[:32], v[96:128]], axis=0)


def whole(edge, middle):
    return jnp.concatenate([edge[:32], middle, edge[32:]], axis=0)


def own_kernel(counts, xnear, xfar, fields, cot, t1, tb, b1, fs, cs, pre, back, hidden, dpre):
    count, lanes = fields.shape[0], pre.shape[1]
    f, c = x_planes(count, fields, cot, xnear, xfar, counts[0])
    for ref, rows in ((fs, f), (cs, c)):
        for p, v in enumerate(rows):
            for n, piece in enumerate(shifted(v)):
                ref[n * v.shape[0]:(n + 1) * v.shape[0], p * Z:(p + 1) * Z] = piece
    fs[192:] = jnp.zeros((64, fs.shape[1]), BF16)
    rows = jnp.concatenate([fs[:, a * 256 + 256:a * 256 + 256 + lanes] for a in range(3)], axis=0)
    first = jnp.dot(t1[:128], rows, preferred_element_type=F32) + b1[:128, :1]
    second = jnp.dot(tb[...], stacked(cs, lanes), preferred_element_type=F32)
    pre[...] = edges(first)
    back[...] = edges(second)
    first, second = first[32:96], second[32:96]
    share = gelu_share(first)
    hidden[...] = (first * share).astype(BF16)
    dpre[...] = (second * gelu_slope(first, share)).astype(BF16)


def rounded(s):
    lost = s - s.astype(BF16).astype(F32)
    row = lax.broadcasted_iota(jnp.int32, s.shape, 0)
    return (s + jnp.where(row == 28, pltpu.roll(lost, 1, 0), 0.0)).astype(BF16)


def two_dots(v, w):
    high = v.astype(BF16)
    low = (v - high.astype(F32)).astype(BF16)
    return jnp.dot(high, w, preferred_element_type=F32) + jnp.dot(low, w, preferred_element_type=F32)


def rim_kernel(counts, rfar, rnear, fs, cs, pre_own, back_own, hidden_own, dpre_own, t1, tb, e1t, e2t, rep1, rep2, y1, y2,
               hidden_out, payload, fr, cr, taps):
    count = hidden_out.shape[0]
    lanes = count * Z
    radial = lax.axis_index("radial")
    at = 0
    for ref, half in ((fr, 16), (cr, 32)):
        for p in range(count + 4):
            low, high = sides(radial, counts[1], rnear[at:at + half], rfar[at:at + half])
            for n, piece in enumerate(shifted(jnp.concatenate([low, high], axis=0))):
                ref[n * 2 * half:(n + 1) * 2 * half, p * Z:(p + 1) * Z] = piece
            at += half
        ref[6 * half:] = jnp.zeros((2 * half, ref.shape[1]), BF16)
    pre = pre_own[...] + jnp.dot(edges(t1), stacked(fr, lanes), preferred_element_type=F32)
    share = gelu_share(pre)
    hidden = whole((pre * share).astype(BF16), hidden_own[...])
    for x in range(count):
        hidden_out[x] = hidden[:, x * Z:(x + 1) * Z]
    back = back_own[...] + jnp.dot(edges(tb), stacked(cr, lanes), preferred_element_type=F32)
    dpre = whole((back * gelu_slope(pre, share)).astype(BF16), dpre_own[...])
    over_lanes = (((1,), (1,)), ((), ()))
    ones, twos = [], []
    sums = [[None] * 3, [None] * 3]
    for pair in range(count // 2 + 2):
        taps_here = [a for a in range(3) if 0 <= pair - a < count // 2]
        at = slice(pair * 256, (pair + 1) * 256)
        shifted_rows = (
            jnp.concatenate([fs[:, (pair + 1) * 256:(pair + 2) * 256], fr[:, at]], axis=0),
            jnp.concatenate([cs[:, at], cr[:, at]], axis=0),
        )
        for here, rows, total in zip((dpre, hidden), shifted_rows, sums):
            here = jnp.concatenate([here[:, (pair - a) * 256:(pair - a + 1) * 256] for a in taps_here], axis=0)
            got = lax.dot_general(here, rows, over_lanes, preferred_element_type=F32)
            for n, a in enumerate(taps_here):
                part = got[n * 128:(n + 1) * 128]
                total[a] = part if total[a] is None else total[a] + part
    for a in range(3):
        g1, g2 = sums[0][a], sums[1][a]
        for b in range(3):
            for g, ys, out in ((g1, y1, ones), (g2, y2, twos)):
                total = jnp.zeros((CH, g.shape[1]), F32)
                for y in range(8):
                    total = jnp.where(ys[...] == float(y + 2 * (b - 1)), g[y * CH:(y + 1) * CH], total)
                out.append(total)
    taps[:, 24:] = jnp.zeros((3, 8, 128), F32)
    for parts, et, rep, at, width in ((ones, e1t, rep1, 0, 128), (twos[::-1], e2t, rep2, 1, 256)):
        sums = two_dots(jnp.concatenate(parts, axis=0), et[...])
        wide = two_dots(sums, rep[...])
        row = lax.broadcasted_iota(jnp.int32, wide.shape, 0) % CH
        lane = lax.broadcasted_iota(jnp.int32, wide.shape, 1) % width
        mine = row == (lane // CI if width == 128 else lane % CH)
        total = jnp.sum(jnp.where(mine, wide, 0.0).reshape(9, CH, 3 * width), axis=1)
        for c in range(3):
            first = c if width == 128 else 2 - c
            for n in range(width // 128):
                taps[at + n, pl.ds(first, 9, stride=3)] = total[:, c * width + n * 128:c * width + (n + 1) * 128]
    bias = jnp.sum(dpre.astype(F32), axis=1, keepdims=True)
    bias = sum(bias[y * CH:(y + 1) * CH] for y in range(8))
    row = lax.broadcasted_iota(jnp.int32, (CH, 128), 0)
    lane = lax.broadcasted_iota(jnp.int32, (CH, 128), 1)
    taps[0, 27:28] = jnp.sum(jnp.where(row == lane, bias, 0.0), axis=0, keepdims=True)
    payload[...] = rounded(jnp.concatenate([taps[n] for n in range(3)], axis=1))


def hidden_rim_kernel(counts, rfar, rnear, rfar_outer, rnear_outer, hidden, fs, t1o, t1d, b1, hidden_out, fr):
    count = hidden.shape[0]
    stream, radial = lax.axis_index("stream"), lax.axis_index("radial")
    for p in range(count + 8):
        end = p if p < 2 else p - count - 4 if p >= count + 6 else None
        if end is None:
            near, outer = (rnear, rfar, (p - 2) * 16), (rnear_outer, rfar_outer, 128 + (p - 2) * 16)
        else:
            near, outer = (rnear_outer, rfar_outer, end * 16), (rnear_outer, rfar_outer, 64 + end * 16)
        parts = [sides(radial, counts[1], n[at:at + 16], f[at:at + 16]) for n, f, at in (near, outer)]
        rows = jnp.concatenate([part[side] for side in range(2) for part in parts], axis=0)
        for n, piece in enumerate(shifted(rows)):
            fr[n * 64:(n + 1) * 64, p * Z:(p + 1) * Z] = piece
    fr[192:] = jnp.zeros((64, fr.shape[1]), BF16)

    def gelu(rows, lanes):
        total = b1[rows, :1]
        for t, ref in ((t1o, fs), (t1d, fr)):
            cells = [jnp.concatenate([ref[:, a * 256 + at:a * 256 + at + size] for at, size in lanes], axis=1) for a in range(3)]
            total = total + jnp.dot(t[rows], jnp.concatenate(cells, axis=0), preferred_element_type=F32)
        return total * gelu_share(total)

    own = gelu(slice(0, 128), ((0, 2 * Z), ((count + 2) * Z, 2 * Z)))
    rims = gelu(slice(128, 192), ((0, (count + 4) * Z),))
    rims = jnp.concatenate([jnp.where(radial > 0, rims[:32], 0.0), jnp.where(radial < counts[1] - 1, rims[32:], 0.0)], axis=0)
    for p in range(count + 4):
        rim_rows = rims[:, p * Z:(p + 1) * Z]
        if 2 <= p < count + 2:
            hidden_out[p, :128] = hidden[p - 2]
            hidden_out[p, 128:] = rim_rows.astype(BF16)
        else:
            at = p if p < 2 else p - count
            inside = stream > 0 if p < 2 else stream < counts[0] - 1
            rows = jnp.concatenate([own[:, at * Z:(at + 1) * Z], rim_rows], axis=0)
            hidden_out[p] = jnp.where(inside, rows, 0.0).astype(BF16)


def closure_kernel(hidden, t2, b2, closure, hs):
    count = closure.shape[2]
    for p in range(count + 4):
        store_wide(hs, p, hidden[p].astype(F32))
    out = (jnp.dot(t2[...], stacked(hs, count * Z), preferred_element_type=F32) + b2[:, :1]).astype(BF16)
    for x in range(count):
        closure[0, :, x] = out[:, x * Z:(x + 1) * Z].reshape(CH, 8, Z)


def summed(parts):
    parts = [part[...].astype(F32) for part in parts]
    while len(parts) > 1:
        parts = [v + w for v, w in zip(parts[::2], parts[1::2])]
    return parts[0]


def add_kernel(*refs):
    refs[-1][...] = rounded(summed(refs[:-1]))


def finish_kernel(norm, *refs):
    *parts, first, second, bias = refs
    scaled = summed(parts) * norm
    flipped = jnp.transpose(scaled)
    first[...] = flipped[:128, :27]
    second[...] = flipped[128:, :27]
    bias[...] = scaled[27:28, :CH] + scaled[28:29, :CH]


def call(kernel, outs, name, scratch=(), flops=10_000_000, **specs):
    return pl.pallas_call(
        kernel,
        out_shape=outs,
        **specs,
        scratch_shapes=list(scratch),
        compiler_params=pltpu.CompilerParams(vmem_limit_bytes=32 * 1024 * 1024),
        cost_estimate=pl.CostEstimate(flops=flops, bytes_accessed=1_000_000, transcendentals=0),
        name=name,
    )


def shape(*dims, dtype=BF16):
    return jax.ShapeDtypeStruct(dims, dtype)


def exchange(near, far, axis, other):
    count, others = lax.axis_size(axis), lax.axis_size(other)
    axes = tuple(name for name in ("stream", "radial", "snap") if name in (axis, other))
    flat = (others, 1) if axes[0] == axis else (1, count)
    pairs = []
    for i in range(count):
        for j in range(others):
            end = i in (0, count - 1)
            to = (i, j ^ 1 if others % 2 == 0 else j) if end else (i - 1 + 2 * (i % 2), j)
            pairs.append((i * flat[0] + j * flat[1], to[0] * flat[0] + to[1] * flat[1]))
    far = lax.ppermute(far, axes, pairs)
    return lax.ppermute(near, axis, [(i, i ^ 1) for i in range(count)]), far


def swap(v, axis, masks):
    count = lax.axis_size(axis)
    return [lax.ppermute(v, axis, [(i, i ^ mask) for i in range(count)]) for mask in masks]


def stream_round(v):
    count, others = lax.axis_size("stream"), lax.axis_size("radial")
    pairs = [(i * others + j, (i ^ (2 + (j + 1) % 2)) * others + j) for i in range(count) for j in range(others)]
    apart = lax.ppermute(v, ("stream", "radial"), pairs)
    return [*swap(v, "stream", [1]), apart, *swap(apart, "radial", [1])]


def add(v, arrived):
    return call(add_kernel, shape(*v.shape), "add_parts")(v, *arrived)


def rounds(axis, most):
    found, step = [], 1
    while step < lax.axis_size(axis):
        masks = [step * n for n in range(1, most if step * most <= lax.axis_size(axis) else 2)]
        found.append((axis, masks))
        step *= len(masks) + 1
    return found


def local(fields, first_weight, first_bias, second_weight, second_bias, cotangent):
    e1t, y1 = table(CI, 384, ((natural, 0, 64), (rim(CI), 256, 32)))
    e2t, y2 = table(CH, 640, ((natural, 0, 128), (rim(CH), 384, 64)))
    rep1, rep2 = np.zeros((128, 384), np.float32), np.zeros((128, 768), np.float32)
    for c in range(3):
        rep1[c * CI:(c + 1) * CI, c * 128:(c + 1) * 128] = np.tile(np.eye(CI), (1, CH))
        rep2[c * CH:(c + 1) * CH, c * 256:(c + 1) * 256] = np.repeat(np.eye(CH), CH, axis=1)

    def const(*arrays, dtype=BF16):
        return [jnp.asarray(v, dtype) for v in arrays]

    planes = fields.shape[2]
    w1 = first_weight.transpose(1, 2, 0).reshape(CH * CI, 27)
    w2 = second_weight.transpose(1, 2, 0).reshape(CH * CH, 27)
    near, far, f_rows, c_rows = call(
        pack_kernel,
        (shape(512, Z), shape(512, Z), shape(planes, CI * 8, Z), shape(planes, CH * 8, Z)),
        "pack_strips",
        flops=4_000_000_000,
    )(jnp.concatenate([fields[0], cotangent[0]], axis=0))
    xnear, xfar = exchange(near, far, "stream", "radial")
    wide = (planes + 4) * Z
    counts = (lax.axis_size("stream"), lax.axis_size("radial"))
    t1o, t1r, t1d, tbo, tbr, t2, b1, b2 = call(
        band_kernel,
        (shape(192, 768), shape(128, 384), shape(192, 768), shape(128, 1152), shape(128, 768), shape(128, 1920),
         shape(192, 128, dtype=F32), shape(128, 128, dtype=F32)),
        "band_matrices",
        flops=4_000_000_000,
    )(w1, w2, first_bias[None], second_bias[None])
    near_own, far_own = call(own_strips_kernel, (shape(planes * 48, Z),) * 2, "own_strips")(f_rows, c_rows)
    xnear, xfar, t1o, tbo = lax.optimization_barrier((xnear, xfar, t1o, tbo))
    inner, outer = shape((planes + 4) * 48, Z), shape(128 + (planes + 4) * 16, Z)
    near, far = call(functools.partial(join_kernel, counts), (inner, inner), "join_strips")(xnear, xfar, near_own, far_own)
    rnear, rfar = exchange(near, far, "radial", "stream")
    half, half_f32 = shape(64, planes * Z), shape(64, planes * Z, dtype=F32)
    fs, cs, pre, back, hidden, dpre = call(
        functools.partial(own_kernel, counts),
        (shape(256, wide + 4 * Z), shape(384, wide), half_f32, half_f32, half, half),
        "own_rows",
        flops=1_000_000_000,
    )(xnear, xfar, f_rows, c_rows, t1o, tbo, b1)
    f_rows, fs = lax.optimization_barrier((f_rows, fs))
    near_outer, far_outer = call(functools.partial(join_outer_kernel, counts), (outer, outer), "join_outer")(
        xnear, xfar, f_rows, c_rows)
    rnear_outer, rfar_outer = exchange(near_outer, far_outer, "radial", "stream")
    hidden, payload = call(
        functools.partial(rim_kernel, counts),
        (shape(planes, 128, Z), shape(32, 384)),
        "gradients",
        (pltpu.VMEM((128, wide), BF16), pltpu.VMEM((256, wide), BF16), pltpu.VMEM((3, 32, 128), F32)),
        flops=2_000_000_000,
    )(rfar, rnear, fs, cs, pre, back, hidden, dpre, t1r, tbr, *const(e1t, e2t, rep1, rep2), *const(y1, y2, dtype=F32))

    steps = rounds("radial", 4) + rounds("stream", 4)[1:] + rounds("snap", 2)
    arrived = swap(payload, *steps[0])
    hidden = call(
        functools.partial(hidden_rim_kernel, counts),
        shape(planes + 4, 192, Z),
        "hidden_rim",
        (pltpu.VMEM((256, wide + 4 * Z), BF16),),
        flops=1_000_000_000,
    )(rfar, rnear, rfar_outer, rnear_outer, hidden, fs, t1o, t1d, b1)
    payload, hidden = lax.optimization_barrier((add(payload, arrived), hidden))
    payload = add(payload, stream_round(payload))
    arrived = swap(payload, *steps[1])
    closure = call(
        closure_kernel, shape(*cotangent.shape), "closure", (pltpu.VMEM((640, wide), BF16),), flops=1_000_000_000
    )(hidden, t2, b2)
    for step in steps[2:]:
        payload = add(payload, arrived)
        arrived = swap(payload, *step)

    cells = fields.shape[0] * fields.shape[2] * fields.shape[3] * fields.shape[4]
    for axis in ("stream", "radial", "snap"):
        cells *= lax.axis_size(axis)
    norm = float(1.0 / np.sqrt(np.float32(cells)))
    first, second, bias = call(
        functools.partial(finish_kernel, norm),
        (shape(CH * CI, 27, dtype=F32), shape(CH * CH, 27, dtype=F32), shape(1, CH, dtype=F32)),
        "finish",
    )(payload, *arrived)
    first = first.reshape(CH, CI, 27).transpose(2, 0, 1)
    second = second.reshape(CH, CH, 27).transpose(2, 0, 1)
    return (closure, first, second, bias[0])


def solution(mesh):
    split = P("snap", None, "stream", "radial", None)
    return jax.shard_map(
        local,
        mesh=mesh,
        in_specs=(split, P(), P(), P(), P(), split),
        out_specs=(split, P(), P(), P()),
        check_vma=False,
    )
```
